32 devices in a mesh: grp: 2 (over y), lsec: 4 (over z), mpo: 2 (over x), rsec: 2 (over core).
Axes of the slice: x: 2, y: 2, z: 4, core: 2. Of those that a mesh axis runs over, the one named last changes fastest.
Arguments:
- wavefunction: float32 [16, 384, 256], P(('grp', 'lsec'), None, 'rsec'), parts along dimension 0, may hold values from -6 to 6
- left_env: float32 [40, 16, 384, 384], P('mpo', ('grp', 'lsec')), parts along dimension 1, may hold values from -0.3125 to 0.3125
- right_env: float32 [40, 16, 256, 256], P('mpo', ('grp', 'lsec'), 'rsec'), parts along dimension 1, may hold values from -0.0625 to 0.0625
- precond_diag: float32 [16, 384, 256], P(('grp', 'lsec'), None, 'rsec'), parts along dimension 0, may hold values from -2 to 6
- down_charge: int32 [16], P('grp'), parts along dimension 0, may hold values from 0 to 2, as said below
- bond_mask: int32 [40, 16], P('mpo', ('grp', 'lsec')), parts along dimension 1, may hold values 0 or 1
- left_size: int32 [16], P(('grp', 'lsec')), parts along dimension 0, may hold values from 1 to 384, 1536 in all
- right_size: int32 [16], P(('grp', 'lsec')), parts along dimension 0, may hold values from 1 to 256, 1024 in all
Outputs:
- basis: float32 [3, 16, 384, 256], P(None, ('grp', 'lsec'), None, 'rsec'), parts along dimension 1
- images: float32 [3, 16, 384, 256], P(None, ('grp', 'lsec'), None, 'rsec'), parts along dimension 1
- projected: float32 [6, 3], P('grp'), parts along dimension 0
The draws below stay inside these ranges and needn't reach their ends.
There are 2 independent parts, one for each index of `grp`. The reference program is written for one: setup_inputs(seed, part) draws one part's arguments, and reference() takes and returns one part's arrays. A program takes and returns all parts, laid end to end along the dimension named above; each array names one. Nothing has to cross between parts.
Inputs may be any that keep to these rules, and one draw needn't show every extreme that they name: `down_charge`: index i of lsec holds sectors 2 * i to 2 * i + 1; their down-spin charges are 2 distinct values. `left_size`: the sizes sum to 1536. `right_size`: the sizes sum to 1024.
All inputs are finite; a program needn't handle non-finite values. No bound on the sum of `bond_mask` or of `left_size` or of `right_size` on one device may be relied on, other than what follows from the above.
Results may differ from the reference program's by a relative error of at most 0.00011.
Values sent between devices are 32-bit elements; how exact they have to be, the bound alone decides.
No kernel may reach another device: no remote copies, remote signals or barrier semaphores. Data moves between devices by JAX's collectives and lax.ppermute only.
A program may use at most 128 MiB of HBM per device.

```python
import math
import jax
import jax.numpy as jnp
import numpy as np
from jax import lax

W = 40
CAP = 384
CAPR = 256
SEC_DEV = 2
MATVECS = 3
SEC = 8


def draw_down_charge(key, part):
    key = jax.random.fold_in(key, 11)
    row_keys = jax.random.split(key, SEC // SEC_DEV)
    orders = jax.vmap(lambda row_key: jax.random.permutation(row_key, SEC_DEV + 1))(row_keys)
    orders = orders[:, :SEC_DEV].astype(jnp.int32)
    first_key = jax.random.fold_in(key, 101)
    second_key = jax.random.fold_in(key, 202)
    lower_row = jax.random.permutation(first_key, SEC_DEV).astype(jnp.int32)
    upper_row = jax.random.permutation(second_key, SEC_DEV).astype(jnp.int32) + 1
    orders = orders.at[0].set(lower_row)
    orders = orders.at[1].set(upper_row)
    return orders.reshape(SEC).astype(jnp.int32)


def place_ends(values, key, smallest, largest):
    extent = values.shape
    spot = [jax.random.randint(jax.random.fold_in(key, axis), (), 0, extent[axis]) for axis in range(len(extent))]
    values = values.at[tuple(spot)].set(smallest)
    longest = extent.index(max(extent))
    spot[longest] = (spot[longest] + 1) % extent[longest]
    return values.at[tuple(spot)].set(largest)


def steps_of(stream_key, extent, cuts, smallest, largest):
    gain = 1.0
    for dim, shards_of in cuts:
        heights = jax.random.uniform(jax.random.fold_in(jax.random.fold_in(stream_key, 6), dim), (shards_of,), jnp.float32, smallest / len(cuts), largest / len(cuts))
        gain = gain * jnp.repeat(jnp.exp(heights), extent[dim] // shards_of).reshape((-1,) + (1,) * (len(extent) - 1 - dim))
    return gain


def split_up(amount, total, reach, skew):
    loads = [(1 << 20) // math.isqrt(rank ** skew) + 1 for rank in range(2, amount + 1)]
    surplus, given = total - reach - (amount - 1), [1] * (amount - 1)
    while surplus > 0:
        candidates = [i for i in range(amount - 1) if given[i] < reach]
        mass, remaining = sum([loads[i] for i in candidates]), surplus
        for i in candidates:
            more = min(reach - given[i], max(1, remaining * loads[i] // mass), surplus)
            given[i] = given[i] + more
            surplus = surplus - more
    return np.array([reach] + given)


def ragged_sizes(own_key, amount, total, most, skew):
    if amount == 2:
        one = jax.random.randint(own_key, (), max(1, total - most), min(most, total - 1) + 1)
        return jnp.stack([one, total - one])
    lengths = jnp.asarray(split_up(amount, total, most, skew), jnp.int32)
    couples = (amount - 1) // 2
    donor, receiver = lengths[1:1 + 2 * couples:2], lengths[2:2 + 2 * couples:2]
    margin = jnp.minimum(donor - 1, most - receiver)
    moved = jax.random.randint(jax.random.fold_in(own_key, 1), (couples,), 0, 1 << 20) % (margin + 1)
    lengths = lengths.at[1:1 + 2 * couples:2].set(donor - moved).at[2:2 + 2 * couples:2].set(receiver + moved)
    return lengths[jax.random.permutation(jax.random.fold_in(own_key, 2), amount)]


def noise(stream_key, shape, deviation, bound, pieces=(), kind=jnp.bfloat16):
    entries = deviation * jax.random.normal(stream_key, shape, jnp.float32)
    if pieces:
        entries = entries * steps_of(stream_key, shape, pieces, -0.22, 0.18)
    return jnp.clip(entries, -bound, bound).astype(kind)


def setup_inputs(seed: int = 0, part: int = 0) -> dict:
    splits = jax.random.split(jax.random.key(seed), 9)
    part_keys = jax.random.split(jax.random.fold_in(splits[8], part), 9)
    wavefunction = noise(part_keys[0], (SEC, CAP, CAPR), 1.0, 6.0, ((0, 4), (2, 2)), jnp.float32)
    left_env = noise(part_keys[1], (W, SEC, CAP, CAP), CAP ** -0.5, 0.3125, ((0, 2), (1, 4)), jnp.float32)
    right_env = noise(part_keys[2], (W, SEC, CAPR, CAPR), (CAPR * W) ** -0.5, 0.0625, ((0, 2), (1, 4), (2, 2)), jnp.float32)
    precond_diag = jnp.clip(-2.0 + 8.0 * jax.random.uniform(part_keys[3], (SEC, CAP, CAPR), jnp.float32) ** steps_of(part_keys[3], (SEC, CAP, CAPR), ((0, 4), (2, 2)), -0.2, 0.2), -2.0, 6.0)
    down_charge = draw_down_charge(jax.random.fold_in(jax.random.fold_in(splits[8], part), 71), part)
    bond_mask = place_ends((jax.random.randint(part_keys[5], (W, SEC), 0, 4) < 3).astype(jnp.int32), jax.random.fold_in(part_keys[5], 1), 0, 1)
    left_size = ragged_sizes(part_keys[6], SEC, SEC * CAP // 2, CAP, 2).astype(jnp.int32)
    right_size = ragged_sizes(part_keys[7], SEC, SEC * CAPR // 2, CAPR, 2).astype(jnp.int32)
    return dict(wavefunction=wavefunction, left_env=left_env, right_env=right_env, precond_diag=precond_diag, down_charge=down_charge, bond_mask=bond_mask, left_size=left_size, right_size=right_size)


EPSILON = 1e-06
HIGHEST = lax.Precision.HIGHEST

def bond_shifts(bond_ids):
    op_class = bond_ids % 5
    shift_up = (op_class == 1).astype(jnp.int32) - (op_class == 2).astype(jnp.int32)
    shift_down = (op_class == 3).astype(jnp.int32) - (op_class == 4).astype(jnp.int32)
    return (shift_up, shift_down)

def reference(wavefunction, left_env, right_env, precond_diag, down_charge, bond_mask, left_size, right_size):
    cell_count = float(SEC * CAP * CAPR)
    row_ids = jnp.arange(CAP, dtype=jnp.int32)
    col_ids = jnp.arange(CAPR, dtype=jnp.int32)
    live_mask = ((row_ids[None, :, None] < left_size[:, None, None]) & (col_ids[None, None, :] < right_size[:, None, None])).astype(jnp.float32)
    sector_ids = jnp.arange(SEC, dtype=jnp.int32)
    up_charge = sector_ids // SEC_DEV
    shift_up, shift_down = bond_shifts(jnp.arange(W, dtype=jnp.int32))
    wanted_up = up_charge[None, :] - shift_up[:, None]
    wanted_down = down_charge[None, :] - shift_down[:, None]
    matches = (up_charge[None, None, :] == wanted_up[:, :, None]) & (down_charge[None, None, :] == wanted_down[:, :, None])
    source = lax.optimization_barrier(jnp.sum(jnp.where(matches, sector_ids[None, None, :], 0), axis=2)).astype(jnp.int32)
    coupling = (jnp.any(matches, axis=2) & (bond_mask > 0)).astype(jnp.float32)

    def apply_operator(operand):

        def one_target(target):
            blocks = operand[source[:, target]]
            inner_block = jnp.einsum('bxr,byr->bxy', blocks, right_env[:, target], precision=HIGHEST)
            weighted = left_env[:, target] * coupling[:, target][:, None, None]
            summed = jnp.einsum('bzx,bxy->zy', weighted, inner_block, precision=HIGHEST)
            return summed * live_mask[target]
        return lax.map(one_target, sector_ids)

    def inner_product(first, second):
        return jnp.sum(first * second) / cell_count
    initial = live_mask * wavefunction
    basis_list = [initial / jnp.sqrt(inner_product(initial, initial) + EPSILON)]
    images = []
    for iteration in range(MATVECS):
        product = apply_operator(basis_list[iteration])
        images.append(product)
        if iteration + 1 < MATVECS:
            rayleigh = inner_product(basis_list[iteration], product)
            correction = (product - rayleigh * basis_list[iteration]) / jnp.maximum(precond_diag - rayleigh, 1.0)
            correlations = [inner_product(member, correction) for member in basis_list]
            for member, correlation in zip(basis_list, correlations):
                correction = correction - correlation * member
            basis_list.append(correction / jnp.sqrt(inner_product(correction, correction) + EPSILON))
    projected = jnp.stack([jnp.stack([inner_product(member, product) for product in images]) for member in basis_list])
    return (jnp.stack(basis_list), jnp.stack(images), projected)
```

```python
import functools

import jax
import jax.numpy as jnp
from jax import lax
from jax.experimental import pallas as pl
from jax.experimental.pallas import tpu as pltpu
from jax.sharding import PartitionSpec as P

EPSILON = 1e-06
MATVECS = 3
F32 = jnp.float32
BF16 = jnp.bfloat16
SIGMA, COUNT, ROWS, COLS, LIST = 0, 1, 2, 3, 8
OWN, SIB, PREV, NEXT = 0, 1, 2, 3
CHUNK = 64
TILE = 128
BUFFERS = 3


def whole_vmem():
    return pl.BlockSpec(memory_space=pltpu.VMEM)


def whole_smem():
    return pl.BlockSpec(memory_space=pltpu.SMEM)


def split(value):
    high = value.astype(BF16)
    return high, (value - high.astype(F32)).astype(BF16)


def orientation(down_ref, place):
    def step(i, flips):
        straight = (down_ref[2 * i] == down_ref[2 * i - 2]) | (
            down_ref[2 * i + 1] == down_ref[2 * i - 1]
        )
        return jnp.where(straight, flips, 1 - flips)

    return lax.fori_loop(1, place + 1, step, jnp.int32(0))


def live_mask(shape, row0, rows, cols):
    row_ids = row0 + lax.broadcasted_iota(jnp.int32, shape, 0)
    col_ids = lax.broadcasted_iota(jnp.int32, shape, 1)
    return (row_ids < rows) & (col_ids < cols)


def prep_kernel(lsec_count, bonds, down_ref, mask_ref, left_size_ref, right_size_ref, wave_ref,
                own_ref, sib_ref, meta_ref):
    place = lax.axis_index("lsec")
    core = lax.axis_index("rsec")
    first_bond = lax.axis_index("mpo") * bonds
    sigma = core ^ orientation(down_ref, place)
    own_down = down_ref[2 * place + sigma]
    sib_down = down_ref[2 * place + 1 - sigma]
    before = jnp.maximum(place - 1, 0)
    after = jnp.minimum(place + 1, lsec_count - 1)
    prev_down = down_ref[2 * before + (core ^ orientation(down_ref, before))]
    next_down = down_ref[2 * after + (core ^ orientation(down_ref, after))]
    has_prev = (place > 0) & (prev_down == own_down)
    has_next = (place < lsec_count - 1) & (next_down == own_down)
    has_lower = sib_down == own_down - 1
    has_upper = sib_down == own_down + 1

    def step(bond, count):
        kind = lax.rem(first_bond + bond, 5)
        slot = jnp.where(kind == 0, OWN, jnp.where(kind == 1, PREV, jnp.where(kind == 2, NEXT, SIB)))
        there = (
            (kind == 0)
            | ((kind == 1) & has_prev)
            | ((kind == 2) & has_next)
            | ((kind == 3) & has_lower)
            | ((kind == 4) & has_upper)
        ) & (mask_ref[bond, sigma] > 0)

        @pl.when(there)
        def _():
            meta_ref[LIST + count] = bond * 4 + slot

        return count + there.astype(jnp.int32)

    count = lax.fori_loop(0, bonds, step, jnp.int32(0))
    rows, cols = left_size_ref[sigma], right_size_ref[sigma]
    meta_ref[SIGMA] = sigma
    meta_ref[COUNT] = count
    meta_ref[ROWS] = rows
    meta_ref[COLS] = cols
    states, width = own_ref.shape
    for ref, slot in ((own_ref, sigma), (sib_ref, 1 - sigma)):

        def mask_rows(i, carry, ref=ref, slot=slot):
            at = pl.ds(pl.multiple_of(i * CHUNK, CHUNK), CHUNK)
            mask = live_mask((CHUNK, width), i * CHUNK, left_size_ref[slot], right_size_ref[slot])
            ref[at, :] = jnp.where(mask, wave_ref[slot, at, :], 0.0)
            return carry

        lax.fori_loop(0, states // CHUNK, mask_rows, 0)


def row(value, index):
    return value[index : index + 1, :]


class Scalars:
    def __init__(self, totals, cells):
        self.proj = {}
        self.gram = {}
        self.norm = []
        self.corr = []
        for k, total in enumerate(totals):
            value = total / cells
            size, inner = row(value, 0), row(value, 1)
            a = [row(value, 2 + j) for j in range(k)]
            e = [row(value, 4 + j) for j in range(k)]
            f = [row(value, 6 + j) for j in range(k)]
            length = size
            theta = inner
            for j in range(k):
                length = length - 2.0 * a[j] * a[j]
                theta = theta - a[j] * e[j] - a[j] * f[j]
            for i in range(k):
                for j in range(k):
                    length = length + a[i] * a[j] * self.gram[i, j]
                    theta = theta + a[i] * a[j] * self.proj[i, j]
            length = jnp.maximum(length, 0.0)
            square = length + EPSILON
            norm = jnp.sqrt(square)
            for j in range(k):
                up, down, both = e[j], f[j], a[j]
                for i in range(k):
                    up = up - a[i] * self.proj[j, i]
                    down = down - a[i] * self.proj[i, j]
                    both = both - a[i] * self.gram[i, j]
                self.proj[j, k] = up / norm
                self.proj[k, j] = down / norm
                self.gram[j, k] = self.gram[k, j] = both / norm
            self.proj[k, k] = theta / square
            self.gram[k, k] = length / square
            self.norm.append(norm)
            self.corr.append(a)

    def basis(self, k, fields):
        done = []
        for step in range(k + 1):
            value = fields[step]
            for j in range(step):
                value = value - self.corr[step][j][:, :1] * done[j]
            done.append(value / self.norm[step][:, :1])
        return done


def matvec_kernel(k, cells, mpo_count, *refs):
    refs = list(refs)
    meta_ref, down_ref = refs.pop(0), None
    left_ref, right_ref, far_ref = refs.pop(0), refs.pop(0), refs.pop(0)
    sums = [[refs.pop(0) for _ in range(4)] for _ in range(1)] if k else []
    old_totals = [refs.pop(0) for _ in range(k - 1)] if k else []
    raw = [[refs.pop(0) for _ in range(4)] for _ in range(max(k, 1))]
    images = [[refs.pop(0) for _ in range(4)] for _ in range(k)]
    precond = [refs.pop(0) for _ in range(4)] if k else []
    out_ref, small_ref = refs.pop(0), refs.pop(0)
    total_ref = refs.pop(0) if k else None
    new_refs = [refs.pop(0) for _ in range(4)] if k else raw[0]
    (left_buf, right_buf, high_ref, low_ref, right_high, right_low, sems) = refs
    states, width = out_ref.shape
    half = right_ref.shape[2]
    sigma, count = meta_ref[SIGMA], meta_ref[COUNT]
    rows, cols = meta_ref[ROWS], meta_ref[COLS]
    core = lax.axis_index("rsec")

    def copies(i):
        bond = meta_ref[LIST + i] // 4
        at = lax.rem(i, BUFFERS)
        near = pl.ds(pl.multiple_of(core * half, half), half)
        away = pl.ds(pl.multiple_of((1 - core) * half, half), half)
        return (
            pltpu.make_async_copy(left_ref.at[bond, sigma], left_buf.at[at], sems.at[0, at]),
            pltpu.make_async_copy(right_ref.at[bond, sigma], right_buf.at[at, near], sems.at[1, at]),
            pltpu.make_async_copy(far_ref.at[bond], right_buf.at[at, away], sems.at[2, at]),
        )

    def start(i):
        @pl.when(i < count)
        def _():
            for copy in copies(i):
                copy.start()

    for i in range(BUFFERS - 1):
        start(jnp.int32(i))

    if k:
        own_sum, one, two, three = [ref[...] for ref in sums[0]]
        total = (own_sum + one) + (two + three)
        total_ref[...] = total
        numbers = Scalars([ref[...] for ref in old_totals] + [total], cells)
        theta = numbers.proj[k - 1, k - 1][:, :1]
    acc_shape = (8, width)

    def fold(value):
        return jnp.sum(value.reshape(CHUNK // 8, 8, width), axis=0)

    local = {}
    for slot in (SIB, PREV, NEXT, OWN):

        def prepare(i, carry, slot=slot):
            at = pl.ds(pl.multiple_of(i * CHUNK, CHUNK), CHUNK)
            if k:
                basis = numbers.basis(k - 1, [r[slot][at, :] for r in raw])
                image = numbers.basis(k - 1, [r[slot][at, :] for r in images])
                value = (image[-1] - theta * basis[-1]) / jnp.maximum(
                    precond[slot][at, :] - theta, 1.0
                )
                new_refs[slot][at, :] = value
            else:
                basis, image = [], []
                value = raw[0][slot][at, :]
            high, low = split(value)
            high_ref[slot, at, :] = high
            low_ref[slot, at, :] = low
            if slot != OWN:
                return carry
            terms = [value * value] + [value * b for b in basis] + [value * g for g in image]
            return tuple(c + fold(t) for c, t in zip(carry, terms))

        zero = jnp.zeros(acc_shape, F32)
        init = (zero,) * (1 + 2 * k) if slot == OWN else 0
        local[slot] = lax.fori_loop(0, states // CHUNK, prepare, init)
    own = local[OWN]

    def clear(i, carry):
        at = pl.ds(pl.multiple_of(i * CHUNK, CHUNK), CHUNK)
        out_ref[at, :] = jnp.zeros((CHUNK, width), F32)
        return carry

    lax.fori_loop(0, states // CHUNK, clear, 0)
    tiles = (rows + TILE - 1) // TILE

    def dot(a, b):
        return jnp.dot(a, b, preferred_element_type=F32)

    def dot_nt(a, b):
        return lax.dot_general(a, b, (((1,), (1,)), ((), ())), preferred_element_type=F32)

    def bond_step(i, carry):
        at = lax.rem(i, BUFFERS)
        slot = lax.rem(meta_ref[LIST + i], 4)
        start(i + BUFFERS - 1)
        for copy in copies(i):
            copy.wait()
        high, low = split(right_buf[at])
        right_high[...] = high
        right_low[...] = low

        def tile_step(t, inner):
            rows_at = pl.ds(pl.multiple_of(t * TILE, TILE), TILE)
            left_high, left_low = split(left_buf[at, rows_at, :])
            mid = (
                dot(left_high, low_ref[slot])
                + dot(left_low, high_ref[slot])
                + dot(left_high, high_ref[slot])
            )
            mid_high, mid_low = split(mid)
            out_ref[rows_at, :] += (
                dot_nt(mid_high, right_low[...])
                + dot_nt(mid_low, right_high[...])
                + dot_nt(mid_high, right_high[...])
            )
            return inner

        lax.fori_loop(0, tiles, tile_step, 0)
        return carry

    lax.fori_loop(0, count, bond_step, 0)

    def finish(i, carry):
        at = pl.ds(pl.multiple_of(i * CHUNK, CHUNK), CHUNK)
        mask = live_mask((CHUNK, width), i * CHUNK, rows, cols)
        value = jnp.where(mask, out_ref[at, :], 0.0)
        out_ref[at, :] = value
        basis = numbers.basis(k - 1, [r[OWN][at, :] for r in raw]) if k else []
        terms = [value * new_refs[OWN][at, :]] + [value * b for b in basis]
        return tuple(c + fold(t) for c, t in zip(carry, terms))

    zero = jnp.zeros(acc_shape, F32)
    late = lax.fori_loop(0, states // CHUNK, finish, (zero,) * (1 + k))

    def whole(value):
        return jnp.sum(jnp.sum(value, axis=1, keepdims=True), axis=0, keepdims=True)

    share = 1.0 / mpo_count
    entries = [whole(own[0]) * share, whole(late[0])]
    for j in range(2):
        entries.append(whole(own[1 + j]) * share if j < k else None)
    for j in range(2):
        entries.append(whole(late[1 + j]) if j < k else None)
    for j in range(2):
        entries.append(whole(own[1 + k + j]) * share if j < k else None)
    row_ids = lax.broadcasted_iota(jnp.int32, small_ref.shape, 0)
    small = jnp.zeros(small_ref.shape, F32)
    for index, entry in enumerate(entries):
        if entry is not None:
            small = jnp.where(row_ids == index, entry, small)
    small_ref[...] = small


def final_kernel(cells, meta_ref, s0, s1, s2, s3, t1, t2, *refs):
    raw = [refs[2 * i : 2 * i + 2] for i in range(MATVECS)]
    images = [refs[2 * (MATVECS + i) : 2 * (MATVECS + i) + 2] for i in range(MATVECS)]
    basis_ref, images_ref, projected_ref = refs[4 * MATVECS :]
    sigma = meta_ref[SIGMA]
    total = (s0[...] + s1[...]) + (s2[...] + s3[...])
    numbers = Scalars([t1[...], t2[...], total], cells)
    states, half = basis_ref.shape[2:]
    core = lax.axis_index("rsec")
    lanes = pl.ds(pl.multiple_of(core * half, half), half)
    for slot in (OWN, SIB):
        sector = sigma if slot == OWN else 1 - sigma

        def step(i, carry, slot=slot, sector=sector):
            at = pl.ds(pl.multiple_of(i * CHUNK, CHUNK), CHUNK)
            for fields, ref in ((raw, basis_ref), (images, images_ref)):
                done = numbers.basis(MATVECS - 1, [f[slot][at, lanes] for f in fields])
                for j, value in enumerate(done):
                    ref[j, sector, at, :] = value
            return carry

        lax.fori_loop(0, states // CHUNK, step, 0)
    shape = projected_ref.shape
    row_ids = lax.broadcasted_iota(jnp.int32, shape, 0)
    col_ids = lax.broadcasted_iota(jnp.int32, shape, 1)
    out = jnp.zeros(shape, F32)
    for i in range(MATVECS):
        for j in range(MATVECS):
            out = jnp.where((row_ids == i) & (col_ids == j), numbers.proj[i, j][:, :1], out)
    projected_ref[...] = out


def per_device(
    wavefunction, left_env, right_env, precond_diag, down_charge, bond_mask, left_size, right_size
):
    sectors, states, columns = wavefunction.shape
    bonds = left_env.shape[0]
    lsec_count = lax.axis_size("lsec")
    mpo_count = lax.axis_size("mpo")
    assert sectors == 2 and lax.axis_size("rsec") == 2
    width = 2 * columns
    cells = float(lsec_count * sectors * states * width)
    field = jax.ShapeDtypeStruct((states, width), F32)
    small = jax.ShapeDtypeStruct((8, 128), F32)
    params = pltpu.CompilerParams(vmem_limit_bytes=48 * 2**20)

    wave_all = lax.all_gather(wavefunction, "rsec", axis=2, tiled=True)
    own, sib, meta = pl.pallas_call(
        functools.partial(prep_kernel, lsec_count, bonds),
        out_shape=(field, field, jax.ShapeDtypeStruct((LIST + bonds,), jnp.int32)),
        in_specs=[whole_smem()] * 4 + [whole_vmem()],
        out_specs=(whole_vmem(), whole_vmem(), whole_smem()),
        compiler_params=params,
        name="prep",
    )(down_charge, bond_mask, left_size, right_size, wave_all)
    sigma = meta[SIGMA]

    up = [(i, i + 1) for i in range(lsec_count - 1)]
    down = [(i + 1, i) for i in range(lsec_count - 1)]
    swap = [(0, 1), (1, 0)]

    def neighbours(value):
        return lax.ppermute(value, "lsec", up), lax.ppermute(value, "lsec", down)

    raw = [(own, sib, *neighbours(own))]
    far_send = lax.dynamic_index_in_dim(right_env, 1 - sigma, 1, keepdims=False)
    far_right = lax.ppermute(far_send, "rsec", swap)
    precond_all = lax.all_gather(precond_diag, "rsec", axis=2, tiled=True)
    precond_own = lax.dynamic_index_in_dim(precond_all, sigma, 0, keepdims=False)
    precond_sib = lax.dynamic_index_in_dim(precond_all, 1 - sigma, 0, keepdims=False)
    precond = (precond_own, precond_sib, *neighbours(precond_own))

    def mpo_sum(value, part):
        if mpo_count != 2:
            return lax.psum(value, "mpo"), lax.psum(part, ("mpo", "rsec"))
        total = value + lax.ppermute(value, "mpo", swap)
        other = lax.ppermute(part, "mpo", swap)
        beside = lax.ppermute(part, "rsec", swap)
        cross = lax.ppermute(
            part, ("mpo", "rsec"), [(0, 3), (1, 2), (2, 1), (3, 0)]
        )
        return total, (part + other) + (beside + cross)

    def lsec_sums(part):
        if lsec_count != 4:
            zero = jnp.zeros_like(part)
            return lax.psum(part, "lsec"), zero, zero, zero
        return (part, *[lax.ppermute(part, "lsec", [(i, i ^ x) for i in range(4)]) for x in (1, 2, 3)])

    def matvec(k, inputs, in_specs):
        extra = 1 + 4 if k else 0
        out_shape = [field, small] + ([small] + [field] * 4 if k else [])
        return pl.pallas_call(
            functools.partial(matvec_kernel, k, cells, mpo_count),
            out_shape=tuple(out_shape),
            in_specs=[whole_smem()] + [pl.BlockSpec(memory_space=pl.ANY)] * 3
            + [whole_vmem()] * (len(inputs)),
            out_specs=tuple([whole_vmem()] * (2 + extra)),
            scratch_shapes=[
                pltpu.VMEM((BUFFERS, states, states), F32),
                pltpu.VMEM((BUFFERS, width, width), F32),
                pltpu.VMEM((4, states, width), BF16),
                pltpu.VMEM((4, states, width), BF16),
                pltpu.VMEM((width, width), BF16),
                pltpu.VMEM((width, width), BF16),
                pltpu.SemaphoreType.DMA((3, BUFFERS)),
            ],
            compiler_params=params,
            name=f"matvec{k}",
        )(meta, left_env, right_env, far_right, *inputs)

    totals = []
    images = []
    for k in range(MATVECS):
        if k == 0:
            value, part = matvec(0, list(raw[0]), None)
        else:
            flat_raw = [x for group in raw for x in group]
            flat_images = [x for group in images for x in group]
            value, part, total, *fresh = matvec(
                k, [*sums, *totals, *flat_raw, *flat_images, *precond], None
            )
            totals.append(total)
            raw.append(tuple(fresh))
        value, part = mpo_sum(value, part)
        sums = lsec_sums(part)
        beside = lax.ppermute(value, "rsec", swap)
        if k + 1 < MATVECS:
            images.append((value, beside, *neighbours(value)))
        else:
            images.append((value, beside))

    flat = [x for group in raw for x in group[:2]] + [x for group in images for x in group[:2]]
    out = jax.ShapeDtypeStruct((MATVECS, sectors, states, columns), F32)
    return pl.pallas_call(
        functools.partial(final_kernel, cells),
        out_shape=(out, out, jax.ShapeDtypeStruct((MATVECS, MATVECS), F32)),
        in_specs=[whole_smem()] + [whole_vmem()] * (6 + len(flat)),
        out_specs=(whole_vmem(),) * 3,
        compiler_params=params,
        name="final",
    )(meta, *sums, *totals, *flat)


def solution(mesh):
    placed = (
        P(("grp", "lsec"), None, "rsec"),
        P("mpo", ("grp", "lsec"), None, None),
        P("mpo", ("grp", "lsec"), "rsec", None),
        P(("grp", "lsec"), None, "rsec"),
        P("grp"),
        P("mpo", ("grp", "lsec")),
        P(("grp", "lsec")),
        P(("grp", "lsec")),
    )
    return jax.shard_map(
        per_device,
        mesh=mesh,
        in_specs=placed,
        out_specs=(
            P(None, ("grp", "lsec"), None, "rsec"),
            P(None, ("grp", "lsec"), None, "rsec"),
            P("grp", None),
        ),
        check_vma=False,
    )
```

```python
import functools

import jax
import jax.numpy as jnp
from jax import lax
from jax.experimental import pallas as pl
from jax.experimental.pallas import tpu as pltpu
from jax.sharding import PartitionSpec as P

EPSILON = 1e-06
MATVECS = 3
F32 = jnp.float32
BF16 = jnp.bfloat16
SIGMA, COUNT, ROWS, COLS, FIRST, LIST = 0, 1, 2, 3, 4, 16
OWN, SIB, PREV, NEXT = 0, 1, 2, 3
CHUNK = 64
TILE = 128
PACK = 256
BUFFERS = 4


def whole_vmem():
    return pl.BlockSpec(memory_space=pltpu.VMEM)


def whole_smem():
    return pl.BlockSpec(memory_space=pltpu.SMEM)


def split(value):
    high = value.astype(BF16)
    return high, (value - high.astype(F32)).astype(BF16)


def orientation(down_ref, place):
    def step(i, flips):
        straight = (down_ref[2 * i] == down_ref[2 * i - 2]) | (
            down_ref[2 * i + 1] == down_ref[2 * i - 1]
        )
        return jnp.where(straight, flips, 1 - flips)

    return lax.fori_loop(1, place + 1, step, jnp.int32(0))


def live_mask(shape, row0, rows, cols):
    row_ids = row0 + lax.broadcasted_iota(jnp.int32, shape, 0)
    col_ids = lax.broadcasted_iota(jnp.int32, shape, 1)
    return (row_ids < rows) & (col_ids < cols)


def prep_kernel(lsec_count, bonds, down_ref, mask_ref, left_size_ref, right_size_ref, wave_ref,
                own_ref, sib_ref, meta_ref):
    place = lax.axis_index("lsec")
    core = lax.axis_index("rsec")
    first_bond = lax.axis_index("mpo") * bonds
    sigma = core ^ orientation(down_ref, place)
    own_down = down_ref[2 * place + sigma]
    sib_down = down_ref[2 * place + 1 - sigma]
    before = jnp.maximum(place - 1, 0)
    after = jnp.minimum(place + 1, lsec_count - 1)
    prev_down = down_ref[2 * before + (core ^ orientation(down_ref, before))]
    next_down = down_ref[2 * after + (core ^ orientation(down_ref, after))]
    has_prev = (place > 0) & (prev_down == own_down)
    has_next = (place < lsec_count - 1) & (next_down == own_down)
    has_lower = sib_down == own_down - 1
    has_upper = sib_down == own_down + 1

    def gather(slot, count):
        meta_ref[FIRST + slot] = count

        def step(bond, count):
            kind = lax.rem(first_bond + bond, 5)
            if slot == OWN:
                there = kind == 0
            elif slot == PREV:
                there = (kind == 1) & has_prev
            elif slot == NEXT:
                there = (kind == 2) & has_next
            else:
                there = ((kind == 3) & has_lower) | ((kind == 4) & has_upper)
            there = there & (mask_ref[bond, sigma] > 0)

            @pl.when(there)
            def _():
                meta_ref[LIST + count] = bond * 4 + slot

            return count + there.astype(jnp.int32)

        return lax.fori_loop(0, bonds, step, count)

    count = jnp.int32(0)
    for slot in (OWN, SIB, PREV, NEXT):
        count = gather(slot, count)
    meta_ref[FIRST + 4] = count
    rows, cols = left_size_ref[sigma], right_size_ref[sigma]
    meta_ref[SIGMA] = sigma
    meta_ref[COUNT] = count
    meta_ref[ROWS] = rows
    meta_ref[COLS] = cols
    states, width = own_ref.shape
    for ref, slot in ((own_ref, sigma), (sib_ref, 1 - sigma)):

        def mask_rows(i, carry, ref=ref, slot=slot):
            at = pl.ds(pl.multiple_of(i * CHUNK, CHUNK), CHUNK)
            mask = live_mask((CHUNK, width), i * CHUNK, left_size_ref[slot], right_size_ref[slot])
            ref[at, :] = jnp.where(mask, wave_ref[slot, at, :], 0.0)
            return carry

        lax.fori_loop(0, states // CHUNK, mask_rows, 0)


def row(value, index):
    return value[index : index + 1, :]


class Scalars:
    def __init__(self, totals, cells):
        self.proj = {}
        self.gram = {}
        self.norm = []
        self.corr = []
        for k, total in enumerate(totals):
            value = total / cells
            size, inner = row(value, 0), row(value, 1)
            a = [row(value, 2 + j) for j in range(k)]
            e = [row(value, 4 + j) for j in range(k)]
            f = [row(value, 6 + j) for j in range(k)]
            length = size
            theta = inner
            for j in range(k):
                length = length - 2.0 * a[j] * a[j]
                theta = theta - a[j] * e[j] - a[j] * f[j]
            for i in range(k):
                for j in range(k):
                    length = length + a[i] * a[j] * self.gram[i, j]
                    theta = theta + a[i] * a[j] * self.proj[i, j]
            length = jnp.maximum(length, 0.0)
            square = length + EPSILON
            norm = jnp.sqrt(square)
            for j in range(k):
                up, down, both = e[j], f[j], a[j]
                for i in range(k):
                    up = up - a[i] * self.proj[j, i]
                    down = down - a[i] * self.proj[i, j]
                    both = both - a[i] * self.gram[i, j]
                self.proj[j, k] = up / norm
                self.proj[k, j] = down / norm
                self.gram[j, k] = self.gram[k, j] = both / norm
            self.proj[k, k] = theta / square
            self.gram[k, k] = length / square
            self.norm.append(norm)
            self.corr.append(a)

    def basis(self, k, fields):
        done = []
        for step in range(k + 1):
            value = fields[step]
            for j in range(step):
                value = value - self.corr[step][j][:, :1] * done[j]
            done.append(value / self.norm[step][:, :1])
        return done


def load_kernel(meta_ref, left_ref, right_ref, far_ref, left_high, left_low, right_high, right_low,
                left_buf, right_buf, sems):
    states, width = left_buf.shape[1], right_buf.shape[1]
    half = right_ref.shape[2]
    sigma, count, rows = meta_ref[SIGMA], meta_ref[COUNT], meta_ref[ROWS]
    stride = packed_rows(rows)
    core = lax.axis_index("rsec")

    def pieces(i):
        bond = meta_ref[LIST + i] // 4
        at = lax.rem(i, BUFFERS)
        near = pl.ds(pl.multiple_of(core * half, half), half)
        away = pl.ds(pl.multiple_of((1 - core) * half, half), half)
        yield None, pltpu.make_async_copy(
            right_ref.at[bond, sigma], right_buf.at[at, near], sems.at[0, at]
        )
        yield None, pltpu.make_async_copy(far_ref.at[bond], right_buf.at[at, away], sems.at[1, at])
        for p in range(states // TILE):
            part = pl.ds(p * TILE, TILE)
            yield p * TILE, pltpu.make_async_copy(
                left_ref.at[bond, sigma, part], left_buf.at[at, part], sems.at[2 + p, at]
            )

    def each(i, act):
        for least, copy in pieces(i):
            if not least:
                act(copy)
            else:
                pl.when(rows > least)(functools.partial(act, copy))

    def start(i):
        @pl.when(i < count)
        def _():
            each(i, lambda copy: copy.start())

    for i in range(BUFFERS - 1):
        start(jnp.int32(i))

    def step(i, carry):
        at = lax.rem(i, BUFFERS)
        start(i + BUFFERS - 1)
        each(i, lambda copy: copy.wait())
        high, low = split(right_buf[at].T)
        right_high[i] = high
        right_low[i] = low

        def chunk(t, inner):
            high, low = split(left_buf[at, pl.ds(pl.multiple_of(t * CHUNK, CHUNK), CHUNK), :])
            to = pl.ds(pl.multiple_of(i * stride + t * CHUNK, 16), CHUNK)
            left_high[to, :] = high
            left_low[to, :] = low
            return inner

        lax.fori_loop(0, (rows + CHUNK - 1) // CHUNK, chunk, 0)
        return carry

    lax.fori_loop(0, count, step, 0)


def packed_rows(rows):
    return ((rows + 15) // 16) * 16


def matvec_kernel(k, cells, mpo_count, *refs):
    refs = list(refs)
    meta_ref = refs.pop(0)
    left_high, left_low, right_high, right_low = [refs.pop(0) for _ in range(4)]
    sums = [refs.pop(0) for _ in range(4)] if k else []
    old_totals = [refs.pop(0) for _ in range(k - 1)] if k else []
    raw = [[refs.pop(0) for _ in range(4)] for _ in range(max(k, 1))]
    images = [[refs.pop(0) for _ in range(4)] for _ in range(k)]
    precond = [refs.pop(0) for _ in range(4)] if k else []
    out_ref, small_ref = refs.pop(0), refs.pop(0)
    total_ref = refs.pop(0) if k else None
    new_refs = [refs.pop(0) for _ in range(4)] if k else raw[0]
    high_ref, low_ref, mid_high, mid_low = refs
    states, width = out_ref.shape
    count, rows, cols = meta_ref[COUNT], meta_ref[ROWS], meta_ref[COLS]
    stride = packed_rows(rows)

    if k:
        own_sum, one, two, three = [ref[...] for ref in sums]
        total = (own_sum + one) + (two + three)
        total_ref[...] = total
        numbers = Scalars([ref[...] for ref in old_totals] + [total], cells)
        theta = numbers.proj[k - 1, k - 1][:, :1]
    zero = jnp.zeros((8, width), F32)

    def fold(value):
        return jnp.sum(value.reshape(CHUNK // 8, 8, width), axis=0)

    def prepare(slot, first, last, carry):
        def step(i, carry):
            at = pl.ds(pl.multiple_of(i * CHUNK, CHUNK), CHUNK)
            if k:
                basis = numbers.basis(k - 1, [r[slot][at, :] for r in raw])
                image = numbers.basis(k - 1, [r[slot][at, :] for r in images])
                value = (image[-1] - theta * basis[-1]) / jnp.maximum(
                    precond[slot][at, :] - theta, 1.0
                )
                new_refs[slot][at, :] = value
            else:
                basis, image = [], []
                value = raw[0][slot][at, :]
            high, low = split(value)
            high_ref[slot, at, :] = high
            low_ref[slot, at, :] = low
            terms = [value * value]
            if slot == OWN:
                terms += [value * b for b in basis] + [value * g for g in image]
            return tuple(c + fold(t) for c, t in zip(carry, terms))

        return lax.fori_loop(first, last, step, carry)

    def dot(a, b):
        return jnp.dot(a, b, preferred_element_type=F32)

    def first_stage(slot, depth):
        begin, end = meta_ref[FIRST + slot], meta_ref[FIRST + 1 + slot]
        tiles = ((end - begin) * stride + PACK - 1) // PACK
        deep = pl.ds(0, depth)

        def step(t, carry):
            at = pl.ds(pl.multiple_of(begin * stride + t * PACK, 16), PACK)
            high, low = left_high[at, deep], left_low[at, deep]
            p_high, p_low = high_ref[slot, deep, :], low_ref[slot, deep, :]
            mid = dot(high, p_low) + dot(low, p_high) + dot(high, p_high)
            mid_high[at, :], mid_low[at, :] = split(mid)
            return carry

        lax.fori_loop(0, tiles, step, 0)

    shallow = min(256, states)
    for slot in (OWN, SIB, PREV, NEXT):

        def work(slot=slot):
            init = (zero,) * (1 + 2 * k if slot == OWN else 1)
            upper = prepare(slot, 0, shallow // CHUNK, init)
            lower = prepare(slot, shallow // CHUNK, states // CHUNK, init)
            deep = jnp.max(lower[0]) > 0.0
            pl.when(deep)(lambda: first_stage(slot, states))
            pl.when(jnp.logical_not(deep))(lambda: first_stage(slot, shallow))
            return [u + l for u, l in zip(upper, lower)]

        if slot == OWN:
            own = work()
        else:
            used = meta_ref[FIRST + 1 + slot] > meta_ref[FIRST + slot]
            pl.when(used | (slot == SIB))(lambda: (work(), None)[1])

    def clear(i, carry):
        at = pl.ds(pl.multiple_of(i * CHUNK, CHUNK), CHUNK)
        out_ref[at, :] = jnp.zeros((CHUNK, width), F32)
        return carry

    lax.fori_loop(0, states // CHUNK, clear, 0)

    def second_stage(size):
        def step(i, carry):
            at = pl.ds(pl.multiple_of(i * stride, 16), size)
            out_ref[pl.ds(0, size), :] += (
                dot(mid_high[at, :], right_low[i])
                + dot(mid_low[at, :], right_high[i])
                + dot(mid_high[at, :], right_high[i])
            )
            return carry

        lax.fori_loop(0, count, step, 0)

    sizes = list(range(TILE, states + 1, TILE))
    for size in sizes:
        pl.when((rows <= size) & (rows > size - TILE))(functools.partial(second_stage, size))

    def finish(i, carry):
        at = pl.ds(pl.multiple_of(i * CHUNK, CHUNK), CHUNK)
        mask = live_mask((CHUNK, width), i * CHUNK, rows, cols)
        value = jnp.where(mask, out_ref[at, :], 0.0)
        out_ref[at, :] = value
        basis = numbers.basis(k - 1, [r[OWN][at, :] for r in raw]) if k else []
        terms = [value * new_refs[OWN][at, :]] + [value * b for b in basis]
        return tuple(c + fold(t) for c, t in zip(carry, terms))

    late = lax.fori_loop(0, states // CHUNK, finish, (zero,) * (1 + k))

    def whole(value):
        return jnp.sum(jnp.sum(value, axis=1, keepdims=True), axis=0, keepdims=True)

    share = 1.0 / mpo_count
    entries = [whole(own[0]) * share, whole(late[0])]
    for j in range(2):
        entries.append(whole(own[1 + j]) * share if j < k else None)
    for j in range(2):
        entries.append(whole(late[1 + j]) if j < k else None)
    for j in range(2):
        entries.append(whole(own[1 + k + j]) * share if j < k else None)
    row_ids = lax.broadcasted_iota(jnp.int32, small_ref.shape, 0)
    small = jnp.zeros(small_ref.shape, F32)
    for index, entry in enumerate(entries):
        if entry is not None:
            small = jnp.where(row_ids == index, entry, small)
    small_ref[...] = small


def join_kernel(a_ref, b_ref, s0, s1, s2, s3, out_ref, small_ref):
    small_ref[...] = (s0[...] + s1[...]) + (s2[...] + s3[...])

    def step(i, carry):
        at = pl.ds(pl.multiple_of(i * CHUNK, CHUNK), CHUNK)
        out_ref[at, :] = a_ref[at, :] + b_ref[at, :]
        return carry

    lax.fori_loop(0, out_ref.shape[0] // CHUNK, step, 0)


def final_kernel(cells, meta_ref, s0, s1, s2, s3, t1, t2, *refs):
    raw = [refs[2 * i : 2 * i + 2] for i in range(MATVECS)]
    images = [refs[2 * (MATVECS + i) : 2 * (MATVECS + i) + 2] for i in range(MATVECS)]
    basis_ref, images_ref, projected_ref = refs[4 * MATVECS :]
    sigma = meta_ref[SIGMA]
    total = (s0[...] + s1[...]) + (s2[...] + s3[...])
    numbers = Scalars([t1[...], t2[...], total], cells)
    states, half = basis_ref.shape[2:]
    core = lax.axis_index("rsec")
    lanes = pl.ds(pl.multiple_of(core * half, half), half)
    for slot in (OWN, SIB):
        sector = sigma if slot == OWN else 1 - sigma

        def step(i, carry, slot=slot, sector=sector):
            at = pl.ds(pl.multiple_of(i * CHUNK, CHUNK), CHUNK)
            for fields, ref in ((raw, basis_ref), (images, images_ref)):
                done = numbers.basis(MATVECS - 1, [f[slot][at, lanes] for f in fields])
                for j, value in enumerate(done):
                    ref[j, sector, at, :] = value
            return carry

        lax.fori_loop(0, states // CHUNK, step, 0)
    shape = projected_ref.shape
    row_ids = lax.broadcasted_iota(jnp.int32, shape, 0)
    col_ids = lax.broadcasted_iota(jnp.int32, shape, 1)
    out = jnp.zeros(shape, F32)
    for i in range(MATVECS):
        for j in range(MATVECS):
            out = jnp.where((row_ids == i) & (col_ids == j), numbers.proj[i, j][:, :1], out)
    projected_ref[...] = out


def per_device(
    wavefunction, left_env, right_env, precond_diag, down_charge, bond_mask, left_size, right_size
):
    sectors, states, columns = wavefunction.shape
    bonds = left_env.shape[0]
    lsec_count = lax.axis_size("lsec")
    mpo_count = lax.axis_size("mpo")
    assert sectors == 2 and lax.axis_size("rsec") == 2
    width = 2 * columns
    cells = float(lsec_count * sectors * states * width)
    field = jax.ShapeDtypeStruct((states, width), F32)
    small = jax.ShapeDtypeStruct((8, 128), F32)
    params = pltpu.CompilerParams(vmem_limit_bytes=24 * 2**20)

    wave_all = lax.all_gather(wavefunction, "rsec", axis=2, tiled=True)
    own, sib, meta = pl.pallas_call(
        functools.partial(prep_kernel, lsec_count, bonds),
        out_shape=(field, field, jax.ShapeDtypeStruct((LIST + bonds,), jnp.int32)),
        in_specs=[whole_smem()] * 4 + [whole_vmem()],
        out_specs=(whole_vmem(), whole_vmem(), whole_smem()),
        compiler_params=params,
        name="prep",
    )(down_charge, bond_mask, left_size, right_size, wave_all)
    sigma = meta[SIGMA]

    up = [(i, i + 1) for i in range(lsec_count - 1)]
    down = [(i + 1, i) for i in range(lsec_count - 1)]
    swap = [(0, 1), (1, 0)]

    def neighbours(value):
        return lax.ppermute(value, "lsec", up), lax.ppermute(value, "lsec", down)

    raw = [(own, sib, *neighbours(own))]
    far_send = lax.dynamic_index_in_dim(right_env, 1 - sigma, 1, keepdims=False)
    far_right = lax.ppermute(far_send, "rsec", swap)
    precond_all = lax.all_gather(precond_diag, "rsec", axis=2, tiled=True)
    precond_own = lax.dynamic_index_in_dim(precond_all, sigma, 0, keepdims=False)
    precond_sib = lax.dynamic_index_in_dim(precond_all, 1 - sigma, 0, keepdims=False)
    precond = (precond_own, precond_sib, *neighbours(precond_own))

    def mpo_sum(value, part):
        if mpo_count != 2:
            return lax.psum(value, "mpo"), lax.psum(part, ("mpo", "rsec"))
        far = lax.ppermute(value, "mpo", swap)
        other = lax.ppermute(part, "mpo", swap)
        beside = lax.ppermute(part, "rsec", swap)
        cross = lax.ppermute(part, ("mpo", "rsec"), [(0, 3), (1, 2), (2, 1), (3, 0)])
        return pl.pallas_call(
            join_kernel,
            out_shape=(field, small),
            in_specs=[whole_vmem()] * 6,
            out_specs=(whole_vmem(),) * 2,
            compiler_params=params,
            name="join",
        )(value, far, part, other, beside, cross)

    def lsec_sums(part):
        if lsec_count != 4:
            zero = jnp.zeros_like(part)
            return lax.psum(part, "lsec"), zero, zero, zero
        return (part, *[lax.ppermute(part, "lsec", [(i, i ^ x) for i in range(4)]) for x in (1, 2, 3)])

    packed = bonds * states + states
    blocks = pl.pallas_call(
        load_kernel,
        out_shape=(
            pltpu.VMEM((packed, states), BF16),
            pltpu.VMEM((packed, states), BF16),
            pltpu.VMEM((bonds, width, width), BF16),
            pltpu.VMEM((bonds, width, width), BF16),
        ),
        in_specs=[whole_smem()] + [pl.BlockSpec(memory_space=pl.ANY)] * 3,
        out_specs=(whole_vmem(),) * 4,
        scratch_shapes=[
            pltpu.VMEM((BUFFERS, states, states), F32),
            pltpu.VMEM((BUFFERS, width, width), F32),
            pltpu.SemaphoreType.DMA((2 + states // TILE, BUFFERS)),
        ],
        compiler_params=params,
        cost_estimate=pl.CostEstimate(flops=0, transcendentals=0, bytes_accessed=bonds * states * states * 4),
        name="load",
    )(meta, left_env, right_env, far_right)

    def matvec(k, inputs):
        out_shape = [field, small] + ([small] + [field] * 4 if k else [])
        return pl.pallas_call(
            functools.partial(matvec_kernel, k, cells, mpo_count),
            out_shape=tuple(out_shape),
            in_specs=[whole_smem()] + [whole_vmem()] * (4 + len(inputs)),
            out_specs=tuple([whole_vmem()] * len(out_shape)),
            scratch_shapes=[
                pltpu.VMEM((4, states, width), BF16),
                pltpu.VMEM((4, states, width), BF16),
                pltpu.VMEM((packed, width), BF16),
                pltpu.VMEM((packed, width), BF16),
            ],
            compiler_params=params,
            cost_estimate=pl.CostEstimate(
                flops=2 * 3 * bonds * states * width * (states + width),
                transcendentals=0,
                bytes_accessed=bonds * states * states,
            ),
            name=f"matvec{k}",
        )(meta, *blocks, *inputs)

    totals = []
    images = []
    for k in range(MATVECS):
        if k == 0:
            value, part = matvec(0, list(raw[0]))
        else:
            flat_raw = [x for group in raw for x in group]
            flat_images = [x for group in images for x in group]
            value, part, total, *fresh = matvec(
                k, [*sums, *totals, *flat_raw, *flat_images, *precond]
            )
            totals.append(total)
            raw.append(tuple(fresh))
        value, part = mpo_sum(value, part)
        sums = lsec_sums(part)
        beside = lax.ppermute(value, "rsec", swap)
        if k + 1 < MATVECS:
            images.append((value, beside, *neighbours(value)))
        else:
            images.append((value, beside))

    flat = [x for group in raw for x in group[:2]] + [x for group in images for x in group[:2]]
    out = jax.ShapeDtypeStruct((MATVECS, sectors, states, columns), F32)
    return pl.pallas_call(
        functools.partial(final_kernel, cells),
        out_shape=(out, out, jax.ShapeDtypeStruct((MATVECS, MATVECS), F32)),
        in_specs=[whole_smem()] + [whole_vmem()] * (6 + len(flat)),
        out_specs=(whole_vmem(),) * 3,
        compiler_params=params,
        name="final",
    )(meta, *sums, *totals, *flat)


def solution(mesh):
    placed = (
        P(("grp", "lsec"), None, "rsec"),
        P("mpo", ("grp", "lsec"), None, None),
        P("mpo", ("grp", "lsec"), "rsec", None),
        P(("grp", "lsec"), None, "rsec"),
        P("grp"),
        P("mpo", ("grp", "lsec")),
        P(("grp", "lsec")),
        P(("grp", "lsec")),
    )
    return jax.shard_map(
        per_device,
        mesh=mesh,
        in_specs=placed,
        out_specs=(
            P(None, ("grp", "lsec"), None, "rsec"),
            P(None, ("grp", "lsec"), None, "rsec"),
            P("grp", None),
        ),
        check_vma=False,
    )
```

```python
import functools

import jax
import jax.numpy as jnp
from jax import lax
from jax.experimental import pallas as pl
from jax.experimental.pallas import tpu as pltpu
from jax.sharding import PartitionSpec as P

EPSILON = 1e-06
MATVECS = 3
F32 = jnp.float32
BF16 = jnp.bfloat16
SIGMA, COUNT, ROWS, COLS, FIRST, LIST = 0, 1, 2, 3, 4, 16
OWN, SIB, FIRST_PAIR, SECOND_PAIR = 0, 1, 2, 3
CHUNK = 64
TILE = 128
PACK = 256
BUFFERS = 4


def whole_vmem():
    return pl.BlockSpec(memory_space=pltpu.VMEM)


def whole_smem():
    return pl.BlockSpec(memory_space=pltpu.SMEM)


def split(value):
    high = value.astype(BF16)
    return high, (value - high.astype(F32)).astype(BF16)


def orientation(down_ref, place):
    def step(i, flips):
        straight = (down_ref[2 * i] == down_ref[2 * i - 2]) | (
            down_ref[2 * i + 1] == down_ref[2 * i - 1]
        )
        return jnp.where(straight, flips, 1 - flips)

    return lax.fori_loop(1, place + 1, step, jnp.int32(0))


def live_mask(shape, row0, rows, cols):
    row_ids = row0 + lax.broadcasted_iota(jnp.int32, shape, 0)
    col_ids = lax.broadcasted_iota(jnp.int32, shape, 1)
    return (row_ids < rows) & (col_ids < cols)


def prep_kernel(lsec_count, bonds, down_in, mask_in, left_in, right_in, wave_ref, wave_far, diag_ref,
                diag_far, own_ref, sib_ref, diag_own, diag_sib, meta_ref, down_ref, mask_ref,
                left_size_ref, right_size_ref, sems):
    copies = [
        pltpu.make_async_copy(source, target, sems.at[i])
        for i, (source, target) in enumerate(
            ((down_in, down_ref), (mask_in, mask_ref), (left_in, left_size_ref), (right_in, right_size_ref))
        )
    ]
    for copy in copies:
        copy.start()
    for copy in copies:
        copy.wait()
    place = lax.axis_index("lsec")
    core = lax.axis_index("rsec")
    first_bond = lax.axis_index("mpo") * bonds
    sigma = core ^ orientation(down_ref, place)
    own_down = down_ref[2 * place + sigma]
    sib_down = down_ref[2 * place + 1 - sigma]
    before = jnp.maximum(place - 1, 0)
    after = jnp.minimum(place + 1, lsec_count - 1)
    prev_down = down_ref[2 * before + (core ^ orientation(down_ref, before))]
    next_down = down_ref[2 * after + (core ^ orientation(down_ref, after))]
    has_prev = (place > 0) & (prev_down == own_down)
    has_next = (place < lsec_count - 1) & (next_down == own_down)
    odd = lax.rem(place, 2)
    has_lower = sib_down == own_down - 1
    has_upper = sib_down == own_down + 1

    def gather(slot, count):
        meta_ref[FIRST + slot] = count

        def step(bond, count):
            kind = lax.rem(first_bond + bond, 5)
            if slot == OWN:
                there = kind == 0
            elif slot == SIB:
                there = ((kind == 3) & has_lower) | ((kind == 4) & has_upper)
            else:
                lower = odd if slot == FIRST_PAIR else 1 - odd
                there = ((kind == 1) & has_prev & (lower == 1)) | (
                    (kind == 2) & has_next & (lower == 0)
                )
            there = there & (mask_ref[bond, sigma] > 0)

            @pl.when(there)
            def _():
                meta_ref[LIST + count] = bond * 4 + slot

            return count + there.astype(jnp.int32)

        return lax.fori_loop(0, bonds, step, count)

    count = jnp.int32(0)
    for slot in (OWN, SIB, FIRST_PAIR, SECOND_PAIR):
        count = gather(slot, count)
    meta_ref[FIRST + 4] = count
    rows, cols = left_size_ref[sigma], right_size_ref[sigma]
    meta_ref[SIGMA] = sigma
    meta_ref[COUNT] = count
    meta_ref[ROWS] = rows
    meta_ref[COLS] = cols
    states, width = own_ref.shape
    half = width // 2
    near = pl.ds(pl.multiple_of(core * half, half), half)
    away = pl.ds(pl.multiple_of((1 - core) * half, half), half)
    for ref, diag, slot in ((own_ref, diag_own, sigma), (sib_ref, diag_sib, 1 - sigma)):

        def fill(i, carry, ref=ref, diag=diag, slot=slot):
            at = pl.ds(pl.multiple_of(i * CHUNK, CHUNK), CHUNK)
            for lanes, place, wave, precond in (
                (near, core, wave_ref, diag_ref),
                (away, 1 - core, wave_far, diag_far),
            ):
                mask = live_mask(
                    (CHUNK, half), i * CHUNK, left_size_ref[slot], right_size_ref[slot] - place * half
                )
                ref[at, lanes] = jnp.where(mask, wave[slot, at, :], 0.0)
                diag[at, lanes] = precond[slot, at, :]
            return carry

        lax.fori_loop(0, states // CHUNK, fill, 0)


def row(value, index):
    return value[index : index + 1, :]


class Scalars:
    def __init__(self, totals, cells):
        self.proj = {}
        self.gram = {}
        self.norm = []
        self.corr = []
        for k, total in enumerate(totals):
            value = total / cells
            size, inner = row(value, 0), row(value, 1)
            a = [row(value, 2 + j) for j in range(k)]
            e = [row(value, 4 + j) for j in range(k)]
            f = [row(value, 6 + j) for j in range(k)]
            length = size
            theta = inner
            for j in range(k):
                length = length - 2.0 * a[j] * a[j]
                theta = theta - a[j] * e[j] - a[j] * f[j]
            for i in range(k):
                for j in range(k):
                    length = length + a[i] * a[j] * self.gram[i, j]
                    theta = theta + a[i] * a[j] * self.proj[i, j]
            length = jnp.maximum(length, 0.0)
            square = length + EPSILON
            norm = jnp.sqrt(square)
            for j in range(k):
                up, down, both = e[j], f[j], a[j]
                for i in range(k):
                    up = up - a[i] * self.proj[j, i]
                    down = down - a[i] * self.proj[i, j]
                    both = both - a[i] * self.gram[i, j]
                self.proj[j, k] = up / norm
                self.proj[k, j] = down / norm
                self.gram[j, k] = self.gram[k, j] = both / norm
            self.proj[k, k] = theta / square
            self.gram[k, k] = length / square
            self.norm.append(norm)
            self.corr.append(a)

    def basis(self, k, fields):
        done = []
        for step in range(k + 1):
            value = fields[step]
            for j in range(step):
                value = value - self.corr[step][j][:, :1] * done[j]
            done.append(value / self.norm[step][:, :1])
        return done


def left_kernel(meta_ref, left_ref, left_high, left_low, left_buf, sems):
    states = left_buf.shape[1]
    sigma, count, rows = meta_ref[SIGMA], meta_ref[COUNT], meta_ref[ROWS]
    stride = packed_rows(rows)

    def each(i, act):
        bond = meta_ref[LIST + i] // 4
        at = lax.rem(i, BUFFERS)
        for p in range(states // TILE):
            part = pl.ds(p * TILE, TILE)

            @pl.when(rows > p * TILE)
            def _(part=part, p=p):
                act(
                    pltpu.make_async_copy(
                        left_ref.at[bond, sigma, part], left_buf.at[at, part], sems.at[p, at]
                    )
                )

    def start(i):
        @pl.when(i < count)
        def _():
            each(i, lambda copy: copy.start())

    for i in range(BUFFERS - 1):
        start(jnp.int32(i))

    def step(i, carry):
        at = lax.rem(i, BUFFERS)
        start(i + BUFFERS - 1)
        each(i, lambda copy: copy.wait())

        def chunk(t, inner):
            high, low = split(left_buf[at, pl.ds(pl.multiple_of(t * CHUNK, CHUNK), CHUNK), :])
            to = pl.ds(pl.multiple_of(i * stride + t * CHUNK, 16), CHUNK)
            left_high[to, :] = high
            left_low[to, :] = low
            return inner

        lax.fori_loop(0, (rows + CHUNK - 1) // CHUNK, chunk, 0)
        return carry

    lax.fori_loop(0, count, step, 0)


def right_kernel(meta_ref, right_ref, far_ref, right_high, right_low, right_buf, sems):
    half = right_ref.shape[2]
    sigma, count = meta_ref[SIGMA], meta_ref[COUNT]
    core = lax.axis_index("rsec")
    near = pl.ds(pl.multiple_of(core * half, half), half)
    away = pl.ds(pl.multiple_of((1 - core) * half, half), half)

    def copies(i):
        bond = meta_ref[LIST + i] // 4
        at = lax.rem(i, BUFFERS)
        return (
            pltpu.make_async_copy(right_ref.at[bond, sigma], right_buf.at[at, near], sems.at[0, at]),
            pltpu.make_async_copy(far_ref.at[bond, sigma], right_buf.at[at, away], sems.at[1, at]),
        )

    def start(i):
        @pl.when(i < count)
        def _():
            for copy in copies(i):
                copy.start()

    for i in range(BUFFERS - 1):
        start(jnp.int32(i))

    def step(i, carry):
        start(i + BUFFERS - 1)
        for copy in copies(i):
            copy.wait()
        right_high[i], right_low[i] = split(right_buf[lax.rem(i, BUFFERS)].T)
        return carry

    lax.fori_loop(0, count, step, 0)


def packed_rows(rows):
    return ((rows + 15) // 16) * 16


def matvec_kernel(k, cells, mpo_count, *refs):
    refs = list(refs)
    meta_ref = refs.pop(0)
    left_high, left_low, right_high, right_low = [refs.pop(0) for _ in range(4)]
    totals = [refs.pop(0) for _ in range(k)]
    raw = [[refs.pop(0) for _ in range(4)] for _ in range(max(k, 1))]
    images = [[refs.pop(0) for _ in range(4)] for _ in range(k)]
    precond = [refs.pop(0) for _ in range(4)] if k else []
    out_ref, small_ref = refs.pop(0), refs.pop(0)
    new_refs = [refs.pop(0) for _ in range(4)] if k else raw[0]
    high_ref, low_ref, mid_high, mid_low = refs
    states, width = out_ref.shape
    count, rows, cols = meta_ref[COUNT], meta_ref[ROWS], meta_ref[COLS]
    stride = packed_rows(rows)

    if k:
        numbers = Scalars([ref[...] for ref in totals], cells)
        theta = numbers.proj[k - 1, k - 1][:, :1]
    zero = jnp.zeros((8, width), F32)

    def fold(value):
        return jnp.sum(value.reshape(CHUNK // 8, 8, width), axis=0)

    def prepare(slot, first, last, carry):
        def step(i, carry):
            at = pl.ds(pl.multiple_of(i * CHUNK, CHUNK), CHUNK)
            if k:
                basis = numbers.basis(k - 1, [r[slot][at, :] for r in raw])
                image = numbers.basis(k - 1, [r[slot][at, :] for r in images])
                value = (image[-1] - theta * basis[-1]) / jnp.maximum(
                    precond[slot][at, :] - theta, 1.0
                )
                new_refs[slot][at, :] = value
            else:
                basis, image = [], []
                value = raw[0][slot][at, :]
            high, low = split(value)
            high_ref[slot, at, :] = high
            low_ref[slot, at, :] = low
            terms = [value * value]
            if slot == OWN:
                terms += [value * b for b in basis] + [value * g for g in image]
            return tuple(c + fold(t) for c, t in zip(carry, terms))

        return lax.fori_loop(first, last, step, carry)

    def dot(a, b):
        return jnp.dot(a, b, preferred_element_type=F32)

    def first_stage(slot, depth):
        begin, end = meta_ref[FIRST + slot], meta_ref[FIRST + 1 + slot]
        tiles = ((end - begin) * stride + PACK - 1) // PACK
        deep = pl.ds(0, depth)

        def step(t, carry):
            at = pl.ds(pl.multiple_of(begin * stride + t * PACK, 16), PACK)
            high, low = left_high[at, deep], left_low[at, deep]
            p_high, p_low = high_ref[slot, deep, :], low_ref[slot, deep, :]
            mid = dot(high, p_low) + dot(low, p_high) + dot(high, p_high)
            mid_high[at, :], mid_low[at, :] = split(mid)
            return carry

        lax.fori_loop(0, tiles, step, 0)

    shallow = min(256, states)
    for slot in (OWN, SIB, FIRST_PAIR, SECOND_PAIR):

        def work(slot=slot):
            init = (zero,) * (1 + 2 * k if slot == OWN else 1)
            upper = prepare(slot, 0, shallow // CHUNK, init)
            lower = prepare(slot, shallow // CHUNK, states // CHUNK, init)
            deep = jnp.max(lower[0]) > 0.0
            pl.when(deep)(lambda: first_stage(slot, states))
            pl.when(jnp.logical_not(deep))(lambda: first_stage(slot, shallow))
            return [u + l for u, l in zip(upper, lower)]

        if slot == OWN:
            own = work()
        else:
            used = meta_ref[FIRST + 1 + slot] > meta_ref[FIRST + slot]
            pl.when(used | (slot == SIB))(lambda: (work(), None)[1])

    def clear(i, carry):
        at = pl.ds(pl.multiple_of(i * CHUNK, CHUNK), CHUNK)
        out_ref[at, :] = jnp.zeros((CHUNK, width), F32)
        return carry

    lax.fori_loop(0, states // CHUNK, clear, 0)

    def second_stage(size):
        def step(i, carry):
            at = pl.ds(pl.multiple_of(i * stride, 16), size)
            out_ref[pl.ds(0, size), :] += (
                dot(mid_high[at, :], right_low[i])
                + dot(mid_low[at, :], right_high[i])
                + dot(mid_high[at, :], right_high[i])
            )
            return carry

        lax.fori_loop(0, count, step, 0)

    sizes = list(range(TILE, states + 1, TILE))
    for size in sizes:
        pl.when((rows <= size) & (rows > size - TILE))(functools.partial(second_stage, size))

    def finish(i, carry):
        at = pl.ds(pl.multiple_of(i * CHUNK, CHUNK), CHUNK)
        mask = live_mask((CHUNK, width), i * CHUNK, rows, cols)
        value = jnp.where(mask, out_ref[at, :], 0.0)
        out_ref[at, :] = value
        basis = numbers.basis(k - 1, [r[OWN][at, :] for r in raw]) if k else []
        terms = [value * new_refs[OWN][at, :]] + [value * b for b in basis]
        return tuple(c + fold(t) for c, t in zip(carry, terms))

    late = lax.fori_loop(0, states // CHUNK, finish, (zero,) * (1 + k))

    def whole(value):
        return jnp.sum(jnp.sum(value, axis=1, keepdims=True), axis=0, keepdims=True)

    share = 1.0 / mpo_count
    entries = [whole(own[0]) * share, whole(late[0])]
    for j in range(2):
        entries.append(whole(own[1 + j]) * share if j < k else None)
    for j in range(2):
        entries.append(whole(late[1 + j]) if j < k else None)
    for j in range(2):
        entries.append(whole(own[1 + k + j]) * share if j < k else None)
    row_ids = lax.broadcasted_iota(jnp.int32, small_ref.shape, 0)
    small = jnp.zeros(small_ref.shape, F32)
    for index, entry in enumerate(entries):
        if entry is not None:
            small = jnp.where(row_ids == index, entry, small)
    small_ref[...] = small


def join_kernel(a_ref, b_ref, s0, s1, s2, s3, out_ref, small_ref):
    small_ref[...] = (s0[...] + s1[...]) + (s2[...] + s3[...])

    def step(i, carry):
        at = pl.ds(pl.multiple_of(i * CHUNK, CHUNK), CHUNK)
        out_ref[at, :] = a_ref[at, :] + b_ref[at, :]
        return carry

    lax.fori_loop(0, out_ref.shape[0] // CHUNK, step, 0)


def final_kernel(cells, meta_ref, *refs):
    totals, refs = refs[:MATVECS], refs[MATVECS:]
    raw = [refs[2 * i : 2 * i + 2] for i in range(MATVECS)]
    images = [refs[2 * (MATVECS + i) : 2 * (MATVECS + i) + 2] for i in range(MATVECS)]
    basis_ref, images_ref, projected_ref = refs[4 * MATVECS :]
    sigma = meta_ref[SIGMA]
    numbers = Scalars([ref[...] for ref in totals], cells)
    states, half = basis_ref.shape[2:]
    core = lax.axis_index("rsec")
    lanes = pl.ds(pl.multiple_of(core * half, half), half)
    for slot in (OWN, SIB):
        sector = sigma if slot == OWN else 1 - sigma

        def step(i, carry, slot=slot, sector=sector):
            at = pl.ds(pl.multiple_of(i * CHUNK, CHUNK), CHUNK)
            for fields, ref in ((raw, basis_ref), (images, images_ref)):
                done = numbers.basis(MATVECS - 1, [f[slot][at, lanes] for f in fields])
                for j, value in enumerate(done):
                    ref[j, sector, at, :] = value
            return carry

        lax.fori_loop(0, states // CHUNK, step, 0)
    shape = projected_ref.shape
    row_ids = lax.broadcasted_iota(jnp.int32, shape, 0)
    col_ids = lax.broadcasted_iota(jnp.int32, shape, 1)
    out = jnp.zeros(shape, F32)
    for i in range(MATVECS):
        for j in range(MATVECS):
            out = jnp.where((row_ids == i) & (col_ids == j), numbers.proj[i, j][:, :1], out)
    projected_ref[...] = out


def per_device(
    wavefunction, left_env, right_env, precond_diag, down_charge, bond_mask, left_size, right_size
):
    sectors, states, columns = wavefunction.shape
    bonds = left_env.shape[0]
    lsec_count = lax.axis_size("lsec")
    mpo_count = lax.axis_size("mpo")
    assert sectors == 2 and lax.axis_size("rsec") == 2
    width = 2 * columns
    cells = float(lsec_count * sectors * states * width)
    field = jax.ShapeDtypeStruct((states, width), F32)
    small = jax.ShapeDtypeStruct((8, 128), F32)
    params = pltpu.CompilerParams(vmem_limit_bytes=24 * 2**20)

    swap = [(0, 1), (1, 0)]
    first_pairs = [(i, i ^ 1) for i in range(lsec_count) if i ^ 1 < lsec_count]
    second_pairs = [(i, j) for a in range(1, lsec_count - 1, 2) for i, j in ((a, a + 1), (a + 1, a))]
    anywhere = pl.BlockSpec(memory_space=pl.ANY)

    def neighbours(value):
        return lax.ppermute(value, "lsec", first_pairs), lax.ppermute(value, "lsec", second_pairs)

    wave_far = lax.ppermute(wavefunction, "rsec", swap)
    diag_far = lax.ppermute(precond_diag, "rsec", swap)
    right_far = lax.ppermute(right_env, "rsec", swap)
    own, sib, diag_own, diag_sib, meta = pl.pallas_call(
        functools.partial(prep_kernel, lsec_count, bonds),
        out_shape=(field,) * 4 + (jax.ShapeDtypeStruct((LIST + bonds,), jnp.int32),),
        in_specs=[anywhere] * 4 + [whole_vmem()] * 4,
        out_specs=(whole_vmem(),) * 4 + (whole_smem(),),
        scratch_shapes=[
            pltpu.SMEM(down_charge.shape, jnp.int32),
            pltpu.SMEM(bond_mask.shape, jnp.int32),
            pltpu.SMEM(left_size.shape, jnp.int32),
            pltpu.SMEM(right_size.shape, jnp.int32),
            pltpu.SemaphoreType.DMA((4,)),
        ],
        compiler_params=params,
        name="prep",
    )(down_charge, bond_mask, left_size, right_size, wavefunction, wave_far, precond_diag, diag_far)
    near_waves = neighbours(own)
    raw = [(own, sib, *near_waves)]
    diag_send, _ = lax.optimization_barrier((diag_own, near_waves))
    precond = (diag_own, diag_sib, *neighbours(diag_send))

    def join(value, part):
        if mpo_count != 2 or lsec_count != 4:
            return lax.psum(value, "mpo"), lax.psum(part, ("lsec", "mpo", "rsec"))
        far = lax.ppermute(value, "mpo", swap)
        other = lax.ppermute(part, "mpo", swap)
        beside = lax.ppermute(part, "rsec", swap)
        cross = lax.ppermute(part, ("mpo", "rsec"), [(0, 3), (1, 2), (2, 1), (3, 0)])
        part = (part + other) + (beside + cross)
        parts = [lax.ppermute(part, "lsec", [(i, i ^ x) for i in range(4)]) for x in (1, 2, 3)]
        return pl.pallas_call(
            join_kernel,
            out_shape=(field, small),
            in_specs=[whole_vmem()] * 6,
            out_specs=(whole_vmem(),) * 2,
            compiler_params=params,
            name="join",
        )(value, far, part, *parts)

    packed = bonds * states + states
    lefts = pl.pallas_call(
        left_kernel,
        out_shape=(pltpu.VMEM((packed, states), BF16),) * 2,
        in_specs=[whole_smem(), anywhere],
        out_specs=(whole_vmem(),) * 2,
        scratch_shapes=[
            pltpu.VMEM((BUFFERS, states, states), F32),
            pltpu.SemaphoreType.DMA((states // TILE, BUFFERS)),
        ],
        compiler_params=params,
        cost_estimate=pl.CostEstimate(flops=0, transcendentals=0, bytes_accessed=bonds * states * states * 4),
        name="left",
    )(meta, left_env)
    rights = pl.pallas_call(
        right_kernel,
        out_shape=(pltpu.VMEM((bonds, width, width), BF16),) * 2,
        in_specs=[whole_smem(), anywhere, anywhere],
        out_specs=(whole_vmem(),) * 2,
        scratch_shapes=[
            pltpu.VMEM((BUFFERS, width, width), F32),
            pltpu.SemaphoreType.DMA((2, BUFFERS)),
        ],
        compiler_params=params,
        cost_estimate=pl.CostEstimate(flops=0, transcendentals=0, bytes_accessed=bonds * width * width * 8),
        name="right",
    )(meta, right_env, right_far)
    blocks = (*lefts, *rights)

    def matvec(k, inputs):
        out_shape = [field, small] + ([field] * 4 if k else [])
        return pl.pallas_call(
            functools.partial(matvec_kernel, k, cells, mpo_count),
            out_shape=tuple(out_shape),
            in_specs=[whole_smem()] + [whole_vmem()] * (4 + len(inputs)),
            out_specs=tuple([whole_vmem()] * len(out_shape)),
            scratch_shapes=[
                pltpu.VMEM((4, states, width), BF16),
                pltpu.VMEM((4, states, width), BF16),
                pltpu.VMEM((packed, width), BF16),
                pltpu.VMEM((packed, width), BF16),
            ],
            compiler_params=params,
            cost_estimate=pl.CostEstimate(
                flops=2 * 3 * bonds * states * width * (states + width),
                transcendentals=0,
                bytes_accessed=bonds * states * states,
            ),
            name=f"matvec{k}",
        )(meta, *blocks, *inputs)

    totals = []
    images = []
    for k in range(MATVECS):
        if k == 0:
            value, part = matvec(0, list(raw[0]))
        else:
            flat_raw = [x for group in raw for x in group]
            flat_images = [x for group in images for x in group]
            value, part, *fresh = matvec(k, [*totals, *flat_raw, *flat_images, *precond])
            raw.append(tuple(fresh))
        value, total = join(value, part)
        totals.append(total)
        beside = lax.ppermute(value, "rsec", swap)
        if k + 1 < MATVECS:
            images.append((value, beside, *neighbours(value)))
        else:
            images.append((value, beside))

    flat = [x for group in raw for x in group[:2]] + [x for group in images for x in group[:2]]
    out = jax.ShapeDtypeStruct((MATVECS, sectors, states, columns), F32)
    return pl.pallas_call(
        functools.partial(final_kernel, cells),
        out_shape=(out, out, jax.ShapeDtypeStruct((MATVECS, MATVECS), F32)),
        in_specs=[whole_smem()] + [whole_vmem()] * (MATVECS + len(flat)),
        out_specs=(whole_vmem(),) * 3,
        compiler_params=params,
        name="final",
    )(meta, *totals, *flat)


def solution(mesh):
    placed = (
        P(("grp", "lsec"), None, "rsec"),
        P("mpo", ("grp", "lsec"), None, None),
        P("mpo", ("grp", "lsec"), "rsec", None),
        P(("grp", "lsec"), None, "rsec"),
        P("grp"),
        P("mpo", ("grp", "lsec")),
        P(("grp", "lsec")),
        P(("grp", "lsec")),
    )
    return jax.shard_map(
        per_device,
        mesh=mesh,
        in_specs=placed,
        out_specs=(
            P(None, ("grp", "lsec"), None, "rsec"),
            P(None, ("grp", "lsec"), None, "rsec"),
            P("grp", None),
        ),
        check_vma=False,
    )
```

```python
import functools

import jax
import jax.numpy as jnp
from jax import lax
from jax.experimental import pallas as pl
from jax.experimental.pallas import tpu as pltpu
from jax.sharding import PartitionSpec as P

EPSILON = 1e-06
MATVECS = 3
F32 = jnp.float32
BF16 = jnp.bfloat16
SIGMA, COUNT, ROWS, COLS, FIRST, LIST = 0, 1, 2, 3, 4, 16
OWN, SIB, FIRST_PAIR, SECOND_PAIR = 0, 1, 2, 3
CHUNK = 64
TILE = 128
PACK = 256
BUFFERS = 4


def whole_vmem():
    return pl.BlockSpec(memory_space=pltpu.VMEM)


def whole_smem():
    return pl.BlockSpec(memory_space=pltpu.SMEM)


def split(value):
    high = value.astype(BF16)
    return high, (value - high.astype(F32)).astype(BF16)


def orientation(down_ref, place):
    def step(i, flips):
        straight = (down_ref[2 * i] == down_ref[2 * i - 2]) | (
            down_ref[2 * i + 1] == down_ref[2 * i - 1]
        )
        return jnp.where(straight, flips, 1 - flips)

    return lax.fori_loop(1, place + 1, step, jnp.int32(0))


def live_mask(shape, row0, rows, cols):
    row_ids = row0 + lax.broadcasted_iota(jnp.int32, shape, 0)
    col_ids = lax.broadcasted_iota(jnp.int32, shape, 1)
    return (row_ids < rows) & (col_ids < cols)


def read_small(pairs, sems):
    copies = [pltpu.make_async_copy(*pair, sems.at[i]) for i, pair in enumerate(pairs)]
    for copy in copies:
        copy.start()
    for copy in copies:
        copy.wait()


def masked_block(out_ref, wave_ref, slot, rows, cols):
    states, width = out_ref.shape

    def fill(i, carry):
        at = pl.ds(pl.multiple_of(i * CHUNK, CHUNK), CHUNK)
        mask = live_mask((CHUNK, width), i * CHUNK, rows, cols)
        out_ref[at, :] = jnp.where(mask, wave_ref[slot, at, :], 0.0)
        return carry

    lax.fori_loop(0, states // CHUNK, fill, 0)


def first_kernel(down_in, left_in, right_in, wave_ref, own_ref, down_ref, left_size_ref,
                 right_size_ref, sems):
    read_small(((down_in, down_ref), (left_in, left_size_ref), (right_in, right_size_ref)), sems)
    sigma = lax.axis_index("rsec") ^ orientation(down_ref, lax.axis_index("lsec"))
    masked_block(own_ref, wave_ref, sigma, left_size_ref[sigma], right_size_ref[sigma])


def prep_kernel(lsec_count, bonds, down_in, mask_in, left_in, right_in, wave_ref, diag_ref, diag_far,
                sib_ref, diag_own, diag_sib, meta_ref, down_ref, mask_ref, left_size_ref,
                right_size_ref, sems):
    read_small(
        ((down_in, down_ref), (mask_in, mask_ref), (left_in, left_size_ref), (right_in, right_size_ref)),
        sems,
    )
    place = lax.axis_index("lsec")
    core = lax.axis_index("rsec")
    first_bond = lax.axis_index("mpo") * bonds
    sigma = core ^ orientation(down_ref, place)
    own_down = down_ref[2 * place + sigma]
    sib_down = down_ref[2 * place + 1 - sigma]
    before = jnp.maximum(place - 1, 0)
    after = jnp.minimum(place + 1, lsec_count - 1)
    prev_down = down_ref[2 * before + (core ^ orientation(down_ref, before))]
    next_down = down_ref[2 * after + (core ^ orientation(down_ref, after))]
    has_prev = (place > 0) & (prev_down == own_down)
    has_next = (place < lsec_count - 1) & (next_down == own_down)
    odd = lax.rem(place, 2)
    has_lower = sib_down == own_down - 1
    has_upper = sib_down == own_down + 1

    def gather(slot, count):
        meta_ref[FIRST + slot] = count

        def step(bond, count):
            kind = lax.rem(first_bond + bond, 5)
            if slot == OWN:
                there = kind == 0
            elif slot == SIB:
                there = ((kind == 3) & has_lower) | ((kind == 4) & has_upper)
            else:
                lower = odd if slot == FIRST_PAIR else 1 - odd
                there = ((kind == 1) & has_prev & (lower == 1)) | (
                    (kind == 2) & has_next & (lower == 0)
                )
            there = there & (mask_ref[sigma, bond] > 0)

            @pl.when(there)
            def _():
                meta_ref[LIST + count] = bond * 4 + slot

            return count + there.astype(jnp.int32)

        return lax.fori_loop(0, bonds, step, count)

    count = jnp.int32(0)
    for slot in (OWN, SIB, FIRST_PAIR, SECOND_PAIR):
        count = gather(slot, count)
    meta_ref[FIRST + 4] = count
    rows, cols = left_size_ref[sigma], right_size_ref[sigma]
    meta_ref[SIGMA] = sigma
    meta_ref[COUNT] = count
    meta_ref[ROWS] = rows
    meta_ref[COLS] = cols
    masked_block(sib_ref, wave_ref, 1 - sigma, left_size_ref[1 - sigma], right_size_ref[1 - sigma])
    states, width = sib_ref.shape
    half = width // 2
    near = pl.ds(pl.multiple_of(core * half, half), half)
    away = pl.ds(pl.multiple_of((1 - core) * half, half), half)
    for out_ref, slot in ((diag_own, sigma), (diag_sib, 1 - sigma)):

        def fill(i, carry, out_ref=out_ref, slot=slot):
            at = pl.ds(pl.multiple_of(i * CHUNK, CHUNK), CHUNK)
            out_ref[at, near] = diag_ref[slot, at, :]
            out_ref[at, away] = diag_far[slot, at, :]
            return carry

        lax.fori_loop(0, states // CHUNK, fill, 0)


def row(value, index):
    return value[index : index + 1, :]


class Scalars:
    def __init__(self, totals, cells):
        self.proj = {}
        self.gram = {}
        self.norm = []
        self.corr = []
        for k, total in enumerate(totals):
            value = (total[0][...] + total[1][...]) / cells
            size, inner = row(value, 0), row(value, 1)
            a = [row(value, 2 + j) for j in range(k)]
            e = [row(value, 4 + j) for j in range(k)]
            f = [row(value, 6 + j) for j in range(k)]
            length = size
            theta = inner
            for j in range(k):
                length = length - 2.0 * a[j] * a[j]
                theta = theta - a[j] * e[j] - a[j] * f[j]
            for i in range(k):
                for j in range(k):
                    length = length + a[i] * a[j] * self.gram[i, j]
                    theta = theta + a[i] * a[j] * self.proj[i, j]
            length = jnp.maximum(length, 0.0)
            square = length + EPSILON
            norm = jnp.sqrt(square)
            for j in range(k):
                up, down, both = e[j], f[j], a[j]
                for i in range(k):
                    up = up - a[i] * self.proj[j, i]
                    down = down - a[i] * self.proj[i, j]
                    both = both - a[i] * self.gram[i, j]
                self.proj[j, k] = up / norm
                self.proj[k, j] = down / norm
                self.gram[j, k] = self.gram[k, j] = both / norm
            self.proj[k, k] = theta / square
            self.gram[k, k] = length / square
            self.norm.append(norm)
            self.corr.append(a)

    def basis(self, k, fields):
        done = []
        for step in range(k + 1):
            value = fields[step]
            for j in range(step):
                value = value - self.corr[step][j][:, :1] * done[j]
            done.append(value / self.norm[step][:, :1])
        return done


def left_kernel(meta_ref, left_ref, left_high, left_low, left_buf, sems):
    states = left_buf.shape[1]
    sigma, count, rows = meta_ref[SIGMA], meta_ref[COUNT], meta_ref[ROWS]
    stride = packed_rows(rows)

    def each(i, act):
        bond = meta_ref[LIST + i] // 4
        at = lax.rem(i, BUFFERS)
        for p in range(states // TILE):
            part = pl.ds(p * TILE, TILE)

            @pl.when(rows > p * TILE)
            def _(part=part, p=p):
                act(
                    pltpu.make_async_copy(
                        left_ref.at[bond, sigma, part], left_buf.at[at, part], sems.at[p, at]
                    )
                )

    def start(i):
        @pl.when(i < count)
        def _():
            each(i, lambda copy: copy.start())

    for i in range(BUFFERS - 1):
        start(jnp.int32(i))

    def step(i, carry):
        at = lax.rem(i, BUFFERS)
        start(i + BUFFERS - 1)
        each(i, lambda copy: copy.wait())

        def chunk(t, inner):
            high, low = split(left_buf[at, pl.ds(pl.multiple_of(t * CHUNK, CHUNK), CHUNK), :])
            to = pl.ds(pl.multiple_of(i * stride + t * CHUNK, 16), CHUNK)
            left_high[to, :] = high
            left_low[to, :] = low
            return inner

        lax.fori_loop(0, (rows + CHUNK - 1) // CHUNK, chunk, 0)
        return carry

    lax.fori_loop(0, count, step, 0)


def right_kernel(meta_ref, right_ref, far_ref, right_high, right_low, right_buf, sems):
    half = right_ref.shape[2]
    sigma, count = meta_ref[SIGMA], meta_ref[COUNT]
    core = lax.axis_index("rsec")
    near = pl.ds(pl.multiple_of(core * half, half), half)
    away = pl.ds(pl.multiple_of((1 - core) * half, half), half)

    def copies(i):
        bond = meta_ref[LIST + i] // 4
        at = lax.rem(i, BUFFERS)
        return (
            pltpu.make_async_copy(right_ref.at[bond, sigma], right_buf.at[at, near], sems.at[0, at]),
            pltpu.make_async_copy(far_ref.at[bond, sigma], right_buf.at[at, away], sems.at[1, at]),
        )

    def start(i):
        @pl.when(i < count)
        def _():
            for copy in copies(i):
                copy.start()

    for i in range(BUFFERS - 1):
        start(jnp.int32(i))

    def step(i, carry):
        start(i + BUFFERS - 1)
        for copy in copies(i):
            copy.wait()
        right_high[i], right_low[i] = split(right_buf[lax.rem(i, BUFFERS)].T)
        return carry

    lax.fori_loop(0, count, step, 0)


def packed_rows(rows):
    return ((rows + 15) // 16) * 16


def matvec_kernel(k, cells, mpo_count, *refs):
    refs = list(refs)
    meta_ref = refs.pop(0)
    left_high, left_low, right_high, right_low = [refs.pop(0) for _ in range(4)]
    totals = [(refs.pop(0), refs.pop(0)) for _ in range(k)]
    raw = [[refs.pop(0) for _ in range(4)] for _ in range(max(k, 1))]
    images = [[refs.pop(0) for _ in range(4)] for _ in range(k)]
    precond = [refs.pop(0) for _ in range(4)] if k else []
    out_ref, small_ref = refs.pop(0), refs.pop(0)
    new_refs = [refs.pop(0) for _ in range(4)] if k else raw[0]
    high_ref, low_ref, mid_high, mid_low = refs
    states, width = out_ref.shape
    count, rows, cols = meta_ref[COUNT], meta_ref[ROWS], meta_ref[COLS]
    stride = packed_rows(rows)

    if k:
        numbers = Scalars(totals, cells)
        theta = numbers.proj[k - 1, k - 1][:, :1]
    zero = jnp.zeros((8, width), F32)

    def fold(value):
        return jnp.sum(value.reshape(CHUNK // 8, 8, width), axis=0)

    def prepare(slot, first, last, carry):
        def step(i, carry):
            at = pl.ds(pl.multiple_of(i * CHUNK, CHUNK), CHUNK)
            if k:
                basis = numbers.basis(k - 1, [r[slot][at, :] for r in raw])
                image = numbers.basis(k - 1, [r[slot][at, :] for r in images])
                value = (image[-1] - theta * basis[-1]) / jnp.maximum(
                    precond[slot][at, :] - theta, 1.0
                )
                new_refs[slot][at, :] = value
            else:
                basis, image = [], []
                value = raw[0][slot][at, :]
            high, low = split(value)
            high_ref[slot, at, :] = high
            low_ref[slot, at, :] = low
            terms = [value * value]
            if slot == OWN:
                terms += [value * b for b in basis] + [value * g for g in image]
            return tuple(c + fold(t) for c, t in zip(carry, terms))

        return lax.fori_loop(first, last, step, carry)

    def dot(a, b):
        return jnp.dot(a, b, preferred_element_type=F32)

    def first_stage(slot, depth):
        begin, end = meta_ref[FIRST + slot], meta_ref[FIRST + 1 + slot]
        tiles = ((end - begin) * stride + PACK - 1) // PACK
        deep = pl.ds(0, depth)

        def step(t, carry):
            at = pl.ds(pl.multiple_of(begin * stride + t * PACK, 16), PACK)
            high, low = left_high[at, deep], left_low[at, deep]
            p_high, p_low = high_ref[slot, deep, :], low_ref[slot, deep, :]
            mid = dot(high, p_low) + dot(low, p_high) + dot(high, p_high)
            mid_high[at, :], mid_low[at, :] = split(mid)
            return carry

        lax.fori_loop(0, tiles, step, 0)

    shallow = min(256, states)
    for slot in (OWN, SIB, FIRST_PAIR, SECOND_PAIR):

        def work(slot=slot):
            init = (zero,) * (1 + 2 * k if slot == OWN else 1)
            upper = prepare(slot, 0, shallow // CHUNK, init)
            lower = prepare(slot, shallow // CHUNK, states // CHUNK, init)
            deep = jnp.max(lower[0]) > 0.0
            pl.when(deep)(lambda: first_stage(slot, states))
            pl.when(jnp.logical_not(deep))(lambda: first_stage(slot, shallow))
            return [u + l for u, l in zip(upper, lower)]

        if slot == OWN:
            own = work()
        else:
            used = meta_ref[FIRST + 1 + slot] > meta_ref[FIRST + slot]
            pl.when(used | (slot == SIB))(lambda: (work(), None)[1])

    def clear(i, carry):
        at = pl.ds(pl.multiple_of(i * CHUNK, CHUNK), CHUNK)
        out_ref[at, :] = jnp.zeros((CHUNK, width), F32)
        return carry

    lax.fori_loop(0, states // CHUNK, clear, 0)

    def second_stage(size):
        def step(i, carry):
            at = pl.ds(pl.multiple_of(i * stride, 16), size)
            out_ref[pl.ds(0, size), :] += (
                dot(mid_high[at, :], right_low[i])
                + dot(mid_low[at, :], right_high[i])
                + dot(mid_high[at, :], right_high[i])
            )
            return carry

        lax.fori_loop(0, count, step, 0)

    sizes = list(range(TILE, states + 1, TILE))
    for size in sizes:
        pl.when((rows <= size) & (rows > size - TILE))(functools.partial(second_stage, size))

    def finish(i, carry):
        at = pl.ds(pl.multiple_of(i * CHUNK, CHUNK), CHUNK)
        mask = live_mask((CHUNK, width), i * CHUNK, rows, cols)
        value = jnp.where(mask, out_ref[at, :], 0.0)
        out_ref[at, :] = value
        basis = numbers.basis(k - 1, [r[OWN][at, :] for r in raw]) if k else []
        terms = [value * new_refs[OWN][at, :]] + [value * b for b in basis]
        return tuple(c + fold(t) for c, t in zip(carry, terms))

    late = lax.fori_loop(0, states // CHUNK, finish, (zero,) * (1 + k))

    def whole(value):
        return jnp.sum(jnp.sum(value, axis=1, keepdims=True), axis=0, keepdims=True)

    share = 1.0 / mpo_count
    entries = [whole(own[0]) * share, whole(late[0])]
    for j in range(2):
        entries.append(whole(own[1 + j]) * share if j < k else None)
    for j in range(2):
        entries.append(whole(late[1 + j]) if j < k else None)
    for j in range(2):
        entries.append(whole(own[1 + k + j]) * share if j < k else None)
    row_ids = lax.broadcasted_iota(jnp.int32, small_ref.shape, 0)
    small = jnp.zeros(small_ref.shape, F32)
    for index, entry in enumerate(entries):
        if entry is not None:
            small = jnp.where(row_ids == index, entry, small)
    small_ref[...] = small


def join_kernel(a_ref, b_ref, s0, s1, s2, s3, out_ref, small_ref):
    small_ref[...] = (s0[...] + s1[...]) + (s2[...] + s3[...])

    def step(i, carry):
        at = pl.ds(pl.multiple_of(i * CHUNK, CHUNK), CHUNK)
        out_ref[at, :] = a_ref[at, :] + b_ref[at, :]
        return carry

    lax.fori_loop(0, out_ref.shape[0] // CHUNK, step, 0)


def final_kernel(cells, meta_ref, *refs):
    totals = [refs[2 * i : 2 * i + 2] for i in range(MATVECS)]
    refs = refs[2 * MATVECS :]
    raw = [refs[2 * i : 2 * i + 2] for i in range(MATVECS)]
    images = [refs[2 * (MATVECS + i) : 2 * (MATVECS + i) + 2] for i in range(MATVECS)]
    basis_ref, images_ref, projected_ref = refs[4 * MATVECS :]
    sigma = meta_ref[SIGMA]
    numbers = Scalars(totals, cells)
    states, half = basis_ref.shape[2:]
    core = lax.axis_index("rsec")
    lanes = pl.ds(pl.multiple_of(core * half, half), half)
    for slot in (OWN, SIB):
        sector = sigma if slot == OWN else 1 - sigma

        def step(i, carry, slot=slot, sector=sector):
            at = pl.ds(pl.multiple_of(i * CHUNK, CHUNK), CHUNK)
            for fields, ref in ((raw, basis_ref), (images, images_ref)):
                done = numbers.basis(MATVECS - 1, [f[slot][at, lanes] for f in fields])
                for j, value in enumerate(done):
                    ref[j, sector, at, :] = value
            return carry

        lax.fori_loop(0, states // CHUNK, step, 0)
    shape = projected_ref.shape
    row_ids = lax.broadcasted_iota(jnp.int32, shape, 0)
    col_ids = lax.broadcasted_iota(jnp.int32, shape, 1)
    out = jnp.zeros(shape, F32)
    for i in range(MATVECS):
        for j in range(MATVECS):
            out = jnp.where((row_ids == i) & (col_ids == j), numbers.proj[i, j][:, :1], out)
    projected_ref[...] = out


def per_device(
    wavefunction, left_env, right_env, precond_diag, down_charge, bond_mask, left_size, right_size
):
    sectors, states, columns = wavefunction.shape
    bonds = left_env.shape[0]
    lsec_count = lax.axis_size("lsec")
    mpo_count = lax.axis_size("mpo")
    assert sectors == 2 and lax.axis_size("rsec") == 2
    width = 2 * columns
    cells = float(lsec_count * sectors * states * width)
    field = jax.ShapeDtypeStruct((states, width), F32)
    small = jax.ShapeDtypeStruct((8, 128), F32)
    params = pltpu.CompilerParams(vmem_limit_bytes=24 * 2**20)

    swap = [(0, 1), (1, 0)]
    first_pairs = [(i, i ^ 1) for i in range(lsec_count) if i ^ 1 < lsec_count]
    second_pairs = [(i, j) for a in range(1, lsec_count - 1, 2) for i, j in ((a, a + 1), (a + 1, a))]
    anywhere = pl.BlockSpec(memory_space=pl.ANY)
    in_hbm = pl.BlockSpec(memory_space=pltpu.HBM)

    def neighbours(value):
        return lax.ppermute(value, "lsec", first_pairs), lax.ppermute(value, "lsec", second_pairs)

    wave_all = lax.all_gather(wavefunction, "rsec", axis=2, tiled=True)
    right_send, diag_send, _ = lax.optimization_barrier((right_env, precond_diag, wave_all))
    diag_far = lax.ppermute(diag_send, "rsec", swap)
    right_far = lax.ppermute(right_send, "rsec", swap)
    mask_rows = bond_mask.T
    down_charge, mask_rows, left_size, right_size, diag_near = [
        pltpu.with_memory_space_constraint(x, pltpu.HBM)
        for x in (down_charge, mask_rows, left_size, right_size, precond_diag)
    ]
    own = pl.pallas_call(
        first_kernel,
        out_shape=field,
        in_specs=[in_hbm] * 3 + [whole_vmem()],
        out_specs=whole_vmem(),
        scratch_shapes=[
            pltpu.SMEM(down_charge.shape, jnp.int32),
            pltpu.SMEM(left_size.shape, jnp.int32),
            pltpu.SMEM(right_size.shape, jnp.int32),
            pltpu.SemaphoreType.DMA((3,)),
        ],
        compiler_params=params,
        name="first",
    )(down_charge, left_size, right_size, wave_all)
    sib, diag_own, diag_sib, meta = pl.pallas_call(
        functools.partial(prep_kernel, lsec_count, bonds),
        out_shape=(field,) * 3 + (jax.ShapeDtypeStruct((LIST + bonds,), jnp.int32),),
        in_specs=[in_hbm] * 4 + [whole_vmem()] * 3,
        out_specs=(whole_vmem(),) * 3 + (whole_smem(),),
        scratch_shapes=[
            pltpu.SMEM(down_charge.shape, jnp.int32),
            pltpu.SMEM(mask_rows.shape, jnp.int32),
            pltpu.SMEM(left_size.shape, jnp.int32),
            pltpu.SMEM(right_size.shape, jnp.int32),
            pltpu.SemaphoreType.DMA((4,)),
        ],
        compiler_params=params,
        name="prep",
    )(down_charge, mask_rows, left_size, right_size, wave_all, diag_near, diag_far)
    near_waves = neighbours(own)
    raw = [(own, sib, *near_waves)]
    diag_send, _ = lax.optimization_barrier((diag_own, near_waves))
    near_diags = neighbours(diag_send)
    precond = (diag_own, diag_sib, *near_diags)

    def join(value, part):
        if mpo_count != 2 or lsec_count != 4:
            total = lax.psum(part, ("lsec", "mpo", "rsec"))
            return lax.psum(value, "mpo"), (total, jnp.zeros_like(total))
        far = lax.ppermute(value, "mpo", swap)
        part = part + lax.ppermute(part, "rsec", swap)
        parts = [lax.ppermute(part, "lsec", [(i, i ^ x) for i in range(4)]) for x in (1, 2, 3)]
        value, part = pl.pallas_call(
            join_kernel,
            out_shape=(field, small),
            in_specs=[whole_vmem()] * 6,
            out_specs=(whole_vmem(),) * 2,
            compiler_params=params,
            name="join",
        )(value, far, part, *parts)
        return value, (part, lax.ppermute(part, "mpo", swap))

    packed = bonds * states + states
    lefts = pl.pallas_call(
        left_kernel,
        out_shape=(pltpu.VMEM((packed, states), BF16),) * 2,
        in_specs=[whole_smem(), anywhere],
        out_specs=(whole_vmem(),) * 2,
        scratch_shapes=[
            pltpu.VMEM((BUFFERS, states, states), F32),
            pltpu.SemaphoreType.DMA((states // TILE, BUFFERS)),
        ],
        compiler_params=params,
        cost_estimate=pl.CostEstimate(flops=0, transcendentals=0, bytes_accessed=bonds * states * states * 4),
        name="left",
    )(meta, left_env)
    rights = pl.pallas_call(
        right_kernel,
        out_shape=(pltpu.VMEM((bonds, width, width), BF16),) * 2,
        in_specs=[whole_smem(), anywhere, anywhere],
        out_specs=(whole_vmem(),) * 2,
        scratch_shapes=[
            pltpu.VMEM((BUFFERS, width, width), F32),
            pltpu.SemaphoreType.DMA((2, BUFFERS)),
        ],
        compiler_params=params,
        cost_estimate=pl.CostEstimate(flops=0, transcendentals=0, bytes_accessed=bonds * width * width * 8),
        name="right",
    )(meta, right_env, right_far)
    blocks = (*lefts, *rights)

    def matvec(k, inputs):
        out_shape = [field, small] + ([field] * 4 if k else [])
        return pl.pallas_call(
            functools.partial(matvec_kernel, k, cells, mpo_count),
            out_shape=tuple(out_shape),
            in_specs=[whole_smem()] + [whole_vmem()] * (4 + len(inputs)),
            out_specs=tuple([whole_vmem()] * len(out_shape)),
            scratch_shapes=[
                pltpu.VMEM((4, states, width), BF16),
                pltpu.VMEM((4, states, width), BF16),
                pltpu.VMEM((packed, width), BF16),
                pltpu.VMEM((packed, width), BF16),
            ],
            compiler_params=params,
            cost_estimate=pl.CostEstimate(
                flops=2 * 3 * bonds * states * width * (states + width),
                transcendentals=0,
                bytes_accessed=bonds * states * states,
            ),
            name=f"matvec{k}",
        )(meta, *blocks, *inputs)

    totals = []
    images = []
    for k in range(MATVECS):
        if k == 0:
            value, part = matvec(0, list(raw[0]))
        else:
            flat_raw = [x for group in raw for x in group]
            flat_images = [x for group in images for x in group]
            value, part, *fresh = matvec(k, [*totals, *flat_raw, *flat_images, *precond])
            raw.append(tuple(fresh))
        if k == 0:
            value, near_diags = lax.optimization_barrier((value, near_diags))
            precond = (diag_own, diag_sib, *near_diags)
        value, total = join(value, part)
        totals += total
        beside = lax.ppermute(value, "rsec", swap)
        if k + 1 < MATVECS:
            images.append((value, beside, *neighbours(value)))
        else:
            images.append((value, beside))

    flat = [x for group in raw for x in group[:2]] + [x for group in images for x in group[:2]]
    out = jax.ShapeDtypeStruct((MATVECS, sectors, states, columns), F32)
    return pl.pallas_call(
        functools.partial(final_kernel, cells),
        out_shape=(out, out, jax.ShapeDtypeStruct((MATVECS, MATVECS), F32)),
        in_specs=[whole_smem()] + [whole_vmem()] * (2 * MATVECS + len(flat)),
        out_specs=(whole_vmem(),) * 3,
        compiler_params=params,
        name="final",
    )(meta, *totals, *flat)


def solution(mesh):
    placed = (
        P(("grp", "lsec"), None, "rsec"),
        P("mpo", ("grp", "lsec"), None, None),
        P("mpo", ("grp", "lsec"), "rsec", None),
        P(("grp", "lsec"), None, "rsec"),
        P("grp"),
        P("mpo", ("grp", "lsec")),
        P(("grp", "lsec")),
        P(("grp", "lsec")),
    )
    return jax.shard_map(
        per_device,
        mesh=mesh,
        in_specs=placed,
        out_specs=(
            P(None, ("grp", "lsec"), None, "rsec"),
            P(None, ("grp", "lsec"), None, "rsec"),
            P("grp", None),
        ),
        check_vma=False,
    )
```

```python
import functools

import jax
import jax.numpy as jnp
from jax import lax
from jax.experimental import pallas as pl
from jax.experimental.pallas import tpu as pltpu
from jax.sharding import PartitionSpec as P

EPSILON = 1e-06
MATVECS = 3
F32 = jnp.float32
BF16 = jnp.bfloat16
SIGMA, COUNT, ROWS, COLS, FIRST, LIST = 0, 1, 2, 3, 4, 16
OWN, SIB, FIRST_PAIR, SECOND_PAIR = 0, 1, 2, 3
CHUNK = 64
TILE = 128
PACK = 256
BUFFERS = 4


def whole_vmem():
    return pl.BlockSpec(memory_space=pltpu.VMEM)


def whole_smem():
    return pl.BlockSpec(memory_space=pltpu.SMEM)


def split(value):
    high = value.astype(BF16)
    return high, (value - high.astype(F32)).astype(BF16)


def orientation(down_ref, place):
    def step(i, flips):
        straight = (down_ref[2 * i] == down_ref[2 * i - 2]) | (
            down_ref[2 * i + 1] == down_ref[2 * i - 1]
        )
        return jnp.where(straight, flips, 1 - flips)

    return lax.fori_loop(1, place + 1, step, jnp.int32(0))


def live_mask(shape, row0, rows, cols):
    row_ids = row0 + lax.broadcasted_iota(jnp.int32, shape, 0)
    col_ids = lax.broadcasted_iota(jnp.int32, shape, 1)
    return (row_ids < rows) & (col_ids < cols)


def read_small(pairs, sems):
    copies = [pltpu.make_async_copy(*pair, sems.at[i]) for i, pair in enumerate(pairs)]
    for copy in copies:
        copy.start()
    for copy in copies:
        copy.wait()


def masked_block(out_ref, wave_ref, slot, rows, cols):
    states, width = out_ref.shape

    def fill(i, carry):
        at = pl.ds(pl.multiple_of(i * CHUNK, CHUNK), CHUNK)
        mask = live_mask((CHUNK, width), i * CHUNK, rows, cols)
        out_ref[at, :] = jnp.where(mask, wave_ref[slot, at, :], 0.0)
        return carry

    lax.fori_loop(0, states // CHUNK, fill, 0)


def first_kernel(down_in, left_in, right_in, wave_ref, own_ref, down_ref, left_size_ref,
                 right_size_ref, sems):
    read_small(((down_in, down_ref), (left_in, left_size_ref), (right_in, right_size_ref)), sems)
    sigma = lax.axis_index("rsec") ^ orientation(down_ref, lax.axis_index("lsec"))
    masked_block(own_ref, wave_ref, sigma, left_size_ref[sigma], right_size_ref[sigma])


def prep_kernel(lsec_count, bonds, down_in, mask_in, left_in, right_in, wave_ref, sib_ref, meta_ref,
                down_ref, mask_ref, left_size_ref, right_size_ref, sems):
    read_small(
        ((down_in, down_ref), (mask_in, mask_ref), (left_in, left_size_ref), (right_in, right_size_ref)),
        sems,
    )
    place = lax.axis_index("lsec")
    core = lax.axis_index("rsec")
    first_bond = lax.axis_index("mpo") * bonds
    sigma = core ^ orientation(down_ref, place)
    own_down = down_ref[2 * place + sigma]
    sib_down = down_ref[2 * place + 1 - sigma]
    before = jnp.maximum(place - 1, 0)
    after = jnp.minimum(place + 1, lsec_count - 1)
    prev_down = down_ref[2 * before + (core ^ orientation(down_ref, before))]
    next_down = down_ref[2 * after + (core ^ orientation(down_ref, after))]
    has_prev = (place > 0) & (prev_down == own_down)
    has_next = (place < lsec_count - 1) & (next_down == own_down)
    odd = lax.rem(place, 2)
    has_lower = sib_down == own_down - 1
    has_upper = sib_down == own_down + 1

    def gather(slot, count):
        meta_ref[FIRST + slot] = count

        def step(bond, count):
            kind = lax.rem(first_bond + bond, 5)
            if slot == OWN:
                there = kind == 0
            elif slot == SIB:
                there = ((kind == 3) & has_lower) | ((kind == 4) & has_upper)
            else:
                lower = odd if slot == FIRST_PAIR else 1 - odd
                there = ((kind == 1) & has_prev & (lower == 1)) | (
                    (kind == 2) & has_next & (lower == 0)
                )
            there = there & (mask_ref[sigma, bond] > 0)

            @pl.when(there)
            def _():
                meta_ref[LIST + count] = bond * 4 + slot

            return count + there.astype(jnp.int32)

        return lax.fori_loop(0, bonds, step, count)

    count = jnp.int32(0)
    for slot in (OWN, SIB, FIRST_PAIR, SECOND_PAIR):
        count = gather(slot, count)
    meta_ref[FIRST + 4] = count
    rows, cols = left_size_ref[sigma], right_size_ref[sigma]
    meta_ref[SIGMA] = sigma
    meta_ref[COUNT] = count
    meta_ref[ROWS] = rows
    meta_ref[COLS] = cols
    masked_block(sib_ref, wave_ref, 1 - sigma, left_size_ref[1 - sigma], right_size_ref[1 - sigma])


def diag_kernel(meta_ref, diag_ref, diag_far, diag_own, diag_sib):
    states, width = diag_own.shape
    half = width // 2
    sigma, core = meta_ref[SIGMA], lax.axis_index("rsec")
    near = pl.ds(pl.multiple_of(core * half, half), half)
    away = pl.ds(pl.multiple_of((1 - core) * half, half), half)
    for out_ref, slot in ((diag_own, sigma), (diag_sib, 1 - sigma)):

        def fill(i, carry, out_ref=out_ref, slot=slot):
            at = pl.ds(pl.multiple_of(i * CHUNK, CHUNK), CHUNK)
            out_ref[at, near] = diag_ref[slot, at, :]
            out_ref[at, away] = diag_far[slot, at, :]
            return carry

        lax.fori_loop(0, states // CHUNK, fill, 0)


def row(value, index):
    return value[index : index + 1, :]


class Scalars:
    def __init__(self, totals, cells):
        self.proj = {}
        self.gram = {}
        self.norm = []
        self.corr = []
        for k, total in enumerate(totals):
            value = (total[0][...] + total[1][...]) / cells
            size, inner = row(value, 0), row(value, 1)
            a = [row(value, 2 + j) for j in range(k)]
            e = [row(value, 4 + j) for j in range(k)]
            f = [row(value, 6 + j) for j in range(k)]
            length = size
            theta = inner
            for j in range(k):
                length = length - 2.0 * a[j] * a[j]
                theta = theta - a[j] * e[j] - a[j] * f[j]
            for i in range(k):
                for j in range(k):
                    length = length + a[i] * a[j] * self.gram[i, j]
                    theta = theta + a[i] * a[j] * self.proj[i, j]
            length = jnp.maximum(length, 0.0)
            square = length + EPSILON
            norm = jnp.sqrt(square)
            for j in range(k):
                up, down, both = e[j], f[j], a[j]
                for i in range(k):
                    up = up - a[i] * self.proj[j, i]
                    down = down - a[i] * self.proj[i, j]
                    both = both - a[i] * self.gram[i, j]
                self.proj[j, k] = up / norm
                self.proj[k, j] = down / norm
                self.gram[j, k] = self.gram[k, j] = both / norm
            self.proj[k, k] = theta / square
            self.gram[k, k] = length / square
            self.norm.append(norm)
            self.corr.append(a)

    def basis(self, k, fields):
        done = []
        for step in range(k + 1):
            value = fields[step]
            for j in range(step):
                value = value - self.corr[step][j][:, :1] * done[j]
            done.append(value / self.norm[step][:, :1])
        return done


def left_kernel(meta_ref, left_ref, left_high, left_low, left_buf, sems):
    states = left_buf.shape[1]
    sigma, count, rows = meta_ref[SIGMA], meta_ref[COUNT], meta_ref[ROWS]
    stride = packed_rows(rows)

    def each(i, act):
        bond = meta_ref[LIST + i] // 4
        at = lax.rem(i, BUFFERS)
        for p in range(states // TILE):
            part = pl.ds(p * TILE, TILE)

            @pl.when(rows > p * TILE)
            def _(part=part, p=p):
                act(
                    pltpu.make_async_copy(
                        left_ref.at[bond, sigma, part], left_buf.at[at, part], sems.at[p, at]
                    )
                )

    def start(i):
        @pl.when(i < count)
        def _():
            each(i, lambda copy: copy.start())

    for i in range(BUFFERS - 1):
        start(jnp.int32(i))

    def step(i, carry):
        at = lax.rem(i, BUFFERS)
        start(i + BUFFERS - 1)
        each(i, lambda copy: copy.wait())

        def chunk(t, inner):
            high, low = split(left_buf[at, pl.ds(pl.multiple_of(t * CHUNK, CHUNK), CHUNK), :])
            to = pl.ds(pl.multiple_of(i * stride + t * CHUNK, 16), CHUNK)
            left_high[to, :] = high
            left_low[to, :] = low
            return inner

        lax.fori_loop(0, (rows + CHUNK - 1) // CHUNK, chunk, 0)
        return carry

    lax.fori_loop(0, count, step, 0)


def right_kernel(meta_ref, right_ref, far_ref, right_high, right_low, right_buf, sems):
    half = right_ref.shape[2]
    sigma, count = meta_ref[SIGMA], meta_ref[COUNT]
    core = lax.axis_index("rsec")
    near = pl.ds(pl.multiple_of(core * half, half), half)
    away = pl.ds(pl.multiple_of((1 - core) * half, half), half)

    def copies(i):
        bond = meta_ref[LIST + i] // 4
        at = lax.rem(i, BUFFERS)
        return (
            pltpu.make_async_copy(right_ref.at[bond, sigma], right_buf.at[at, near], sems.at[0, at]),
            pltpu.make_async_copy(far_ref.at[bond, sigma], right_buf.at[at, away], sems.at[1, at]),
        )

    def start(i):
        @pl.when(i < count)
        def _():
            for copy in copies(i):
                copy.start()

    for i in range(BUFFERS - 1):
        start(jnp.int32(i))

    def step(i, carry):
        start(i + BUFFERS - 1)
        for copy in copies(i):
            copy.wait()
        right_high[i], right_low[i] = split(right_buf[lax.rem(i, BUFFERS)].T)
        return carry

    lax.fori_loop(0, count, step, 0)


def packed_rows(rows):
    return ((rows + 15) // 16) * 16


def matvec_kernel(k, cells, mpo_count, *refs):
    refs = list(refs)
    meta_ref = refs.pop(0)
    left_high, left_low, right_high, right_low = [refs.pop(0) for _ in range(4)]
    totals = [(refs.pop(0), refs.pop(0)) for _ in range(k)]
    raw = [[refs.pop(0) for _ in range(4)] for _ in range(max(k, 1))]
    images = [[refs.pop(0) for _ in range(4)] for _ in range(k)]
    precond = [refs.pop(0) for _ in range(4)] if k else []
    out_ref, small_ref = refs.pop(0), refs.pop(0)
    new_refs = [refs.pop(0) for _ in range(4)] if k else raw[0]
    high_ref, low_ref, mid_high, mid_low = refs
    states, width = out_ref.shape
    count, rows, cols = meta_ref[COUNT], meta_ref[ROWS], meta_ref[COLS]
    stride = packed_rows(rows)

    if k:
        numbers = Scalars(totals, cells)
        theta = numbers.proj[k - 1, k - 1][:, :1]
    zero = jnp.zeros((8, width), F32)

    def fold(value):
        return jnp.sum(value.reshape(CHUNK // 8, 8, width), axis=0)

    def prepare(slot, first, last, carry):
        def step(i, carry):
            at = pl.ds(pl.multiple_of(i * CHUNK, CHUNK), CHUNK)
            if k:
                basis = numbers.basis(k - 1, [r[slot][at, :] for r in raw])
                image = numbers.basis(k - 1, [r[slot][at, :] for r in images])
                value = (image[-1] - theta * basis[-1]) / jnp.maximum(
                    precond[slot][at, :] - theta, 1.0
                )
                new_refs[slot][at, :] = value
            else:
                basis, image = [], []
                value = raw[0][slot][at, :]
            high, low = split(value)
            high_ref[slot, at, :] = high
            low_ref[slot, at, :] = low
            terms = [value * value]
            if slot == OWN:
                terms += [value * b for b in basis] + [value * g for g in image]
            return tuple(c + fold(t) for c, t in zip(carry, terms))

        return lax.fori_loop(first, last, step, carry)

    def dot(a, b):
        return jnp.dot(a, b, preferred_element_type=F32)

    def first_stage(slot, depth):
        begin, end = meta_ref[FIRST + slot], meta_ref[FIRST + 1 + slot]
        tiles = ((end - begin) * stride + PACK - 1) // PACK
        deep = pl.ds(0, depth)

        def step(t, carry):
            at = pl.ds(pl.multiple_of(begin * stride + t * PACK, 16), PACK)
            high, low = left_high[at, deep], left_low[at, deep]
            p_high, p_low = high_ref[slot, deep, :], low_ref[slot, deep, :]
            mid = dot(high, p_low) + dot(low, p_high) + dot(high, p_high)
            mid_high[at, :], mid_low[at, :] = split(mid)
            return carry

        lax.fori_loop(0, tiles, step, 0)

    shallow = min(256, states)
    for slot in (OWN, SIB, FIRST_PAIR, SECOND_PAIR):

        def work(slot=slot):
            init = (zero,) * (1 + 2 * k if slot == OWN else 1)
            upper = prepare(slot, 0, shallow // CHUNK, init)
            lower = prepare(slot, shallow // CHUNK, states // CHUNK, init)
            deep = jnp.max(lower[0]) > 0.0
            pl.when(deep)(lambda: first_stage(slot, states))
            pl.when(jnp.logical_not(deep))(lambda: first_stage(slot, shallow))
            return [u + l for u, l in zip(upper, lower)]

        if slot == OWN:
            own = work()
        else:
            used = meta_ref[FIRST + 1 + slot] > meta_ref[FIRST + slot]
            pl.when(used | (slot == SIB))(lambda: (work(), None)[1])

    def clear(i, carry):
        at = pl.ds(pl.multiple_of(i * CHUNK, CHUNK), CHUNK)
        out_ref[at, :] = jnp.zeros((CHUNK, width), F32)
        return carry

    lax.fori_loop(0, states // CHUNK, clear, 0)

    def second_stage(size):
        def step(i, carry):
            at = pl.ds(pl.multiple_of(i * stride, 16), size)
            out_ref[pl.ds(0, size), :] += (
                dot(mid_high[at, :], right_low[i])
                + dot(mid_low[at, :], right_high[i])
                + dot(mid_high[at, :], right_high[i])
            )
            return carry

        lax.fori_loop(0, count, step, 0)

    sizes = list(range(TILE, states + 1, TILE))
    for size in sizes:
        pl.when((rows <= size) & (rows > size - TILE))(functools.partial(second_stage, size))

    def finish(i, carry):
        at = pl.ds(pl.multiple_of(i * CHUNK, CHUNK), CHUNK)
        mask = live_mask((CHUNK, width), i * CHUNK, rows, cols)
        value = jnp.where(mask, out_ref[at, :], 0.0)
        out_ref[at, :] = value
        basis = numbers.basis(k - 1, [r[OWN][at, :] for r in raw]) if k else []
        terms = [value * new_refs[OWN][at, :]] + [value * b for b in basis]
        return tuple(c + fold(t) for c, t in zip(carry, terms))

    late = lax.fori_loop(0, states // CHUNK, finish, (zero,) * (1 + k))

    def whole(value):
        return jnp.sum(jnp.sum(value, axis=1, keepdims=True), axis=0, keepdims=True)

    share = 1.0 / mpo_count
    entries = [whole(own[0]) * share, whole(late[0])]
    for j in range(2):
        entries.append(whole(own[1 + j]) * share if j < k else None)
    for j in range(2):
        entries.append(whole(late[1 + j]) if j < k else None)
    for j in range(2):
        entries.append(whole(own[1 + k + j]) * share if j < k else None)
    row_ids = lax.broadcasted_iota(jnp.int32, small_ref.shape, 0)
    small = jnp.zeros(small_ref.shape, F32)
    for index, entry in enumerate(entries):
        if entry is not None:
            small = jnp.where(row_ids == index, entry, small)
    small_ref[...] = small


def final_kernel(cells, meta_ref, *refs):
    totals = [refs[2 * i : 2 * i + 2] for i in range(MATVECS)]
    refs = refs[2 * MATVECS :]
    raw = [refs[2 * i : 2 * i + 2] for i in range(MATVECS)]
    images = [refs[2 * (MATVECS + i) : 2 * (MATVECS + i) + 2] for i in range(MATVECS)]
    basis_ref, images_ref, projected_ref = refs[4 * MATVECS :]
    sigma = meta_ref[SIGMA]
    numbers = Scalars(totals, cells)
    states, half = basis_ref.shape[2:]
    core = lax.axis_index("rsec")
    lanes = pl.ds(pl.multiple_of(core * half, half), half)
    for slot in (OWN, SIB):
        sector = sigma if slot == OWN else 1 - sigma

        def step(i, carry, slot=slot, sector=sector):
            at = pl.ds(pl.multiple_of(i * CHUNK, CHUNK), CHUNK)
            for fields, ref in ((raw, basis_ref), (images, images_ref)):
                done = numbers.basis(MATVECS - 1, [f[slot][at, lanes] for f in fields])
                for j, value in enumerate(done):
                    ref[j, sector, at, :] = value
            return carry

        lax.fori_loop(0, states // CHUNK, step, 0)
    shape = projected_ref.shape
    row_ids = lax.broadcasted_iota(jnp.int32, shape, 0)
    col_ids = lax.broadcasted_iota(jnp.int32, shape, 1)
    out = jnp.zeros(shape, F32)
    for i in range(MATVECS):
        for j in range(MATVECS):
            out = jnp.where((row_ids == i) & (col_ids == j), numbers.proj[i, j][:, :1], out)
    projected_ref[...] = out


def per_device(
    wavefunction, left_env, right_env, precond_diag, down_charge, bond_mask, left_size, right_size
):
    sectors, states, columns = wavefunction.shape
    bonds = left_env.shape[0]
    lsec_count = lax.axis_size("lsec")
    mpo_count = lax.axis_size("mpo")
    assert sectors == 2 and lax.axis_size("rsec") == 2
    width = 2 * columns
    cells = float(lsec_count * sectors * states * width)
    field = jax.ShapeDtypeStruct((states, width), F32)
    small = jax.ShapeDtypeStruct((8, 128), F32)
    params = pltpu.CompilerParams(vmem_limit_bytes=24 * 2**20)

    swap = [(0, 1), (1, 0)]
    first_pairs = [(i, i ^ 1) for i in range(lsec_count) if i ^ 1 < lsec_count]
    second_pairs = [(i, j) for a in range(1, lsec_count - 1, 2) for i, j in ((a, a + 1), (a + 1, a))]
    anywhere = pl.BlockSpec(memory_space=pl.ANY)
    in_hbm = pl.BlockSpec(memory_space=pltpu.HBM)

    def neighbours(value):
        return lax.ppermute(value, "lsec", first_pairs), lax.ppermute(value, "lsec", second_pairs)

    wave_all = lax.all_gather(wavefunction, "rsec", axis=2, tiled=True)
    right_send, _ = lax.optimization_barrier((right_env, wave_all))
    right_far = lax.ppermute(right_send, "rsec", swap)
    mask_rows = bond_mask.T
    down_charge, mask_rows, left_size, right_size = [
        pltpu.with_memory_space_constraint(x, pltpu.HBM)
        for x in (down_charge, mask_rows, left_size, right_size)
    ]
    own = pl.pallas_call(
        first_kernel,
        out_shape=field,
        in_specs=[in_hbm] * 3 + [whole_vmem()],
        out_specs=whole_vmem(),
        scratch_shapes=[
            pltpu.SMEM(down_charge.shape, jnp.int32),
            pltpu.SMEM(left_size.shape, jnp.int32),
            pltpu.SMEM(right_size.shape, jnp.int32),
            pltpu.SemaphoreType.DMA((3,)),
        ],
        compiler_params=params,
        name="first",
    )(down_charge, left_size, right_size, wave_all)
    near_waves = neighbours(own)
    sib, meta = pl.pallas_call(
        functools.partial(prep_kernel, lsec_count, bonds),
        out_shape=(field, jax.ShapeDtypeStruct((LIST + bonds,), jnp.int32)),
        in_specs=[in_hbm] * 4 + [whole_vmem()],
        out_specs=(whole_vmem(), whole_smem()),
        scratch_shapes=[
            pltpu.SMEM(down_charge.shape, jnp.int32),
            pltpu.SMEM(mask_rows.shape, jnp.int32),
            pltpu.SMEM(left_size.shape, jnp.int32),
            pltpu.SMEM(right_size.shape, jnp.int32),
            pltpu.SemaphoreType.DMA((4,)),
        ],
        compiler_params=params,
        name="prep",
    )(down_charge, mask_rows, left_size, right_size, wave_all)
    raw = [(own, sib, *near_waves)]
    diag_send, _ = lax.optimization_barrier((precond_diag, sib))
    diag_far = lax.ppermute(diag_send, "rsec", swap)
    diag_own, diag_sib = pl.pallas_call(
        diag_kernel,
        out_shape=(field,) * 2,
        in_specs=[whole_smem()] + [whole_vmem()] * 2,
        out_specs=(whole_vmem(),) * 2,
        compiler_params=params,
        name="diag",
    )(meta, pltpu.with_memory_space_constraint(precond_diag, pltpu.HBM), diag_far)

    def join(value, part):
        if mpo_count != 2 or lsec_count != 4:
            total = lax.psum(part, ("lsec", "mpo", "rsec"))
            return lax.psum(value, "mpo"), (total, jnp.zeros_like(total))
        far = lax.ppermute(value, "mpo", swap)
        part = part + lax.ppermute(part, "rsec", swap)
        parts = [lax.ppermute(part, "lsec", [(i, i ^ x) for i in range(4)]) for x in (1, 2, 3)]
        part = (part + parts[0]) + (parts[1] + parts[2])
        return value + far, (part, lax.ppermute(part, "mpo", swap))

    packed = bonds * states + states
    lefts = pl.pallas_call(
        left_kernel,
        out_shape=(pltpu.VMEM((packed, states), BF16),) * 2,
        in_specs=[whole_smem(), anywhere],
        out_specs=(whole_vmem(),) * 2,
        scratch_shapes=[
            pltpu.VMEM((BUFFERS, states, states), F32),
            pltpu.SemaphoreType.DMA((states // TILE, BUFFERS)),
        ],
        compiler_params=params,
        cost_estimate=pl.CostEstimate(flops=0, transcendentals=0, bytes_accessed=bonds * states * states * 4),
        name="left",
    )(meta, left_env)
    rights = pl.pallas_call(
        right_kernel,
        out_shape=(pltpu.VMEM((bonds, width, width), BF16),) * 2,
        in_specs=[whole_smem(), anywhere, anywhere],
        out_specs=(whole_vmem(),) * 2,
        scratch_shapes=[
            pltpu.VMEM((BUFFERS, width, width), F32),
            pltpu.SemaphoreType.DMA((2, BUFFERS)),
        ],
        compiler_params=params,
        cost_estimate=pl.CostEstimate(flops=0, transcendentals=0, bytes_accessed=bonds * width * width * 8),
        name="right",
    )(meta, right_env, right_far)
    blocks = (*lefts, *rights)

    def matvec(k, inputs):
        out_shape = [field, small] + ([field] * 4 if k else [])
        return pl.pallas_call(
            functools.partial(matvec_kernel, k, cells, mpo_count),
            out_shape=tuple(out_shape),
            in_specs=[whole_smem()] + [whole_vmem()] * (4 + len(inputs)),
            out_specs=tuple([whole_vmem()] * len(out_shape)),
            scratch_shapes=[
                pltpu.VMEM((4, states, width), BF16),
                pltpu.VMEM((4, states, width), BF16),
                pltpu.VMEM((packed, width), BF16),
                pltpu.VMEM((packed, width), BF16),
            ],
            compiler_params=params,
            cost_estimate=pl.CostEstimate(
                flops=2 * 3 * bonds * states * width * (states + width),
                transcendentals=0,
                bytes_accessed=bonds * states * states,
            ),
            name=f"matvec{k}",
        )(meta, *blocks, *inputs)

    totals = []
    images = []
    for k in range(MATVECS):
        if k == 0:
            value, part = matvec(0, list(raw[0]))
        else:
            flat_raw = [x for group in raw for x in group]
            flat_images = [x for group in images for x in group]
            value, part, *fresh = matvec(k, [*totals, *flat_raw, *flat_images, *precond])
            raw.append(tuple(fresh))
        if k == 0:
            diag_send, value = lax.optimization_barrier((diag_own, value))
            near_diags = neighbours(diag_send)
        value, total = join(value, part)
        if k == 0:
            value, near_diags = lax.optimization_barrier((value, near_diags))
            precond = (diag_own, diag_sib, *near_diags)
        totals += total
        beside = lax.ppermute(value, "rsec", swap)
        if k + 1 < MATVECS:
            images.append((value, beside, *neighbours(value)))
        else:
            images.append((value, beside))

    flat = [x for group in raw for x in group[:2]] + [x for group in images for x in group[:2]]
    out = jax.ShapeDtypeStruct((MATVECS, sectors, states, columns), F32)
    return pl.pallas_call(
        functools.partial(final_kernel, cells),
        out_shape=(out, out, jax.ShapeDtypeStruct((MATVECS, MATVECS), F32)),
        in_specs=[whole_smem()] + [whole_vmem()] * (2 * MATVECS + len(flat)),
        out_specs=(whole_vmem(),) * 3,
        compiler_params=params,
        name="final",
    )(meta, *totals, *flat)


def solution(mesh):
    placed = (
        P(("grp", "lsec"), None, "rsec"),
        P("mpo", ("grp", "lsec"), None, None),
        P("mpo", ("grp", "lsec"), "rsec", None),
        P(("grp", "lsec"), None, "rsec"),
        P("grp"),
        P("mpo", ("grp", "lsec")),
        P(("grp", "lsec")),
        P(("grp", "lsec")),
    )
    return jax.shard_map(
        per_device,
        mesh=mesh,
        in_specs=placed,
        out_specs=(
            P(None, ("grp", "lsec"), None, "rsec"),
            P(None, ("grp", "lsec"), None, "rsec"),
            P("grp", None),
        ),
        check_vma=False,
    )
```

```python
import functools

import jax
import jax.numpy as jnp
from jax import lax
from jax.experimental import pallas as pl
from jax.experimental.pallas import tpu as pltpu
from jax.sharding import PartitionSpec as P

EPSILON = 1e-06
MATVECS = 3
F32 = jnp.float32
BF16 = jnp.bfloat16
SIGMA, COUNT, ROWS, COLS, FIRST, SIB_ROWS, SIB_COLS, LIST = 0, 1, 2, 3, 4, 9, 10, 16
OWN, SIB, FIRST_PAIR, SECOND_PAIR = 0, 1, 2, 3
CHUNK = 64
TILE = 128
SIDE = 256
HALF = 128
NOTE = 8
PACK = 256
BUFFERS = 4


def whole_vmem():
    return pl.BlockSpec(memory_space=pltpu.VMEM)


def whole_smem():
    return pl.BlockSpec(memory_space=pltpu.SMEM)


def split(value):
    high = value.astype(BF16)
    return high, (value - high.astype(F32)).astype(BF16)


def orientation(down_ref, place):
    def step(i, flips):
        straight = (down_ref[2 * i] == down_ref[2 * i - 2]) | (
            down_ref[2 * i + 1] == down_ref[2 * i - 1]
        )
        return jnp.where(straight, flips, 1 - flips)

    return lax.fori_loop(1, place + 1, step, jnp.int32(0))


def live_mask(shape, row0, rows, cols):
    row_ids = row0 + lax.broadcasted_iota(jnp.int32, shape, 0)
    col_ids = lax.broadcasted_iota(jnp.int32, shape, 1)
    return (row_ids < rows) & (col_ids < cols)


def read_small(pairs, sems):
    copies = [pltpu.make_async_copy(*pair, sems.at[i]) for i, pair in enumerate(pairs)]
    for copy in copies:
        copy.start()
    for copy in copies:
        copy.wait()


def masked_block(out_ref, wave_ref, slot, rows, cols):
    states, width = wave_ref.shape[1:]

    def fill(i, carry):
        at = pl.ds(pl.multiple_of(i * CHUNK, CHUNK), CHUNK)
        mask = live_mask((CHUNK, width), i * CHUNK, rows, cols)
        out_ref[at, :] = jnp.where(mask, wave_ref[slot, at, :], 0.0)
        return carry

    lax.fori_loop(0, states // CHUNK, fill, 0)


def first_kernel(down_in, left_in, right_in, wave_ref, own_ref, down_ref, left_size_ref,
                 right_size_ref, sems):
    read_small(((down_in, down_ref), (left_in, left_size_ref), (right_in, right_size_ref)), sems)
    sigma = lax.axis_index("rsec") ^ orientation(down_ref, lax.axis_index("lsec"))
    rows, cols = left_size_ref[sigma], right_size_ref[sigma]
    masked_block(own_ref, wave_ref, sigma, rows, cols)
    note = (NOTE, own_ref.shape[1])
    row_ids = lax.broadcasted_iota(jnp.int32, note, 0)
    states = wave_ref.shape[1]
    own_ref[pl.ds(states, NOTE), :] = jnp.where(row_ids == 0, rows, cols).astype(F32)


def prep_kernel(lsec_count, bonds, down_in, mask_in, left_in, right_in, wave_ref, own_ref,
                sib_ref, meta_ref, down_ref, mask_ref, left_size_ref, right_size_ref, sems):
    read_small(
        ((down_in, down_ref), (mask_in, mask_ref), (left_in, left_size_ref), (right_in, right_size_ref)),
        sems,
    )
    place = lax.axis_index("lsec")
    core = lax.axis_index("rsec")
    first_bond = lax.axis_index("mpo") * bonds
    sigma = core ^ orientation(down_ref, place)
    own_down = down_ref[2 * place + sigma]
    sib_down = down_ref[2 * place + 1 - sigma]
    before = jnp.maximum(place - 1, 0)
    after = jnp.minimum(place + 1, lsec_count - 1)
    prev_down = down_ref[2 * before + (core ^ orientation(down_ref, before))]
    next_down = down_ref[2 * after + (core ^ orientation(down_ref, after))]
    has_prev = (place > 0) & (prev_down == own_down)
    has_next = (place < lsec_count - 1) & (next_down == own_down)
    odd = lax.rem(place, 2)
    has_lower = sib_down == own_down - 1
    has_upper = sib_down == own_down + 1

    def gather(slot, count):
        meta_ref[FIRST + slot] = count

        def step(bond, count):
            kind = lax.rem(first_bond + bond, 5)
            if slot == OWN:
                there = kind == 0
            elif slot == SIB:
                there = ((kind == 3) & has_lower) | ((kind == 4) & has_upper)
            else:
                lower = odd if slot == FIRST_PAIR else 1 - odd
                there = ((kind == 1) & has_prev & (lower == 1)) | (
                    (kind == 2) & has_next & (lower == 0)
                )
            there = there & (mask_ref[sigma, bond] > 0)

            @pl.when(there)
            def _():
                meta_ref[LIST + count] = bond * 4 + slot

            return count + there.astype(jnp.int32)

        return lax.fori_loop(0, bonds, step, count)

    count = jnp.int32(0)
    for slot in (OWN, SIB, FIRST_PAIR, SECOND_PAIR):
        count = gather(slot, count)
    meta_ref[FIRST + 4] = count
    rows, cols = left_size_ref[sigma], right_size_ref[sigma]
    meta_ref[SIGMA] = sigma
    meta_ref[COUNT] = count
    meta_ref[ROWS] = rows
    meta_ref[COLS] = cols
    meta_ref[SIB_ROWS] = left_size_ref[1 - sigma]
    meta_ref[SIB_COLS] = right_size_ref[1 - sigma]
    masked_block(sib_ref, wave_ref, 1 - sigma, left_size_ref[1 - sigma], right_size_ref[1 - sigma])


def diag_kernel(meta_ref, diag_ref, diag_far, diag_own, diag_sib):
    states, width = diag_own.shape
    half = width // 2
    sigma, core = meta_ref[SIGMA], lax.axis_index("rsec")
    near = pl.ds(pl.multiple_of(core * half, half), half)
    away = pl.ds(pl.multiple_of((1 - core) * half, half), half)
    for out_ref, slot in ((diag_own, sigma), (diag_sib, 1 - sigma)):

        def fill(i, carry, out_ref=out_ref, slot=slot):
            at = pl.ds(pl.multiple_of(i * CHUNK, CHUNK), CHUNK)
            out_ref[at, near] = diag_ref[slot, at, :]
            out_ref[at, away] = diag_far[slot, at, :]
            return carry

        lax.fori_loop(0, states // CHUNK, fill, 0)


def row(value, index):
    return value[index : index + 1, :]


class Scalars:
    def __init__(self, totals, cells):
        self.proj = {}
        self.gram = {}
        self.norm = []
        self.corr = []
        for k, total in enumerate(totals):
            value = (total[0][...] + total[1][...]) / cells
            size, inner = row(value, 0), row(value, 1)
            a = [row(value, 2 + j) for j in range(k)]
            e = [row(value, 4 + j) for j in range(k)]
            f = [row(value, 6 + j) for j in range(k)]
            length = size
            theta = inner
            for j in range(k):
                length = length - 2.0 * a[j] * a[j]
                theta = theta - a[j] * e[j] - a[j] * f[j]
            for i in range(k):
                for j in range(k):
                    length = length + a[i] * a[j] * self.gram[i, j]
                    theta = theta + a[i] * a[j] * self.proj[i, j]
            length = jnp.maximum(length, 0.0)
            square = length + EPSILON
            norm = jnp.sqrt(square)
            for j in range(k):
                up, down, both = e[j], f[j], a[j]
                for i in range(k):
                    up = up - a[i] * self.proj[j, i]
                    down = down - a[i] * self.proj[i, j]
                    both = both - a[i] * self.gram[i, j]
                self.proj[j, k] = up / norm
                self.proj[k, j] = down / norm
                self.gram[j, k] = self.gram[k, j] = both / norm
            self.proj[k, k] = theta / square
            self.gram[k, k] = length / square
            self.norm.append(norm)
            self.corr.append(a)

    def basis(self, k, fields):
        done = []
        for step in range(k + 1):
            value = fields[step]
            for j in range(step):
                value = value - self.corr[step][j][:, :1] * done[j]
            done.append(value / self.norm[step][:, :1])
        return done


def left_kernel(meta_ref, left_ref, left_high, left_low, left_tail, left_buf, sems):
    states = left_buf.shape[1]
    sigma, count, rows = meta_ref[SIGMA], meta_ref[COUNT], meta_ref[ROWS]
    stride = packed_rows(rows)

    def each(i, act):
        bond = meta_ref[LIST + i] // 4
        at = lax.rem(i, BUFFERS)
        for p in range(states // TILE):
            part = pl.ds(p * TILE, TILE)

            @pl.when(rows > p * TILE)
            def _(part=part, p=p):
                act(
                    pltpu.make_async_copy(
                        left_ref.at[bond, sigma, part], left_buf.at[at, part], sems.at[p, at]
                    )
                )

    def start(i):
        @pl.when(i < count)
        def _():
            each(i, lambda copy: copy.start())

    for i in range(BUFFERS - 1):
        start(jnp.int32(i))

    def step(i, carry):
        at = lax.rem(i, BUFFERS)
        start(i + BUFFERS - 1)
        each(i, lambda copy: copy.wait())

        def chunk(t, inner):
            high, low = split(left_buf[at, pl.ds(pl.multiple_of(t * CHUNK, CHUNK), CHUNK), :])
            to = pl.ds(pl.multiple_of(i * stride + t * CHUNK, 16), CHUNK)
            left_high[to, :] = high[:, :SIDE]
            left_low[to, :] = low[:, :SIDE]
            left_tail[to, :] = jnp.concatenate([high[:, SIDE:], low[:, SIDE:]], axis=1)
            return inner

        lax.fori_loop(0, (rows + CHUNK - 1) // CHUNK, chunk, 0)
        return carry

    lax.fori_loop(0, count, step, 0)


def right_kernel(meta_ref, right_ref, far_ref, right_high, right_low, right_buf, sems):
    half = right_ref.shape[2]
    sigma, count = meta_ref[SIGMA], meta_ref[COUNT]
    core = lax.axis_index("rsec")
    narrow = meta_ref[COLS] <= HALF

    def each(i, act):
        bond = meta_ref[LIST + i] // 4
        at = lax.rem(i, BUFFERS)
        for ref, place, sem in ((right_ref, core, 0), (far_ref, 1 - core, 1)):
            part = pl.ds(pl.multiple_of(place * half, half), half)

            @pl.when(jnp.logical_not(narrow) | (place == 0))
            def _(ref=ref, part=part, sem=sem):
                act(
                    pltpu.make_async_copy(
                        ref.at[bond, sigma], right_buf.at[at, part], sems.at[sem, at]
                    )
                )

    def start(i):
        @pl.when(i < count)
        def _():
            each(i, lambda copy: copy.start())

    for i in range(BUFFERS - 1):
        start(jnp.int32(i))

    def step(i, carry):
        at = lax.rem(i, BUFFERS)
        start(i + BUFFERS - 1)
        each(i, lambda copy: copy.wait())

        @pl.when(narrow)
        def _():
            high, low = split(right_buf[at, pl.ds(0, HALF), :].T)
            right_high[i] = jnp.concatenate([high, low], axis=1)

        @pl.when(jnp.logical_not(narrow))
        def _():
            right_high[i], right_low[i] = split(right_buf[at].T)

        return carry

    lax.fori_loop(0, count, step, 0)


def packed_rows(rows):
    return ((rows + 15) // 16) * 16


def matvec_kernel(k, cells, mpo_count, *refs):
    refs = list(refs)
    meta_ref = refs.pop(0)
    left_high, left_low, left_tail, right_high, right_low = [refs.pop(0) for _ in range(5)]
    size_ref = refs.pop(0) if k else None
    totals = [(refs.pop(0), refs.pop(0)) for _ in range(k)]
    raw = [[refs.pop(0) for _ in range(4)] for _ in range(max(k, 1))]
    images = [[refs.pop(0) for _ in range(4)] for _ in range(k)]
    precond = [refs.pop(0) for _ in range(4)] if k else []
    out_ref, small_ref = refs.pop(0), refs.pop(0)
    size_ref = size_ref if k else refs.pop(0)
    new_refs = [refs.pop(0) for _ in range(4)] if k else raw[0]
    high_ref, low_ref, tail_ref, mid_high, mid_low = refs
    states, width = out_ref.shape
    count, rows, cols = meta_ref[COUNT], meta_ref[ROWS], meta_ref[COLS]
    stride = packed_rows(rows)

    if k:
        numbers = Scalars(totals, cells)
        theta = numbers.proj[k - 1, k - 1][:, :1]
    zero = jnp.zeros((8, width), F32)

    def fold(value):
        return jnp.sum(value.reshape(CHUNK // 8, 8, width), axis=0)

    def prepare(slot, first, last, carry):
        def step(i, carry):
            at = pl.ds(pl.multiple_of(i * CHUNK, CHUNK), CHUNK)
            if k:
                basis = numbers.basis(k - 1, [r[slot][at, :] for r in raw])
                image = numbers.basis(k - 1, [r[slot][at, :] for r in images])
                value = (image[-1] - theta * basis[-1]) / jnp.maximum(
                    precond[slot][at, :] - theta, 1.0
                )
                new_refs[slot][at, :] = value
            else:
                basis, image = [], []
                value = raw[0][slot][at, :]
            high, low = split(value)
            high_ref[slot, at, :] = high
            low_ref[slot, at, :] = low
            terms = [value * value]
            if slot == OWN:
                terms += [value * b for b in basis] + [value * g for g in image]
            return tuple(c + fold(t) for c, t in zip(carry, terms))

        return lax.fori_loop(first, last, step, carry)

    def dot(a, b):
        return jnp.dot(a, b, preferred_element_type=F32)

    if not k:
        size_ref[2 * OWN], size_ref[2 * OWN + 1] = rows, cols
        size_ref[2 * SIB], size_ref[2 * SIB + 1] = meta_ref[SIB_ROWS], meta_ref[SIB_COLS]
        for slot in (FIRST_PAIR, SECOND_PAIR):
            note = raw[0][slot][pl.ds(states, NOTE), :HALF]
            size_ref[2 * slot] = jnp.max(note[:1]).astype(jnp.int32)
            size_ref[2 * slot + 1] = jnp.max(note[1:]).astype(jnp.int32)
    twice = functools.partial(jnp.concatenate, axis=0)

    def first_stage(slot, deep, narrow):
        begin, end = meta_ref[FIRST + slot], meta_ref[FIRST + 1 + slot]
        tiles = ((end - begin) * stride + PACK - 1) // PACK
        top, rest = pl.ds(0, SIDE), pl.ds(SIDE, states - SIDE)
        if narrow:
            high_ref[slot, :, HALF:] = low_ref[slot, :, :HALF]
        if deep:
            tail = high_ref[slot, rest, :]
            tail_ref[...] = twice([tail, tail])

        def step(t, carry):
            at = pl.ds(pl.multiple_of(begin * stride + t * PACK, 16), PACK)
            high, low = left_high[at, :], left_low[at, :]
            mid = dot(high, high_ref[slot, top, :])
            if deep:
                mid = mid + dot(left_tail[at, :], tail_ref[...])
            if narrow:
                mid = mid[:, :HALF] + mid[:, HALF:] + dot(low, high_ref[slot, top, :HALF])
                mid_high[at, :] = jnp.concatenate(split(mid), axis=1)
            else:
                mid = mid + dot(low, high_ref[slot, top, :]) + dot(high, low_ref[slot, top, :])
                if deep:
                    mid = mid + dot(left_tail[at, : states - SIDE], low_ref[slot, rest, :])
                mid_high[at, :], mid_low[at, :] = split(mid)
            return carry

        lax.fori_loop(0, tiles, step, 0)

    def both(test, action):
        pl.when(test)(lambda: action(True))
        pl.when(jnp.logical_not(test))(lambda: action(False))

    for slot in (OWN, SIB, FIRST_PAIR, SECOND_PAIR):

        def work(slot=slot):
            sums = prepare(slot, 0, states // CHUNK, (zero,) * (1 + 2 * k if slot == OWN else 1))
            both(
                size_ref[2 * slot] > SIDE,
                lambda deep: both(
                    size_ref[2 * slot + 1] <= HALF, lambda narrow: first_stage(slot, deep, narrow)
                ),
            )
            return sums

        if slot == OWN:
            own = work()
        else:
            used = meta_ref[FIRST + 1 + slot] > meta_ref[FIRST + slot]
            pl.when(used | (slot == SIB))(lambda: (work(), None)[1])

    def clear(i, carry):
        at = pl.ds(pl.multiple_of(i * CHUNK, CHUNK), CHUNK)
        out_ref[at, :] = jnp.zeros((CHUNK, width), F32)
        return carry

    lax.fori_loop(0, states // CHUNK, clear, 0)

    def second_stage(size, thin):
        to = pl.ds(0, size)

        def step(i, carry):
            at = pl.ds(pl.multiple_of(i * stride, 16), size)
            slot = lax.rem(meta_ref[LIST + i], 4)

            def add(narrow):
                high = mid_high[at, :]
                if narrow:
                    part = right_high[i, :HALF, :]
                    value = dot(high, twice([part, part]))
                    if not thin:
                        value = value + dot(high[:, :HALF], right_low[i, :HALF, :])
                else:
                    value = dot(high, right_high[i])
                    if not thin:
                        value = value + dot(high, right_low[i]) + dot(mid_low[at, :], right_high[i])
                if thin:
                    value = value[:, :HALF] + value[:, HALF:]
                    if not narrow:
                        value = value + dot(mid_low[at, :], right_high[i, :, :HALF])
                    out_ref[to, :HALF] += value
                else:
                    out_ref[to, :] += value

            both(size_ref[2 * slot + 1] <= HALF, add)
            return carry

        lax.fori_loop(0, count, step, 0)

    for size in range(TILE, states + 1, TILE):
        pl.when((rows <= size) & (rows > size - TILE))(
            lambda size=size: both(cols <= HALF, functools.partial(second_stage, size))
        )

    def finish(i, carry):
        at = pl.ds(pl.multiple_of(i * CHUNK, CHUNK), CHUNK)
        mask = live_mask((CHUNK, width), i * CHUNK, rows, cols)
        value = jnp.where(mask, out_ref[at, :], 0.0)
        out_ref[at, :] = value
        basis = numbers.basis(k - 1, [r[OWN][at, :] for r in raw]) if k else []
        terms = [value * new_refs[OWN][at, :]] + [value * b for b in basis]
        return tuple(c + fold(t) for c, t in zip(carry, terms))

    late = lax.fori_loop(0, states // CHUNK, finish, (zero,) * (1 + k))

    def whole(value):
        return jnp.sum(jnp.sum(value, axis=1, keepdims=True), axis=0, keepdims=True)

    share = 1.0 / mpo_count
    entries = [whole(own[0]) * share, whole(late[0])]
    for j in range(2):
        entries.append(whole(own[1 + j]) * share if j < k else None)
    for j in range(2):
        entries.append(whole(late[1 + j]) if j < k else None)
    for j in range(2):
        entries.append(whole(own[1 + k + j]) * share if j < k else None)
    row_ids = lax.broadcasted_iota(jnp.int32, small_ref.shape, 0)
    small = jnp.zeros(small_ref.shape, F32)
    for index, entry in enumerate(entries):
        if entry is not None:
            small = jnp.where(row_ids == index, entry, small)
    small_ref[...] = small


def join_kernel(a_ref, b_ref, s0, s1, s2, s3, out_ref, small_ref):
    small_ref[...] = (s0[...] + s1[...]) + (s2[...] + s3[...])

    def step(i, carry):
        at = pl.ds(pl.multiple_of(i * CHUNK, CHUNK), CHUNK)
        out_ref[at, :] = a_ref[at, :] + b_ref[at, :]
        return carry

    lax.fori_loop(0, out_ref.shape[0] // CHUNK, step, 0)


def final_kernel(cells, meta_ref, *refs):
    totals = [refs[2 * i : 2 * i + 2] for i in range(MATVECS)]
    refs = refs[2 * MATVECS :]
    raw = [refs[2 * i : 2 * i + 2] for i in range(MATVECS)]
    images = [refs[2 * (MATVECS + i) : 2 * (MATVECS + i) + 2] for i in range(MATVECS)]
    basis_ref, images_ref, projected_ref = refs[4 * MATVECS :]
    sigma = meta_ref[SIGMA]
    numbers = Scalars(totals, cells)
    states, half = basis_ref.shape[2:]
    core = lax.axis_index("rsec")
    lanes = pl.ds(pl.multiple_of(core * half, half), half)
    for slot in (OWN, SIB):
        sector = sigma if slot == OWN else 1 - sigma

        def step(i, carry, slot=slot, sector=sector):
            at = pl.ds(pl.multiple_of(i * CHUNK, CHUNK), CHUNK)
            for fields, ref in ((raw, basis_ref), (images, images_ref)):
                done = numbers.basis(MATVECS - 1, [f[slot][at, lanes] for f in fields])
                for j, value in enumerate(done):
                    ref[j, sector, at, :] = value
            return carry

        lax.fori_loop(0, states // CHUNK, step, 0)
    shape = projected_ref.shape
    row_ids = lax.broadcasted_iota(jnp.int32, shape, 0)
    col_ids = lax.broadcasted_iota(jnp.int32, shape, 1)
    out = jnp.zeros(shape, F32)
    for i in range(MATVECS):
        for j in range(MATVECS):
            out = jnp.where((row_ids == i) & (col_ids == j), numbers.proj[i, j][:, :1], out)
    projected_ref[...] = out


def per_device(
    wavefunction, left_env, right_env, precond_diag, down_charge, bond_mask, left_size, right_size
):
    sectors, states, columns = wavefunction.shape
    bonds = left_env.shape[0]
    lsec_count = lax.axis_size("lsec")
    mpo_count = lax.axis_size("mpo")
    assert sectors == 2 and lax.axis_size("rsec") == 2
    width = 2 * columns
    cells = float(lsec_count * sectors * states * width)
    field = jax.ShapeDtypeStruct((states, width), F32)
    small = jax.ShapeDtypeStruct((8, 128), F32)
    params = pltpu.CompilerParams(vmem_limit_bytes=24 * 2**20)

    swap = [(0, 1), (1, 0)]
    first_pairs = [(i, i ^ 1) for i in range(lsec_count) if i ^ 1 < lsec_count]
    second_pairs = [(i, j) for a in range(1, lsec_count - 1, 2) for i, j in ((a, a + 1), (a + 1, a))]
    anywhere = pl.BlockSpec(memory_space=pl.ANY)
    in_hbm = pl.BlockSpec(memory_space=pltpu.HBM)

    def neighbours(value):
        return lax.ppermute(value, "lsec", first_pairs), lax.ppermute(value, "lsec", second_pairs)

    wave_all = lax.all_gather(wavefunction, "rsec", axis=2, tiled=True)
    right_send, _ = lax.optimization_barrier((right_env, wave_all))
    right_far = lax.ppermute(right_send, "rsec", swap)
    mask_rows = bond_mask.T
    down_charge, mask_rows, left_size, right_size = [
        pltpu.with_memory_space_constraint(x, pltpu.HBM)
        for x in (down_charge, mask_rows, left_size, right_size)
    ]
    own = pl.pallas_call(
        first_kernel,
        out_shape=jax.ShapeDtypeStruct((states + NOTE, width), F32),
        in_specs=[in_hbm] * 3 + [whole_vmem()],
        out_specs=whole_vmem(),
        scratch_shapes=[
            pltpu.SMEM(down_charge.shape, jnp.int32),
            pltpu.SMEM(left_size.shape, jnp.int32),
            pltpu.SMEM(right_size.shape, jnp.int32),
            pltpu.SemaphoreType.DMA((3,)),
        ],
        compiler_params=params,
        name="first",
    )(down_charge, left_size, right_size, wave_all)
    near_waves = neighbours(own)
    sib, meta = pl.pallas_call(
        functools.partial(prep_kernel, lsec_count, bonds),
        out_shape=(field, jax.ShapeDtypeStruct((LIST + bonds,), jnp.int32)),
        in_specs=[in_hbm] * 4 + [whole_vmem(), anywhere],
        out_specs=(whole_vmem(), whole_smem()),
        scratch_shapes=[
            pltpu.SMEM(down_charge.shape, jnp.int32),
            pltpu.SMEM(mask_rows.shape, jnp.int32),
            pltpu.SMEM(left_size.shape, jnp.int32),
            pltpu.SMEM(right_size.shape, jnp.int32),
            pltpu.SemaphoreType.DMA((4,)),
        ],
        compiler_params=params,
        name="prep",
    )(down_charge, mask_rows, left_size, right_size, wave_all, own)
    raw = [(own, sib, *near_waves)]
    diag_send, _ = lax.optimization_barrier((precond_diag, sib))
    diag_far = lax.ppermute(diag_send, "rsec", swap)
    diag_own, diag_sib = pl.pallas_call(
        diag_kernel,
        out_shape=(field,) * 2,
        in_specs=[whole_smem()] + [whole_vmem()] * 2,
        out_specs=(whole_vmem(),) * 2,
        compiler_params=params,
        name="diag",
    )(meta, pltpu.with_memory_space_constraint(precond_diag, pltpu.HBM), diag_far)

    near_diags = neighbours(diag_own)

    def join(value, part):
        if mpo_count != 2 or lsec_count != 4:
            total = lax.psum(part, ("lsec", "mpo", "rsec"))
            return lax.psum(value, "mpo"), (total, jnp.zeros_like(total))
        far = lax.ppermute(value, "mpo", swap)
        part = part + lax.ppermute(part, "rsec", swap)
        parts = [lax.ppermute(part, "lsec", [(i, i ^ x) for i in range(4)]) for x in (1, 2, 3)]
        value, part = pl.pallas_call(
            join_kernel,
            out_shape=(field, small),
            in_specs=[whole_vmem()] * 6,
            out_specs=(whole_vmem(),) * 2,
            compiler_params=params,
            name="join",
        )(value, far, part, *parts)
        return value, (part, lax.ppermute(part, "mpo", swap))

    packed = bonds * states + states
    lefts = pl.pallas_call(
        left_kernel,
        out_shape=(
            pltpu.VMEM((packed, SIDE), BF16),
            pltpu.VMEM((packed, SIDE), BF16),
            pltpu.VMEM((packed, 2 * (states - SIDE)), BF16),
        ),
        in_specs=[whole_smem(), anywhere],
        out_specs=(whole_vmem(),) * 3,
        scratch_shapes=[
            pltpu.VMEM((BUFFERS, states, states), F32),
            pltpu.SemaphoreType.DMA((states // TILE, BUFFERS)),
        ],
        compiler_params=params,
        cost_estimate=pl.CostEstimate(flops=0, transcendentals=0, bytes_accessed=bonds * states * states * 4),
        name="left",
    )(meta, left_env)
    rights = pl.pallas_call(
        right_kernel,
        out_shape=(pltpu.VMEM((bonds, width, width), BF16),) * 2,
        in_specs=[whole_smem(), anywhere, anywhere],
        out_specs=(whole_vmem(),) * 2,
        scratch_shapes=[
            pltpu.VMEM((BUFFERS, width, width), F32),
            pltpu.SemaphoreType.DMA((2, BUFFERS)),
        ],
        compiler_params=params,
        cost_estimate=pl.CostEstimate(flops=0, transcendentals=0, bytes_accessed=bonds * width * width * 8),
        name="right",
    )(meta, right_env, right_far)
    blocks = (*lefts, *rights)

    sizes = []

    def matvec(k, inputs):
        out_shape = [field, small]
        out_specs = [whole_vmem()] * 2
        if k:
            out_shape += [field] * 4
            out_specs += [whole_vmem()] * 4
        else:
            out_shape.append(jax.ShapeDtypeStruct((8,), jnp.int32))
            out_specs.append(whole_smem())
        return pl.pallas_call(
            functools.partial(matvec_kernel, k, cells, mpo_count),
            out_shape=tuple(out_shape),
            in_specs=[whole_smem()] + [whole_vmem()] * len(blocks) + [whole_smem()] * len(sizes)
            + [whole_vmem()] * len(inputs),
            out_specs=tuple(out_specs),
            scratch_shapes=[
                pltpu.VMEM((4, states, width), BF16),
                pltpu.VMEM((4, states, width), BF16),
                pltpu.VMEM((2 * (states - SIDE), width), BF16),
                pltpu.VMEM((packed, width), BF16),
                pltpu.VMEM((packed, width), BF16),
            ],
            compiler_params=params,
            cost_estimate=pl.CostEstimate(
                flops=2 * 3 * bonds * states * width * (states + width),
                transcendentals=0,
                bytes_accessed=bonds * states * states,
            ),
            name=f"matvec{k}",
        )(meta, *blocks, *sizes, *inputs)

    totals = []
    images = []
    for k in range(MATVECS):
        if k == 0:
            value, part, size = matvec(0, list(raw[0]))
            sizes.append(size)
        else:
            flat_raw = [x for group in raw for x in group]
            flat_images = [x for group in images for x in group]
            value, part, *fresh = matvec(k, [*totals, *flat_raw, *flat_images, *precond])
            raw.append(tuple(fresh))
        if k == 0:
            value, near_diags = lax.optimization_barrier((value, near_diags))
            precond = (diag_own, diag_sib, *near_diags)
        value, total = join(value, part)
        totals += total
        beside = lax.ppermute(value, "rsec", swap)
        if k + 1 < MATVECS:
            images.append((value, beside, *neighbours(value)))
        else:
            images.append((value, beside))

    flat = [x for group in raw for x in group[:2]] + [x for group in images for x in group[:2]]
    out = jax.ShapeDtypeStruct((MATVECS, sectors, states, columns), F32)
    return pl.pallas_call(
        functools.partial(final_kernel, cells),
        out_shape=(out, out, jax.ShapeDtypeStruct((MATVECS, MATVECS), F32)),
        in_specs=[whole_smem()] + [whole_vmem()] * (2 * MATVECS + len(flat)),
        out_specs=(whole_vmem(),) * 3,
        compiler_params=params,
        name="final",
    )(meta, *totals, *flat)


def solution(mesh):
    placed = (
        P(("grp", "lsec"), None, "rsec"),
        P("mpo", ("grp", "lsec"), None, None),
        P("mpo", ("grp", "lsec"), "rsec", None),
        P(("grp", "lsec"), None, "rsec"),
        P("grp"),
        P("mpo", ("grp", "lsec")),
        P(("grp", "lsec")),
        P(("grp", "lsec")),
    )
    return jax.shard_map(
        per_device,
        mesh=mesh,
        in_specs=placed,
        out_specs=(
            P(None, ("grp", "lsec"), None, "rsec"),
            P(None, ("grp", "lsec"), None, "rsec"),
            P("grp", None),
        ),
        check_vma=False,
    )
```

```python
import functools

import jax
import jax.numpy as jnp
from jax import lax
from jax.experimental import pallas as pl
from jax.experimental.pallas import tpu as pltpu
from jax.sharding import PartitionSpec as P

EPSILON = 1e-06
MATVECS = 3
F32 = jnp.float32
BF16 = jnp.bfloat16
SIGMA, COUNT, ROWS, COLS, FIRST, SIB_ROWS, SIB_COLS, LIST = 0, 1, 2, 3, 4, 9, 10, 16
OWN, SIB, FIRST_PAIR, SECOND_PAIR = 0, 1, 2, 3
CHUNK = 64
TILE = 128
SIDE = 256
HALF = 128
NOTE = 8
PACK = 256
BUFFERS = 4


def whole_vmem():
    return pl.BlockSpec(memory_space=pltpu.VMEM)


def whole_smem():
    return pl.BlockSpec(memory_space=pltpu.SMEM)


def split(value):
    high = value.astype(BF16)
    return high, (value - high.astype(F32)).astype(BF16)


def orientation(down_ref, place):
    def step(i, flips):
        straight = (down_ref[2 * i] == down_ref[2 * i - 2]) | (
            down_ref[2 * i + 1] == down_ref[2 * i - 1]
        )
        return jnp.where(straight, flips, 1 - flips)

    return lax.fori_loop(1, place + 1, step, jnp.int32(0))


def live_mask(shape, row0, rows, cols):
    row_ids = row0 + lax.broadcasted_iota(jnp.int32, shape, 0)
    col_ids = lax.broadcasted_iota(jnp.int32, shape, 1)
    return (row_ids < rows) & (col_ids < cols)


def read_small(pairs, sems):
    copies = [pltpu.make_async_copy(*pair, sems.at[i]) for i, pair in enumerate(pairs)]
    for copy in copies:
        copy.start()
    for copy in copies:
        copy.wait()


def masked_block(out_ref, wave_ref, slot, rows, cols):
    states, width = wave_ref.shape[1:]

    def fill(i, carry):
        at = pl.ds(pl.multiple_of(i * CHUNK, CHUNK), CHUNK)
        mask = live_mask((CHUNK, width), i * CHUNK, rows, cols)
        out_ref[at, :] = jnp.where(mask, wave_ref[slot, at, :], 0.0)
        return carry

    lax.fori_loop(0, states // CHUNK, fill, 0)


def first_kernel(down_in, left_in, right_in, wave_ref, own_ref, down_ref, left_size_ref,
                 right_size_ref, sems):
    read_small(((down_in, down_ref), (left_in, left_size_ref), (right_in, right_size_ref)), sems)
    sigma = lax.axis_index("rsec") ^ orientation(down_ref, lax.axis_index("lsec"))
    rows, cols = left_size_ref[sigma], right_size_ref[sigma]
    masked_block(own_ref, wave_ref, sigma, rows, cols)
    note = (NOTE, own_ref.shape[1])
    row_ids = lax.broadcasted_iota(jnp.int32, note, 0)
    states = wave_ref.shape[1]
    own_ref[pl.ds(states, NOTE), :] = jnp.where(row_ids == 0, rows, cols).astype(F32)


def prep_kernel(lsec_count, bonds, down_in, mask_in, left_in, right_in, wave_ref, own_ref,
                sib_ref, meta_ref, down_ref, mask_ref, left_size_ref, right_size_ref, sems):
    read_small(
        ((down_in, down_ref), (mask_in, mask_ref), (left_in, left_size_ref), (right_in, right_size_ref)),
        sems,
    )
    place = lax.axis_index("lsec")
    core = lax.axis_index("rsec")
    first_bond = lax.axis_index("mpo") * bonds
    sigma = core ^ orientation(down_ref, place)
    own_down = down_ref[2 * place + sigma]
    sib_down = down_ref[2 * place + 1 - sigma]
    before = jnp.maximum(place - 1, 0)
    after = jnp.minimum(place + 1, lsec_count - 1)
    prev_down = down_ref[2 * before + (core ^ orientation(down_ref, before))]
    next_down = down_ref[2 * after + (core ^ orientation(down_ref, after))]
    has_prev = (place > 0) & (prev_down == own_down)
    has_next = (place < lsec_count - 1) & (next_down == own_down)
    odd = lax.rem(place, 2)
    has_lower = sib_down == own_down - 1
    has_upper = sib_down == own_down + 1

    def gather(slot, count):
        meta_ref[FIRST + slot] = count

        def step(bond, count):
            kind = lax.rem(first_bond + bond, 5)
            if slot == OWN:
                there = kind == 0
            elif slot == SIB:
                there = ((kind == 3) & has_lower) | ((kind == 4) & has_upper)
            else:
                lower = odd if slot == FIRST_PAIR else 1 - odd
                there = ((kind == 1) & has_prev & (lower == 1)) | (
                    (kind == 2) & has_next & (lower == 0)
                )
            there = there & (mask_ref[sigma, bond] > 0)

            @pl.when(there)
            def _():
                meta_ref[LIST + count] = bond * 4 + slot

            return count + there.astype(jnp.int32)

        return lax.fori_loop(0, bonds, step, count)

    count = jnp.int32(0)
    for slot in (OWN, SIB, FIRST_PAIR, SECOND_PAIR):
        count = gather(slot, count)
    meta_ref[FIRST + 4] = count
    rows, cols = left_size_ref[sigma], right_size_ref[sigma]
    meta_ref[SIGMA] = sigma
    meta_ref[COUNT] = count
    meta_ref[ROWS] = rows
    meta_ref[COLS] = cols
    meta_ref[SIB_ROWS] = left_size_ref[1 - sigma]
    meta_ref[SIB_COLS] = right_size_ref[1 - sigma]
    masked_block(sib_ref, wave_ref, 1 - sigma, left_size_ref[1 - sigma], right_size_ref[1 - sigma])


def diag_kernel(meta_ref, diag_ref, diag_far, diag_own, diag_sib):
    states, width = diag_own.shape
    half = width // 2
    sigma, core = meta_ref[SIGMA], lax.axis_index("rsec")
    near = pl.ds(pl.multiple_of(core * half, half), half)
    away = pl.ds(pl.multiple_of((1 - core) * half, half), half)
    for out_ref, slot in ((diag_own, sigma), (diag_sib, 1 - sigma)):

        def fill(i, carry, out_ref=out_ref, slot=slot):
            at = pl.ds(pl.multiple_of(i * CHUNK, CHUNK), CHUNK)
            out_ref[at, near] = diag_ref[slot, at, :]
            out_ref[at, away] = diag_far[slot, at, :]
            return carry

        lax.fori_loop(0, states // CHUNK, fill, 0)


def row(value, index):
    return value[index : index + 1, :]


class Scalars:
    def __init__(self, totals, cells):
        self.proj = {}
        self.gram = {}
        self.norm = []
        self.corr = []
        for k, total in enumerate(totals):
            value = (total[0][...] + total[1][...]) / cells
            size, inner = row(value, 0), row(value, 1)
            a = [row(value, 2 + j) for j in range(k)]
            e = [row(value, 4 + j) for j in range(k)]
            f = [row(value, 6 + j) for j in range(k)]
            length = size
            theta = inner
            for j in range(k):
                length = length - 2.0 * a[j] * a[j]
                theta = theta - a[j] * e[j] - a[j] * f[j]
            for i in range(k):
                for j in range(k):
                    length = length + a[i] * a[j] * self.gram[i, j]
                    theta = theta + a[i] * a[j] * self.proj[i, j]
            length = jnp.maximum(length, 0.0)
            square = length + EPSILON
            norm = jnp.sqrt(square)
            for j in range(k):
                up, down, both = e[j], f[j], a[j]
                for i in range(k):
                    up = up - a[i] * self.proj[j, i]
                    down = down - a[i] * self.proj[i, j]
                    both = both - a[i] * self.gram[i, j]
                self.proj[j, k] = up / norm
                self.proj[k, j] = down / norm
                self.gram[j, k] = self.gram[k, j] = both / norm
            self.proj[k, k] = theta / square
            self.gram[k, k] = length / square
            self.norm.append(norm)
            self.corr.append(a)

    def basis(self, k, fields):
        done = []
        for step in range(k + 1):
            value = fields[step]
            for j in range(step):
                value = value - self.corr[step][j][:, :1] * done[j]
            done.append(value / self.norm[step][:, :1])
        return done


def left_kernel(meta_ref, left_ref, left_high, left_low, left_tail, left_buf, sems):
    states = left_buf.shape[1]
    sigma, count, rows = meta_ref[SIGMA], meta_ref[COUNT], meta_ref[ROWS]
    stride = packed_rows(rows)

    def each(i, act):
        bond = meta_ref[LIST + i] // 4
        at = lax.rem(i, BUFFERS)
        for p in range(states // TILE):
            part = pl.ds(p * TILE, TILE)

            @pl.when(rows > p * TILE)
            def _(part=part, p=p):
                act(
                    pltpu.make_async_copy(
                        left_ref.at[bond, sigma, part], left_buf.at[at, part], sems.at[p, at]
                    )
                )

    def start(i):
        @pl.when(i < count)
        def _():
            each(i, lambda copy: copy.start())

    for i in range(BUFFERS - 1):
        start(jnp.int32(i))

    def step(i, carry):
        at = lax.rem(i, BUFFERS)
        start(i + BUFFERS - 1)
        each(i, lambda copy: copy.wait())

        def chunk(t, inner):
            high, low = split(left_buf[at, pl.ds(pl.multiple_of(t * CHUNK, CHUNK), CHUNK), :])
            to = pl.ds(pl.multiple_of(i * stride + t * CHUNK, 16), CHUNK)
            left_high[to, :] = high[:, :SIDE]
            left_low[to, :] = low[:, :SIDE]
            left_tail[to, :] = jnp.concatenate([high[:, SIDE:], low[:, SIDE:]], axis=1)
            return inner

        lax.fori_loop(0, (rows + CHUNK - 1) // CHUNK, chunk, 0)
        return carry

    lax.fori_loop(0, count, step, 0)


def right_kernel(meta_ref, right_ref, far_ref, right_high, right_low, right_buf, sems):
    half = right_ref.shape[2]
    sigma, count = meta_ref[SIGMA], meta_ref[COUNT]
    core = lax.axis_index("rsec")
    narrow = meta_ref[COLS] <= HALF

    def each(i, act):
        bond = meta_ref[LIST + i] // 4
        at = lax.rem(i, BUFFERS)
        for ref, place, sem in ((right_ref, core, 0), (far_ref, 1 - core, 1)):
            part = pl.ds(pl.multiple_of(place * half, half), half)

            @pl.when(jnp.logical_not(narrow) | (place == 0))
            def _(ref=ref, part=part, sem=sem):
                act(
                    pltpu.make_async_copy(
                        ref.at[bond, sigma], right_buf.at[at, part], sems.at[sem, at]
                    )
                )

    def start(i):
        @pl.when(i < count)
        def _():
            each(i, lambda copy: copy.start())

    for i in range(BUFFERS - 1):
        start(jnp.int32(i))

    def step(i, carry):
        at = lax.rem(i, BUFFERS)
        start(i + BUFFERS - 1)
        each(i, lambda copy: copy.wait())

        @pl.when(narrow)
        def _():
            right_high[i] = jnp.concatenate(split(right_buf[at, pl.ds(0, HALF), :]), axis=0)

        @pl.when(jnp.logical_not(narrow))
        def _():
            right_high[i], right_low[i] = split(right_buf[at])

        return carry

    lax.fori_loop(0, count, step, 0)


def packed_rows(rows):
    return ((rows + 15) // 16) * 16


def matvec_kernel(k, cells, mpo_count, *refs):
    refs = list(refs)
    meta_ref = refs.pop(0)
    left_high, left_low, left_tail, right_high, right_low = [refs.pop(0) for _ in range(5)]
    size_ref = refs.pop(0) if k else None
    totals = [(refs.pop(0), refs.pop(0)) for _ in range(k)]
    raw = [[refs.pop(0) for _ in range(4)] for _ in range(max(k, 1))]
    images = [[refs.pop(0) for _ in range(4)] for _ in range(k)]
    precond = [refs.pop(0) for _ in range(4)] if k else []
    out_ref, small_ref = refs.pop(0), refs.pop(0)
    size_ref = size_ref if k else refs.pop(0)
    new_refs = [refs.pop(0) for _ in range(4)] if k else raw[0]
    high_ref, low_ref, tail_ref, mid_high, mid_low = refs
    states, width = out_ref.shape
    count, rows, cols = meta_ref[COUNT], meta_ref[ROWS], meta_ref[COLS]
    stride = packed_rows(rows)

    if k:
        numbers = Scalars(totals, cells)
        theta = numbers.proj[k - 1, k - 1][:, :1]
    zero = jnp.zeros((8, width), F32)

    def fold(value):
        return jnp.sum(value.reshape(CHUNK // 8, 8, width), axis=0)

    def prepare(slot, first, last, carry):
        def step(i, carry):
            at = pl.ds(pl.multiple_of(i * CHUNK, CHUNK), CHUNK)
            if k:
                basis = numbers.basis(k - 1, [r[slot][at, :] for r in raw])
                image = numbers.basis(k - 1, [r[slot][at, :] for r in images])
                value = (image[-1] - theta * basis[-1]) / jnp.maximum(
                    precond[slot][at, :] - theta, 1.0
                )
                new_refs[slot][at, :] = value
            else:
                basis, image = [], []
                value = raw[0][slot][at, :]
            high, low = split(value)
            high_ref[slot, at, :] = high
            low_ref[slot, at, :] = low
            terms = [value * value]
            if slot == OWN:
                terms += [value * b for b in basis] + [value * g for g in image]
            return tuple(c + fold(t) for c, t in zip(carry, terms))

        return lax.fori_loop(first, last, step, carry)

    def dot(a, b):
        return jnp.dot(a, b, preferred_element_type=F32)

    def dot_nt(a, b):
        return lax.dot_general(a, b, (((1,), (1,)), ((), ())), preferred_element_type=F32)

    if not k:
        size_ref[2 * OWN], size_ref[2 * OWN + 1] = rows, cols
        size_ref[2 * SIB], size_ref[2 * SIB + 1] = meta_ref[SIB_ROWS], meta_ref[SIB_COLS]
        for slot in (FIRST_PAIR, SECOND_PAIR):
            note = raw[0][slot][pl.ds(states, NOTE), :HALF]
            size_ref[2 * slot] = jnp.max(note[:1]).astype(jnp.int32)
            size_ref[2 * slot + 1] = jnp.max(note[1:]).astype(jnp.int32)
    twice = functools.partial(jnp.concatenate, axis=0)

    def first_stage(slot, deep, narrow):
        begin, end = meta_ref[FIRST + slot], meta_ref[FIRST + 1 + slot]
        tiles = ((end - begin) * stride + PACK - 1) // PACK
        top, rest = pl.ds(0, SIDE), pl.ds(SIDE, states - SIDE)
        if narrow:
            high_ref[slot, :, HALF:] = low_ref[slot, :, :HALF]
        if deep:
            tail = high_ref[slot, rest, :]
            tail_ref[...] = twice([tail, tail])

        def step(t, carry):
            at = pl.ds(pl.multiple_of(begin * stride + t * PACK, 16), PACK)
            high, low = left_high[at, :], left_low[at, :]
            mid = dot(high, high_ref[slot, top, :])
            if deep:
                mid = mid + dot(left_tail[at, :], tail_ref[...])
            if narrow:
                mid = mid[:, :HALF] + mid[:, HALF:] + dot(low, high_ref[slot, top, :HALF])
                mid_high[at, :] = jnp.concatenate(split(mid), axis=1)
            else:
                mid = mid + dot(low, high_ref[slot, top, :]) + dot(high, low_ref[slot, top, :])
                if deep:
                    mid = mid + dot(left_tail[at, : states - SIDE], low_ref[slot, rest, :])
                mid_high[at, :], mid_low[at, :] = split(mid)
            return carry

        lax.fori_loop(0, tiles, step, 0)

    def both(test, action):
        pl.when(test)(lambda: action(True))
        pl.when(jnp.logical_not(test))(lambda: action(False))

    for slot in (OWN, SIB, FIRST_PAIR, SECOND_PAIR):

        def work(slot=slot):
            sums = prepare(slot, 0, states // CHUNK, (zero,) * (1 + 2 * k if slot == OWN else 1))
            both(
                size_ref[2 * slot] > SIDE,
                lambda deep: both(
                    size_ref[2 * slot + 1] <= HALF, lambda narrow: first_stage(slot, deep, narrow)
                ),
            )
            return sums

        if slot == OWN:
            own = work()
        else:
            used = meta_ref[FIRST + 1 + slot] > meta_ref[FIRST + slot]
            pl.when(used | (slot == SIB))(lambda: (work(), None)[1])

    def clear(i, carry):
        at = pl.ds(pl.multiple_of(i * CHUNK, CHUNK), CHUNK)
        out_ref[at, :] = jnp.zeros((CHUNK, width), F32)
        return carry

    lax.fori_loop(0, states // CHUNK, clear, 0)

    def second_stage(size, thin):
        to = pl.ds(0, size)

        def step(i, carry):
            at = pl.ds(pl.multiple_of(i * stride, 16), size)
            slot = lax.rem(meta_ref[LIST + i], 4)

            def add(narrow):
                high = mid_high[at, :]
                if narrow:
                    part = right_high[i, :, :HALF]
                    value = dot_nt(high, jnp.concatenate([part, part], axis=1))
                    if not thin:
                        value = value + dot_nt(high[:, :HALF], right_low[i, :, :HALF])
                else:
                    value = dot_nt(high, right_high[i])
                    if not thin:
                        value = value + dot_nt(high, right_low[i]) + dot_nt(mid_low[at, :], right_high[i])
                if thin:
                    value = value[:, :HALF] + value[:, HALF:]
                    if not narrow:
                        value = value + dot_nt(mid_low[at, :], right_high[i, :HALF, :])
                    out_ref[to, :HALF] += value
                else:
                    out_ref[to, :] += value

            both(size_ref[2 * slot + 1] <= HALF, add)
            return carry

        lax.fori_loop(0, count, step, 0)

    for size in range(TILE, states + 1, TILE):
        pl.when((rows <= size) & (rows > size - TILE))(
            lambda size=size: both(cols <= HALF, functools.partial(second_stage, size))
        )

    def finish(i, carry):
        at = pl.ds(pl.multiple_of(i * CHUNK, CHUNK), CHUNK)
        mask = live_mask((CHUNK, width), i * CHUNK, rows, cols)
        value = jnp.where(mask, out_ref[at, :], 0.0)
        out_ref[at, :] = value
        basis = numbers.basis(k - 1, [r[OWN][at, :] for r in raw]) if k else []
        terms = [value * new_refs[OWN][at, :]] + [value * b for b in basis]
        return tuple(c + fold(t) for c, t in zip(carry, terms))

    late = lax.fori_loop(0, states // CHUNK, finish, (zero,) * (1 + k))

    def whole(value):
        return jnp.sum(jnp.sum(value, axis=1, keepdims=True), axis=0, keepdims=True)

    share = 1.0 / mpo_count
    entries = [whole(own[0]) * share, whole(late[0])]
    for j in range(2):
        entries.append(whole(own[1 + j]) * share if j < k else None)
    for j in range(2):
        entries.append(whole(late[1 + j]) if j < k else None)
    for j in range(2):
        entries.append(whole(own[1 + k + j]) * share if j < k else None)
    row_ids = lax.broadcasted_iota(jnp.int32, small_ref.shape, 0)
    small = jnp.zeros(small_ref.shape, F32)
    for index, entry in enumerate(entries):
        if entry is not None:
            small = jnp.where(row_ids == index, entry, small)
    small_ref[...] = small


def join_kernel(a_ref, b_ref, s0, s1, s2, s3, out_ref, small_ref):
    small_ref[...] = (s0[...] + s1[...]) + (s2[...] + s3[...])

    def step(i, carry):
        at = pl.ds(pl.multiple_of(i * CHUNK, CHUNK), CHUNK)
        out_ref[at, :] = a_ref[at, :] + b_ref[at, :]
        return carry

    lax.fori_loop(0, out_ref.shape[0] // CHUNK, step, 0)


def fill_kernel(steps, cells, *refs):
    known = max(steps) + 1
    refs = list(refs)
    meta_ref = refs.pop(0)
    totals = [(refs.pop(0), refs.pop(0)) for _ in range(known)]
    raw = [(refs.pop(0), refs.pop(0)) for _ in range(known)]
    images = [(refs.pop(0), refs.pop(0)) for _ in range(known)]
    *rest, basis_buf, images_buf, sems = refs
    last = known == MATVECS
    outs = rest[-3:] if last else rest[-2:]
    sigma = meta_ref[SIGMA]
    numbers = Scalars(totals, cells)
    states, half = outs[0].shape[2:]
    core = lax.axis_index("rsec")
    lanes = pl.ds(pl.multiple_of(core * half, half), half)
    for slot in (OWN, SIB):
        sector = sigma if slot == OWN else 1 - sigma

        def step(i, carry, slot=slot, sector=sector):
            at = pl.ds(pl.multiple_of(i * CHUNK, CHUNK), CHUNK)
            for fields, ref in ((raw, basis_buf), (images, images_buf)):
                done = numbers.basis(known - 1, [f[slot][at, lanes] for f in fields])
                for j in steps:
                    ref[j - steps[0], sector, at, :] = done[j]
            return carry

        lax.fori_loop(0, states // CHUNK, step, 0)
    part = pl.ds(steps[0], len(steps))
    copies = [
        pltpu.make_async_copy(buf, out.at[part], sems.at[i])
        for i, (buf, out) in enumerate(((basis_buf, outs[0]), (images_buf, outs[1])))
    ]
    for copy in copies:
        copy.start()
    if last:
        projected_ref = outs[2]
        shape = projected_ref.shape
        row_ids = lax.broadcasted_iota(jnp.int32, shape, 0)
        col_ids = lax.broadcasted_iota(jnp.int32, shape, 1)
        value = jnp.zeros(shape, F32)
        for i in range(MATVECS):
            for j in range(MATVECS):
                value = jnp.where((row_ids == i) & (col_ids == j), numbers.proj[i, j][:, :1], value)
        projected_ref[...] = value
    for copy in copies:
        copy.wait()


def per_device(
    wavefunction, left_env, right_env, precond_diag, down_charge, bond_mask, left_size, right_size
):
    sectors, states, columns = wavefunction.shape
    bonds = left_env.shape[0]
    lsec_count = lax.axis_size("lsec")
    mpo_count = lax.axis_size("mpo")
    assert sectors == 2 and lax.axis_size("rsec") == 2
    width = 2 * columns
    cells = float(lsec_count * sectors * states * width)
    field = jax.ShapeDtypeStruct((states, width), F32)
    small = jax.ShapeDtypeStruct((8, 128), F32)
    params = pltpu.CompilerParams(vmem_limit_bytes=24 * 2**20)

    swap = [(0, 1), (1, 0)]
    first_pairs = [(i, i ^ 1) for i in range(lsec_count) if i ^ 1 < lsec_count]
    second_pairs = [(i, j) for a in range(1, lsec_count - 1, 2) for i, j in ((a, a + 1), (a + 1, a))]
    anywhere = pl.BlockSpec(memory_space=pl.ANY)
    in_hbm = pl.BlockSpec(memory_space=pltpu.HBM)

    def neighbours(value):
        return lax.ppermute(value, "lsec", first_pairs), lax.ppermute(value, "lsec", second_pairs)

    wave_all = lax.all_gather(wavefunction, "rsec", axis=2, tiled=True)
    right_send, _ = lax.optimization_barrier((right_env, wave_all))
    right_far = lax.ppermute(right_send, "rsec", swap)
    mask_rows = bond_mask.T
    down_charge, mask_rows, left_size, right_size = [
        pltpu.with_memory_space_constraint(x, pltpu.HBM)
        for x in (down_charge, mask_rows, left_size, right_size)
    ]
    own = pl.pallas_call(
        first_kernel,
        out_shape=jax.ShapeDtypeStruct((states + NOTE, width), F32),
        in_specs=[in_hbm] * 3 + [whole_vmem()],
        out_specs=whole_vmem(),
        scratch_shapes=[
            pltpu.SMEM(down_charge.shape, jnp.int32),
            pltpu.SMEM(left_size.shape, jnp.int32),
            pltpu.SMEM(right_size.shape, jnp.int32),
            pltpu.SemaphoreType.DMA((3,)),
        ],
        compiler_params=params,
        name="first",
    )(down_charge, left_size, right_size, wave_all)
    near_waves = neighbours(own)
    sib, meta = pl.pallas_call(
        functools.partial(prep_kernel, lsec_count, bonds),
        out_shape=(field, jax.ShapeDtypeStruct((LIST + bonds,), jnp.int32)),
        in_specs=[in_hbm] * 4 + [whole_vmem(), anywhere],
        out_specs=(whole_vmem(), whole_smem()),
        scratch_shapes=[
            pltpu.SMEM(down_charge.shape, jnp.int32),
            pltpu.SMEM(mask_rows.shape, jnp.int32),
            pltpu.SMEM(left_size.shape, jnp.int32),
            pltpu.SMEM(right_size.shape, jnp.int32),
            pltpu.SemaphoreType.DMA((4,)),
        ],
        compiler_params=params,
        name="prep",
    )(down_charge, mask_rows, left_size, right_size, wave_all, own)
    raw = [(own, sib, *near_waves)]
    diag_send, _ = lax.optimization_barrier((precond_diag, sib))
    diag_far = lax.ppermute(diag_send, "rsec", swap)
    diag_own, diag_sib = pl.pallas_call(
        diag_kernel,
        out_shape=(field,) * 2,
        in_specs=[whole_smem()] + [whole_vmem()] * 2,
        out_specs=(whole_vmem(),) * 2,
        compiler_params=params,
        name="diag",
    )(meta, pltpu.with_memory_space_constraint(precond_diag, pltpu.HBM), diag_far)

    near_diags = neighbours(diag_own)

    def join(value, part):
        if mpo_count != 2 or lsec_count != 4:
            total = lax.psum(part, ("lsec", "mpo", "rsec"))
            return lax.psum(value, "mpo"), (total, jnp.zeros_like(total))
        far = lax.ppermute(value, "mpo", swap)
        part = part + lax.ppermute(part, "rsec", swap)
        parts = [lax.ppermute(part, "lsec", [(i, i ^ x) for i in range(4)]) for x in (1, 2, 3)]
        value, part = pl.pallas_call(
            join_kernel,
            out_shape=(field, small),
            in_specs=[whole_vmem()] * 6,
            out_specs=(whole_vmem(),) * 2,
            compiler_params=params,
            name="join",
        )(value, far, part, *parts)
        return value, (part, lax.ppermute(part, "mpo", swap))

    packed = bonds * states + states
    lefts = pl.pallas_call(
        left_kernel,
        out_shape=(
            pltpu.VMEM((packed, SIDE), BF16),
            pltpu.VMEM((packed, SIDE), BF16),
            pltpu.VMEM((packed, 2 * (states - SIDE)), BF16),
        ),
        in_specs=[whole_smem(), anywhere],
        out_specs=(whole_vmem(),) * 3,
        scratch_shapes=[
            pltpu.VMEM((BUFFERS, states, states), F32),
            pltpu.SemaphoreType.DMA((states // TILE, BUFFERS)),
        ],
        compiler_params=params,
        cost_estimate=pl.CostEstimate(flops=0, transcendentals=0, bytes_accessed=bonds * states * states * 4),
        name="left",
    )(meta, left_env)
    rights = pl.pallas_call(
        right_kernel,
        out_shape=(pltpu.VMEM((bonds, width, width), BF16),) * 2,
        in_specs=[whole_smem(), anywhere, anywhere],
        out_specs=(whole_vmem(),) * 2,
        scratch_shapes=[
            pltpu.VMEM((BUFFERS, width, width), F32),
            pltpu.SemaphoreType.DMA((2, BUFFERS)),
        ],
        compiler_params=params,
        cost_estimate=pl.CostEstimate(flops=0, transcendentals=0, bytes_accessed=bonds * width * width * 8),
        name="right",
    )(meta, right_env, right_far)
    blocks = (*lefts, *rights)

    sizes = []

    def matvec(k, inputs):
        out_shape = [field, small]
        out_specs = [whole_vmem()] * 2
        if k:
            out_shape += [field] * 4
            out_specs += [whole_vmem()] * 4
        else:
            out_shape.append(jax.ShapeDtypeStruct((8,), jnp.int32))
            out_specs.append(whole_smem())
        return pl.pallas_call(
            functools.partial(matvec_kernel, k, cells, mpo_count),
            out_shape=tuple(out_shape),
            in_specs=[whole_smem()] + [whole_vmem()] * len(blocks) + [whole_smem()] * len(sizes)
            + [whole_vmem()] * len(inputs),
            out_specs=tuple(out_specs),
            scratch_shapes=[
                pltpu.VMEM((4, states, width), BF16),
                pltpu.VMEM((4, states, width), BF16),
                pltpu.VMEM((2 * (states - SIDE), width), BF16),
                pltpu.VMEM((packed, width), BF16),
                pltpu.VMEM((packed, width), BF16),
            ],
            compiler_params=params,
            cost_estimate=pl.CostEstimate(
                flops=2 * 3 * bonds * states * width * (states + width),
                transcendentals=0,
                bytes_accessed=bonds * states * states,
            ),
            name=f"matvec{k}",
        )(meta, *blocks, *sizes, *inputs)

    out = jax.ShapeDtypeStruct((MATVECS, sectors, states, columns), F32)

    def fill(steps, totals, raw, images, extra):
        steps = list(steps)
        last = len(raw) == MATVECS
        fields = [x for group in (*raw, *images) for x in group[:2]]
        count = 1 + len(totals) + len(fields)
        return pl.pallas_call(
            functools.partial(fill_kernel, steps, cells),
            out_shape=(out, out) + ((jax.ShapeDtypeStruct((MATVECS, MATVECS), F32),) if last else ()),
            in_specs=[whole_smem()] + [whole_vmem()] * (count - 1) + [anywhere] * len(extra),
            out_specs=(anywhere, anywhere) + ((whole_vmem(),) if last else ()),
            scratch_shapes=[
                pltpu.VMEM((len(steps), sectors, states, columns), F32),
                pltpu.VMEM((len(steps), sectors, states, columns), F32),
                pltpu.SemaphoreType.DMA((2,)),
            ],
            input_output_aliases={count: 0, count + 1: 1} if last else {},
            compiler_params=params,
            name="fill_last" if last else "fill_first",
        )(meta, *totals, *fields, *extra)

    totals = []
    images = []
    for k in range(MATVECS):
        if k == 0:
            value, part, size = matvec(0, list(raw[0]))
            sizes.append(size)
        else:
            flat_raw = [x for group in raw for x in group]
            flat_images = [x for group in images for x in group]
            value, part, *fresh = matvec(k, [*totals, *flat_raw, *flat_images, *precond])
            raw.append(tuple(fresh))
        if k == 0:
            value, near_diags = lax.optimization_barrier((value, near_diags))
            precond = (diag_own, diag_sib, *near_diags)
        if k + 1 == MATVECS:
            partial = fill(range(MATVECS - 1), totals, raw[:-1], images, [value])
        value, total = join(value, part)
        totals += total
        beside = lax.ppermute(value, "rsec", swap)
        if k + 1 < MATVECS:
            images.append((value, beside, *neighbours(value)))
        else:
            images.append((value, beside))
    return fill([MATVECS - 1], totals, raw, images, partial)


def solution(mesh):
    placed = (
        P(("grp", "lsec"), None, "rsec"),
        P("mpo", ("grp", "lsec"), None, None),
        P("mpo", ("grp", "lsec"), "rsec", None),
        P(("grp", "lsec"), None, "rsec"),
        P("grp"),
        P("mpo", ("grp", "lsec")),
        P(("grp", "lsec")),
        P(("grp", "lsec")),
    )
    return jax.shard_map(
        per_device,
        mesh=mesh,
        in_specs=placed,
        out_specs=(
            P(None, ("grp", "lsec"), None, "rsec"),
            P(None, ("grp", "lsec"), None, "rsec"),
            P("grp", None),
        ),
        check_vma=False,
    )
```

```python
import functools

import jax
import jax.numpy as jnp
from jax import lax
from jax.experimental import pallas as pl
from jax.experimental.pallas import tpu as pltpu
from jax.sharding import PartitionSpec as P

EPSILON = 1e-06
MATVECS = 3
F32 = jnp.float32
BF16 = jnp.bfloat16
SIGMA, COUNT, ROWS, COLS, FIRST, SIB_ROWS, SIB_COLS, LIST = 0, 1, 2, 3, 4, 9, 10, 16
OWN, SIB, FIRST_PAIR, SECOND_PAIR = 0, 1, 2, 3
CHUNK = 64
TILE = 128
SIDE = 256
HALF = 128
NOTE = 8
PACK = 512
BUFFERS = 4


def whole_vmem():
    return pl.BlockSpec(memory_space=pltpu.VMEM)


def whole_smem():
    return pl.BlockSpec(memory_space=pltpu.SMEM)


def split(value):
    high = value.astype(BF16)
    return high, (value - high.astype(F32)).astype(BF16)


def orientation(down_ref, place):
    def step(i, flips):
        straight = (down_ref[2 * i] == down_ref[2 * i - 2]) | (
            down_ref[2 * i + 1] == down_ref[2 * i - 1]
        )
        return jnp.where(straight, flips, 1 - flips)

    return lax.fori_loop(1, place + 1, step, jnp.int32(0))


def live_mask(shape, row0, rows, cols):
    row_ids = row0 + lax.broadcasted_iota(jnp.int32, shape, 0)
    col_ids = lax.broadcasted_iota(jnp.int32, shape, 1)
    return (row_ids < rows) & (col_ids < cols)


def read_small(pairs, sems):
    copies = [pltpu.make_async_copy(*pair, sems.at[i]) for i, pair in enumerate(pairs)]
    for copy in copies:
        copy.start()
    for copy in copies:
        copy.wait()


def masked_block(out_ref, wave_ref, slot, rows, cols):
    states, width = wave_ref.shape[1:]

    def fill(i, carry):
        at = pl.ds(pl.multiple_of(i * CHUNK, CHUNK), CHUNK)
        mask = live_mask((CHUNK, width), i * CHUNK, rows, cols)
        out_ref[at, :] = jnp.where(mask, wave_ref[slot, at, :], 0.0)
        return carry

    lax.fori_loop(0, states // CHUNK, fill, 0)


def first_kernel(down_in, left_in, right_in, wave_ref, own_ref, down_ref, left_size_ref,
                 right_size_ref, sems):
    read_small(((down_in, down_ref), (left_in, left_size_ref), (right_in, right_size_ref)), sems)
    sigma = lax.axis_index("rsec") ^ orientation(down_ref, lax.axis_index("lsec"))
    rows, cols = left_size_ref[sigma], right_size_ref[sigma]
    masked_block(own_ref, wave_ref, sigma, rows, cols)
    note = (NOTE, own_ref.shape[1])
    row_ids = lax.broadcasted_iota(jnp.int32, note, 0)
    states = wave_ref.shape[1]
    own_ref[pl.ds(states, NOTE), :] = jnp.where(row_ids == 0, rows, cols).astype(F32)


def prep_kernel(lsec_count, bonds, down_in, mask_in, left_in, right_in, wave_ref, own_ref,
                sib_ref, meta_ref, down_ref, mask_ref, left_size_ref, right_size_ref, sems):
    read_small(
        ((down_in, down_ref), (mask_in, mask_ref), (left_in, left_size_ref), (right_in, right_size_ref)),
        sems,
    )
    place = lax.axis_index("lsec")
    core = lax.axis_index("rsec")
    first_bond = lax.axis_index("mpo") * bonds
    sigma = core ^ orientation(down_ref, place)
    own_down = down_ref[2 * place + sigma]
    sib_down = down_ref[2 * place + 1 - sigma]
    before = jnp.maximum(place - 1, 0)
    after = jnp.minimum(place + 1, lsec_count - 1)
    prev_down = down_ref[2 * before + (core ^ orientation(down_ref, before))]
    next_down = down_ref[2 * after + (core ^ orientation(down_ref, after))]
    has_prev = (place > 0) & (prev_down == own_down)
    has_next = (place < lsec_count - 1) & (next_down == own_down)
    odd = lax.rem(place, 2)
    has_lower = sib_down == own_down - 1
    has_upper = sib_down == own_down + 1

    def gather(slot, count):
        meta_ref[FIRST + slot] = count

        def step(bond, count):
            kind = lax.rem(first_bond + bond, 5)
            if slot == OWN:
                there = kind == 0
            elif slot == SIB:
                there = ((kind == 3) & has_lower) | ((kind == 4) & has_upper)
            else:
                lower = odd if slot == FIRST_PAIR else 1 - odd
                there = ((kind == 1) & has_prev & (lower == 1)) | (
                    (kind == 2) & has_next & (lower == 0)
                )
            there = there & (mask_ref[sigma, bond] > 0)

            @pl.when(there)
            def _():
                meta_ref[LIST + count] = bond * 4 + slot

            return count + there.astype(jnp.int32)

        return lax.fori_loop(0, bonds, step, count)

    count = jnp.int32(0)
    for slot in (OWN, SIB, FIRST_PAIR, SECOND_PAIR):
        count = gather(slot, count)
    meta_ref[FIRST + 4] = count
    rows, cols = left_size_ref[sigma], right_size_ref[sigma]
    meta_ref[SIGMA] = sigma
    meta_ref[COUNT] = count
    meta_ref[ROWS] = rows
    meta_ref[COLS] = cols
    meta_ref[SIB_ROWS] = left_size_ref[1 - sigma]
    meta_ref[SIB_COLS] = right_size_ref[1 - sigma]
    masked_block(sib_ref, wave_ref, 1 - sigma, left_size_ref[1 - sigma], right_size_ref[1 - sigma])


def diag_kernel(meta_ref, diag_ref, diag_far, diag_own, diag_sib):
    states, width = diag_own.shape
    half = width // 2
    sigma, core = meta_ref[SIGMA], lax.axis_index("rsec")
    near = pl.ds(pl.multiple_of(core * half, half), half)
    away = pl.ds(pl.multiple_of((1 - core) * half, half), half)
    for out_ref, slot in ((diag_own, sigma), (diag_sib, 1 - sigma)):

        def fill(i, carry, out_ref=out_ref, slot=slot):
            at = pl.ds(pl.multiple_of(i * CHUNK, CHUNK), CHUNK)
            out_ref[at, near] = diag_ref[slot, at, :]
            out_ref[at, away] = diag_far[slot, at, :]
            return carry

        lax.fori_loop(0, states // CHUNK, fill, 0)


def row(value, index):
    return value[index : index + 1, :]


class Scalars:
    def __init__(self, totals, cells):
        self.proj = {}
        self.gram = {}
        self.norm = []
        self.corr = []
        for k, total in enumerate(totals):
            value = (total[0][...] + total[1][...]) / cells
            size, inner = row(value, 0), row(value, 1)
            a = [row(value, 2 + j) for j in range(k)]
            e = [row(value, 4 + j) for j in range(k)]
            f = [row(value, 6 + j) for j in range(k)]
            length = size
            theta = inner
            for j in range(k):
                length = length - 2.0 * a[j] * a[j]
                theta = theta - a[j] * e[j] - a[j] * f[j]
            for i in range(k):
                for j in range(k):
                    length = length + a[i] * a[j] * self.gram[i, j]
                    theta = theta + a[i] * a[j] * self.proj[i, j]
            length = jnp.maximum(length, 0.0)
            square = length + EPSILON
            norm = jnp.sqrt(square)
            for j in range(k):
                up, down, both = e[j], f[j], a[j]
                for i in range(k):
                    up = up - a[i] * self.proj[j, i]
                    down = down - a[i] * self.proj[i, j]
                    both = both - a[i] * self.gram[i, j]
                self.proj[j, k] = up / norm
                self.proj[k, j] = down / norm
                self.gram[j, k] = self.gram[k, j] = both / norm
            self.proj[k, k] = theta / square
            self.gram[k, k] = length / square
            self.norm.append(norm)
            self.corr.append(a)

    def basis(self, k, fields):
        done = []
        for step in range(k + 1):
            value = fields[step]
            for j in range(step):
                value = value - self.corr[step][j][:, :1] * done[j]
            done.append(value / self.norm[step][:, :1])
        return done


def left_kernel(meta_ref, left_ref, left_high, left_low, left_tail, left_buf, sems):
    states = left_buf.shape[1]
    sigma, count, rows = meta_ref[SIGMA], meta_ref[COUNT], meta_ref[ROWS]
    stride = packed_rows(rows)

    def each(i, act):
        bond = meta_ref[LIST + i] // 4
        at = lax.rem(i, BUFFERS)
        for p in range(states // TILE):
            part = pl.ds(p * TILE, TILE)

            @pl.when(rows > p * TILE)
            def _(part=part, p=p):
                act(
                    pltpu.make_async_copy(
                        left_ref.at[bond, sigma, part], left_buf.at[at, part], sems.at[p, at]
                    )
                )

    def start(i):
        @pl.when(i < count)
        def _():
            each(i, lambda copy: copy.start())

    for i in range(BUFFERS - 1):
        start(jnp.int32(i))

    def step(i, carry):
        at = lax.rem(i, BUFFERS)
        start(i + BUFFERS - 1)
        each(i, lambda copy: copy.wait())

        def chunk(t, inner):
            high, low = split(left_buf[at, pl.ds(pl.multiple_of(t * CHUNK, CHUNK), CHUNK), :])
            to = pl.ds(pl.multiple_of(i * stride + t * CHUNK, 16), CHUNK)
            left_high[to, :] = high[:, :SIDE]
            left_low[to, :] = low[:, :SIDE]
            left_tail[to, :] = jnp.concatenate([high[:, SIDE:], low[:, SIDE:]], axis=1)
            return inner

        lax.fori_loop(0, (rows + CHUNK - 1) // CHUNK, chunk, 0)
        return carry

    lax.fori_loop(0, count, step, 0)


def packed_rows(rows):
    return ((rows + 15) // 16) * 16


def matvec_kernel(k, cells, mpo_count, *refs):
    refs = list(refs)
    meta_ref = refs.pop(0)
    left_high, left_low, left_tail = [refs.pop(0) for _ in range(3)]
    if k:
        right_high, right_low, size_ref = [refs.pop(0) for _ in range(3)]
    else:
        right_ref, far_ref = refs.pop(0), refs.pop(0)
    totals = [(refs.pop(0), refs.pop(0)) for _ in range(k)]
    raw = [[refs.pop(0) for _ in range(4)] for _ in range(max(k, 1))]
    images = [[refs.pop(0) for _ in range(4)] for _ in range(k)]
    precond = [refs.pop(0) for _ in range(4)] if k else []
    out_ref, small_ref = refs.pop(0), refs.pop(0)
    if k:
        new_refs = [refs.pop(0) for _ in range(4)]
    else:
        new_refs = raw[0]
        right_high, right_low, size_ref = [refs.pop(0) for _ in range(3)]
    last = k + 1 == MATVECS
    if last:
        known_ref, basis_out, images_out = [refs.pop(0) for _ in range(3)]
    high_ref, low_ref, tail_ref, mid_high, mid_low = refs[:5]
    if not k:
        right_buf, sems = refs[5:]
    elif last:
        sems = refs[5]
    states, width = out_ref.shape
    count, rows, cols = meta_ref[COUNT], meta_ref[ROWS], meta_ref[COLS]
    stride = packed_rows(rows)

    core = lax.axis_index("rsec")
    if not k:
        half = right_ref.shape[2]
        sigma = meta_ref[SIGMA]

        def each_right(i, act):
            bond = meta_ref[LIST + i] // 4
            at = lax.rem(i, BUFFERS)
            for ref, place, sem in ((right_ref, core, 0), (far_ref, 1 - core, 1)):
                part = pl.ds(pl.multiple_of(place * half, half), half)

                @pl.when((cols > HALF) | (place == 0))
                def _(ref=ref, part=part, sem=sem):
                    act(
                        pltpu.make_async_copy(
                            ref.at[bond, sigma], right_buf.at[at, part], sems.at[sem, at]
                        )
                    )

        def start_right(i):
            @pl.when(i < count)
            def _():
                each_right(i, lambda copy: copy.start())

        for i in range(BUFFERS):
            start_right(jnp.int32(i))

    if k:
        numbers = Scalars(totals, cells)
        theta = numbers.proj[k - 1, k - 1][:, :1]
    zero = jnp.zeros((8, width), F32)

    def fold(value):
        return jnp.sum(value.reshape(CHUNK // 8, 8, width), axis=0)

    def prepare(slot, carry):
        def step(i, carry):
            at = pl.ds(pl.multiple_of(i * CHUNK, CHUNK), CHUNK)
            if k:
                basis = numbers.basis(k - 1, [r[slot][at, :] for r in raw])
                image = numbers.basis(k - 1, [r[slot][at, :] for r in images])
                value = (image[-1] - theta * basis[-1]) / jnp.maximum(
                    precond[slot][at, :] - theta, 1.0
                )
                new_refs[slot][at, :] = value
                if last and slot in (OWN, SIB):
                    for which, group in enumerate((basis, image)):
                        for j, block in enumerate(group):
                            block = jnp.where(core == 0, block[:, :HALF], block[:, HALF:])
                            known_ref[which, slot, j, at, :] = block
            else:
                basis, image = [], []
                value = raw[0][slot][at, :]
            high, low = split(value)
            high_ref[slot, at, :] = high
            low_ref[slot, at, :] = low
            terms = [value * value]
            if slot == OWN:
                terms += [value * b for b in basis] + [value * g for g in image]
            return tuple(c + fold(t) for c, t in zip(carry, terms))

        return lax.fori_loop(0, states // CHUNK, step, carry)

    def dot(a, b):
        return jnp.dot(a, b, preferred_element_type=F32)

    def dot_nt(a, b):
        return lax.dot_general(a, b, (((1,), (1,)), ((), ())), preferred_element_type=F32)

    if not k:
        size_ref[2 * OWN], size_ref[2 * OWN + 1] = rows, cols
        size_ref[2 * SIB], size_ref[2 * SIB + 1] = meta_ref[SIB_ROWS], meta_ref[SIB_COLS]
        for slot in (FIRST_PAIR, SECOND_PAIR):
            note = raw[0][slot][pl.ds(states, NOTE), :HALF]
            size_ref[2 * slot] = jnp.max(note[:1]).astype(jnp.int32)
            size_ref[2 * slot + 1] = jnp.max(note[1:]).astype(jnp.int32)
    twice = functools.partial(jnp.concatenate, axis=0)

    def first_stage(slot, deep, narrow):
        begin, end = meta_ref[FIRST + slot], meta_ref[FIRST + 1 + slot]
        total = (end - begin) * stride
        top, rest = pl.ds(0, SIDE), pl.ds(SIDE, states - SIDE)
        if narrow:
            high_ref[slot, :, HALF:] = low_ref[slot, :, :HALF]
        if deep:
            tail = high_ref[slot, rest, :]
            tail_ref[...] = twice([tail, tail])

        def tile(first, size):
            at = pl.ds(pl.multiple_of(begin * stride + first, 16), size)
            high, low = left_high[at, :], left_low[at, :]
            mid = dot(high, high_ref[slot, top, :])
            if deep:
                mid = mid + dot(left_tail[at, :], tail_ref[...])
            if narrow:
                mid = mid[:, :HALF] + mid[:, HALF:] + dot(low, high_ref[slot, top, :HALF])
                mid_high[at, :] = jnp.concatenate(split(mid), axis=1)
            else:
                mid = mid + dot(low, high_ref[slot, top, :]) + dot(high, low_ref[slot, top, :])
                if deep:
                    mid = mid + dot(left_tail[at, : states - SIDE], low_ref[slot, rest, :])
                mid_high[at, :], mid_low[at, :] = split(mid)

        def step(t, carry):
            tile(t * PACK, PACK)
            return carry

        tiles = (total + PACK // 2 - 1) // PACK
        lax.fori_loop(0, tiles, step, 0)
        pl.when(total > tiles * PACK)(lambda: tile(tiles * PACK, PACK // 2))

    def both(test, action):
        pl.when(test)(lambda: action(True))
        pl.when(jnp.logical_not(test))(lambda: action(False))

    for slot in (OWN, SIB, FIRST_PAIR, SECOND_PAIR):

        def work(slot=slot):
            sums = prepare(slot, (zero,) * (1 + 2 * k if slot == OWN else 1))
            both(
                size_ref[2 * slot] > SIDE,
                lambda deep: both(
                    size_ref[2 * slot + 1] <= HALF, lambda narrow: first_stage(slot, deep, narrow)
                ),
            )
            return sums

        if slot == OWN:
            own = work()
        else:
            used = meta_ref[FIRST + 1 + slot] > meta_ref[FIRST + slot]
            pl.when(used | (slot == SIB))(lambda: (work(), None)[1])

    if last:
        sigma = meta_ref[SIGMA]
        outputs = [
            pltpu.make_async_copy(
                known_ref.at[which, slot],
                out.at[pl.ds(0, MATVECS - 1), sigma if slot == OWN else 1 - sigma],
                sems.at[which, slot],
            )
            for which, out in enumerate((basis_out, images_out))
            for slot in (OWN, SIB)
        ]
        for copy in outputs:
            copy.start()

    def clear(i, carry):
        at = pl.ds(pl.multiple_of(i * CHUNK, CHUNK), CHUNK)
        out_ref[at, :] = jnp.zeros((CHUNK, width), F32)
        return carry

    lax.fori_loop(0, states // CHUNK, clear, 0)

    def second_stage(size, thin):
        to = pl.ds(0, size)

        def right_block(i):
            if k:
                return right_high[i], None if thin else right_low[i]
            at = lax.rem(i, BUFFERS)
            each_right(i, lambda copy: copy.wait())
            if thin:
                high, low = jnp.concatenate(split(right_buf[at, pl.ds(0, HALF), :]), axis=0), None
            else:
                high, low = split(right_buf[at])
                right_low[i] = low
            right_high[i] = high
            return high, low

        def product(i, narrow):
            at = pl.ds(pl.multiple_of(i * stride, 16), size)
            high = mid_high[at, :]
            right, right_rest = right_block(i)
            if narrow:
                part = right[:, :HALF]
                value = dot_nt(high, jnp.concatenate([part, part], axis=1))
                if not thin:
                    value = value + dot_nt(high[:, :HALF], right_rest[:, :HALF])
            else:
                value = dot_nt(high, right)
                if not thin:
                    value = value + dot_nt(high, right_rest) + dot_nt(mid_low[at, :], right)
            if thin:
                value = value[:, :HALF] + value[:, HALF:]
                if not narrow:
                    value = value + dot_nt(mid_low[at, :], right[:HALF, :])
            return value

        def bonds(indices, narrow):
            value = product(indices[0], narrow)
            for i in indices[1:]:
                value = value + product(i, narrow)
            if thin:
                out_ref[to, :HALF] += value
            else:
                out_ref[to, :] += value
            if not k:
                for i in indices:
                    start_right(i + BUFFERS)

        def from_slot(slot, carry):
            begin, end = meta_ref[FIRST + slot], meta_ref[FIRST + 1 + slot]

            def run(narrow):
                def pair(p, inner):
                    bonds([begin + 2 * p, begin + 2 * p + 1], narrow)
                    return inner

                lax.fori_loop(0, (end - begin) // 2, pair, 0)
                pl.when(lax.rem(end - begin, 2) == 1)(lambda: bonds([end - 1], narrow))

            both(size_ref[2 * slot + 1] <= HALF, run)
            return carry

        lax.fori_loop(0, 4, from_slot, 0)

    for size in range(TILE, states + 1, TILE):
        pl.when((rows <= size) & (rows > size - TILE))(
            lambda size=size: both(cols <= HALF, functools.partial(second_stage, size))
        )

    def finish(i, carry):
        at = pl.ds(pl.multiple_of(i * CHUNK, CHUNK), CHUNK)
        mask = live_mask((CHUNK, width), i * CHUNK, rows, cols)
        value = jnp.where(mask, out_ref[at, :], 0.0)
        out_ref[at, :] = value
        basis = numbers.basis(k - 1, [r[OWN][at, :] for r in raw]) if k else []
        terms = [value * new_refs[OWN][at, :]] + [value * b for b in basis]
        return tuple(c + fold(t) for c, t in zip(carry, terms))

    late = lax.fori_loop(0, states // CHUNK, finish, (zero,) * (1 + k))

    def whole(value):
        return jnp.sum(jnp.sum(value, axis=1, keepdims=True), axis=0, keepdims=True)

    share = 1.0 / mpo_count
    entries = [whole(own[0]) * share, whole(late[0])]
    for j in range(2):
        entries.append(whole(own[1 + j]) * share if j < k else None)
    for j in range(2):
        entries.append(whole(late[1 + j]) if j < k else None)
    for j in range(2):
        entries.append(whole(own[1 + k + j]) * share if j < k else None)
    row_ids = lax.broadcasted_iota(jnp.int32, small_ref.shape, 0)
    small = jnp.zeros(small_ref.shape, F32)
    for index, entry in enumerate(entries):
        if entry is not None:
            small = jnp.where(row_ids == index, entry, small)
    small_ref[...] = small
    if last:
        for copy in outputs:
            copy.wait()


def join_kernel(a_ref, b_ref, s0, s1, s2, s3, out_ref, small_ref):
    small_ref[...] = (s0[...] + s1[...]) + (s2[...] + s3[...])

    def step(i, carry):
        at = pl.ds(pl.multiple_of(i * CHUNK, CHUNK), CHUNK)
        out_ref[at, :] = a_ref[at, :] + b_ref[at, :]
        return carry

    lax.fori_loop(0, out_ref.shape[0] // CHUNK, step, 0)


def fill_kernel(cells, meta_ref, *refs):
    totals = [refs[2 * i : 2 * i + 2] for i in range(MATVECS)]
    known_ref, raw_own, raw_sib, image_own, image_sib = refs[2 * MATVECS : 2 * MATVECS + 5]
    basis_out, images_out, projected_ref, basis_buf, images_buf, sems = refs[-6:]
    last = MATVECS - 1
    sigma = meta_ref[SIGMA]
    numbers = Scalars(totals, cells)
    core = lax.axis_index("rsec")
    states, half = basis_buf.shape[1:]
    lanes = pl.ds(pl.multiple_of(core * half, half), half)
    inverse = 1.0 / numbers.norm[last][:, :1]
    corr = [a[:, :1] for a in numbers.corr[last]]
    copies = []
    for slot, fields in ((OWN, (raw_own, image_own)), (SIB, (raw_sib, image_sib))):

        def step(i, carry, slot=slot, fields=fields):
            at = pl.ds(pl.multiple_of(i * CHUNK, CHUNK), CHUNK)
            for which, buf in enumerate((basis_buf, images_buf)):
                value = fields[which][at, lanes]
                for j in range(last):
                    value = value - corr[j] * known_ref[which, slot, j, at, :]
                buf[slot, at, :] = value * inverse
            return carry

        lax.fori_loop(0, states // CHUNK, step, 0)
        sector = sigma if slot == OWN else 1 - sigma
        for which, (buf, out) in enumerate(((basis_buf, basis_out), (images_buf, images_out))):
            copies.append(
                pltpu.make_async_copy(buf.at[slot], out.at[last, sector], sems.at[which, slot])
            )
            copies[-1].start()
    shape = projected_ref.shape
    row_ids = lax.broadcasted_iota(jnp.int32, shape, 0)
    col_ids = lax.broadcasted_iota(jnp.int32, shape, 1)
    value = jnp.zeros(shape, F32)
    for i in range(MATVECS):
        for j in range(MATVECS):
            value = jnp.where((row_ids == i) & (col_ids == j), numbers.proj[i, j][:, :1], value)
    projected_ref[...] = value
    for copy in copies:
        copy.wait()


def per_device(
    wavefunction, left_env, right_env, precond_diag, down_charge, bond_mask, left_size, right_size
):
    sectors, states, columns = wavefunction.shape
    bonds = left_env.shape[0]
    lsec_count = lax.axis_size("lsec")
    mpo_count = lax.axis_size("mpo")
    assert sectors == 2 and lax.axis_size("rsec") == 2
    width = 2 * columns
    cells = float(lsec_count * sectors * states * width)
    field = jax.ShapeDtypeStruct((states, width), F32)
    small = jax.ShapeDtypeStruct((8, 128), F32)
    params = pltpu.CompilerParams(vmem_limit_bytes=24 * 2**20)

    swap = [(0, 1), (1, 0)]
    first_pairs = [(i, i ^ 1) for i in range(lsec_count) if i ^ 1 < lsec_count]
    second_pairs = [(i, j) for a in range(1, lsec_count - 1, 2) for i, j in ((a, a + 1), (a + 1, a))]
    anywhere = pl.BlockSpec(memory_space=pl.ANY)
    in_hbm = pl.BlockSpec(memory_space=pltpu.HBM)

    def hold(value):
        return pltpu.with_memory_space_constraint(value, pltpu.HBM)

    def neighbours(value):
        return lax.ppermute(value, "lsec", first_pairs), lax.ppermute(value, "lsec", second_pairs)

    wave_all = lax.all_gather(wavefunction, "rsec", axis=2, tiled=True)
    right_send, _ = lax.optimization_barrier((right_env, wave_all))
    right_far = lax.ppermute(right_send, "rsec", swap)
    mask_rows = bond_mask.T
    down_charge, mask_rows, left_size, right_size = [
        hold(x) for x in (down_charge, mask_rows, left_size, right_size)
    ]
    own = pl.pallas_call(
        first_kernel,
        out_shape=jax.ShapeDtypeStruct((states + NOTE, width), F32),
        in_specs=[in_hbm] * 3 + [whole_vmem()],
        out_specs=whole_vmem(),
        scratch_shapes=[
            pltpu.SMEM(down_charge.shape, jnp.int32),
            pltpu.SMEM(left_size.shape, jnp.int32),
            pltpu.SMEM(right_size.shape, jnp.int32),
            pltpu.SemaphoreType.DMA((3,)),
        ],
        compiler_params=params,
        name="first",
    )(down_charge, left_size, right_size, wave_all)
    near_waves = neighbours(own)
    sib, meta = pl.pallas_call(
        functools.partial(prep_kernel, lsec_count, bonds),
        out_shape=(field, jax.ShapeDtypeStruct((LIST + bonds,), jnp.int32)),
        in_specs=[in_hbm] * 4 + [whole_vmem(), anywhere],
        out_specs=(whole_vmem(), whole_smem()),
        scratch_shapes=[
            pltpu.SMEM(down_charge.shape, jnp.int32),
            pltpu.SMEM(mask_rows.shape, jnp.int32),
            pltpu.SMEM(left_size.shape, jnp.int32),
            pltpu.SMEM(right_size.shape, jnp.int32),
            pltpu.SemaphoreType.DMA((4,)),
        ],
        compiler_params=params,
        name="prep",
    )(down_charge, mask_rows, left_size, right_size, wave_all, own)
    raw = [(own, sib, *near_waves)]
    diag_send, _ = lax.optimization_barrier((precond_diag, sib))
    diag_far = lax.ppermute(diag_send, "rsec", swap)
    diag_own, diag_sib = pl.pallas_call(
        diag_kernel,
        out_shape=(field,) * 2,
        in_specs=[whole_smem()] + [whole_vmem()] * 2,
        out_specs=(whole_vmem(),) * 2,
        compiler_params=params,
        name="diag",
    )(meta, hold(precond_diag), diag_far)

    near_diags = neighbours(diag_own)

    def join(value, part):
        if mpo_count != 2 or lsec_count != 4:
            total = lax.psum(part, ("lsec", "mpo", "rsec"))
            return lax.psum(value, "mpo"), (total, jnp.zeros_like(total))
        far = lax.ppermute(value, "mpo", swap)
        part = part + lax.ppermute(part, "rsec", swap)
        parts = [lax.ppermute(part, "lsec", [(i, i ^ x) for i in range(4)]) for x in (1, 2, 3)]
        value, part = pl.pallas_call(
            join_kernel,
            out_shape=(field, small),
            in_specs=[whole_vmem()] * 6,
            out_specs=(whole_vmem(),) * 2,
            compiler_params=params,
            name="join",
        )(value, far, part, *parts)
        return value, (part, lax.ppermute(part, "mpo", swap))

    packed = bonds * states + PACK
    lefts = pl.pallas_call(
        left_kernel,
        out_shape=(
            pltpu.VMEM((packed, SIDE), BF16),
            pltpu.VMEM((packed, SIDE), BF16),
            pltpu.VMEM((packed, 2 * (states - SIDE)), BF16),
        ),
        in_specs=[whole_smem(), anywhere],
        out_specs=(whole_vmem(),) * 3,
        scratch_shapes=[
            pltpu.VMEM((BUFFERS, states, states), F32),
            pltpu.SemaphoreType.DMA((states // TILE, BUFFERS)),
        ],
        compiler_params=params,
        cost_estimate=pl.CostEstimate(flops=0, transcendentals=0, bytes_accessed=bonds * states * states * 4),
        name="left",
    )(meta, hold(left_env))
    out = jax.ShapeDtypeStruct((MATVECS, sectors, states, columns), F32)
    known = jax.ShapeDtypeStruct((2, sectors, MATVECS - 1, states, columns), F32)

    def matvec(k, rights, inputs):
        out_shape = [field, small] + [field] * (4 if k else 0)
        out_specs = [whole_vmem()] * len(out_shape)
        scratch = [
            pltpu.VMEM((4, states, width), BF16),
            pltpu.VMEM((4, states, width), BF16),
            pltpu.VMEM((2 * (states - SIDE), width), BF16),
            pltpu.VMEM((packed, width), BF16),
            pltpu.VMEM((packed, width), BF16),
        ]
        if k == 0:
            out_shape += [pltpu.VMEM((bonds, width, width), BF16)] * 2
            out_shape += [jax.ShapeDtypeStruct((8,), jnp.int32)]
            out_specs += [whole_vmem()] * 2 + [whole_smem()]
            scratch += [
                pltpu.VMEM((BUFFERS, width, width), F32),
                pltpu.SemaphoreType.DMA((2, BUFFERS)),
            ]
            right_specs = [anywhere] * 2
        else:
            right_specs = [whole_vmem()] * 2 + [whole_smem()]
        if k + 1 == MATVECS:
            out_shape += [known, out, out]
            out_specs += [whole_vmem(), anywhere, anywhere]
            scratch += [pltpu.SemaphoreType.DMA((2, 2))]
        return pl.pallas_call(
            functools.partial(matvec_kernel, k, cells, mpo_count),
            out_shape=tuple(out_shape),
            in_specs=[whole_smem()] + [whole_vmem()] * 3 + right_specs + [whole_vmem()] * len(inputs),
            out_specs=tuple(out_specs),
            scratch_shapes=scratch,
            compiler_params=params,
            cost_estimate=pl.CostEstimate(
                flops=2 * 3 * bonds * states * width * (states + width),
                transcendentals=0,
                bytes_accessed=bonds * states * states,
            ),
            name=f"matvec{k}",
        )(meta, *lefts, *rights, *inputs)

    totals = []
    images = []
    for k in range(MATVECS):
        if k == 0:
            value, part, *rights = matvec(0, [hold(right_env), hold(right_far)], list(raw[0]))
            value, near_diags = lax.optimization_barrier((value, near_diags))
            precond = (diag_own, diag_sib, *near_diags)
        else:
            flat_raw = [x for group in raw for x in group]
            flat_images = [x for group in images for x in group]
            inputs = [*totals, *flat_raw, *flat_images, *precond]
            value, part, *fresh = matvec(k, rights, inputs)
            raw.append(tuple(fresh[:4]))
        value, total = join(value, part)
        totals += total
        beside = lax.ppermute(value, "rsec", swap)
        if k + 1 < MATVECS:
            images.append((value, beside, *neighbours(value)))
    operands = [*totals, fresh[4], *raw[-1][:2], value, beside]
    return pl.pallas_call(
        functools.partial(fill_kernel, cells),
        out_shape=(out, out, jax.ShapeDtypeStruct((MATVECS, MATVECS), F32)),
        in_specs=[whole_smem()] + [whole_vmem()] * len(operands) + [anywhere] * 2,
        out_specs=(anywhere, anywhere, whole_vmem()),
        scratch_shapes=[
            pltpu.VMEM((sectors, states, columns), F32),
            pltpu.VMEM((sectors, states, columns), F32),
            pltpu.SemaphoreType.DMA((2, 2)),
        ],
        input_output_aliases={1 + len(operands): 0, 2 + len(operands): 1},
        compiler_params=params,
        name="fill",
    )(meta, *operands, *fresh[5:])


def solution(mesh):
    placed = (
        P(("grp", "lsec"), None, "rsec"),
        P("mpo", ("grp", "lsec"), None, None),
        P("mpo", ("grp", "lsec"), "rsec", None),
        P(("grp", "lsec"), None, "rsec"),
        P("grp"),
        P("mpo", ("grp", "lsec")),
        P(("grp", "lsec")),
        P(("grp", "lsec")),
    )
    return jax.shard_map(
        per_device,
        mesh=mesh,
        in_specs=placed,
        out_specs=(
            P(None, ("grp", "lsec"), None, "rsec"),
            P(None, ("grp", "lsec"), None, "rsec"),
            P("grp", None),
        ),
        check_vma=False,
    )
```

```python
import functools

import jax
import jax.numpy as jnp
from jax import lax
from jax.experimental import pallas as pl
from jax.experimental.pallas import tpu as pltpu
from jax.sharding import PartitionSpec as P

EPSILON = 1e-06
MATVECS = 3
F32 = jnp.float32
BF16 = jnp.bfloat16
SIGMA, COUNT, ROWS, COLS, FIRST, SIB_ROWS, SIB_COLS, LIST = 0, 1, 2, 3, 4, 9, 10, 16
OWN, SIB, FIRST_PAIR, SECOND_PAIR = 0, 1, 2, 3
CHUNK = 64
TILE = 128
SIDE = 256
HALF = 128
NOTE = 8
PACK = 512
BUFFERS = 4


def whole_vmem():
    return pl.BlockSpec(memory_space=pltpu.VMEM)


def whole_smem():
    return pl.BlockSpec(memory_space=pltpu.SMEM)


def split(value):
    high = value.astype(BF16)
    return high, (value - high.astype(F32)).astype(BF16)


def orientation(down_ref, place):
    def step(i, flips):
        straight = (down_ref[2 * i] == down_ref[2 * i - 2]) | (
            down_ref[2 * i + 1] == down_ref[2 * i - 1]
        )
        return jnp.where(straight, flips, 1 - flips)

    return lax.fori_loop(1, place + 1, step, jnp.int32(0))


def live_mask(shape, row0, rows, cols):
    row_ids = row0 + lax.broadcasted_iota(jnp.int32, shape, 0)
    col_ids = lax.broadcasted_iota(jnp.int32, shape, 1)
    return (row_ids < rows) & (col_ids < cols)


def read_small(pairs, sems):
    copies = [pltpu.make_async_copy(*pair, sems.at[i]) for i, pair in enumerate(pairs)]
    for copy in copies:
        copy.start()
    for copy in copies:
        copy.wait()


def masked_block(out_ref, wave_ref, slot, rows, cols):
    states, width = wave_ref.shape[1:]

    def fill(i, carry):
        at = pl.ds(pl.multiple_of(i * CHUNK, CHUNK), CHUNK)
        mask = live_mask((CHUNK, width), i * CHUNK, rows, cols)
        out_ref[at, :] = jnp.where(mask, wave_ref[slot, at, :], 0.0)
        return carry

    lax.fori_loop(0, states // CHUNK, fill, 0)


def first_kernel(down_in, left_in, right_in, wave_ref, own_ref, down_ref, left_size_ref,
                 right_size_ref, sems):
    read_small(((down_in, down_ref), (left_in, left_size_ref), (right_in, right_size_ref)), sems)
    sigma = lax.axis_index("rsec") ^ orientation(down_ref, lax.axis_index("lsec"))
    rows, cols = left_size_ref[sigma], right_size_ref[sigma]
    masked_block(own_ref, wave_ref, sigma, rows, cols)
    note = (NOTE, own_ref.shape[1])
    row_ids = lax.broadcasted_iota(jnp.int32, note, 0)
    states = wave_ref.shape[1]
    own_ref[pl.ds(states, NOTE), :] = jnp.where(row_ids == 0, rows, cols).astype(F32)


def prep_kernel(lsec_count, bonds, down_in, mask_in, left_in, right_in, wave_ref, own_ref,
                sib_ref, meta_ref, down_ref, mask_ref, left_size_ref, right_size_ref, sems):
    read_small(
        ((down_in, down_ref), (mask_in, mask_ref), (left_in, left_size_ref), (right_in, right_size_ref)),
        sems,
    )
    place = lax.axis_index("lsec")
    core = lax.axis_index("rsec")
    first_bond = lax.axis_index("mpo") * bonds
    sigma = core ^ orientation(down_ref, place)
    own_down = down_ref[2 * place + sigma]
    sib_down = down_ref[2 * place + 1 - sigma]
    before = jnp.maximum(place - 1, 0)
    after = jnp.minimum(place + 1, lsec_count - 1)
    prev_down = down_ref[2 * before + (core ^ orientation(down_ref, before))]
    next_down = down_ref[2 * after + (core ^ orientation(down_ref, after))]
    has_prev = (place > 0) & (prev_down == own_down)
    has_next = (place < lsec_count - 1) & (next_down == own_down)
    odd = lax.rem(place, 2)
    has_lower = sib_down == own_down - 1
    has_upper = sib_down == own_down + 1

    def gather(slot, count):
        meta_ref[FIRST + slot] = count

        def step(bond, count):
            kind = lax.rem(first_bond + bond, 5)
            if slot == OWN:
                there = kind == 0
            elif slot == SIB:
                there = ((kind == 3) & has_lower) | ((kind == 4) & has_upper)
            else:
                lower = odd if slot == FIRST_PAIR else 1 - odd
                there = ((kind == 1) & has_prev & (lower == 1)) | (
                    (kind == 2) & has_next & (lower == 0)
                )
            there = there & (mask_ref[sigma, bond] > 0)

            @pl.when(there)
            def _():
                meta_ref[LIST + count] = bond * 4 + slot

            return count + there.astype(jnp.int32)

        return lax.fori_loop(0, bonds, step, count)

    count = jnp.int32(0)
    for slot in (OWN, SIB, FIRST_PAIR, SECOND_PAIR):
        count = gather(slot, count)
    meta_ref[FIRST + 4] = count
    rows, cols = left_size_ref[sigma], right_size_ref[sigma]
    meta_ref[SIGMA] = sigma
    meta_ref[COUNT] = count
    meta_ref[ROWS] = rows
    meta_ref[COLS] = cols
    meta_ref[SIB_ROWS] = left_size_ref[1 - sigma]
    meta_ref[SIB_COLS] = right_size_ref[1 - sigma]
    masked_block(sib_ref, wave_ref, 1 - sigma, left_size_ref[1 - sigma], right_size_ref[1 - sigma])


def diag_kernel(meta_ref, diag_ref, diag_far, diag_own, diag_sib):
    states, width = diag_own.shape
    half = width // 2
    sigma, core = meta_ref[SIGMA], lax.axis_index("rsec")
    near = pl.ds(pl.multiple_of(core * half, half), half)
    away = pl.ds(pl.multiple_of((1 - core) * half, half), half)
    for out_ref, slot in ((diag_own, sigma), (diag_sib, 1 - sigma)):

        def fill(i, carry, out_ref=out_ref, slot=slot):
            at = pl.ds(pl.multiple_of(i * CHUNK, CHUNK), CHUNK)
            out_ref[at, near] = diag_ref[slot, at, :]
            out_ref[at, away] = diag_far[slot, at, :]
            return carry

        lax.fori_loop(0, states // CHUNK, fill, 0)


def row(value, index):
    return value[index : index + 1, :]


class Scalars:
    def __init__(self, totals, cells):
        self.proj = {}
        self.gram = {}
        self.norm = []
        self.corr = []
        for k, total in enumerate(totals):
            value = (total[0][...] + total[1][...]) / cells
            size, inner = row(value, 0), row(value, 1)
            a = [row(value, 2 + j) for j in range(k)]
            e = [row(value, 4 + j) for j in range(k)]
            f = [row(value, 6 + j) for j in range(k)]
            length = size
            theta = inner
            for j in range(k):
                length = length - 2.0 * a[j] * a[j]
                theta = theta - a[j] * e[j] - a[j] * f[j]
            for i in range(k):
                for j in range(k):
                    length = length + a[i] * a[j] * self.gram[i, j]
                    theta = theta + a[i] * a[j] * self.proj[i, j]
            length = jnp.maximum(length, 0.0)
            square = length + EPSILON
            norm = jnp.sqrt(square)
            for j in range(k):
                up, down, both = e[j], f[j], a[j]
                for i in range(k):
                    up = up - a[i] * self.proj[j, i]
                    down = down - a[i] * self.proj[i, j]
                    both = both - a[i] * self.gram[i, j]
                self.proj[j, k] = up / norm
                self.proj[k, j] = down / norm
                self.gram[j, k] = self.gram[k, j] = both / norm
            self.proj[k, k] = theta / square
            self.gram[k, k] = length / square
            self.norm.append(norm)
            self.corr.append(a)

    def basis(self, k, fields):
        done = []
        for step in range(k + 1):
            value = fields[step]
            for j in range(step):
                value = value - self.corr[step][j][:, :1] * done[j]
            done.append(value / self.norm[step][:, :1])
        return done


def left_kernel(meta_ref, left_ref, left_high, left_low, left_tail, left_buf, sems):
    states = left_buf.shape[1]
    sigma, count, rows = meta_ref[SIGMA], meta_ref[COUNT], meta_ref[ROWS]
    stride = packed_rows(rows)

    def each(i, act):
        bond = meta_ref[LIST + i] // 4
        at = lax.rem(i, BUFFERS)
        for p in range(states // TILE):
            part = pl.ds(p * TILE, TILE)

            @pl.when(rows > p * TILE)
            def _(part=part, p=p):
                act(
                    pltpu.make_async_copy(
                        left_ref.at[bond, sigma, part], left_buf.at[at, part], sems.at[p, at]
                    )
                )

    def start(i):
        @pl.when(i < count)
        def _():
            each(i, lambda copy: copy.start())

    for i in range(BUFFERS - 1):
        start(jnp.int32(i))

    def step(i, carry):
        at = lax.rem(i, BUFFERS)
        start(i + BUFFERS - 1)
        each(i, lambda copy: copy.wait())

        def chunk(t, inner):
            high, low = split(left_buf[at, pl.ds(pl.multiple_of(t * CHUNK, CHUNK), CHUNK), :])
            to = pl.ds(pl.multiple_of(i * stride + t * CHUNK, 16), CHUNK)
            left_high[to, :] = high[:, :SIDE]
            left_low[to, :] = low[:, :SIDE]
            left_tail[to, :] = jnp.concatenate([high[:, SIDE:], low[:, SIDE:]], axis=1)
            return inner

        lax.fori_loop(0, (rows + CHUNK - 1) // CHUNK, chunk, 0)
        return carry

    lax.fori_loop(0, count, step, 0)


def packed_rows(rows):
    return ((rows + 15) // 16) * 16


def matvec_kernel(k, cells, mpo_count, *refs):
    refs = list(refs)
    meta_ref = refs.pop(0)
    left_high, left_low, left_tail = [refs.pop(0) for _ in range(3)]
    if k:
        right_high, right_low, size_ref = [refs.pop(0) for _ in range(3)]
    else:
        right_ref, far_ref = refs.pop(0), refs.pop(0)
    totals = [(refs.pop(0), refs.pop(0)) for _ in range(k)]
    raw = [[refs.pop(0) for _ in range(4)] for _ in range(max(k, 1))]
    images = [[refs.pop(0) for _ in range(4)] for _ in range(k)]
    precond = [refs.pop(0) for _ in range(4)] if k else []
    last = k + 1 == MATVECS
    halves = [refs.pop(0), refs.pop(0)] if last else []
    out_ref = None if last else refs.pop(0)
    small_ref = refs.pop(0)
    if k:
        new_refs = [refs.pop(0) for _ in range(4)]
    else:
        new_refs = raw[0]
        right_high, right_low, size_ref = [refs.pop(0) for _ in range(3)]
    if last:
        known_ref, basis_out, images_out = [refs.pop(0) for _ in range(3)]
    high_ref, low_ref, tail_ref, mid_high, mid_low, order_ref = refs[:6]
    if not k:
        right_buf, sems = refs[6:]
    elif last:
        out_ref, sems = refs[6:]
    states, width = out_ref.shape
    count, rows, cols = meta_ref[COUNT], meta_ref[ROWS], meta_ref[COLS]
    stride = packed_rows(rows)

    core = lax.axis_index("rsec")
    if not k:
        size_ref[2 * OWN], size_ref[2 * OWN + 1] = rows, cols
        size_ref[2 * SIB], size_ref[2 * SIB + 1] = meta_ref[SIB_ROWS], meta_ref[SIB_COLS]
        for slot in (FIRST_PAIR, SECOND_PAIR):
            note = raw[0][slot][pl.ds(states, NOTE), :HALF]
            size_ref[2 * slot] = jnp.max(note[:1]).astype(jnp.int32)
            size_ref[2 * slot + 1] = jnp.max(note[1:]).astype(jnp.int32)
    def list_bonds(narrow):
        def step(i, place):
            hit = (size_ref[2 * lax.rem(meta_ref[LIST + i], 4) + 1] <= HALF) == narrow

            @pl.when(hit)
            def _():
                order_ref[place] = i

            return place + hit.astype(jnp.int32)

        return step

    thin_sources = lax.fori_loop(0, count, list_bonds(True), jnp.int32(0))
    lax.fori_loop(0, count, list_bonds(False), thin_sources)
    if not k:
        half = right_ref.shape[2]
        sigma = meta_ref[SIGMA]

        def each_right(i, act):
            bond = meta_ref[LIST + order_ref[i]] // 4
            at = lax.rem(i, BUFFERS)
            for ref, place, sem in ((right_ref, core, 0), (far_ref, 1 - core, 1)):
                part = pl.ds(pl.multiple_of(place * half, half), half)

                @pl.when((cols > HALF) | (place == 0))
                def _(ref=ref, part=part, sem=sem):
                    act(
                        pltpu.make_async_copy(
                            ref.at[bond, sigma], right_buf.at[at, part], sems.at[sem, at]
                        )
                    )

        def start_right(i):
            @pl.when(i < count)
            def _():
                each_right(i, lambda copy: copy.start())

        for i in range(BUFFERS):
            start_right(jnp.int32(i))

    if k:
        numbers = Scalars(totals, cells)
        theta = numbers.proj[k - 1, k - 1][:, :1]
    zero = jnp.zeros((8, width), F32)

    def fold(value):
        return jnp.sum(value.reshape(CHUNK // 8, 8, width), axis=0)

    def prepare(slot, carry):
        def step(i, carry):
            at = pl.ds(pl.multiple_of(i * CHUNK, CHUNK), CHUNK)
            if k:
                basis = numbers.basis(k - 1, [r[slot][at, :] for r in raw])
                image = numbers.basis(k - 1, [r[slot][at, :] for r in images])
                value = (image[-1] - theta * basis[-1]) / jnp.maximum(
                    precond[slot][at, :] - theta, 1.0
                )
                new_refs[slot][at, :] = value
                if last and slot in (OWN, SIB):
                    for which, group in enumerate((basis, image)):
                        for j, block in enumerate(group):
                            block = jnp.where(core == 0, block[:, :HALF], block[:, HALF:])
                            known_ref[which, slot, j, at, :] = block
            else:
                basis, image = [], []
                value = raw[0][slot][at, :]
            high, low = split(value)
            high_ref[slot, at, :] = high
            low_ref[slot, at, :] = low
            terms = [value * value]
            if slot == OWN:
                terms += [value * b for b in basis] + [value * g for g in image]
            return tuple(c + fold(t) for c, t in zip(carry, terms))

        return lax.fori_loop(0, states // CHUNK, step, carry)

    def dot(a, b):
        return jnp.dot(a, b, preferred_element_type=F32)

    def dot_nt(a, b):
        return lax.dot_general(a, b, (((1,), (1,)), ((), ())), preferred_element_type=F32)

    twice = functools.partial(jnp.concatenate, axis=0)

    def first_stage(slot, deep, narrow):
        begin, end = meta_ref[FIRST + slot], meta_ref[FIRST + 1 + slot]
        total = (end - begin) * stride
        top, rest = pl.ds(0, SIDE), pl.ds(SIDE, states - SIDE)
        if narrow:
            high_ref[slot, :, HALF:] = low_ref[slot, :, :HALF]
        if deep:
            tail = high_ref[slot, rest, :]
            tail_ref[...] = twice([tail, tail])

        def tile(first, size):
            at = pl.ds(pl.multiple_of(begin * stride + first, 16), size)
            high, low = left_high[at, :], left_low[at, :]
            mid = dot(high, high_ref[slot, top, :])
            if deep:
                mid = mid + dot(left_tail[at, :], tail_ref[...])
            if narrow:
                mid = mid[:, :HALF] + mid[:, HALF:] + dot(low, high_ref[slot, top, :HALF])
                mid_high[at, :] = jnp.concatenate(split(mid), axis=1)
            else:
                mid = mid + dot(low, high_ref[slot, top, :]) + dot(high, low_ref[slot, top, :])
                if deep:
                    mid = mid + dot(left_tail[at, : states - SIDE], low_ref[slot, rest, :])
                mid_high[at, :], mid_low[at, :] = split(mid)

        def step(t, carry):
            tile(t * PACK, PACK)
            return carry

        tiles = (total + PACK // 2 - 1) // PACK
        lax.fori_loop(0, tiles, step, 0)
        pl.when(total > tiles * PACK)(lambda: tile(tiles * PACK, PACK // 2))

    def both(test, action):
        pl.when(test)(lambda: action(True))
        pl.when(jnp.logical_not(test))(lambda: action(False))

    for slot in (OWN, SIB, FIRST_PAIR, SECOND_PAIR):
        if slot == OWN:
            own = prepare(slot, (zero,) * (1 + 2 * k))
        else:
            used = meta_ref[FIRST + 1 + slot] > meta_ref[FIRST + slot]
            pl.when(used | (slot == SIB))(lambda slot=slot: (prepare(slot, (zero,)), None)[1])

    def from_slot(slot, carry):
        both(
            size_ref[2 * slot] > SIDE,
            lambda deep: both(
                size_ref[2 * slot + 1] <= HALF, lambda narrow: first_stage(slot, deep, narrow)
            ),
        )
        return carry

    lax.fori_loop(0, 4, from_slot, 0)
    if last:
        sigma = meta_ref[SIGMA]
        outputs = [
            pltpu.make_async_copy(
                known_ref.at[which, slot],
                out.at[pl.ds(0, MATVECS - 1), sigma if slot == OWN else 1 - sigma],
                sems.at[which, slot],
            )
            for which, out in enumerate((basis_out, images_out))
            for slot in (OWN, SIB)
        ]
        for copy in outputs:
            copy.start()

    def clear(i, carry):
        at = pl.ds(pl.multiple_of(i * CHUNK, CHUNK), CHUNK)
        out_ref[at, :] = jnp.zeros((CHUNK, width), F32)
        return carry

    lax.fori_loop(0, states // CHUNK, clear, 0)
    zeros_at = mid_high.shape[0] - states
    for ref in (mid_high, mid_low):
        ref[pl.ds(zeros_at, states), :] = jnp.zeros((states, width), BF16)

    def second_stage(size, thin):
        to = pl.ds(0, size)

        def right_block(i, bond):
            if k:
                return right_high[bond], None if thin else right_low[bond]
            at = lax.rem(i, BUFFERS)
            if thin:
                high, low = jnp.concatenate(split(right_buf[at, pl.ds(0, HALF), :]), axis=0), None
            else:
                high, low = split(right_buf[at])
                right_low[bond] = low
            right_high[bond] = high
            return high, low

        def product(i, real, narrow):
            bond = order_ref[i]
            at = pl.ds(pl.multiple_of(jnp.where(real, bond * stride, zeros_at), 16), size)
            high = mid_high[at, :]
            right, right_rest = right_block(i, bond)
            if narrow:
                part = right[:, :HALF]
                value = dot_nt(high, jnp.concatenate([part, part], axis=1))
                if not thin:
                    value = value + dot_nt(high[:, :HALF], right_rest[:, :HALF])
            else:
                value = dot_nt(high, right)
                if not thin:
                    value = value + dot_nt(high, right_rest) + dot_nt(mid_low[at, :], right)
            if thin:
                value = value[:, :HALF] + value[:, HALF:]
                if not narrow:
                    value = value + dot_nt(mid_low[at, :], right[:HALF, :])
            return value

        def run(begin, end, narrow):
            def pair(p, carry):
                one = begin + 2 * p
                real = one + 1 < end
                two = jnp.where(real, one + 1, one)
                if not k:
                    each_right(one, lambda copy: copy.wait())
                    pl.when(real)(lambda: each_right(two, lambda copy: copy.wait()))
                value = product(one, True, narrow) + product(two, real, narrow)
                if thin:
                    out_ref[to, :HALF] += value
                else:
                    out_ref[to, :] += value
                if not k:
                    start_right(one + BUFFERS)
                    pl.when(real)(lambda: start_right(two + BUFFERS))
                return carry

            lax.fori_loop(0, (end - begin + 1) // 2, pair, 0)

        run(0, thin_sources, True)
        run(thin_sources, count, False)

    for size in range(TILE, states + 1, TILE):
        pl.when((rows <= size) & (rows > size - TILE))(
            lambda size=size: both(cols <= HALF, functools.partial(second_stage, size))
        )

    def finish(i, carry):
        at = pl.ds(pl.multiple_of(i * CHUNK, CHUNK), CHUNK)
        mask = live_mask((CHUNK, width), i * CHUNK, rows, cols)
        value = jnp.where(mask, out_ref[at, :], 0.0)
        if last:
            halves[0][at, :] = jnp.where(core == 0, value[:, :HALF], value[:, HALF:])
            halves[1][at, :] = jnp.where(core == 0, value[:, HALF:], value[:, :HALF])
        else:
            out_ref[at, :] = value
        basis = numbers.basis(k - 1, [r[OWN][at, :] for r in raw]) if k else []
        terms = [value * new_refs[OWN][at, :]] + [value * b for b in basis]
        return tuple(c + fold(t) for c, t in zip(carry, terms))

    late = lax.fori_loop(0, states // CHUNK, finish, (zero,) * (1 + k))

    def whole(value):
        return jnp.sum(jnp.sum(value, axis=1, keepdims=True), axis=0, keepdims=True)

    share = 1.0 / mpo_count
    entries = [whole(own[0]) * share, whole(late[0])]
    for j in range(2):
        entries.append(whole(own[1 + j]) * share if j < k else None)
    for j in range(2):
        entries.append(whole(late[1 + j]) if j < k else None)
    for j in range(2):
        entries.append(whole(own[1 + k + j]) * share if j < k else None)
    row_ids = lax.broadcasted_iota(jnp.int32, small_ref.shape, 0)
    small = jnp.zeros(small_ref.shape, F32)
    for index, entry in enumerate(entries):
        if entry is not None:
            small = jnp.where(row_ids == index, entry, small)
    small_ref[...] = small
    if last:
        for copy in outputs:
            copy.wait()


def join_kernel(a_ref, b_ref, parts_ref, out_ref, small_ref):
    add_parts(parts_ref, small_ref)

    def step(i, carry):
        at = pl.ds(pl.multiple_of(i * CHUNK, CHUNK), CHUNK)
        out_ref[at, :] = a_ref[at, :] + b_ref[at, :]
        return carry

    lax.fori_loop(0, out_ref.shape[0] // CHUNK, step, 0)


def add_parts(parts_ref, small_ref):
    total = parts_ref[0]
    for i in range(1, parts_ref.shape[0]):
        total = total + parts_ref[i]
    small_ref[...] = total


def fill_kernel(cells, meta_ref, *refs):
    totals = [refs[2 * i : 2 * i + 2] for i in range(MATVECS)]
    known_ref, raw_own, raw_sib, *parts = refs[2 * MATVECS : 2 * MATVECS + 7]
    basis_out, images_out, projected_ref, basis_buf, images_buf, sems = refs[-6:]
    last = MATVECS - 1
    sigma = meta_ref[SIGMA]
    numbers = Scalars(totals, cells)
    core = lax.axis_index("rsec")
    states, half = basis_buf.shape[1:]
    lanes = pl.ds(pl.multiple_of(core * half, half), half)
    inverse = 1.0 / numbers.norm[last][:, :1]
    corr = [a[:, :1] for a in numbers.corr[last]]
    copies = []
    for slot, raw, image in ((OWN, raw_own, parts[:2]), (SIB, raw_sib, parts[2:])):

        def step(i, carry, slot=slot, raw=raw, image=image):
            at = pl.ds(pl.multiple_of(i * CHUNK, CHUNK), CHUNK)
            fields = (raw[at, lanes], image[0][at, :] + image[1][at, :])
            for which, buf in enumerate((basis_buf, images_buf)):
                value = fields[which]
                for j in range(last):
                    value = value - corr[j] * known_ref[which, slot, j, at, :]
                buf[slot, at, :] = value * inverse
            return carry

        lax.fori_loop(0, states // CHUNK, step, 0)
        sector = sigma if slot == OWN else 1 - sigma
        for which, (buf, out) in enumerate(((basis_buf, basis_out), (images_buf, images_out))):
            copies.append(
                pltpu.make_async_copy(buf.at[slot], out.at[last, sector], sems.at[which, slot])
            )
            copies[-1].start()
    shape = projected_ref.shape
    row_ids = lax.broadcasted_iota(jnp.int32, shape, 0)
    col_ids = lax.broadcasted_iota(jnp.int32, shape, 1)
    value = jnp.zeros(shape, F32)
    for i in range(MATVECS):
        for j in range(MATVECS):
            value = jnp.where((row_ids == i) & (col_ids == j), numbers.proj[i, j][:, :1], value)
    projected_ref[...] = value
    for copy in copies:
        copy.wait()


def per_device(
    wavefunction, left_env, right_env, precond_diag, down_charge, bond_mask, left_size, right_size
):
    sectors, states, columns = wavefunction.shape
    bonds = left_env.shape[0]
    lsec_count = lax.axis_size("lsec")
    mpo_count = lax.axis_size("mpo")
    assert sectors == 2 and lax.axis_size("rsec") == 2
    width = 2 * columns
    cells = float(lsec_count * sectors * states * width)
    field = jax.ShapeDtypeStruct((states, width), F32)
    half_field = jax.ShapeDtypeStruct((states, columns), F32)
    small = jax.ShapeDtypeStruct((8, 128), F32)
    params = pltpu.CompilerParams(vmem_limit_bytes=16 * 2**20)

    swap = [(0, 1), (1, 0)]
    first_pairs = [(i, i ^ 1) for i in range(lsec_count) if i ^ 1 < lsec_count]
    second_pairs = [(i, j) for a in range(1, lsec_count - 1, 2) for i, j in ((a, a + 1), (a + 1, a))]
    anywhere = pl.BlockSpec(memory_space=pl.ANY)
    in_hbm = pl.BlockSpec(memory_space=pltpu.HBM)

    def hold(value):
        return pltpu.with_memory_space_constraint(value, pltpu.HBM)

    def neighbours(value):
        return lax.ppermute(value, "lsec", first_pairs), lax.ppermute(value, "lsec", second_pairs)

    wave_all = lax.all_gather(wavefunction, "rsec", axis=2, tiled=True)
    right_send, _ = lax.optimization_barrier((right_env, wave_all))
    right_far = lax.ppermute(right_send, "rsec", swap)
    mask_rows = bond_mask.T
    down_charge, mask_rows, left_size, right_size = [
        hold(x) for x in (down_charge, mask_rows, left_size, right_size)
    ]
    own = pl.pallas_call(
        first_kernel,
        out_shape=jax.ShapeDtypeStruct((states + NOTE, width), F32),
        in_specs=[in_hbm] * 3 + [whole_vmem()],
        out_specs=whole_vmem(),
        scratch_shapes=[
            pltpu.SMEM(down_charge.shape, jnp.int32),
            pltpu.SMEM(left_size.shape, jnp.int32),
            pltpu.SMEM(right_size.shape, jnp.int32),
            pltpu.SemaphoreType.DMA((3,)),
        ],
        compiler_params=params,
        name="first",
    )(down_charge, left_size, right_size, wave_all)
    near_waves = neighbours(own)
    sib, meta = pl.pallas_call(
        functools.partial(prep_kernel, lsec_count, bonds),
        out_shape=(field, jax.ShapeDtypeStruct((LIST + bonds,), jnp.int32)),
        in_specs=[in_hbm] * 4 + [whole_vmem(), anywhere],
        out_specs=(whole_vmem(), whole_smem()),
        scratch_shapes=[
            pltpu.SMEM(down_charge.shape, jnp.int32),
            pltpu.SMEM(mask_rows.shape, jnp.int32),
            pltpu.SMEM(left_size.shape, jnp.int32),
            pltpu.SMEM(right_size.shape, jnp.int32),
            pltpu.SemaphoreType.DMA((4,)),
        ],
        compiler_params=params,
        name="prep",
    )(down_charge, mask_rows, left_size, right_size, wave_all, own)
    raw = [(own, sib, *near_waves)]
    diag_send, _ = lax.optimization_barrier((precond_diag, sib))
    diag_far = lax.ppermute(diag_send, "rsec", swap)
    diag_own, diag_sib = pl.pallas_call(
        diag_kernel,
        out_shape=(field,) * 2,
        in_specs=[whole_smem()] + [whole_vmem()] * 2,
        out_specs=(whole_vmem(),) * 2,
        compiler_params=params,
        name="diag",
    )(meta, hold(precond_diag), diag_far)

    near_diags = neighbours(diag_own)

    def mpo_pair(value):
        if mpo_count != 2:
            value = lax.psum(value, "mpo")
            return value, jnp.zeros_like(value)
        return value, lax.ppermute(value, "mpo", swap)

    def join(value, part):
        parts = lax.all_gather(part, ("lsec", "rsec"))
        value, part = pl.pallas_call(
            join_kernel,
            out_shape=(field, small),
            in_specs=[whole_vmem()] * 3,
            out_specs=(whole_vmem(),) * 2,
            compiler_params=params,
            name="join",
        )(*mpo_pair(value), parts)
        return value, mpo_pair(part)

    most = bonds - bonds // 5 if bonds % 5 == 0 else bonds
    packed = most * states + PACK
    lefts = pl.pallas_call(
        left_kernel,
        out_shape=(
            pltpu.VMEM((packed, SIDE), BF16),
            pltpu.VMEM((packed, SIDE), BF16),
            pltpu.VMEM((packed, 2 * (states - SIDE)), BF16),
        ),
        in_specs=[whole_smem(), anywhere],
        out_specs=(whole_vmem(),) * 3,
        scratch_shapes=[
            pltpu.VMEM((BUFFERS, states, states), F32),
            pltpu.SemaphoreType.DMA((states // TILE, BUFFERS)),
        ],
        compiler_params=params,
        cost_estimate=pl.CostEstimate(flops=0, transcendentals=0, bytes_accessed=bonds * states * states * 4),
        name="left",
    )(meta, hold(left_env))
    out = jax.ShapeDtypeStruct((MATVECS, sectors, states, columns), F32)
    known = jax.ShapeDtypeStruct((2, sectors, MATVECS - 1, states, columns), F32)

    def matvec(k, rights, inputs):
        last = k + 1 == MATVECS
        out_shape = [half_field] * 2 if last else [field]
        out_shape += [small] + [field] * (4 if k else 0)
        out_specs = [whole_vmem()] * len(out_shape)
        scratch = [
            pltpu.VMEM((4, states, width), BF16),
            pltpu.VMEM((4, states, width), BF16),
            pltpu.VMEM((2 * (states - SIDE), width), BF16),
            pltpu.VMEM((packed + states, width), BF16),
            pltpu.VMEM((packed + states, width), BF16),
            pltpu.SMEM((bonds,), jnp.int32),
        ]
        if k == 0:
            out_shape += [pltpu.VMEM((most, width, width), BF16)] * 2
            out_shape += [jax.ShapeDtypeStruct((8,), jnp.int32)]
            out_specs += [whole_vmem()] * 2 + [whole_smem()]
            scratch += [
                pltpu.VMEM((BUFFERS, width, width), F32),
                pltpu.SemaphoreType.DMA((2, BUFFERS)),
            ]
            right_specs = [anywhere] * 2
        else:
            right_specs = [whole_vmem()] * 2 + [whole_smem()]
        if last:
            out_shape += [known, out, out]
            out_specs += [whole_vmem(), anywhere, anywhere]
            scratch += [pltpu.VMEM((states, width), F32), pltpu.SemaphoreType.DMA((2, 2))]
        return pl.pallas_call(
            functools.partial(matvec_kernel, k, cells, mpo_count),
            out_shape=tuple(out_shape),
            in_specs=[whole_smem()] + [whole_vmem()] * 3 + right_specs + [whole_vmem()] * len(inputs),
            out_specs=tuple(out_specs),
            scratch_shapes=scratch,
            compiler_params=params,
            cost_estimate=pl.CostEstimate(
                flops=2 * 3 * bonds * states * width * (states + width),
                transcendentals=0,
                bytes_accessed=bonds * states * states,
            ),
            name=f"matvec{k}",
        )(meta, *lefts, *rights, *inputs)

    def flatten(groups):
        return [x for group in groups for x in group]

    totals = []
    images = []
    for k in range(MATVECS - 1):
        if k == 0:
            value, part, *rights = matvec(0, [hold(right_env), right_far], list(raw[0]))
            value, near_diags = lax.optimization_barrier((value, near_diags))
            precond = (diag_own, diag_sib, *near_diags)
        else:
            value, part, *fresh = matvec(k, rights, [*totals, *flatten(raw), *flatten(images), *precond])
            raw.append(tuple(fresh))
        value, total = join(value, part)
        totals += total
        images.append((value, lax.ppermute(value, "rsec", swap), *neighbours(value)))

    inputs = [*totals, *flatten(raw), *flatten(images), *precond]
    near, away, part, own, sib, _, _, known_blocks, *outs = matvec(MATVECS - 1, rights, inputs)
    own_half = mpo_pair(near)
    sib_half = mpo_pair(lax.ppermute(away, "rsec", swap))
    parts = lax.all_gather(part, ("lsec", "rsec"))
    totals += mpo_pair(
        pl.pallas_call(
            add_parts,
            out_shape=small,
            in_specs=[whole_vmem()],
            out_specs=whole_vmem(),
            compiler_params=params,
            name="add",
        )(parts)
    )
    operands = [*totals, known_blocks, own, sib, *own_half, *sib_half]
    return pl.pallas_call(
        functools.partial(fill_kernel, cells),
        out_shape=(out, out, jax.ShapeDtypeStruct((MATVECS, MATVECS), F32)),
        in_specs=[whole_smem()] + [whole_vmem()] * len(operands) + [anywhere] * 2,
        out_specs=(anywhere, anywhere, whole_vmem()),
        scratch_shapes=[
            pltpu.VMEM((sectors, states, columns), F32),
            pltpu.VMEM((sectors, states, columns), F32),
            pltpu.SemaphoreType.DMA((2, 2)),
        ],
        input_output_aliases={1 + len(operands): 0, 2 + len(operands): 1},
        compiler_params=params,
        name="fill",
    )(meta, *operands, *outs)


def solution(mesh):
    placed = (
        P(("grp", "lsec"), None, "rsec"),
        P("mpo", ("grp", "lsec"), None, None),
        P("mpo", ("grp", "lsec"), "rsec", None),
        P(("grp", "lsec"), None, "rsec"),
        P("grp"),
        P("mpo", ("grp", "lsec")),
        P(("grp", "lsec")),
        P(("grp", "lsec")),
    )
    return jax.shard_map(
        per_device,
        mesh=mesh,
        in_specs=placed,
        out_specs=(
            P(None, ("grp", "lsec"), None, "rsec"),
            P(None, ("grp", "lsec"), None, "rsec"),
            P("grp", None),
        ),
        check_vma=False,
    )
```

```python
import functools

import jax
import jax.numpy as jnp
from jax import lax
from jax.experimental import pallas as pl
from jax.experimental.pallas import tpu as pltpu
from jax.sharding import PartitionSpec as P

EPSILON = 1e-06
MATVECS = 3
F32 = jnp.float32
BF16 = jnp.bfloat16
SIGMA, COUNT, ROWS, COLS, FIRST, SIB_ROWS, SIB_COLS, LIST = 0, 1, 2, 3, 4, 9, 10, 16
OWN, SIB, FIRST_PAIR, SECOND_PAIR = 0, 1, 2, 3
CHUNK = 64
TILE = 128
SIDE = 256
HALF = 128
NOTE = 8
PACK = 512
BUFFERS = 8


def whole_vmem():
    return pl.BlockSpec(memory_space=pltpu.VMEM)


def whole_smem():
    return pl.BlockSpec(memory_space=pltpu.SMEM)


def split(value):
    high = value.astype(BF16)
    return high, (value - high.astype(F32)).astype(BF16)


def orientation(down_ref, place):
    def step(i, flips):
        straight = (down_ref[2 * i] == down_ref[2 * i - 2]) | (
            down_ref[2 * i + 1] == down_ref[2 * i - 1]
        )
        return jnp.where(straight, flips, 1 - flips)

    return lax.fori_loop(1, place + 1, step, jnp.int32(0))


def live_mask(shape, row0, rows, cols):
    row_ids = row0 + lax.broadcasted_iota(jnp.int32, shape, 0)
    col_ids = lax.broadcasted_iota(jnp.int32, shape, 1)
    return (row_ids < rows) & (col_ids < cols)


def read_small(pairs, sems):
    copies = [pltpu.make_async_copy(*pair, sems.at[i]) for i, pair in enumerate(pairs)]
    for copy in copies:
        copy.start()
    for copy in copies:
        copy.wait()


def masked_block(out_ref, wave_ref, slot, rows, cols):
    states, width = wave_ref.shape[1:]

    def fill(i, carry):
        at = pl.ds(pl.multiple_of(i * CHUNK, CHUNK), CHUNK)
        mask = live_mask((CHUNK, width), i * CHUNK, rows, cols)
        out_ref[at, :] = jnp.where(mask, wave_ref[slot, at, :], 0.0)
        return carry

    lax.fori_loop(0, states // CHUNK, fill, 0)


def first_kernel(down_in, left_in, right_in, wave_ref, own_ref, down_ref, left_size_ref,
                 right_size_ref, sems):
    read_small(((down_in, down_ref), (left_in, left_size_ref), (right_in, right_size_ref)), sems)
    sigma = lax.axis_index("rsec") ^ orientation(down_ref, lax.axis_index("lsec"))
    rows, cols = left_size_ref[sigma], right_size_ref[sigma]
    masked_block(own_ref, wave_ref, sigma, rows, cols)
    note = (NOTE, own_ref.shape[1])
    row_ids = lax.broadcasted_iota(jnp.int32, note, 0)
    states = wave_ref.shape[1]
    own_ref[pl.ds(states, NOTE), :] = jnp.where(row_ids == 0, rows, cols).astype(F32)


def prep_kernel(lsec_count, bonds, down_in, mask_in, left_in, right_in, wave_ref, own_ref,
                sib_ref, meta_ref, down_ref, mask_ref, left_size_ref, right_size_ref, sems):
    read_small(
        ((down_in, down_ref), (mask_in, mask_ref), (left_in, left_size_ref), (right_in, right_size_ref)),
        sems,
    )
    place = lax.axis_index("lsec")
    core = lax.axis_index("rsec")
    first_bond = lax.axis_index("mpo") * bonds
    sigma = core ^ orientation(down_ref, place)
    own_down = down_ref[2 * place + sigma]
    sib_down = down_ref[2 * place + 1 - sigma]
    before = jnp.maximum(place - 1, 0)
    after = jnp.minimum(place + 1, lsec_count - 1)
    prev_down = down_ref[2 * before + (core ^ orientation(down_ref, before))]
    next_down = down_ref[2 * after + (core ^ orientation(down_ref, after))]
    has_prev = (place > 0) & (prev_down == own_down)
    has_next = (place < lsec_count - 1) & (next_down == own_down)
    odd = lax.rem(place, 2)
    has_lower = sib_down == own_down - 1
    has_upper = sib_down == own_down + 1

    def gather(slot, count):
        meta_ref[FIRST + slot] = count

        def step(bond, count):
            kind = lax.rem(first_bond + bond, 5)
            if slot == OWN:
                there = kind == 0
            elif slot == SIB:
                there = ((kind == 3) & has_lower) | ((kind == 4) & has_upper)
            else:
                lower = odd if slot == FIRST_PAIR else 1 - odd
                there = ((kind == 1) & has_prev & (lower == 1)) | (
                    (kind == 2) & has_next & (lower == 0)
                )
            there = there & (mask_ref[sigma, bond] > 0)

            @pl.when(there)
            def _():
                meta_ref[LIST + count] = bond * 4 + slot

            return count + there.astype(jnp.int32)

        return lax.fori_loop(0, bonds, step, count)

    count = jnp.int32(0)
    for slot in (OWN, SIB, FIRST_PAIR, SECOND_PAIR):
        count = gather(slot, count)
    meta_ref[FIRST + 4] = count
    rows, cols = left_size_ref[sigma], right_size_ref[sigma]
    meta_ref[SIGMA] = sigma
    meta_ref[COUNT] = count
    meta_ref[ROWS] = rows
    meta_ref[COLS] = cols
    meta_ref[SIB_ROWS] = left_size_ref[1 - sigma]
    meta_ref[SIB_COLS] = right_size_ref[1 - sigma]
    masked_block(sib_ref, wave_ref, 1 - sigma, left_size_ref[1 - sigma], right_size_ref[1 - sigma])


def diag_kernel(meta_ref, diag_ref, diag_far, diag_own, diag_sib):
    states, width = diag_own.shape
    half = width // 2
    sigma, core = meta_ref[SIGMA], lax.axis_index("rsec")
    near = pl.ds(pl.multiple_of(core * half, half), half)
    away = pl.ds(pl.multiple_of((1 - core) * half, half), half)
    for out_ref, slot in ((diag_own, sigma), (diag_sib, 1 - sigma)):

        def fill(i, carry, out_ref=out_ref, slot=slot):
            at = pl.ds(pl.multiple_of(i * CHUNK, CHUNK), CHUNK)
            out_ref[at, near] = diag_ref[slot, at, :]
            out_ref[at, away] = diag_far[slot, at, :]
            return carry

        lax.fori_loop(0, states // CHUNK, fill, 0)


def row(value, index):
    return value[index : index + 1, :]


class Scalars:
    def __init__(self, totals, cells):
        self.proj = {}
        self.gram = {}
        self.norm = []
        self.corr = []
        for k, total in enumerate(totals):
            value = (total[0][...] + total[1][...]) / cells
            size, inner = row(value, 0), row(value, 1)
            a = [row(value, 2 + j) for j in range(k)]
            e = [row(value, 4 + j) for j in range(k)]
            f = [row(value, 6 + j) for j in range(k)]
            length = size
            theta = inner
            for j in range(k):
                length = length - 2.0 * a[j] * a[j]
                theta = theta - a[j] * e[j] - a[j] * f[j]
            for i in range(k):
                for j in range(k):
                    length = length + a[i] * a[j] * self.gram[i, j]
                    theta = theta + a[i] * a[j] * self.proj[i, j]
            length = jnp.maximum(length, 0.0)
            square = length + EPSILON
            norm = jnp.sqrt(square)
            for j in range(k):
                up, down, both = e[j], f[j], a[j]
                for i in range(k):
                    up = up - a[i] * self.proj[j, i]
                    down = down - a[i] * self.proj[i, j]
                    both = both - a[i] * self.gram[i, j]
                self.proj[j, k] = up / norm
                self.proj[k, j] = down / norm
                self.gram[j, k] = self.gram[k, j] = both / norm
            self.proj[k, k] = theta / square
            self.gram[k, k] = length / square
            self.norm.append(norm)
            self.corr.append(a)

    def basis(self, k, fields):
        done = []
        for step in range(k + 1):
            value = fields[step]
            for j in range(step):
                value = value - self.corr[step][j][:, :1] * done[j]
            done.append(value / self.norm[step][:, :1])
        return done


def left_kernel(meta_ref, left_ref, left_high, left_low, left_tail, left_buf, sems):
    states = left_buf.shape[1]
    sigma, count, rows = meta_ref[SIGMA], meta_ref[COUNT], meta_ref[ROWS]
    stride = packed_rows(rows)

    def each(i, act):
        bond = meta_ref[LIST + i] // 4
        at = lax.rem(i, BUFFERS)
        for p in range(states // TILE):
            part = pl.ds(p * TILE, TILE)

            @pl.when(rows > p * TILE)
            def _(part=part, p=p):
                act(
                    pltpu.make_async_copy(
                        left_ref.at[bond, sigma, part], left_buf.at[at, part], sems.at[p, at]
                    )
                )

    def start(i):
        @pl.when(i < count)
        def _():
            each(i, lambda copy: copy.start())

    for i in range(BUFFERS - 1):
        start(jnp.int32(i))

    def step(i, carry):
        at = lax.rem(i, BUFFERS)
        start(i + BUFFERS - 1)
        each(i, lambda copy: copy.wait())

        def chunk(t, inner):
            high, low = split(left_buf[at, pl.ds(pl.multiple_of(t * CHUNK, CHUNK), CHUNK), :])
            to = pl.ds(pl.multiple_of(i * stride + t * CHUNK, 16), CHUNK)
            left_high[to, :] = high[:, :SIDE]
            left_low[to, :] = low[:, :SIDE]
            left_tail[to, :] = jnp.concatenate([high[:, SIDE:], low[:, SIDE:]], axis=1)
            return inner

        lax.fori_loop(0, (rows + CHUNK - 1) // CHUNK, chunk, 0)
        return carry

    lax.fori_loop(0, count, step, 0)


def packed_rows(rows):
    return ((rows + 15) // 16) * 16


def matvec_kernel(k, cells, mpo_count, *refs):
    refs = list(refs)
    meta_ref = refs.pop(0)
    left_high, left_low, left_tail = [refs.pop(0) for _ in range(3)]
    if k:
        right_high, right_low, size_ref = [refs.pop(0) for _ in range(3)]
    else:
        right_ref, far_ref = refs.pop(0), refs.pop(0)
    totals = [(refs.pop(0), refs.pop(0)) for _ in range(k)]
    raw = [[refs.pop(0) for _ in range(4)] for _ in range(max(k, 1))]
    images = [[refs.pop(0) for _ in range(4)] for _ in range(k)]
    precond = [refs.pop(0) for _ in range(4)] if k else []
    last = k + 1 == MATVECS
    halves = [refs.pop(0), refs.pop(0)] if last else []
    out_ref = None if last else refs.pop(0)
    small_ref = refs.pop(0)
    if k:
        new_refs = [refs.pop(0) for _ in range(4)]
    else:
        new_refs = raw[0]
        right_high, right_low, size_ref = [refs.pop(0) for _ in range(3)]
    if last:
        known_ref, basis_out, images_out = [refs.pop(0) for _ in range(3)]
    high_ref, low_ref, tail_ref, mid_high, mid_low, order_ref = refs[:6]
    if not k:
        right_buf, sems = refs[6:]
    elif last:
        out_ref, sems = refs[6:]
    states, width = out_ref.shape
    count, rows, cols = meta_ref[COUNT], meta_ref[ROWS], meta_ref[COLS]
    stride = packed_rows(rows)

    core = lax.axis_index("rsec")
    if not k:
        size_ref[2 * OWN], size_ref[2 * OWN + 1] = rows, cols
        size_ref[2 * SIB], size_ref[2 * SIB + 1] = meta_ref[SIB_ROWS], meta_ref[SIB_COLS]
        for slot in (FIRST_PAIR, SECOND_PAIR):
            note = raw[0][slot][pl.ds(states, NOTE), :HALF]
            size_ref[2 * slot] = jnp.max(note[:1]).astype(jnp.int32)
            size_ref[2 * slot + 1] = jnp.max(note[1:]).astype(jnp.int32)
    def list_bonds(narrow):
        def step(i, place):
            hit = (size_ref[2 * lax.rem(meta_ref[LIST + i], 4) + 1] <= HALF) == narrow

            @pl.when(hit)
            def _():
                order_ref[place] = i

            return place + hit.astype(jnp.int32)

        return step

    thin_sources = lax.fori_loop(0, count, list_bonds(True), jnp.int32(0))
    lax.fori_loop(0, count, list_bonds(False), thin_sources)
    if not k:
        half = right_ref.shape[2]
        sigma = meta_ref[SIGMA]

        def each_right(i, act):
            bond = meta_ref[LIST + order_ref[i]] // 4
            for ref, place, sem in ((right_ref, core, 0), (far_ref, 1 - core, 1)):
                part = pl.ds(pl.multiple_of(place * half, half), half)

                @pl.when((cols > HALF) | (place == 0))
                def _(ref=ref, part=part, sem=sem):
                    act(
                        pltpu.make_async_copy(
                            ref.at[bond, sigma], right_buf.at[i, part], sems.at[sem, i]
                        )
                    )

        def start_right(i, carry):
            each_right(i, lambda copy: copy.start())
            return carry

        lax.fori_loop(0, count, start_right, 0)

    if k:
        numbers = Scalars(totals, cells)
        theta = numbers.proj[k - 1, k - 1][:, :1]
    zero = jnp.zeros((8, width), F32)

    def fold(value):
        return jnp.sum(value.reshape(CHUNK // 8, 8, width), axis=0)

    def prepare(slot, carry):
        def step(i, carry):
            at = pl.ds(pl.multiple_of(i * CHUNK, CHUNK), CHUNK)
            if k:
                basis = numbers.basis(k - 1, [r[slot][at, :] for r in raw])
                image = numbers.basis(k - 1, [r[slot][at, :] for r in images])
                value = (image[-1] - theta * basis[-1]) / jnp.maximum(
                    precond[slot][at, :] - theta, 1.0
                )
                new_refs[slot][at, :] = value
                if last and slot in (OWN, SIB):
                    for which, group in enumerate((basis, image)):
                        for j, block in enumerate(group):
                            block = jnp.where(core == 0, block[:, :HALF], block[:, HALF:])
                            known_ref[which, slot, j, at, :] = block
            else:
                basis, image = [], []
                value = raw[0][slot][at, :]
            high, low = split(value)
            high_ref[slot, at, :] = high
            low_ref[slot, at, :] = low
            terms = [value * value]
            if slot == OWN:
                terms += [value * b for b in basis] + [value * g for g in image]
            return tuple(c + fold(t) for c, t in zip(carry, terms))

        return lax.fori_loop(0, states // CHUNK, step, carry)

    def dot(a, b):
        return jnp.dot(a, b, preferred_element_type=F32)

    def dot_nt(a, b):
        return lax.dot_general(a, b, (((1,), (1,)), ((), ())), preferred_element_type=F32)

    twice = functools.partial(jnp.concatenate, axis=0)

    def first_stage(slot, deep, narrow):
        begin, end = meta_ref[FIRST + slot], meta_ref[FIRST + 1 + slot]
        total = (end - begin) * stride
        top, rest = pl.ds(0, SIDE), pl.ds(SIDE, states - SIDE)
        if narrow:
            high_ref[slot, :, HALF:] = low_ref[slot, :, :HALF]
        if deep:
            tail = high_ref[slot, rest, :]
            tail_ref[...] = twice([tail, tail])

        def tile(first, size):
            at = pl.ds(pl.multiple_of(begin * stride + first, 16), size)
            high, low = left_high[at, :], left_low[at, :]
            mid = dot(high, high_ref[slot, top, :])
            if deep:
                mid = mid + dot(left_tail[at, :], tail_ref[...])
            if narrow:
                mid = mid[:, :HALF] + mid[:, HALF:] + dot(low, high_ref[slot, top, :HALF])
                mid_high[at, :] = jnp.concatenate(split(mid), axis=1)
            else:
                mid = mid + dot(low, high_ref[slot, top, :]) + dot(high, low_ref[slot, top, :])
                if deep:
                    mid = mid + dot(left_tail[at, : states - SIDE], low_ref[slot, rest, :])
                mid_high[at, :], mid_low[at, :] = split(mid)

        def step(t, carry):
            tile(t * PACK, PACK)
            return carry

        tiles = (total + PACK // 2 - 1) // PACK
        lax.fori_loop(0, tiles, step, 0)
        pl.when(total > tiles * PACK)(lambda: tile(tiles * PACK, PACK // 2))

    def both(test, action):
        pl.when(test)(lambda: action(True))
        pl.when(jnp.logical_not(test))(lambda: action(False))

    for slot in (OWN, SIB, FIRST_PAIR, SECOND_PAIR):
        if slot == OWN:
            own = prepare(slot, (zero,) * (1 + 2 * k))
        else:
            used = meta_ref[FIRST + 1 + slot] > meta_ref[FIRST + slot]
            pl.when(used | (slot == SIB))(lambda slot=slot: (prepare(slot, (zero,)), None)[1])

    def from_slot(slot, carry):
        both(
            size_ref[2 * slot] > SIDE,
            lambda deep: both(
                size_ref[2 * slot + 1] <= HALF, lambda narrow: first_stage(slot, deep, narrow)
            ),
        )
        return carry

    lax.fori_loop(0, 4, from_slot, 0)
    if last:
        sigma = meta_ref[SIGMA]
        outputs = [
            pltpu.make_async_copy(
                known_ref.at[which, slot],
                out.at[pl.ds(0, MATVECS - 1), sigma if slot == OWN else 1 - sigma],
                sems.at[which, slot],
            )
            for which, out in enumerate((basis_out, images_out))
            for slot in (OWN, SIB)
        ]
        for copy in outputs:
            copy.start()

    def clear(i, carry):
        at = pl.ds(pl.multiple_of(i * CHUNK, CHUNK), CHUNK)
        out_ref[at, :] = jnp.zeros((CHUNK, width), F32)
        return carry

    lax.fori_loop(0, states // CHUNK, clear, 0)
    zeros_at = mid_high.shape[0] - states
    for ref in (mid_high, mid_low):
        ref[pl.ds(zeros_at, states), :] = jnp.zeros((states, width), BF16)

    def second_stage(size, thin):
        to = pl.ds(0, size)

        def right_block(i, bond):
            if k:
                return right_high[bond], None if thin else right_low[bond]
            if thin:
                high, low = jnp.concatenate(split(right_buf[i, pl.ds(0, HALF), :]), axis=0), None
            else:
                high, low = split(right_buf[i])
                right_low[bond] = low
            right_high[bond] = high
            return high, low

        def product(i, real, narrow):
            bond = order_ref[i]
            at = pl.ds(pl.multiple_of(jnp.where(real, bond * stride, zeros_at), 16), size)
            high = mid_high[at, :]
            right, right_rest = right_block(i, bond)
            if narrow:
                part = right[:, :HALF]
                value = dot_nt(high, jnp.concatenate([part, part], axis=1))
                if not thin:
                    value = value + dot_nt(high[:, :HALF], right_rest[:, :HALF])
            else:
                value = dot_nt(high, right)
                if not thin:
                    value = value + dot_nt(high, right_rest) + dot_nt(mid_low[at, :], right)
            if thin:
                value = value[:, :HALF] + value[:, HALF:]
                if not narrow:
                    value = value + dot_nt(mid_low[at, :], right[:HALF, :])
            return value

        def run(begin, end, narrow):
            def pair(p, carry):
                one = begin + 2 * p
                real = one + 1 < end
                two = jnp.where(real, one + 1, one)
                if not k:
                    each_right(one, lambda copy: copy.wait())
                    pl.when(real)(lambda: each_right(two, lambda copy: copy.wait()))
                value = product(one, True, narrow) + product(two, real, narrow)
                if thin:
                    out_ref[to, :HALF] += value
                else:
                    out_ref[to, :] += value
                return carry

            lax.fori_loop(0, (end - begin + 1) // 2, pair, 0)

        run(0, thin_sources, True)
        run(thin_sources, count, False)

    for size in range(TILE, states + 1, TILE):
        pl.when((rows <= size) & (rows > size - TILE))(
            lambda size=size: both(cols <= HALF, functools.partial(second_stage, size))
        )

    def finish(i, carry):
        at = pl.ds(pl.multiple_of(i * CHUNK, CHUNK), CHUNK)
        mask = live_mask((CHUNK, width), i * CHUNK, rows, cols)
        value = jnp.where(mask, out_ref[at, :], 0.0)
        if last:
            halves[0][at, :] = jnp.where(core == 0, value[:, :HALF], value[:, HALF:])
            halves[1][at, :] = jnp.where(core == 0, value[:, HALF:], value[:, :HALF])
        else:
            out_ref[at, :] = value
        basis = numbers.basis(k - 1, [r[OWN][at, :] for r in raw]) if k else []
        terms = [value * new_refs[OWN][at, :]] + [value * b for b in basis]
        return tuple(c + fold(t) for c, t in zip(carry, terms))

    late = lax.fori_loop(0, states // CHUNK, finish, (zero,) * (1 + k))

    def whole(value):
        return jnp.sum(jnp.sum(value, axis=1, keepdims=True), axis=0, keepdims=True)

    share = 1.0 / mpo_count
    entries = [whole(own[0]) * share, whole(late[0])]
    for j in range(2):
        entries.append(whole(own[1 + j]) * share if j < k else None)
    for j in range(2):
        entries.append(whole(late[1 + j]) if j < k else None)
    for j in range(2):
        entries.append(whole(own[1 + k + j]) * share if j < k else None)
    row_ids = lax.broadcasted_iota(jnp.int32, small_ref.shape, 0)
    small = jnp.zeros(small_ref.shape, F32)
    for index, entry in enumerate(entries):
        if entry is not None:
            small = jnp.where(row_ids == index, entry, small)
    small_ref[...] = small
    if last:
        for copy in outputs:
            copy.wait()


def join_kernel(a_ref, b_ref, s0, s1, s2, s3, out_ref):
    states = a_ref.shape[0]
    total = (s0[...] + s1[...]) + (s2[...] + s3[...])
    out_ref[pl.ds(states, NOTE), :HALF] = total
    out_ref[pl.ds(states, NOTE), HALF:] = total

    def step(i, carry):
        at = pl.ds(pl.multiple_of(i * CHUNK, CHUNK), CHUNK)
        out_ref[at, :] = a_ref[at, :] + b_ref[at, :]
        return carry

    lax.fori_loop(0, states // CHUNK, step, 0)


def fill_kernel(cells, meta_ref, *refs):
    totals = [refs[2 * i : 2 * i + 2] for i in range(MATVECS)]
    known_ref, raw_own, raw_sib, *parts = refs[2 * MATVECS : 2 * MATVECS + 7]
    basis_out, images_out, projected_ref, basis_buf, images_buf, sems = refs[-6:]
    last = MATVECS - 1
    sigma = meta_ref[SIGMA]
    numbers = Scalars(totals, cells)
    core = lax.axis_index("rsec")
    states, half = basis_buf.shape[1:]
    lanes = pl.ds(pl.multiple_of(core * half, half), half)
    inverse = 1.0 / numbers.norm[last][:, :1]
    corr = [a[:, :1] for a in numbers.corr[last]]
    copies = []
    for slot, raw, image in ((OWN, raw_own, parts[:2]), (SIB, raw_sib, parts[2:])):

        def step(i, carry, slot=slot, raw=raw, image=image):
            at = pl.ds(pl.multiple_of(i * CHUNK, CHUNK), CHUNK)
            fields = (raw[at, lanes], image[0][at, :] + image[1][at, :])
            for which, buf in enumerate((basis_buf, images_buf)):
                value = fields[which]
                for j in range(last):
                    value = value - corr[j] * known_ref[which, slot, j, at, :]
                buf[slot, at, :] = value * inverse
            return carry

        lax.fori_loop(0, states // CHUNK, step, 0)
        sector = sigma if slot == OWN else 1 - sigma
        for which, (buf, out) in enumerate(((basis_buf, basis_out), (images_buf, images_out))):
            copies.append(
                pltpu.make_async_copy(buf.at[slot], out.at[last, sector], sems.at[which, slot])
            )
            copies[-1].start()
    shape = projected_ref.shape
    row_ids = lax.broadcasted_iota(jnp.int32, shape, 0)
    col_ids = lax.broadcasted_iota(jnp.int32, shape, 1)
    value = jnp.zeros(shape, F32)
    for i in range(MATVECS):
        for j in range(MATVECS):
            value = jnp.where((row_ids == i) & (col_ids == j), numbers.proj[i, j][:, :1], value)
    projected_ref[...] = value
    for copy in copies:
        copy.wait()


def per_device(
    wavefunction, left_env, right_env, precond_diag, down_charge, bond_mask, left_size, right_size
):
    sectors, states, columns = wavefunction.shape
    bonds = left_env.shape[0]
    lsec_count = lax.axis_size("lsec")
    mpo_count = lax.axis_size("mpo")
    assert sectors == 2 and lax.axis_size("rsec") == 2
    width = 2 * columns
    cells = float(lsec_count * sectors * states * width)
    field = jax.ShapeDtypeStruct((states, width), F32)
    noted = jax.ShapeDtypeStruct((states + NOTE, width), F32)
    half_field = jax.ShapeDtypeStruct((states, columns), F32)
    small = jax.ShapeDtypeStruct((8, 128), F32)
    params = pltpu.CompilerParams(vmem_limit_bytes=18 * 2**20)

    swap = [(0, 1), (1, 0)]
    first_pairs = [(i, i ^ 1) for i in range(lsec_count) if i ^ 1 < lsec_count]
    second_pairs = [(i, j) for a in range(1, lsec_count - 1, 2) for i, j in ((a, a + 1), (a + 1, a))]
    anywhere = pl.BlockSpec(memory_space=pl.ANY)
    in_hbm = pl.BlockSpec(memory_space=pltpu.HBM)

    def hold(value):
        return pltpu.with_memory_space_constraint(value, pltpu.HBM)

    def neighbours(value):
        return lax.ppermute(value, "lsec", first_pairs), lax.ppermute(value, "lsec", second_pairs)

    wave_all = lax.all_gather(wavefunction, "rsec", axis=2, tiled=True)
    right_send, _ = lax.optimization_barrier((right_env, wave_all))
    right_far = lax.ppermute(right_send, "rsec", swap)
    mask_rows = bond_mask.T
    down_charge, mask_rows, left_size, right_size = [
        hold(x) for x in (down_charge, mask_rows, left_size, right_size)
    ]
    own = pl.pallas_call(
        first_kernel,
        out_shape=noted,
        in_specs=[in_hbm] * 3 + [whole_vmem()],
        out_specs=whole_vmem(),
        scratch_shapes=[
            pltpu.SMEM(down_charge.shape, jnp.int32),
            pltpu.SMEM(left_size.shape, jnp.int32),
            pltpu.SMEM(right_size.shape, jnp.int32),
            pltpu.SemaphoreType.DMA((3,)),
        ],
        compiler_params=params,
        name="first",
    )(down_charge, left_size, right_size, wave_all)
    near_waves = neighbours(own)
    sib, meta = pl.pallas_call(
        functools.partial(prep_kernel, lsec_count, bonds),
        out_shape=(field, jax.ShapeDtypeStruct((LIST + bonds,), jnp.int32)),
        in_specs=[in_hbm] * 4 + [whole_vmem(), anywhere],
        out_specs=(whole_vmem(), whole_smem()),
        scratch_shapes=[
            pltpu.SMEM(down_charge.shape, jnp.int32),
            pltpu.SMEM(mask_rows.shape, jnp.int32),
            pltpu.SMEM(left_size.shape, jnp.int32),
            pltpu.SMEM(right_size.shape, jnp.int32),
            pltpu.SemaphoreType.DMA((4,)),
        ],
        compiler_params=params,
        name="prep",
    )(down_charge, mask_rows, left_size, right_size, wave_all, own)
    raw = [(own, sib, *near_waves)]
    diag_send, _ = lax.optimization_barrier((precond_diag, sib))
    diag_far = lax.ppermute(diag_send, "rsec", swap)
    diag_own, diag_sib = pl.pallas_call(
        diag_kernel,
        out_shape=(field,) * 2,
        in_specs=[whole_smem()] + [whole_vmem()] * 2,
        out_specs=(whole_vmem(),) * 2,
        compiler_params=params,
        name="diag",
    )(meta, hold(precond_diag), diag_far)

    near_diags = neighbours(diag_own)

    def mpo_pair(value):
        if mpo_count != 2:
            value = lax.psum(value, "mpo")
            return value, jnp.zeros_like(value)
        return value, lax.ppermute(value, "mpo", swap)

    def lsec_parts(part):
        if lsec_count != 4:
            zero = jnp.zeros_like(part)
            return lax.psum(part, "lsec"), zero, zero, zero
        return (part, *[lax.ppermute(part, "lsec", [(i, i ^ x) for i in range(4)]) for x in (1, 2, 3)])

    def join(value, part):
        return pl.pallas_call(
            join_kernel,
            out_shape=noted,
            in_specs=[whole_vmem()] * 6,
            out_specs=whole_vmem(),
            compiler_params=params,
            name="join",
        )(*mpo_pair(value), *lsec_parts(part))

    most = bonds - bonds // 5 if bonds % 5 == 0 else bonds
    packed = most * states + PACK
    lefts = pl.pallas_call(
        left_kernel,
        out_shape=(
            pltpu.VMEM((packed, SIDE), BF16),
            pltpu.VMEM((packed, SIDE), BF16),
            pltpu.VMEM((packed, 2 * (states - SIDE)), BF16),
        ),
        in_specs=[whole_smem(), anywhere],
        out_specs=(whole_vmem(),) * 3,
        scratch_shapes=[
            pltpu.VMEM((BUFFERS, states, states), F32),
            pltpu.SemaphoreType.DMA((states // TILE, BUFFERS)),
        ],
        compiler_params=params,
        cost_estimate=pl.CostEstimate(flops=0, transcendentals=0, bytes_accessed=bonds * states * states * 4),
        name="left",
    )(meta, hold(left_env))
    out = jax.ShapeDtypeStruct((MATVECS, sectors, states, columns), F32)
    known = jax.ShapeDtypeStruct((2, sectors, MATVECS - 1, states, columns), F32)

    def matvec(k, rights, inputs):
        last = k + 1 == MATVECS
        out_shape = [half_field] * 2 if last else [field]
        out_shape += [small] + [field] * (4 if k else 0)
        out_specs = [whole_vmem()] * len(out_shape)
        scratch = [
            pltpu.VMEM((4, states, width), BF16),
            pltpu.VMEM((4, states, width), BF16),
            pltpu.VMEM((2 * (states - SIDE), width), BF16),
            pltpu.VMEM((packed + states, width), BF16),
            pltpu.VMEM((packed + states, width), BF16),
            pltpu.SMEM((bonds,), jnp.int32),
        ]
        if k == 0:
            out_shape += [pltpu.VMEM((most, width, width), BF16)] * 2
            out_shape += [jax.ShapeDtypeStruct((8,), jnp.int32)]
            out_specs += [whole_vmem()] * 2 + [whole_smem()]
            scratch += [
                pltpu.VMEM((most, width, width), F32),
                pltpu.SemaphoreType.DMA((2, most)),
            ]
            right_specs = [anywhere] * 2
        else:
            right_specs = [whole_vmem()] * 2 + [whole_smem()]
        if last:
            out_shape += [known, out, out]
            out_specs += [whole_vmem(), anywhere, anywhere]
            scratch += [pltpu.VMEM((states, width), F32), pltpu.SemaphoreType.DMA((2, 2))]
        return pl.pallas_call(
            functools.partial(matvec_kernel, k, cells, mpo_count),
            out_shape=tuple(out_shape),
            in_specs=[whole_smem()] + [whole_vmem()] * 3 + right_specs + [whole_vmem()] * len(inputs),
            out_specs=tuple(out_specs),
            scratch_shapes=scratch,
            compiler_params=params,
            cost_estimate=pl.CostEstimate(
                flops=2 * 3 * bonds * states * width * (states + width),
                transcendentals=0,
                bytes_accessed=bonds * states * states,
            ),
            name=f"matvec{k}",
        )(meta, *lefts, *rights, *inputs)

    def flatten(groups):
        return [x for group in groups for x in group]

    totals = []
    images = []
    for k in range(MATVECS - 1):
        if k == 0:
            value, part, *rights = matvec(0, [hold(right_env), right_far], list(raw[0]))
            value, near_diags = lax.optimization_barrier((value, near_diags))
            precond = (diag_own, diag_sib, *near_diags)
        else:
            value, part, *fresh = matvec(k, rights, [*totals, *flatten(raw), *flatten(images), *precond])
            raw.append(tuple(fresh))
        value = join(value, part)
        beside = lax.ppermute(value, "rsec", swap)
        images.append((value, beside, *neighbours(value)))
        totals += mpo_pair(value[states:, :HALF] + beside[states:, :HALF])

    inputs = [*totals, *flatten(raw), *flatten(images), *precond]
    near, away, part, own, sib, _, _, known_blocks, *outs = matvec(MATVECS - 1, rights, inputs)
    own_half = mpo_pair(near)
    sib_half = mpo_pair(lax.ppermute(away, "rsec", swap))
    one, two, three, four = lsec_parts(part)
    part = (one + two) + (three + four)
    totals += mpo_pair(part + lax.ppermute(part, "rsec", swap))
    operands = [*totals, known_blocks, own, sib, *own_half, *sib_half]
    return pl.pallas_call(
        functools.partial(fill_kernel, cells),
        out_shape=(out, out, jax.ShapeDtypeStruct((MATVECS, MATVECS), F32)),
        in_specs=[whole_smem()] + [whole_vmem()] * len(operands) + [anywhere] * 2,
        out_specs=(anywhere, anywhere, whole_vmem()),
        scratch_shapes=[
            pltpu.VMEM((sectors, states, columns), F32),
            pltpu.VMEM((sectors, states, columns), F32),
            pltpu.SemaphoreType.DMA((2, 2)),
        ],
        input_output_aliases={1 + len(operands): 0, 2 + len(operands): 1},
        compiler_params=params,
        name="fill",
    )(meta, *operands, *outs)


def solution(mesh):
    placed = (
        P(("grp", "lsec"), None, "rsec"),
        P("mpo", ("grp", "lsec"), None, None),
        P("mpo", ("grp", "lsec"), "rsec", None),
        P(("grp", "lsec"), None, "rsec"),
        P("grp"),
        P("mpo", ("grp", "lsec")),
        P(("grp", "lsec")),
        P(("grp", "lsec")),
    )
    return jax.shard_map(
        per_device,
        mesh=mesh,
        in_specs=placed,
        out_specs=(
            P(None, ("grp", "lsec"), None, "rsec"),
            P(None, ("grp", "lsec"), None, "rsec"),
            P("grp", None),
        ),
        check_vma=False,
    )
```

```python
import functools

import jax
import jax.numpy as jnp
from jax import lax
from jax.experimental import pallas as pl
from jax.experimental.pallas import tpu as pltpu
from jax.sharding import PartitionSpec as P

EPSILON = 1e-06
MATVECS = 3
F32 = jnp.float32
BF16 = jnp.bfloat16
SIGMA, COUNT, ROWS, COLS, FIRST, SIB_ROWS, SIB_COLS, LIST = 0, 1, 2, 3, 4, 9, 10, 16
OWN, SIB, FIRST_PAIR, SECOND_PAIR = 0, 1, 2, 3
CHUNK = 64
UPPER = 128
TILE = 128
SIDE = 256
HALF = 128
NOTE = 8
PACK = 512
BUFFERS = 8


def whole_vmem():
    return pl.BlockSpec(memory_space=pltpu.VMEM)


def whole_smem():
    return pl.BlockSpec(memory_space=pltpu.SMEM)


def split(value):
    high = value.astype(BF16)
    return high, (value - high.astype(F32)).astype(BF16)


def orientation(down_ref, place):
    def step(i, flips):
        straight = (down_ref[2 * i] == down_ref[2 * i - 2]) | (
            down_ref[2 * i + 1] == down_ref[2 * i - 1]
        )
        return jnp.where(straight, flips, 1 - flips)

    return lax.fori_loop(1, place + 1, step, jnp.int32(0))


def live_mask(shape, row0, rows, cols):
    row_ids = row0 + lax.broadcasted_iota(jnp.int32, shape, 0)
    col_ids = lax.broadcasted_iota(jnp.int32, shape, 1)
    return (row_ids < rows) & (col_ids < cols)


def read_small(pairs, sems):
    copies = [pltpu.make_async_copy(*pair, sems.at[i]) for i, pair in enumerate(pairs)]
    for copy in copies:
        copy.start()
    for copy in copies:
        copy.wait()


def masked_block(out_ref, wave_ref, slot, rows, cols):
    states, width = wave_ref.shape[1:]

    def fill(i, carry):
        at = pl.ds(pl.multiple_of(i * CHUNK, CHUNK), CHUNK)
        mask = live_mask((CHUNK, width), i * CHUNK, rows, cols)
        out_ref[at, :] = jnp.where(mask, wave_ref[slot, at, :], 0.0)
        return carry

    lax.fori_loop(0, states // CHUNK, fill, 0)


def first_kernel(down_in, left_in, right_in, wave_ref, own_ref, down_ref, left_size_ref,
                 right_size_ref, sems):
    read_small(((down_in, down_ref), (left_in, left_size_ref), (right_in, right_size_ref)), sems)
    sigma = lax.axis_index("rsec") ^ orientation(down_ref, lax.axis_index("lsec"))
    rows, cols = left_size_ref[sigma], right_size_ref[sigma]
    masked_block(own_ref, wave_ref, sigma, rows, cols)
    note = (NOTE, own_ref.shape[1])
    row_ids = lax.broadcasted_iota(jnp.int32, note, 0)
    states = wave_ref.shape[1]
    own_ref[pl.ds(states, NOTE), :] = jnp.where(row_ids == 0, rows, cols).astype(F32)


def prep_kernel(lsec_count, bonds, down_in, mask_in, left_in, right_in, wave_ref, own_ref,
                sib_ref, meta_ref, down_ref, mask_ref, left_size_ref, right_size_ref, sems):
    read_small(
        ((down_in, down_ref), (mask_in, mask_ref), (left_in, left_size_ref), (right_in, right_size_ref)),
        sems,
    )
    place = lax.axis_index("lsec")
    core = lax.axis_index("rsec")
    first_bond = lax.axis_index("mpo") * bonds
    sigma = core ^ orientation(down_ref, place)
    own_down = down_ref[2 * place + sigma]
    sib_down = down_ref[2 * place + 1 - sigma]
    before = jnp.maximum(place - 1, 0)
    after = jnp.minimum(place + 1, lsec_count - 1)
    prev_down = down_ref[2 * before + (core ^ orientation(down_ref, before))]
    next_down = down_ref[2 * after + (core ^ orientation(down_ref, after))]
    has_prev = (place > 0) & (prev_down == own_down)
    has_next = (place < lsec_count - 1) & (next_down == own_down)
    odd = lax.rem(place, 2)
    has_lower = sib_down == own_down - 1
    has_upper = sib_down == own_down + 1

    def gather(slot, count):
        meta_ref[FIRST + slot] = count

        def step(bond, count):
            kind = lax.rem(first_bond + bond, 5)
            if slot == OWN:
                there = kind == 0
            elif slot == SIB:
                there = ((kind == 3) & has_lower) | ((kind == 4) & has_upper)
            else:
                lower = odd if slot == FIRST_PAIR else 1 - odd
                there = ((kind == 1) & has_prev & (lower == 1)) | (
                    (kind == 2) & has_next & (lower == 0)
                )
            there = there & (mask_ref[sigma, bond] > 0)

            @pl.when(there)
            def _():
                meta_ref[LIST + count] = bond * 4 + slot

            return count + there.astype(jnp.int32)

        return lax.fori_loop(0, bonds, step, count)

    count = jnp.int32(0)
    for slot in (OWN, SIB, FIRST_PAIR, SECOND_PAIR):
        count = gather(slot, count)
    meta_ref[FIRST + 4] = count
    rows, cols = left_size_ref[sigma], right_size_ref[sigma]
    meta_ref[SIGMA] = sigma
    meta_ref[COUNT] = count
    meta_ref[ROWS] = rows
    meta_ref[COLS] = cols
    meta_ref[SIB_ROWS] = left_size_ref[1 - sigma]
    meta_ref[SIB_COLS] = right_size_ref[1 - sigma]
    masked_block(sib_ref, wave_ref, 1 - sigma, left_size_ref[1 - sigma], right_size_ref[1 - sigma])


def diag_kernel(meta_ref, diag_ref, diag_far, diag_own, diag_sib):
    states, width = diag_own.shape
    half = width // 2
    sigma, core = meta_ref[SIGMA], lax.axis_index("rsec")
    near = pl.ds(pl.multiple_of(core * half, half), half)
    away = pl.ds(pl.multiple_of((1 - core) * half, half), half)
    for out_ref, slot in ((diag_own, sigma), (diag_sib, 1 - sigma)):

        def fill(i, carry, out_ref=out_ref, slot=slot):
            at = pl.ds(pl.multiple_of(i * CHUNK, CHUNK), CHUNK)
            out_ref[at, near] = diag_ref[slot, at, :]
            out_ref[at, away] = diag_far[slot, at, :]
            return carry

        lax.fori_loop(0, states // CHUNK, fill, 0)


def row(value, index):
    return value[index : index + 1, :]


class Scalars:
    def __init__(self, totals, cells):
        self.proj = {}
        self.gram = {}
        self.norm = []
        self.corr = []
        for k, total in enumerate(totals):
            value = (total[0][...] + total[1][...]) / cells
            size, inner = row(value, 0), row(value, 1)
            a = [row(value, 2 + j) for j in range(k)]
            e = [row(value, 4 + j) for j in range(k)]
            f = [row(value, 6 + j) for j in range(k)]
            length = size
            theta = inner
            for j in range(k):
                length = length - 2.0 * a[j] * a[j]
                theta = theta - a[j] * e[j] - a[j] * f[j]
            for i in range(k):
                for j in range(k):
                    length = length + a[i] * a[j] * self.gram[i, j]
                    theta = theta + a[i] * a[j] * self.proj[i, j]
            length = jnp.maximum(length, 0.0)
            square = length + EPSILON
            norm = jnp.sqrt(square)
            for j in range(k):
                up, down, both = e[j], f[j], a[j]
                for i in range(k):
                    up = up - a[i] * self.proj[j, i]
                    down = down - a[i] * self.proj[i, j]
                    both = both - a[i] * self.gram[i, j]
                self.proj[j, k] = up / norm
                self.proj[k, j] = down / norm
                self.gram[j, k] = self.gram[k, j] = both / norm
            self.proj[k, k] = theta / square
            self.gram[k, k] = length / square
            self.norm.append(norm)
            self.corr.append(a)

    def basis(self, k, fields):
        done = []
        for step in range(k + 1):
            value = fields[step]
            for j in range(step):
                value = value - self.corr[step][j][:, :1] * done[j]
            done.append(value / self.norm[step][:, :1])
        return done


def left_kernel(meta_ref, left_ref, left_high, left_low, left_tail, left_buf, sems):
    states = left_buf.shape[1]
    sigma, count, rows = meta_ref[SIGMA], meta_ref[COUNT], meta_ref[ROWS]
    stride = packed_rows(rows)

    def each(i, act):
        bond = meta_ref[LIST + i] // 4
        at = lax.rem(i, BUFFERS)
        for p in range(states // TILE):
            part = pl.ds(p * TILE, TILE)

            @pl.when(rows > p * TILE)
            def _(part=part, p=p):
                act(
                    pltpu.make_async_copy(
                        left_ref.at[bond, sigma, part], left_buf.at[at, part], sems.at[p, at]
                    )
                )

    def start(i):
        @pl.when(i < count)
        def _():
            each(i, lambda copy: copy.start())

    for i in range(BUFFERS - 1):
        start(jnp.int32(i))

    def step(i, carry):
        at = lax.rem(i, BUFFERS)
        start(i + BUFFERS - 1)
        each(i, lambda copy: copy.wait())

        def chunk(t, inner):
            high, low = split(left_buf[at, pl.ds(pl.multiple_of(t * CHUNK, CHUNK), CHUNK), :])
            to = pl.ds(pl.multiple_of(i * stride + t * CHUNK, 16), CHUNK)
            left_high[to, :] = high[:, :SIDE]
            left_low[to, :] = low[:, :SIDE]
            left_tail[to, :] = jnp.concatenate([high[:, SIDE:], low[:, SIDE:]], axis=1)
            return inner

        lax.fori_loop(0, (rows + CHUNK - 1) // CHUNK, chunk, 0)
        return carry

    lax.fori_loop(0, count, step, 0)


def packed_rows(rows):
    return ((rows + 15) // 16) * 16


def matvec_kernel(k, cells, mpo_count, *refs):
    refs = list(refs)
    meta_ref = refs.pop(0)
    left_high, left_low, left_tail = [refs.pop(0) for _ in range(3)]
    if k:
        right_high, right_low, size_ref = [refs.pop(0) for _ in range(3)]
    else:
        right_ref, far_ref = refs.pop(0), refs.pop(0)
    totals = [(refs.pop(0), refs.pop(0)) for _ in range(k)]
    raw = [[refs.pop(0) for _ in range(4)] for _ in range(max(k, 1))]
    images = [
        [[refs.pop(0)] * 2 if slot in (OWN, SIB) else [refs.pop(0), refs.pop(0)] for slot in range(4)]
        for _ in range(k)
    ]
    precond = [refs.pop(0) for _ in range(4)] if k else []
    last = k + 1 == MATVECS
    halves = [refs.pop(0), refs.pop(0)]
    small_ref = refs.pop(0)
    if k:
        new_refs = [refs.pop(0) for _ in range(4)]
    else:
        new_refs = raw[0]
        right_high, right_low, size_ref = [refs.pop(0) for _ in range(3)]
    if last:
        known_ref, basis_out, images_out = [refs.pop(0) for _ in range(3)]
    high_ref, low_ref, tail_ref, mid_high, mid_low, order_ref, out_ref = refs[:7]
    if not k:
        right_buf, sems = refs[7:]
    elif last:
        sems = refs[7]
    states, width = out_ref.shape
    count, rows, cols = meta_ref[COUNT], meta_ref[ROWS], meta_ref[COLS]
    stride = packed_rows(rows)

    core = lax.axis_index("rsec")
    if not k:
        size_ref[2 * OWN], size_ref[2 * OWN + 1] = rows, cols
        size_ref[2 * SIB], size_ref[2 * SIB + 1] = meta_ref[SIB_ROWS], meta_ref[SIB_COLS]
        for slot in (FIRST_PAIR, SECOND_PAIR):
            note = raw[0][slot][pl.ds(states, NOTE), :HALF]
            size_ref[2 * slot] = jnp.max(note[:1]).astype(jnp.int32)
            size_ref[2 * slot + 1] = jnp.max(note[1:]).astype(jnp.int32)
    def list_bonds(narrow):
        def step(i, place):
            hit = (size_ref[2 * lax.rem(meta_ref[LIST + i], 4) + 1] <= HALF) == narrow

            @pl.when(hit)
            def _():
                order_ref[place] = i

            return place + hit.astype(jnp.int32)

        return step

    thin_sources = lax.fori_loop(0, count, list_bonds(True), jnp.int32(0))
    lax.fori_loop(0, count, list_bonds(False), thin_sources)
    if not k:
        half = right_ref.shape[2]
        sigma = meta_ref[SIGMA]

        def each_right(i, act):
            bond = meta_ref[LIST + order_ref[i]] // 4
            for ref, place, sem in ((right_ref, core, 0), (far_ref, 1 - core, 1)):
                part = pl.ds(pl.multiple_of(place * half, half), half)

                @pl.when((cols > HALF) | (place == 0))
                def _(ref=ref, part=part, sem=sem):
                    act(
                        pltpu.make_async_copy(
                            ref.at[bond, sigma], right_buf.at[i, part], sems.at[sem, i]
                        )
                    )

        def start_right(i, carry):
            each_right(i, lambda copy: copy.start())
            return carry

        lax.fori_loop(0, count, start_right, 0)

    if k:
        numbers = Scalars(totals, cells)
        theta = numbers.proj[k - 1, k - 1][:, :1]
    zero = jnp.zeros((8, width), F32)
    parts = ((0, UPPER // CHUNK), (UPPER // CHUNK, states // CHUNK))

    def fold(value):
        return jnp.sum(value.reshape(CHUNK // 8, 8, width), axis=0)

    def prepare(slot, carry):
        def step(part, i, carry):
            at = pl.ds(pl.multiple_of(i * CHUNK, CHUNK), CHUNK)
            if k:
                base = 0 if slot in (OWN, SIB) else parts[part][0]
                within = pl.ds(pl.multiple_of((i - base) * CHUNK, CHUNK), CHUNK)
                basis = numbers.basis(k - 1, [r[slot][at, :] for r in raw])
                image = numbers.basis(k - 1, [r[slot][part][within, :] for r in images])
                value = (image[-1] - theta * basis[-1]) / jnp.maximum(
                    precond[slot][at, :] - theta, 1.0
                )
                new_refs[slot][at, :] = value
                if last and slot in (OWN, SIB):
                    for which, group in enumerate((basis, image)):
                        for j, block in enumerate(group):
                            block = jnp.where(core == 0, block[:, :HALF], block[:, HALF:])
                            known_ref[which, slot, j, at, :] = block
            else:
                basis, image = [], []
                value = raw[0][slot][at, :]
            high, low = split(value)
            high_ref[slot, at, :] = high
            low_ref[slot, at, :] = low
            terms = [value * value]
            if slot == OWN:
                terms += [value * b for b in basis] + [value * g for g in image]
            return tuple(c + fold(t) for c, t in zip(carry, terms))

        for part, (begin, end) in enumerate(parts):
            carry = lax.fori_loop(begin, end, functools.partial(step, part), carry)
        return carry

    def dot(a, b):
        return jnp.dot(a, b, preferred_element_type=F32)

    def dot_nt(a, b):
        return lax.dot_general(a, b, (((1,), (1,)), ((), ())), preferred_element_type=F32)

    twice = functools.partial(jnp.concatenate, axis=0)

    def first_stage(slot, deep, narrow):
        begin, end = meta_ref[FIRST + slot], meta_ref[FIRST + 1 + slot]
        total = (end - begin) * stride
        top, rest = pl.ds(0, SIDE), pl.ds(SIDE, states - SIDE)
        if narrow:
            high_ref[slot, :, HALF:] = low_ref[slot, :, :HALF]
        if deep:
            tail = high_ref[slot, rest, :]
            tail_ref[...] = twice([tail, tail])

        def tile(first, size):
            at = pl.ds(pl.multiple_of(begin * stride + first, 16), size)
            high, low = left_high[at, :], left_low[at, :]
            mid = dot(high, high_ref[slot, top, :])
            if deep:
                mid = mid + dot(left_tail[at, :], tail_ref[...])
            if narrow:
                mid = mid[:, :HALF] + mid[:, HALF:] + dot(low, high_ref[slot, top, :HALF])
                mid_high[at, :] = jnp.concatenate(split(mid), axis=1)
            else:
                mid = mid + dot(low, high_ref[slot, top, :]) + dot(high, low_ref[slot, top, :])
                if deep:
                    mid = mid + dot(left_tail[at, : states - SIDE], low_ref[slot, rest, :])
                mid_high[at, :], mid_low[at, :] = split(mid)

        def step(t, carry):
            tile(t * PACK, PACK)
            return carry

        tiles = (total + PACK // 2 - 1) // PACK
        lax.fori_loop(0, tiles, step, 0)
        pl.when(total > tiles * PACK)(lambda: tile(tiles * PACK, PACK // 2))

    def both(test, action):
        pl.when(test)(lambda: action(True))
        pl.when(jnp.logical_not(test))(lambda: action(False))

    for slot in (OWN, SIB, FIRST_PAIR, SECOND_PAIR):
        if slot == OWN:
            own = prepare(slot, (zero,) * (1 + 2 * k))
        else:
            used = meta_ref[FIRST + 1 + slot] > meta_ref[FIRST + slot]
            pl.when(used | (slot == SIB))(lambda slot=slot: (prepare(slot, (zero,)), None)[1])

    def from_slot(slot, carry):
        both(
            size_ref[2 * slot] > SIDE,
            lambda deep: both(
                size_ref[2 * slot + 1] <= HALF, lambda narrow: first_stage(slot, deep, narrow)
            ),
        )
        return carry

    lax.fori_loop(0, 4, from_slot, 0)
    if last:
        sigma = meta_ref[SIGMA]
        outputs = [
            pltpu.make_async_copy(
                known_ref.at[which, slot],
                out.at[pl.ds(0, MATVECS - 1), sigma if slot == OWN else 1 - sigma],
                sems.at[which, slot],
            )
            for which, out in enumerate((basis_out, images_out))
            for slot in (OWN, SIB)
        ]
        for copy in outputs:
            copy.start()

    def clear(i, carry):
        at = pl.ds(pl.multiple_of(i * CHUNK, CHUNK), CHUNK)
        out_ref[at, :] = jnp.zeros((CHUNK, width), F32)
        return carry

    lax.fori_loop(0, states // CHUNK, clear, 0)
    zeros_at = mid_high.shape[0] - states
    for ref in (mid_high, mid_low):
        ref[pl.ds(zeros_at, states), :] = jnp.zeros((states, width), BF16)

    def second_stage(size, thin):
        to = pl.ds(0, size)

        def right_block(i, bond):
            if k:
                return right_high[bond], None if thin else right_low[bond]
            if thin:
                high, low = jnp.concatenate(split(right_buf[i, pl.ds(0, HALF), :]), axis=0), None
            else:
                high, low = split(right_buf[i])
                right_low[bond] = low
            right_high[bond] = high
            return high, low

        def product(i, real, narrow):
            bond = order_ref[i]
            at = pl.ds(pl.multiple_of(jnp.where(real, bond * stride, zeros_at), 16), size)
            high = mid_high[at, :]
            right, right_rest = right_block(i, bond)
            if narrow:
                part = right[:, :HALF]
                value = dot_nt(high, jnp.concatenate([part, part], axis=1))
                if not thin:
                    value = value + dot_nt(high[:, :HALF], right_rest[:, :HALF])
            else:
                value = dot_nt(high, right)
                if not thin:
                    value = value + dot_nt(high, right_rest) + dot_nt(mid_low[at, :], right)
            if thin:
                value = value[:, :HALF] + value[:, HALF:]
                if not narrow:
                    value = value + dot_nt(mid_low[at, :], right[:HALF, :])
            return value

        def run(begin, end, narrow):
            def pair(p, carry):
                one = begin + 2 * p
                real = one + 1 < end
                two = jnp.where(real, one + 1, one)
                if not k:
                    each_right(one, lambda copy: copy.wait())
                    pl.when(real)(lambda: each_right(two, lambda copy: copy.wait()))
                value = product(one, True, narrow) + product(two, real, narrow)
                if thin:
                    out_ref[to, :HALF] += value
                else:
                    out_ref[to, :] += value
                return carry

            lax.fori_loop(0, (end - begin + 1) // 2, pair, 0)

        run(0, thin_sources, True)
        run(thin_sources, count, False)

    for size in range(TILE, states + 1, TILE):
        pl.when((rows <= size) & (rows > size - TILE))(
            lambda size=size: both(cols <= HALF, functools.partial(second_stage, size))
        )

    def finish(part, i, carry):
        at = pl.ds(pl.multiple_of(i * CHUNK, CHUNK), CHUNK)
        mask = live_mask((CHUNK, width), i * CHUNK, rows, cols)
        value = jnp.where(mask, out_ref[at, :], 0.0)
        if last:
            halves[0][at, :] = jnp.where(core == 0, value[:, :HALF], value[:, HALF:])
            halves[1][at, :] = jnp.where(core == 0, value[:, HALF:], value[:, :HALF])
        else:
            within = pl.ds(pl.multiple_of((i - parts[part][0]) * CHUNK, CHUNK), CHUNK)
            halves[part][within, :] = value
        basis = numbers.basis(k - 1, [r[OWN][at, :] for r in raw]) if k else []
        terms = [value * new_refs[OWN][at, :]] + [value * b for b in basis]
        return tuple(c + fold(t) for c, t in zip(carry, terms))

    late = (zero,) * (1 + k)
    for part, (begin, end) in enumerate(parts):
        late = lax.fori_loop(begin, end, functools.partial(finish, part), late)

    def whole(value):
        return jnp.sum(jnp.sum(value, axis=1, keepdims=True), axis=0, keepdims=True)

    share = 1.0 / mpo_count
    entries = [whole(own[0]) * share, whole(late[0])]
    for j in range(2):
        entries.append(whole(own[1 + j]) * share if j < k else None)
    for j in range(2):
        entries.append(whole(late[1 + j]) if j < k else None)
    for j in range(2):
        entries.append(whole(own[1 + k + j]) * share if j < k else None)
    row_ids = lax.broadcasted_iota(jnp.int32, small_ref.shape, 0)
    small = jnp.zeros(small_ref.shape, F32)
    for index, entry in enumerate(entries):
        if entry is not None:
            small = jnp.where(row_ids == index, entry, small)
    small_ref[...] = small
    if last:
        for copy in outputs:
            copy.wait()


def upper_kernel(a_ref, b_ref, _, out_ref):
    def step(i, carry):
        at = pl.ds(pl.multiple_of(i * CHUNK, CHUNK), CHUNK)
        out_ref[at, :] = a_ref[at, :] + b_ref[at, :]
        return carry

    lax.fori_loop(0, out_ref.shape[0] // CHUNK, step, 0)


def lower_kernel(a_ref, b_ref, upper_ref, small_ref, _, __, out_ref, whole_ref):
    above, states = upper_ref.shape[0], a_ref.shape[0]
    small = small_ref[...]
    whole_ref[pl.ds(above + states, NOTE), :HALF] = small
    whole_ref[pl.ds(above + states, NOTE), HALF:] = small

    def copy(i, carry):
        at = pl.ds(pl.multiple_of(i * CHUNK, CHUNK), CHUNK)
        whole_ref[at, :] = upper_ref[at, :]
        return carry

    def step(i, carry):
        at = pl.ds(pl.multiple_of(i * CHUNK, CHUNK), CHUNK)
        value = a_ref[at, :] + b_ref[at, :]
        out_ref[at, :] = value
        whole_ref[pl.ds(pl.multiple_of(above + i * CHUNK, CHUNK), CHUNK), :] = value
        return carry

    lax.fori_loop(0, above // CHUNK, copy, 0)
    lax.fori_loop(0, states // CHUNK, step, 0)


def fill_kernel(cells, meta_ref, *refs):
    totals = [refs[2 * i : 2 * i + 2] for i in range(MATVECS)]
    known_ref, raw_own, raw_sib, *parts = refs[2 * MATVECS : 2 * MATVECS + 7]
    basis_out, images_out, projected_ref, basis_buf, images_buf, sems = refs[-6:]
    last = MATVECS - 1
    sigma = meta_ref[SIGMA]
    numbers = Scalars(totals, cells)
    core = lax.axis_index("rsec")
    states, half = basis_buf.shape[1:]
    lanes = pl.ds(pl.multiple_of(core * half, half), half)
    inverse = 1.0 / numbers.norm[last][:, :1]
    corr = [a[:, :1] for a in numbers.corr[last]]
    copies = []
    for slot, raw, image in ((OWN, raw_own, parts[:2]), (SIB, raw_sib, parts[2:])):

        def step(i, carry, slot=slot, raw=raw, image=image):
            at = pl.ds(pl.multiple_of(i * CHUNK, CHUNK), CHUNK)
            fields = (raw[at, lanes], image[0][at, :] + image[1][at, :])
            for which, buf in enumerate((basis_buf, images_buf)):
                value = fields[which]
                for j in range(last):
                    value = value - corr[j] * known_ref[which, slot, j, at, :]
                buf[slot, at, :] = value * inverse
            return carry

        lax.fori_loop(0, states // CHUNK, step, 0)
        sector = sigma if slot == OWN else 1 - sigma
        for which, (buf, out) in enumerate(((basis_buf, basis_out), (images_buf, images_out))):
            copies.append(
                pltpu.make_async_copy(buf.at[slot], out.at[last, sector], sems.at[which, slot])
            )
            copies[-1].start()
    shape = projected_ref.shape
    row_ids = lax.broadcasted_iota(jnp.int32, shape, 0)
    col_ids = lax.broadcasted_iota(jnp.int32, shape, 1)
    value = jnp.zeros(shape, F32)
    for i in range(MATVECS):
        for j in range(MATVECS):
            value = jnp.where((row_ids == i) & (col_ids == j), numbers.proj[i, j][:, :1], value)
    projected_ref[...] = value
    for copy in copies:
        copy.wait()


def per_device(
    wavefunction, left_env, right_env, precond_diag, down_charge, bond_mask, left_size, right_size
):
    sectors, states, columns = wavefunction.shape
    bonds = left_env.shape[0]
    lsec_count = lax.axis_size("lsec")
    mpo_count = lax.axis_size("mpo")
    assert sectors == 2 and lax.axis_size("rsec") == 2
    width = 2 * columns
    cells = float(lsec_count * sectors * states * width)
    field = jax.ShapeDtypeStruct((states, width), F32)
    upper_rows = jax.ShapeDtypeStruct((UPPER, width), F32)
    lower_rows = jax.ShapeDtypeStruct((states - UPPER, width), F32)
    noted = jax.ShapeDtypeStruct((states + NOTE, width), F32)
    half_field = jax.ShapeDtypeStruct((states, columns), F32)
    small = jax.ShapeDtypeStruct((8, 128), F32)
    params = pltpu.CompilerParams(vmem_limit_bytes=18 * 2**20)

    swap = [(0, 1), (1, 0)]
    first_pairs = [(i, i ^ 1) for i in range(lsec_count) if i ^ 1 < lsec_count]
    second_pairs = [(i, j) for a in range(1, lsec_count - 1, 2) for i, j in ((a, a + 1), (a + 1, a))]
    anywhere = pl.BlockSpec(memory_space=pl.ANY)
    in_hbm = pl.BlockSpec(memory_space=pltpu.HBM)

    def hold(value):
        return pltpu.with_memory_space_constraint(value, pltpu.HBM)

    def neighbours(value):
        return lax.ppermute(value, "lsec", first_pairs), lax.ppermute(value, "lsec", second_pairs)

    wave_all = lax.all_gather(wavefunction, "rsec", axis=2, tiled=True)
    right_send, _ = lax.optimization_barrier((right_env, wave_all))
    right_far = lax.ppermute(right_send, "rsec", swap)
    mask_rows = bond_mask.T
    down_charge, mask_rows, left_size, right_size = [
        hold(x) for x in (down_charge, mask_rows, left_size, right_size)
    ]
    own = pl.pallas_call(
        first_kernel,
        out_shape=noted,
        in_specs=[in_hbm] * 3 + [whole_vmem()],
        out_specs=whole_vmem(),
        scratch_shapes=[
            pltpu.SMEM(down_charge.shape, jnp.int32),
            pltpu.SMEM(left_size.shape, jnp.int32),
            pltpu.SMEM(right_size.shape, jnp.int32),
            pltpu.SemaphoreType.DMA((3,)),
        ],
        compiler_params=params,
        name="first",
    )(down_charge, left_size, right_size, wave_all)
    near_waves = neighbours(own)
    sib, meta = pl.pallas_call(
        functools.partial(prep_kernel, lsec_count, bonds),
        out_shape=(field, jax.ShapeDtypeStruct((LIST + bonds,), jnp.int32)),
        in_specs=[in_hbm] * 4 + [whole_vmem(), anywhere],
        out_specs=(whole_vmem(), whole_smem()),
        scratch_shapes=[
            pltpu.SMEM(down_charge.shape, jnp.int32),
            pltpu.SMEM(mask_rows.shape, jnp.int32),
            pltpu.SMEM(left_size.shape, jnp.int32),
            pltpu.SMEM(right_size.shape, jnp.int32),
            pltpu.SemaphoreType.DMA((4,)),
        ],
        compiler_params=params,
        name="prep",
    )(down_charge, mask_rows, left_size, right_size, wave_all, own)
    raw = [(own, sib, *near_waves)]
    diag_send, _ = lax.optimization_barrier((precond_diag, sib))
    diag_far = lax.ppermute(diag_send, "rsec", swap)
    diag_own, diag_sib = pl.pallas_call(
        diag_kernel,
        out_shape=(field,) * 2,
        in_specs=[whole_smem()] + [whole_vmem()] * 2,
        out_specs=(whole_vmem(),) * 2,
        compiler_params=params,
        name="diag",
    )(meta, hold(precond_diag), diag_far)

    near_diags = neighbours(diag_own)

    def mpo_pair(value):
        if mpo_count != 2:
            value = lax.psum(value, "mpo")
            return value, jnp.zeros_like(value)
        return value, lax.ppermute(value, "mpo", swap)

    def lsec_sum(part):
        if lsec_count & (lsec_count - 1):
            return lax.psum(part, "lsec"), part
        first = None
        for bit in range(lsec_count.bit_length() - 1):
            part = part + lax.ppermute(
                part, "lsec", [(i, i ^ (1 << bit)) for i in range(lsec_count)]
            )
            first = part if first is None else first
        return part, first

    def join(kernel, out_shape, *operands):
        return pl.pallas_call(
            kernel,
            out_shape=out_shape,
            in_specs=[whole_vmem()] * len(operands[:4]) + [anywhere] * len(operands[4:]),
            out_specs=jax.tree.map(lambda _: whole_vmem(), out_shape),
            compiler_params=params,
            name=kernel.__name__,
        )(*operands)

    most = bonds - bonds // 5 if bonds % 5 == 0 else bonds
    packed = most * states + PACK
    lefts = pl.pallas_call(
        left_kernel,
        out_shape=(
            pltpu.VMEM((packed, SIDE), BF16),
            pltpu.VMEM((packed, SIDE), BF16),
            pltpu.VMEM((packed, 2 * (states - SIDE)), BF16),
        ),
        in_specs=[whole_smem(), anywhere],
        out_specs=(whole_vmem(),) * 3,
        scratch_shapes=[
            pltpu.VMEM((BUFFERS, states, states), F32),
            pltpu.SemaphoreType.DMA((states // TILE, BUFFERS)),
        ],
        compiler_params=params,
        cost_estimate=pl.CostEstimate(flops=0, transcendentals=0, bytes_accessed=bonds * states * states * 4),
        name="left",
    )(meta, hold(left_env))
    out = jax.ShapeDtypeStruct((MATVECS, sectors, states, columns), F32)
    known = jax.ShapeDtypeStruct((2, sectors, MATVECS - 1, states, columns), F32)

    def matvec(k, rights, inputs):
        last = k + 1 == MATVECS
        out_shape = [half_field] * 2 if last else [upper_rows, lower_rows]
        out_shape += [small] + [field] * (4 if k else 0)
        out_specs = [whole_vmem()] * len(out_shape)
        scratch = [
            pltpu.VMEM((4, states, width), BF16),
            pltpu.VMEM((4, states, width), BF16),
            pltpu.VMEM((2 * (states - SIDE), width), BF16),
            pltpu.VMEM((packed + states, width), BF16),
            pltpu.VMEM((packed + states, width), BF16),
            pltpu.SMEM((bonds,), jnp.int32),
            pltpu.VMEM((states, width), F32),
        ]
        if k == 0:
            out_shape += [pltpu.VMEM((most, width, width), BF16)] * 2
            out_shape += [jax.ShapeDtypeStruct((8,), jnp.int32)]
            out_specs += [whole_vmem()] * 2 + [whole_smem()]
            scratch += [
                pltpu.VMEM((most, width, width), F32),
                pltpu.SemaphoreType.DMA((2, most)),
            ]
            right_specs = [anywhere] * 2
        else:
            right_specs = [whole_vmem()] * 2 + [whole_smem()]
        if last:
            out_shape += [known, out, out]
            out_specs += [whole_vmem(), anywhere, anywhere]
            scratch += [pltpu.SemaphoreType.DMA((2, 2))]
        return pl.pallas_call(
            functools.partial(matvec_kernel, k, cells, mpo_count),
            out_shape=tuple(out_shape),
            in_specs=[whole_smem()] + [whole_vmem()] * 3 + right_specs + [whole_vmem()] * len(inputs),
            out_specs=tuple(out_specs),
            scratch_shapes=scratch,
            compiler_params=params,
            cost_estimate=pl.CostEstimate(
                flops=2 * 3 * bonds * states * width * (states + width),
                transcendentals=0,
                bytes_accessed=bonds * states * states,
            ),
            name=f"matvec{k}",
        )(meta, *lefts, *rights, *inputs)

    def flatten(groups):
        return [x for group in groups for x in group]

    totals = []
    images = []
    for k in range(MATVECS - 1):
        if k == 0:
            upper, lower, part, *rights = matvec(0, [hold(right_env), right_far], list(raw[0]))
            upper, near_diags = lax.optimization_barrier((upper, near_diags))
            precond = (diag_own, diag_sib, *near_diags)
        else:
            inputs = [*totals, *flatten(raw), *flatten(images), *precond]
            upper, lower, part, *fresh = matvec(k, rights, inputs)
            raw.append(tuple(fresh))
        upper, lower = mpo_pair(upper), mpo_pair(lower)
        small_sum, small_first = lsec_sum(part)
        upper = join(upper_kernel, upper_rows, *upper, small_first)
        far_upper = neighbours(upper)
        lower, whole = join(lower_kernel, (lower_rows, noted), *lower, upper, small_sum, *far_upper)
        far_lower = neighbours(lower)
        beside = lax.ppermute(whole, "rsec", swap)
        images.append([whole, beside, *flatten(zip(far_upper, far_lower))])
        totals += mpo_pair(whole[states:, :HALF] + beside[states:, :HALF])

    inputs = [*totals, *flatten(raw), *flatten(images), *precond]
    near, away, part, own, sib, _, _, known_blocks, *outs = matvec(MATVECS - 1, rights, inputs)
    own_half = mpo_pair(near)
    sib_half = mpo_pair(lax.ppermute(away, "rsec", swap))
    part, _ = lsec_sum(part)
    totals += mpo_pair(part + lax.ppermute(part, "rsec", swap))
    operands = [*totals, known_blocks, own, sib, *own_half, *sib_half]
    return pl.pallas_call(
        functools.partial(fill_kernel, cells),
        out_shape=(out, out, jax.ShapeDtypeStruct((MATVECS, MATVECS), F32)),
        in_specs=[whole_smem()] + [whole_vmem()] * len(operands) + [anywhere] * 2,
        out_specs=(anywhere, anywhere, whole_vmem()),
        scratch_shapes=[
            pltpu.VMEM((sectors, states, columns), F32),
            pltpu.VMEM((sectors, states, columns), F32),
            pltpu.SemaphoreType.DMA((2, 2)),
        ],
        input_output_aliases={1 + len(operands): 0, 2 + len(operands): 1},
        compiler_params=params,
        name="fill",
    )(meta, *operands, *outs)


def solution(mesh):
    placed = (
        P(("grp", "lsec"), None, "rsec"),
        P("mpo", ("grp", "lsec"), None, None),
        P("mpo", ("grp", "lsec"), "rsec", None),
        P(("grp", "lsec"), None, "rsec"),
        P("grp"),
        P("mpo", ("grp", "lsec")),
        P(("grp", "lsec")),
        P(("grp", "lsec")),
    )
    return jax.shard_map(
        per_device,
        mesh=mesh,
        in_specs=placed,
        out_specs=(
            P(None, ("grp", "lsec"), None, "rsec"),
            P(None, ("grp", "lsec"), None, "rsec"),
            P("grp", None),
        ),
        check_vma=False,
    )
```

```python
import functools

import jax
import jax.numpy as jnp
from jax import lax
from jax.experimental import pallas as pl
from jax.experimental.pallas import tpu as pltpu
from jax.sharding import PartitionSpec as P

EPSILON = 1e-06
MATVECS = 3
F32 = jnp.float32
BF16 = jnp.bfloat16
SIGMA, COUNT, ROWS, COLS, FIRST, SIB_ROWS, SIB_COLS, LIST = 0, 1, 2, 3, 4, 9, 10, 16
OWN, SIB, FIRST_PAIR, SECOND_PAIR = 0, 1, 2, 3
CHUNK = 64
TILE = 128
SIDE = 256
HALF = 128
NOTE = 8
PACK = 512
BUFFERS = 8


def whole_vmem():
    return pl.BlockSpec(memory_space=pltpu.VMEM)


def whole_smem():
    return pl.BlockSpec(memory_space=pltpu.SMEM)


def split(value):
    high = value.astype(BF16)
    return high, (value - high.astype(F32)).astype(BF16)


def orientation(down_ref, place):
    def step(i, flips):
        straight = (down_ref[2 * i] == down_ref[2 * i - 2]) | (
            down_ref[2 * i + 1] == down_ref[2 * i - 1]
        )
        return jnp.where(straight, flips, 1 - flips)

    return lax.fori_loop(1, place + 1, step, jnp.int32(0))


def live_mask(shape, row0, rows, cols):
    row_ids = row0 + lax.broadcasted_iota(jnp.int32, shape, 0)
    col_ids = lax.broadcasted_iota(jnp.int32, shape, 1)
    return (row_ids < rows) & (col_ids < cols)


def read_small(pairs, sems):
    copies = [pltpu.make_async_copy(*pair, sems.at[i]) for i, pair in enumerate(pairs)]
    for copy in copies:
        copy.start()
    for copy in copies:
        copy.wait()


def masked_block(out_ref, wave_ref, slot, rows, cols):
    states, width = wave_ref.shape[1:]

    def fill(i, carry):
        at = pl.ds(pl.multiple_of(i * CHUNK, CHUNK), CHUNK)
        mask = live_mask((CHUNK, width), i * CHUNK, rows, cols)
        out_ref[at, :] = jnp.where(mask, wave_ref[slot, at, :], 0.0)
        return carry

    lax.fori_loop(0, states // CHUNK, fill, 0)


def first_kernel(down_in, left_in, right_in, wave_ref, own_ref, down_ref, left_size_ref,
                 right_size_ref, sems):
    read_small(((down_in, down_ref), (left_in, left_size_ref), (right_in, right_size_ref)), sems)
    sigma = lax.axis_index("rsec") ^ orientation(down_ref, lax.axis_index("lsec"))
    rows, cols = left_size_ref[sigma], right_size_ref[sigma]
    masked_block(own_ref, wave_ref, sigma, rows, cols)
    note = (NOTE, own_ref.shape[1])
    row_ids = lax.broadcasted_iota(jnp.int32, note, 0)
    states = wave_ref.shape[1]
    own_ref[pl.ds(states, NOTE), :] = jnp.where(row_ids == 0, rows, cols).astype(F32)


def prep_kernel(lsec_count, bonds, down_in, mask_in, left_in, right_in, wave_ref, own_ref,
                sib_ref, meta_ref, down_ref, mask_ref, left_size_ref, right_size_ref, sems):
    read_small(
        ((down_in, down_ref), (mask_in, mask_ref), (left_in, left_size_ref), (right_in, right_size_ref)),
        sems,
    )
    place = lax.axis_index("lsec")
    core = lax.axis_index("rsec")
    first_bond = lax.axis_index("mpo") * bonds
    sigma = core ^ orientation(down_ref, place)
    own_down = down_ref[2 * place + sigma]
    sib_down = down_ref[2 * place + 1 - sigma]
    before = jnp.maximum(place - 1, 0)
    after = jnp.minimum(place + 1, lsec_count - 1)
    prev_down = down_ref[2 * before + (core ^ orientation(down_ref, before))]
    next_down = down_ref[2 * after + (core ^ orientation(down_ref, after))]
    has_prev = (place > 0) & (prev_down == own_down)
    has_next = (place < lsec_count - 1) & (next_down == own_down)
    odd = lax.rem(place, 2)
    has_lower = sib_down == own_down - 1
    has_upper = sib_down == own_down + 1

    def gather(slot, count):
        meta_ref[FIRST + slot] = count

        def step(bond, count):
            kind = lax.rem(first_bond + bond, 5)
            if slot == OWN:
                there = kind == 0
            elif slot == SIB:
                there = ((kind == 3) & has_lower) | ((kind == 4) & has_upper)
            else:
                lower = odd if slot == FIRST_PAIR else 1 - odd
                there = ((kind == 1) & has_prev & (lower == 1)) | (
                    (kind == 2) & has_next & (lower == 0)
                )
            there = there & (mask_ref[sigma, bond] > 0)

            @pl.when(there)
            def _():
                meta_ref[LIST + count] = bond * 4 + slot

            return count + there.astype(jnp.int32)

        return lax.fori_loop(0, bonds, step, count)

    count = jnp.int32(0)
    for slot in (OWN, SIB, FIRST_PAIR, SECOND_PAIR):
        count = gather(slot, count)
    meta_ref[FIRST + 4] = count
    rows, cols = left_size_ref[sigma], right_size_ref[sigma]
    meta_ref[SIGMA] = sigma
    meta_ref[COUNT] = count
    meta_ref[ROWS] = rows
    meta_ref[COLS] = cols
    meta_ref[SIB_ROWS] = left_size_ref[1 - sigma]
    meta_ref[SIB_COLS] = right_size_ref[1 - sigma]
    masked_block(sib_ref, wave_ref, 1 - sigma, left_size_ref[1 - sigma], right_size_ref[1 - sigma])


def diag_kernel(meta_ref, diag_ref, diag_far, diag_own, diag_sib):
    states, width = diag_own.shape
    half = width // 2
    sigma, core = meta_ref[SIGMA], lax.axis_index("rsec")
    near = pl.ds(pl.multiple_of(core * half, half), half)
    away = pl.ds(pl.multiple_of((1 - core) * half, half), half)
    for out_ref, slot in ((diag_own, sigma), (diag_sib, 1 - sigma)):

        def fill(i, carry, out_ref=out_ref, slot=slot):
            at = pl.ds(pl.multiple_of(i * CHUNK, CHUNK), CHUNK)
            out_ref[at, near] = diag_ref[slot, at, :]
            out_ref[at, away] = diag_far[slot, at, :]
            return carry

        lax.fori_loop(0, states // CHUNK, fill, 0)


def row(value, index):
    return value[index : index + 1, :]


def stack_rows(shape, rows):
    row_ids = lax.broadcasted_iota(jnp.int32, shape, 0)
    value = jnp.zeros(shape, F32)
    for index, entry in enumerate(rows):
        if entry is not None:
            value = jnp.where(row_ids == index, entry, value)
    return value


class Scalars:
    def __init__(self, totals, cells, state=None):
        self.proj = {}
        self.gram = {}
        self.norm = []
        self.corr = []
        known = 0
        if state is not None:
            known = MATVECS - 1
            places = [(i, j) for i in range(known) for j in range(known)]
            for index, place in enumerate(places):
                self.proj[place] = row(state, index)
                self.gram[place] = row(state, len(places) + index)
        for k, total in enumerate(totals, known):
            value = (total[0][...] + total[1][...]) / cells
            size, inner = row(value, 0), row(value, 1)
            a = [row(value, 2 + j) for j in range(k)]
            e = [row(value, 4 + j) for j in range(k)]
            f = [row(value, 6 + j) for j in range(k)]
            length = size
            theta = inner
            for j in range(k):
                length = length - 2.0 * a[j] * a[j]
                theta = theta - a[j] * e[j] - a[j] * f[j]
            for i in range(k):
                for j in range(k):
                    length = length + a[i] * a[j] * self.gram[i, j]
                    theta = theta + a[i] * a[j] * self.proj[i, j]
            length = jnp.maximum(length, 0.0)
            square = length + EPSILON
            norm = jnp.sqrt(square)
            for j in range(k):
                up, down, both = e[j], f[j], a[j]
                for i in range(k):
                    up = up - a[i] * self.proj[j, i]
                    down = down - a[i] * self.proj[i, j]
                    both = both - a[i] * self.gram[i, j]
                self.proj[j, k] = up / norm
                self.proj[k, j] = down / norm
                self.gram[j, k] = self.gram[k, j] = both / norm
            self.proj[k, k] = theta / square
            self.gram[k, k] = length / square
            self.norm.append(norm)
            self.corr.append(a)

    def state(self, shape):
        known = MATVECS - 1
        places = [(i, j) for i in range(known) for j in range(known)]
        rows = [self.proj[place] for place in places] + [self.gram[place] for place in places]
        return stack_rows(shape, rows)

    def basis(self, k, fields):
        done = []
        for step in range(k + 1):
            value = fields[step]
            for j in range(step):
                value = value - self.corr[step][j][:, :1] * done[j]
            done.append(value / self.norm[step][:, :1])
        return done


def left_kernel(meta_ref, left_ref, left_high, left_low, left_tail, left_buf, sems):
    states = left_buf.shape[1]
    sigma, count, rows = meta_ref[SIGMA], meta_ref[COUNT], meta_ref[ROWS]
    stride = packed_rows(rows)

    def each(i, act):
        bond = meta_ref[LIST + i] // 4
        at = lax.rem(i, BUFFERS)
        for p in range(states // TILE):
            part = pl.ds(p * TILE, TILE)

            @pl.when(rows > p * TILE)
            def _(part=part, p=p):
                act(
                    pltpu.make_async_copy(
                        left_ref.at[bond, sigma, part], left_buf.at[at, part], sems.at[p, at]
                    )
                )

    def start(i):
        @pl.when(i < count)
        def _():
            each(i, lambda copy: copy.start())

    for i in range(BUFFERS - 1):
        start(jnp.int32(i))

    def step(i, carry):
        at = lax.rem(i, BUFFERS)
        start(i + BUFFERS - 1)
        each(i, lambda copy: copy.wait())

        def chunk(t, inner):
            high, low = split(left_buf[at, pl.ds(pl.multiple_of(t * CHUNK, CHUNK), CHUNK), :])
            to = pl.ds(pl.multiple_of(i * stride + t * CHUNK, 16), CHUNK)
            left_high[to, :] = high[:, :SIDE]
            left_low[to, :] = low[:, :SIDE]
            left_tail[to, :] = jnp.concatenate([high[:, SIDE:], low[:, SIDE:]], axis=1)
            return inner

        lax.fori_loop(0, (rows + CHUNK - 1) // CHUNK, chunk, 0)
        return carry

    lax.fori_loop(0, count, step, 0)


def packed_rows(rows):
    return ((rows + 15) // 16) * 16


def fold(value):
    return jnp.sum(value.reshape(CHUNK // 8, 8, value.shape[1]), axis=0)


def dots_kernel(k, cells, mpo_count, meta_ref, early_ref, *refs):
    refs, small_ref = list(refs[:-1]), refs[-1]
    totals = [(refs.pop(0), refs.pop(0)) for _ in range(k)]
    raw = [refs.pop(0) for _ in range(k + 1)]
    numbers = Scalars(totals, cells) if k else None
    core = lax.axis_index("rsec")
    zero = jnp.zeros(early_ref.shape[1:], F32)

    def step(i, carry):
        at = pl.ds(pl.multiple_of(i * CHUNK, CHUNK), CHUNK)
        blocks = [ref[at, :] for ref in refs]
        if len(blocks) == 2:
            near, away = blocks
            first, second = jnp.where(core == 0, near, away), jnp.where(core == 0, away, near)
            value = jnp.concatenate([first, second], axis=1)
        else:
            value = blocks[0]
        basis = numbers.basis(k - 1, [ref[at, :] for ref in raw[:k]]) if k else []
        return tuple(c + fold(value * b) for c, b in zip(carry, [raw[k][at, :], *basis]))

    live = (meta_ref[ROWS] + CHUNK - 1) // CHUNK
    late = lax.fori_loop(0, live, step, (zero,) * (1 + k))

    def whole(value):
        return jnp.sum(jnp.sum(value, axis=1, keepdims=True), axis=0, keepdims=True)

    share = 1.0 / mpo_count
    entries = [whole(early_ref[0]) * share, whole(late[0])]
    for j in range(2):
        entries.append(whole(early_ref[1 + j]) * share if j < k else None)
    for j in range(2):
        entries.append(whole(late[1 + j]) if j < k else None)
    for j in range(2):
        entries.append(whole(early_ref[1 + k + j]) * share if j < k else None)
    small_ref[...] = stack_rows(small_ref.shape, entries)


def matvec_kernel(k, cells, *refs):
    refs = list(refs)
    meta_ref = refs.pop(0)
    left_high, left_low, left_tail = [refs.pop(0) for _ in range(3)]
    if k:
        right_high, right_low, size_ref = [refs.pop(0) for _ in range(3)]
    else:
        right_ref, far_ref = refs.pop(0), refs.pop(0)
    totals = [(refs.pop(0), refs.pop(0)) for _ in range(k)]
    raw = [[refs.pop(0) for _ in range(4)] for _ in range(max(k, 1))]
    images = [[refs.pop(0) for _ in range(4)] for _ in range(k)]
    precond = [refs.pop(0) for _ in range(4)] if k else []
    last = k + 1 == MATVECS
    halves = [refs.pop(0), refs.pop(0)] if last else []
    out_ref = None if last else refs.pop(0)
    early_ref = refs.pop(0)
    if k:
        new_refs = [refs.pop(0) for _ in range(4)]
    else:
        new_refs = raw[0]
        right_high, right_low, size_ref = [refs.pop(0) for _ in range(3)]
    if last:
        known_ref, state_ref, basis_out, images_out = [refs.pop(0) for _ in range(4)]
    high_ref, low_ref, tail_ref, mid_high, mid_low, order_ref = refs[:6]
    if not k:
        right_buf, sems = refs[6:]
    elif last:
        out_ref, sems = refs[6:]
    states, width = out_ref.shape
    count, rows, cols = meta_ref[COUNT], meta_ref[ROWS], meta_ref[COLS]
    stride = packed_rows(rows)

    core = lax.axis_index("rsec")
    if not k:
        size_ref[2 * OWN], size_ref[2 * OWN + 1] = rows, cols
        size_ref[2 * SIB], size_ref[2 * SIB + 1] = meta_ref[SIB_ROWS], meta_ref[SIB_COLS]
        for slot in (FIRST_PAIR, SECOND_PAIR):
            note = raw[0][slot][pl.ds(states, NOTE), :HALF]
            size_ref[2 * slot] = jnp.max(note[:1]).astype(jnp.int32)
            size_ref[2 * slot + 1] = jnp.max(note[1:]).astype(jnp.int32)
    def list_bonds(narrow):
        def step(i, place):
            hit = (size_ref[2 * lax.rem(meta_ref[LIST + i], 4) + 1] <= HALF) == narrow

            @pl.when(hit)
            def _():
                order_ref[place] = i

            return place + hit.astype(jnp.int32)

        return step

    thin_sources = lax.fori_loop(0, count, list_bonds(True), jnp.int32(0))
    lax.fori_loop(0, count, list_bonds(False), thin_sources)
    if not k:
        half = right_ref.shape[2]
        sigma = meta_ref[SIGMA]

        def each_right(i, act):
            bond = meta_ref[LIST + order_ref[i]] // 4
            for ref, place, sem in ((right_ref, core, 0), (far_ref, 1 - core, 1)):
                part = pl.ds(pl.multiple_of(place * half, half), half)

                @pl.when((cols > HALF) | (place == 0))
                def _(ref=ref, part=part, sem=sem):
                    act(
                        pltpu.make_async_copy(
                            ref.at[bond, sigma], right_buf.at[i, part], sems.at[sem, i]
                        )
                    )

        def start_right(i, carry):
            each_right(i, lambda copy: copy.start())
            return carry

        lax.fori_loop(0, count, start_right, 0)

    if k:
        numbers = Scalars(totals, cells)
        theta = numbers.proj[k - 1, k - 1][:, :1]
    zero = jnp.zeros((8, width), F32)

    def prepare(slot, carry):
        def step(i, carry):
            at = pl.ds(pl.multiple_of(i * CHUNK, CHUNK), CHUNK)
            if k:
                basis = numbers.basis(k - 1, [r[slot][at, :] for r in raw])
                image = numbers.basis(k - 1, [r[slot][at, :] for r in images])
                value = (image[-1] - theta * basis[-1]) / jnp.maximum(
                    precond[slot][at, :] - theta, 1.0
                )
                new_refs[slot][at, :] = value
                if last and slot in (OWN, SIB):
                    for which, group in enumerate((basis, image)):
                        for j, block in enumerate(group):
                            block = jnp.where(core == 0, block[:, :HALF], block[:, HALF:])
                            known_ref[which, slot, j, at, :] = block
            else:
                basis, image = [], []
                value = raw[0][slot][at, :]
            high, low = split(value)
            high_ref[slot, at, :] = high
            low_ref[slot, at, :] = low
            terms = [value * value]
            if slot == OWN:
                terms += [value * b for b in basis] + [value * g for g in image]
            return tuple(c + fold(t) for c, t in zip(carry, terms))

        def dead(i, inner):
            at = pl.ds(pl.multiple_of(i * CHUNK, CHUNK), CHUNK)
            high_ref[slot, at, :] = jnp.zeros((CHUNK, width), BF16)
            low_ref[slot, at, :] = jnp.zeros((CHUNK, width), BF16)
            if last and slot in (OWN, SIB):
                for which in range(2):
                    for j in range(k):
                        known_ref[which, slot, j, at, :] = jnp.zeros((CHUNK, HALF), F32)
            return inner

        live = (size_ref[2 * slot] + CHUNK - 1) // CHUNK
        lax.fori_loop(live, states // CHUNK, dead, 0)
        return lax.fori_loop(0, live, step, carry)

    def dot(a, b):
        return jnp.dot(a, b, preferred_element_type=F32)

    def dot_nt(a, b):
        return lax.dot_general(a, b, (((1,), (1,)), ((), ())), preferred_element_type=F32)

    twice = functools.partial(jnp.concatenate, axis=0)

    def first_stage(slot, deep, narrow):
        begin, end = meta_ref[FIRST + slot], meta_ref[FIRST + 1 + slot]
        total = (end - begin) * stride
        top, rest = pl.ds(0, SIDE), pl.ds(SIDE, states - SIDE)
        if narrow:
            high_ref[slot, :, HALF:] = low_ref[slot, :, :HALF]
        if deep:
            tail = high_ref[slot, rest, :]
            tail_ref[...] = twice([tail, tail])

        def tile(first, size):
            at = pl.ds(pl.multiple_of(begin * stride + first, 16), size)
            high, low = left_high[at, :], left_low[at, :]
            mid = dot(high, high_ref[slot, top, :])
            if deep:
                mid = mid + dot(left_tail[at, :], tail_ref[...])
            if narrow:
                mid = mid[:, :HALF] + mid[:, HALF:] + dot(low, high_ref[slot, top, :HALF])
                mid_high[at, :] = jnp.concatenate(split(mid), axis=1)
            else:
                mid = mid + dot(low, high_ref[slot, top, :]) + dot(high, low_ref[slot, top, :])
                if deep:
                    mid = mid + dot(left_tail[at, : states - SIDE], low_ref[slot, rest, :])
                mid_high[at, :], mid_low[at, :] = split(mid)

        def step(t, carry):
            tile(t * PACK, PACK)
            return carry

        tiles = (total + PACK // 2 - 1) // PACK
        lax.fori_loop(0, tiles, step, 0)
        pl.when(total > tiles * PACK)(lambda: tile(tiles * PACK, PACK // 2))

    def both(test, action):
        pl.when(test)(lambda: action(True))
        pl.when(jnp.logical_not(test))(lambda: action(False))

    for slot in (OWN, SIB, FIRST_PAIR, SECOND_PAIR):
        if slot == OWN:
            own = prepare(slot, (zero,) * (1 + 2 * k))
        else:
            used = meta_ref[FIRST + 1 + slot] > meta_ref[FIRST + slot]
            pl.when(used | (slot == SIB))(lambda slot=slot: (prepare(slot, (zero,)), None)[1])

    def from_slot(slot, carry):
        both(
            size_ref[2 * slot] > SIDE,
            lambda deep: both(
                size_ref[2 * slot + 1] <= HALF, lambda narrow: first_stage(slot, deep, narrow)
            ),
        )
        return carry

    lax.fori_loop(0, 4, from_slot, 0)
    if last:
        sigma = meta_ref[SIGMA]
        outputs = [
            pltpu.make_async_copy(
                known_ref.at[which, slot],
                out.at[pl.ds(0, MATVECS - 1), sigma if slot == OWN else 1 - sigma],
                sems.at[which, slot],
            )
            for which, out in enumerate((basis_out, images_out))
            for slot in (OWN, SIB)
        ]
        for copy in outputs:
            copy.start()
        state_ref[...] = numbers.state(state_ref.shape)

    def clear(i, carry):
        at = pl.ds(pl.multiple_of(i * CHUNK, CHUNK), CHUNK)
        out_ref[at, :] = jnp.zeros((CHUNK, width), F32)
        return carry

    lax.fori_loop(0, states // CHUNK, clear, 0)
    zeros_at = mid_high.shape[0] - states
    for ref in (mid_high, mid_low):
        ref[pl.ds(zeros_at, states), :] = jnp.zeros((states, width), BF16)

    def second_stage(size, thin):
        to = pl.ds(0, size)

        def right_block(i, bond, narrow):
            lanes = pl.ds(0, HALF if narrow else width)
            if not k:
                for first in range(0, HALF if thin else width, CHUNK):
                    at = pl.ds(first, CHUNK)
                    high, low = split(right_buf[i, at, lanes])
                    right_high[bond, at, lanes] = high
                    if thin:
                        right_high[bond, pl.ds(HALF + first, CHUNK), lanes] = low
                    else:
                        right_low[bond, at, lanes] = low
            return right_high[bond, :, lanes], None if thin else right_low[bond, :, lanes]

        def product(i, real, narrow):
            bond = order_ref[i]
            at = pl.ds(pl.multiple_of(jnp.where(real, bond * stride, zeros_at), 16), size)
            high = mid_high[at, :]
            right, right_rest = right_block(i, bond, narrow)
            if narrow:
                value = dot_nt(high, jnp.concatenate([right, right], axis=1))
                if not thin:
                    value = value + dot_nt(high[:, :HALF], right_rest)
            else:
                value = dot_nt(high, right)
                if not thin:
                    value = value + dot_nt(high, right_rest) + dot_nt(mid_low[at, :], right)
            if thin:
                value = value[:, :HALF] + value[:, HALF:]
                if not narrow:
                    value = value + dot_nt(mid_low[at, :], right[:HALF, :])
            return value

        def run(begin, end, narrow):
            def pair(p, carry):
                one = begin + 2 * p
                real = one + 1 < end
                two = jnp.where(real, one + 1, one)
                if not k:
                    each_right(one, lambda copy: copy.wait())
                    pl.when(real)(lambda: each_right(two, lambda copy: copy.wait()))
                value = product(one, True, narrow) + product(two, real, narrow)
                if thin:
                    out_ref[to, :HALF] += value
                else:
                    out_ref[to, :] += value
                return carry

            lax.fori_loop(0, (end - begin + 1) // 2, pair, 0)

        run(0, thin_sources, True)
        run(thin_sources, count, False)

    for size in range(TILE, states + 1, TILE):
        pl.when((rows <= size) & (rows > size - TILE))(
            lambda size=size: both(cols <= HALF, functools.partial(second_stage, size))
        )

    def finish(i, carry):
        at = pl.ds(pl.multiple_of(i * CHUNK, CHUNK), CHUNK)
        mask = live_mask((CHUNK, width), i * CHUNK, rows, cols)
        value = jnp.where(mask, out_ref[at, :], 0.0)
        if last:
            halves[0][at, :] = jnp.where(core == 0, value[:, :HALF], value[:, HALF:])
            halves[1][at, :] = jnp.where(core == 0, value[:, HALF:], value[:, :HALF])
        else:
            out_ref[at, :] = value
        return carry

    lax.fori_loop(0, (rows + CHUNK - 1) // CHUNK, finish, 0)
    for index, entry in enumerate(own):
        early_ref[index] = entry
    if last:
        for copy in outputs:
            copy.wait()


def join_kernel(a_ref, b_ref, s0, s1, s2, s3, *refs):
    out_ref = refs[-1]
    states = a_ref.shape[0]
    total = (s0[...] + s1[...]) + (s2[...] + s3[...])
    out_ref[pl.ds(states, NOTE), :HALF] = total
    out_ref[pl.ds(states, NOTE), HALF:] = total

    def step(i, carry):
        at = pl.ds(pl.multiple_of(i * CHUNK, CHUNK), CHUNK)
        out_ref[at, :] = a_ref[at, :] + b_ref[at, :]
        return carry

    lax.fori_loop(0, states // CHUNK, step, 0)


def fill_kernel(cells, meta_ref, *refs):
    total, state_ref = refs[:2], refs[2]
    known_ref, raw_own, raw_sib, *parts = refs[3:9]
    basis_out, images_out, projected_ref, basis_buf, images_buf, sems = refs[-6:]
    last = MATVECS - 1
    sigma = meta_ref[SIGMA]
    numbers = Scalars([total], cells, state_ref[...])
    core = lax.axis_index("rsec")
    states, half = basis_buf.shape[1:]
    lanes = pl.ds(pl.multiple_of(core * half, half), half)
    inverse = 1.0 / numbers.norm[0][:, :1]
    corr = [a[:, :1] for a in numbers.corr[0]]
    copies = []
    chunks = states // CHUNK
    for slot, raw, image, rows in (
        (OWN, raw_own, parts[:2], meta_ref[ROWS]),
        (SIB, raw_sib, parts[2:], meta_ref[SIB_ROWS]),
    ):

        def step(i, carry, slot=slot, raw=raw, image=image):
            at = pl.ds(pl.multiple_of(i * CHUNK, CHUNK), CHUNK)
            fields = (raw[at, lanes], sum(ref[at, :] for ref in image[1:]) + image[0][at, :])
            for which, buf in enumerate((basis_buf, images_buf)):
                value = fields[which]
                for j in range(last):
                    value = value - corr[j] * known_ref[which, slot, j, at, :]
                buf[slot, at, :] = value * inverse
            return carry

        def dead(i, carry, slot=slot):
            at = pl.ds(pl.multiple_of(i * CHUNK, CHUNK), CHUNK)
            for buf in (basis_buf, images_buf):
                buf[slot, at, :] = jnp.zeros((CHUNK, half), F32)
            return carry

        live = (rows + CHUNK - 1) // CHUNK
        lax.fori_loop(0, live, step, 0)
        lax.fori_loop(live, chunks, dead, 0)
        sector = sigma if slot == OWN else 1 - sigma
        for which, (buf, out) in enumerate(((basis_buf, basis_out), (images_buf, images_out))):
            copies.append(
                pltpu.make_async_copy(buf.at[slot], out.at[last, sector], sems.at[which, slot])
            )
            copies[-1].start()
    shape = projected_ref.shape
    row_ids = lax.broadcasted_iota(jnp.int32, shape, 0)
    col_ids = lax.broadcasted_iota(jnp.int32, shape, 1)
    value = jnp.zeros(shape, F32)
    for i in range(MATVECS):
        for j in range(MATVECS):
            value = jnp.where((row_ids == i) & (col_ids == j), numbers.proj[i, j][:, :1], value)
    projected_ref[...] = value
    for copy in copies:
        copy.wait()


def per_device(
    wavefunction, left_env, right_env, precond_diag, down_charge, bond_mask, left_size, right_size
):
    sectors, states, columns = wavefunction.shape
    bonds = left_env.shape[0]
    lsec_count = lax.axis_size("lsec")
    mpo_count = lax.axis_size("mpo")
    assert sectors == 2 and lax.axis_size("rsec") == 2
    width = 2 * columns
    cells = float(lsec_count * sectors * states * width)
    field = jax.ShapeDtypeStruct((states, width), F32)
    noted = jax.ShapeDtypeStruct((states + NOTE, width), F32)
    half_field = jax.ShapeDtypeStruct((states, columns), F32)
    small = jax.ShapeDtypeStruct((8, 128), F32)
    params = pltpu.CompilerParams(vmem_limit_bytes=18 * 2**20)

    swap = [(0, 1), (1, 0)]
    first_pairs = [(i, i ^ 1) for i in range(lsec_count) if i ^ 1 < lsec_count]
    second_pairs = [(i, j) for a in range(1, lsec_count - 1, 2) for i, j in ((a, a + 1), (a + 1, a))]
    anywhere = pl.BlockSpec(memory_space=pl.ANY)
    in_hbm = pl.BlockSpec(memory_space=pltpu.HBM)

    def hold(value):
        return pltpu.with_memory_space_constraint(value, pltpu.HBM)

    def neighbours(value):
        return lax.ppermute(value, "lsec", first_pairs), lax.ppermute(value, "lsec", second_pairs)

    wave_all = lax.all_gather(wavefunction, "rsec", axis=2, tiled=True)
    right_send, _ = lax.optimization_barrier((right_env, wave_all))
    right_far = lax.ppermute(right_send, "rsec", swap)
    mask_rows = bond_mask.T
    down_charge, mask_rows, left_size, right_size = [
        hold(x) for x in (down_charge, mask_rows, left_size, right_size)
    ]
    own = pl.pallas_call(
        first_kernel,
        out_shape=noted,
        in_specs=[in_hbm] * 3 + [whole_vmem()],
        out_specs=whole_vmem(),
        scratch_shapes=[
            pltpu.SMEM(down_charge.shape, jnp.int32),
            pltpu.SMEM(left_size.shape, jnp.int32),
            pltpu.SMEM(right_size.shape, jnp.int32),
            pltpu.SemaphoreType.DMA((3,)),
        ],
        compiler_params=params,
        name="first",
    )(down_charge, left_size, right_size, wave_all)
    near_waves = neighbours(own)
    sib, meta = pl.pallas_call(
        functools.partial(prep_kernel, lsec_count, bonds),
        out_shape=(field, jax.ShapeDtypeStruct((LIST + bonds,), jnp.int32)),
        in_specs=[in_hbm] * 4 + [whole_vmem(), anywhere],
        out_specs=(whole_vmem(), whole_smem()),
        scratch_shapes=[
            pltpu.SMEM(down_charge.shape, jnp.int32),
            pltpu.SMEM(mask_rows.shape, jnp.int32),
            pltpu.SMEM(left_size.shape, jnp.int32),
            pltpu.SMEM(right_size.shape, jnp.int32),
            pltpu.SemaphoreType.DMA((4,)),
        ],
        compiler_params=params,
        name="prep",
    )(down_charge, mask_rows, left_size, right_size, wave_all, own)
    raw = [(own, sib, *near_waves)]
    diag_send, _ = lax.optimization_barrier((precond_diag, sib))
    diag_far = lax.ppermute(diag_send, "rsec", swap)
    diag_own, diag_sib = pl.pallas_call(
        diag_kernel,
        out_shape=(field,) * 2,
        in_specs=[whole_smem()] + [whole_vmem()] * 2,
        out_specs=(whole_vmem(),) * 2,
        compiler_params=params,
        name="diag",
    )(meta, hold(precond_diag), diag_far)

    near_diags = neighbours(diag_own)

    def mpo_pair(value):
        if mpo_count != 2:
            value = lax.psum(value, "mpo")
            return value, jnp.zeros_like(value)
        return value, lax.ppermute(value, "mpo", swap)

    def lsec_parts(part):
        if lsec_count != 4:
            zero = jnp.zeros_like(part)
            return lax.psum(part, "lsec"), zero, zero, zero
        return (part, *[lax.ppermute(part, "lsec", [(i, i ^ x) for i in range(4)]) for x in (1, 2, 3)])

    def join(value, part, after):
        return pl.pallas_call(
            join_kernel,
            out_shape=noted,
            in_specs=[whole_vmem()] * 6 + [anywhere] * len(after),
            out_specs=whole_vmem(),
            compiler_params=params,
            name="join",
        )(*mpo_pair(value), *lsec_parts(part), *after)

    most = bonds - bonds // 5 if bonds % 5 == 0 else bonds
    packed = most * states + PACK
    lefts = pl.pallas_call(
        left_kernel,
        out_shape=(
            pltpu.VMEM((packed, SIDE), BF16),
            pltpu.VMEM((packed, SIDE), BF16),
            pltpu.VMEM((packed, 2 * (states - SIDE)), BF16),
        ),
        in_specs=[whole_smem(), anywhere],
        out_specs=(whole_vmem(),) * 3,
        scratch_shapes=[
            pltpu.VMEM((BUFFERS, states, states), F32),
            pltpu.SemaphoreType.DMA((states // TILE, BUFFERS)),
        ],
        compiler_params=params,
        cost_estimate=pl.CostEstimate(flops=0, transcendentals=0, bytes_accessed=bonds * states * states * 4),
        name="left",
    )(meta, hold(left_env))
    def dots(k, early, values):
        operands = [early, *totals, *[group[0] for group in raw], *values]
        return pl.pallas_call(
            functools.partial(dots_kernel, k, cells, mpo_count),
            out_shape=small,
            in_specs=[whole_smem()] + [whole_vmem()] * len(operands),
            out_specs=whole_vmem(),
            compiler_params=params,
            cost_estimate=pl.CostEstimate(
                flops=4 * states * width, transcendentals=0, bytes_accessed=4 * states * width
            ),
            name=f"dots{k}",
        )(meta, *operands)

    out = jax.ShapeDtypeStruct((MATVECS, sectors, states, columns), F32)
    known = jax.ShapeDtypeStruct((2, sectors, MATVECS - 1, states, columns), F32)

    def matvec(k, rights, inputs):
        last = k + 1 == MATVECS
        out_shape = [half_field] * 2 if last else [field]
        out_shape += [jax.ShapeDtypeStruct((1 + 2 * k, 8, width), F32)] + [field] * (4 if k else 0)
        out_specs = [whole_vmem()] * len(out_shape)
        scratch = [
            pltpu.VMEM((4, states, width), BF16),
            pltpu.VMEM((4, states, width), BF16),
            pltpu.VMEM((2 * (states - SIDE), width), BF16),
            pltpu.VMEM((packed + states, width), BF16),
            pltpu.VMEM((packed + states, width), BF16),
            pltpu.SMEM((bonds,), jnp.int32),
        ]
        if k == 0:
            out_shape += [pltpu.VMEM((most, width, width), BF16)] * 2
            out_shape += [jax.ShapeDtypeStruct((8,), jnp.int32)]
            out_specs += [whole_vmem()] * 2 + [whole_smem()]
            scratch += [
                pltpu.VMEM((most, width, width), F32),
                pltpu.SemaphoreType.DMA((2, most)),
            ]
            right_specs = [anywhere] * 2
        else:
            right_specs = [whole_vmem()] * 2 + [whole_smem()]
        if last:
            out_shape += [known, small, out, out]
            out_specs += [whole_vmem(), whole_vmem(), anywhere, anywhere]
            scratch += [pltpu.VMEM((states, width), F32), pltpu.SemaphoreType.DMA((2, 2))]
        return pl.pallas_call(
            functools.partial(matvec_kernel, k, cells),
            out_shape=tuple(out_shape),
            in_specs=[whole_smem()] + [whole_vmem()] * 3 + right_specs + [whole_vmem()] * len(inputs),
            out_specs=tuple(out_specs),
            scratch_shapes=scratch,
            compiler_params=params,
            cost_estimate=pl.CostEstimate(
                flops=2 * 3 * bonds * states * width * (states + width),
                transcendentals=0,
                bytes_accessed=bonds * states * states,
            ),
            name=f"matvec{k}",
        )(meta, *lefts, *rights, *inputs)

    def flatten(groups):
        return [x for group in groups for x in group]

    totals = []
    images = []
    for k in range(MATVECS - 1):
        if k == 0:
            value, early, *rights = matvec(0, [hold(right_env), right_far], list(raw[0]))
            precond = (diag_own, diag_sib, *near_diags)
        else:
            value, early, *fresh = matvec(k, rights, [*totals, *flatten(raw), *flatten(images), *precond])
            raw.append(tuple(fresh))
        part = dots(k, early, [value])
        value = join(value, part, [] if k else near_diags)
        beside = lax.ppermute(value, "rsec", swap)
        images.append((value, beside, *neighbours(value)))
        totals += mpo_pair(value[states:, :HALF] + beside[states:, :HALF])

    inputs = [*totals, *flatten(raw), *flatten(images), *precond]
    near, away, early, own, sib, _, _, known_blocks, state, *outs = matvec(MATVECS - 1, rights, inputs)
    raw.append((own, sib))
    part = dots(MATVECS - 1, early, [near, away])
    away, far_away = mpo_pair(away)
    sib_half = lax.ppermute(away + far_away, "rsec", swap)
    own_half = mpo_pair(near)
    one, two, three, four = lsec_parts(part)
    part = (one + two) + (three + four)
    total = mpo_pair(part + lax.ppermute(part, "rsec", swap))
    operands = [*total, state, known_blocks, own, sib, *own_half, sib_half]
    return pl.pallas_call(
        functools.partial(fill_kernel, cells),
        out_shape=(out, out, jax.ShapeDtypeStruct((MATVECS, MATVECS), F32)),
        in_specs=[whole_smem()] + [whole_vmem()] * len(operands) + [anywhere] * 2,
        out_specs=(anywhere, anywhere, whole_vmem()),
        scratch_shapes=[
            pltpu.VMEM((sectors, states, columns), F32),
            pltpu.VMEM((sectors, states, columns), F32),
            pltpu.SemaphoreType.DMA((2, 2)),
        ],
        input_output_aliases={1 + len(operands): 0, 2 + len(operands): 1},
        compiler_params=params,
        name="fill",
    )(meta, *operands, *outs)


def solution(mesh):
    placed = (
        P(("grp", "lsec"), None, "rsec"),
        P("mpo", ("grp", "lsec"), None, None),
        P("mpo", ("grp", "lsec"), "rsec", None),
        P(("grp", "lsec"), None, "rsec"),
        P("grp"),
        P("mpo", ("grp", "lsec")),
        P(("grp", "lsec")),
        P(("grp", "lsec")),
    )
    return jax.shard_map(
        per_device,
        mesh=mesh,
        in_specs=placed,
        out_specs=(
            P(None, ("grp", "lsec"), None, "rsec"),
            P(None, ("grp", "lsec"), None, "rsec"),
            P("grp", None),
        ),
        check_vma=False,
    )
```

```python
import functools

import jax
import jax.numpy as jnp
from jax import lax
from jax.experimental import pallas as pl
from jax.experimental.pallas import tpu as pltpu
from jax.sharding import PartitionSpec as P

EPSILON = 1e-06
MATVECS = 3
F32 = jnp.float32
BF16 = jnp.bfloat16
SIGMA, COUNT, ROWS, COLS, FIRST, SIB_ROWS, SIB_COLS, LIST = 0, 1, 2, 3, 4, 9, 10, 16
OWN, SIB, FIRST_PAIR, SECOND_PAIR = 0, 1, 2, 3
CHUNK = 64
TILE = 128
SIDE = 256
HALF = 128
NOTE = 8
PACK = 512
BUFFERS = 8


def whole_vmem():
    return pl.BlockSpec(memory_space=pltpu.VMEM)


def whole_smem():
    return pl.BlockSpec(memory_space=pltpu.SMEM)


def split(value):
    high = value.astype(BF16)
    return high, (value - high.astype(F32)).astype(BF16)


def orientation(down_ref, place):
    def step(i, flips):
        straight = (down_ref[2 * i] == down_ref[2 * i - 2]) | (
            down_ref[2 * i + 1] == down_ref[2 * i - 1]
        )
        return jnp.where(straight, flips, 1 - flips)

    return lax.fori_loop(1, place + 1, step, jnp.int32(0))


def live_mask(shape, row0, rows, cols):
    row_ids = row0 + lax.broadcasted_iota(jnp.int32, shape, 0)
    col_ids = lax.broadcasted_iota(jnp.int32, shape, 1)
    return (row_ids < rows) & (col_ids < cols)


def read_small(pairs, sems):
    copies = [pltpu.make_async_copy(*pair, sems.at[i]) for i, pair in enumerate(pairs)]
    for copy in copies:
        copy.start()
    for copy in copies:
        copy.wait()


def first_kernel(meta_ref, wave_ref, wave_far, own_ref, sib_ref):
    states, half = wave_ref.shape[1:]
    sigma, core = meta_ref[SIGMA], lax.axis_index("rsec")
    for out_ref, slot, rows, cols in (
        (own_ref, sigma, meta_ref[ROWS], meta_ref[COLS]),
        (sib_ref, 1 - sigma, meta_ref[SIB_ROWS], meta_ref[SIB_COLS]),
    ):

        def fill(i, carry, out_ref=out_ref, slot=slot, rows=rows, cols=cols):
            at = pl.ds(pl.multiple_of(i * CHUNK, CHUNK), CHUNK)
            for place, wave in ((core, wave_ref), (1 - core, wave_far)):
                lanes = pl.ds(pl.multiple_of(place * half, half), half)
                mask = live_mask((CHUNK, half), i * CHUNK, rows, cols - place * half)
                out_ref[at, lanes] = jnp.where(mask, wave[slot, at, :], 0.0)
            return carry

        lax.fori_loop(0, states // CHUNK, fill, 0)
    note = (NOTE, own_ref.shape[1])
    row_ids = lax.broadcasted_iota(jnp.int32, note, 0)
    own_ref[pl.ds(states, NOTE), :] = jnp.where(
        row_ids == 0, meta_ref[ROWS], meta_ref[COLS]
    ).astype(F32)


def prep_kernel(lsec_count, bonds, down_in, mask_in, left_in, right_in, wave_in, meta_ref, wave_ref,
                down_ref, mask_ref, left_size_ref, right_size_ref, sems, wave_sem):
    wave_copy = pltpu.make_async_copy(wave_in, wave_ref, wave_sem)
    wave_copy.start()
    read_small(
        ((down_in, down_ref), (mask_in, mask_ref), (left_in, left_size_ref), (right_in, right_size_ref)),
        sems,
    )
    place = lax.axis_index("lsec")
    core = lax.axis_index("rsec")
    first_bond = lax.axis_index("mpo") * bonds
    sigma = core ^ orientation(down_ref, place)
    own_down = down_ref[2 * place + sigma]
    sib_down = down_ref[2 * place + 1 - sigma]
    before = jnp.maximum(place - 1, 0)
    after = jnp.minimum(place + 1, lsec_count - 1)
    prev_down = down_ref[2 * before + (core ^ orientation(down_ref, before))]
    next_down = down_ref[2 * after + (core ^ orientation(down_ref, after))]
    has_prev = (place > 0) & (prev_down == own_down)
    has_next = (place < lsec_count - 1) & (next_down == own_down)
    odd = lax.rem(place, 2)
    has_lower = sib_down == own_down - 1
    has_upper = sib_down == own_down + 1

    def gather(slot, count):
        meta_ref[FIRST + slot] = count

        def step(bond, count):
            kind = lax.rem(first_bond + bond, 5)
            if slot == OWN:
                there = kind == 0
            elif slot == SIB:
                there = ((kind == 3) & has_lower) | ((kind == 4) & has_upper)
            else:
                lower = odd if slot == FIRST_PAIR else 1 - odd
                there = ((kind == 1) & has_prev & (lower == 1)) | (
                    (kind == 2) & has_next & (lower == 0)
                )
            there = there & (mask_ref[sigma, bond] > 0)

            @pl.when(there)
            def _():
                meta_ref[LIST + count] = bond * 4 + slot

            return count + there.astype(jnp.int32)

        return lax.fori_loop(0, bonds, step, count)

    count = jnp.int32(0)
    for slot in (OWN, SIB, FIRST_PAIR, SECOND_PAIR):
        count = gather(slot, count)
    meta_ref[FIRST + 4] = count
    rows, cols = left_size_ref[sigma], right_size_ref[sigma]
    meta_ref[SIGMA] = sigma
    meta_ref[COUNT] = count
    meta_ref[ROWS] = rows
    meta_ref[COLS] = cols
    meta_ref[SIB_ROWS] = left_size_ref[1 - sigma]
    meta_ref[SIB_COLS] = right_size_ref[1 - sigma]
    wave_copy.wait()


def diag_kernel(meta_ref, diag_ref, diag_far, diag_own, diag_sib):
    states, width = diag_own.shape
    half = width // 2
    sigma, core = meta_ref[SIGMA], lax.axis_index("rsec")
    near = pl.ds(pl.multiple_of(core * half, half), half)
    away = pl.ds(pl.multiple_of((1 - core) * half, half), half)
    for out_ref, slot in ((diag_own, sigma), (diag_sib, 1 - sigma)):

        def fill(i, carry, out_ref=out_ref, slot=slot):
            at = pl.ds(pl.multiple_of(i * CHUNK, CHUNK), CHUNK)
            out_ref[at, near] = diag_ref[slot, at, :]
            out_ref[at, away] = diag_far[slot, at, :]
            return carry

        lax.fori_loop(0, states // CHUNK, fill, 0)


def row(value, index):
    return value[index : index + 1, :]


def stack_rows(shape, rows):
    row_ids = lax.broadcasted_iota(jnp.int32, shape, 0)
    value = jnp.zeros(shape, F32)
    for index, entry in enumerate(rows):
        if entry is not None:
            value = jnp.where(row_ids == index, entry, value)
    return value


class Scalars:
    def __init__(self, totals, cells, state=None):
        self.proj = {}
        self.gram = {}
        self.norm = []
        self.corr = []
        known = 0
        if state is not None:
            known = MATVECS - 1
            places = [(i, j) for i in range(known) for j in range(known)]
            for index, place in enumerate(places):
                self.proj[place] = row(state, index)
                self.gram[place] = row(state, len(places) + index)
        for k, total in enumerate(totals, known):
            value = (total[0][...] + total[1][...]) / cells
            size, inner = row(value, 0), row(value, 1)
            a = [row(value, 2 + j) for j in range(k)]
            e = [row(value, 4 + j) for j in range(k)]
            f = [row(value, 6 + j) for j in range(k)]
            length = size
            theta = inner
            for j in range(k):
                length = length - 2.0 * a[j] * a[j]
                theta = theta - a[j] * e[j] - a[j] * f[j]
            for i in range(k):
                for j in range(k):
                    length = length + a[i] * a[j] * self.gram[i, j]
                    theta = theta + a[i] * a[j] * self.proj[i, j]
            length = jnp.maximum(length, 0.0)
            square = length + EPSILON
            norm = jnp.sqrt(square)
            for j in range(k):
                up, down, both = e[j], f[j], a[j]
                for i in range(k):
                    up = up - a[i] * self.proj[j, i]
                    down = down - a[i] * self.proj[i, j]
                    both = both - a[i] * self.gram[i, j]
                self.proj[j, k] = up / norm
                self.proj[k, j] = down / norm
                self.gram[j, k] = self.gram[k, j] = both / norm
            self.proj[k, k] = theta / square
            self.gram[k, k] = length / square
            self.norm.append(norm)
            self.corr.append(a)

    def state(self, shape):
        known = MATVECS - 1
        places = [(i, j) for i in range(known) for j in range(known)]
        rows = [self.proj[place] for place in places] + [self.gram[place] for place in places]
        return stack_rows(shape, rows)

    def basis(self, k, fields):
        done = []
        for step in range(k + 1):
            value = fields[step]
            for j in range(step):
                value = value - self.corr[step][j][:, :1] * done[j]
            done.append(value / self.norm[step][:, :1])
        return done


def left_kernel(meta_ref, left_ref, left_high, left_low, left_tail, left_buf, sems):
    states = left_buf.shape[1]
    sigma, count, rows = meta_ref[SIGMA], meta_ref[COUNT], meta_ref[ROWS]
    stride = packed_rows(rows)

    def each(i, act):
        bond = meta_ref[LIST + i] // 4
        at = lax.rem(i, BUFFERS)
        for p in range(states // TILE):
            part = pl.ds(p * TILE, TILE)

            @pl.when(rows > p * TILE)
            def _(part=part, p=p):
                act(
                    pltpu.make_async_copy(
                        left_ref.at[bond, sigma, part], left_buf.at[at, part], sems.at[p, at]
                    )
                )

    def start(i):
        @pl.when(i < count)
        def _():
            each(i, lambda copy: copy.start())

    for i in range(BUFFERS - 1):
        start(jnp.int32(i))

    def step(i, carry):
        at = lax.rem(i, BUFFERS)
        start(i + BUFFERS - 1)
        each(i, lambda copy: copy.wait())

        def chunk(t, inner):
            high, low = split(left_buf[at, pl.ds(pl.multiple_of(t * CHUNK, CHUNK), CHUNK), :])
            to = pl.ds(pl.multiple_of(i * stride + t * CHUNK, 16), CHUNK)
            left_high[to, :] = high[:, :SIDE]
            left_low[to, :] = low[:, :SIDE]
            left_tail[to, :] = jnp.concatenate([high[:, SIDE:], low[:, SIDE:]], axis=1)
            return inner

        lax.fori_loop(0, (rows + CHUNK - 1) // CHUNK, chunk, 0)
        return carry

    lax.fori_loop(0, count, step, 0)


def right_kernel(meta_ref, right_ref, far_ref, right_high, right_low, right_buf, sems):
    width, half = right_buf.shape[1], right_ref.shape[2]
    sigma, count = meta_ref[SIGMA], meta_ref[COUNT]
    core = lax.axis_index("rsec")
    thin = meta_ref[COLS] <= HALF

    def each(i, act):
        bond = meta_ref[LIST + i] // 4
        for ref, place, sem in ((right_ref, core, 0), (far_ref, 1 - core, 1)):
            part = pl.ds(pl.multiple_of(place * half, half), half)

            @pl.when(jnp.logical_not(thin) | (place == 0))
            def _(ref=ref, part=part, sem=sem):
                act(
                    pltpu.make_async_copy(ref.at[bond, sigma], right_buf.at[i, part], sems.at[sem, i])
                )

    def start(i, carry):
        each(i, lambda copy: copy.start())
        return carry

    lax.fori_loop(0, count, start, 0)

    def step(i, carry):
        each(i, lambda copy: copy.wait())

        @pl.when(thin)
        def _():
            for first in range(0, HALF, CHUNK):
                high, low = split(right_buf[i, pl.ds(first, CHUNK), :])
                right_high[i, pl.ds(first, CHUNK), :] = high
                right_high[i, pl.ds(HALF + first, CHUNK), :] = low

        @pl.when(jnp.logical_not(thin))
        def _():
            for first in range(0, width, CHUNK):
                at = pl.ds(first, CHUNK)
                right_high[i, at, :], right_low[i, at, :] = split(right_buf[i, at, :])

        return carry

    lax.fori_loop(0, count, step, 0)


def packed_rows(rows):
    return ((rows + 15) // 16) * 16


def fold(value):
    return jnp.sum(value.reshape(CHUNK // 8, 8, value.shape[1]), axis=0)


def dots_kernel(k, cells, mpo_count, meta_ref, early_ref, *refs):
    refs, small_ref = list(refs[:-1]), refs[-1]
    totals = [(refs.pop(0), refs.pop(0)) for _ in range(k)]
    raw = [refs.pop(0) for _ in range(k + 1)]
    numbers = Scalars(totals, cells) if k else None
    core = lax.axis_index("rsec")
    zero = jnp.zeros(early_ref.shape[1:], F32)

    def step(i, carry):
        at = pl.ds(pl.multiple_of(i * CHUNK, CHUNK), CHUNK)
        blocks = [ref[at, :] for ref in refs]
        if len(blocks) == 2:
            near, away = blocks
            first, second = jnp.where(core == 0, near, away), jnp.where(core == 0, away, near)
            value = jnp.concatenate([first, second], axis=1)
        else:
            value = blocks[0]
        basis = numbers.basis(k - 1, [ref[at, :] for ref in raw[:k]]) if k else []
        return tuple(c + fold(value * b) for c, b in zip(carry, [raw[k][at, :], *basis]))

    live = (meta_ref[ROWS] + CHUNK - 1) // CHUNK
    late = lax.fori_loop(0, live, step, (zero,) * (1 + k))

    def whole(value):
        return jnp.sum(jnp.sum(value, axis=1, keepdims=True), axis=0, keepdims=True)

    share = 1.0 / mpo_count
    entries = [whole(early_ref[0]) * share, whole(late[0])]
    for j in range(2):
        entries.append(whole(early_ref[1 + j]) * share if j < k else None)
    for j in range(2):
        entries.append(whole(late[1 + j]) if j < k else None)
    for j in range(2):
        entries.append(whole(early_ref[1 + k + j]) * share if j < k else None)
    small_ref[...] = stack_rows(small_ref.shape, entries)


def matvec_kernel(k, cells, *refs):
    refs = list(refs)
    meta_ref = refs.pop(0)
    left_high, left_low, left_tail = [refs.pop(0) for _ in range(3)]
    right_high, right_low = refs.pop(0), refs.pop(0)
    size_ref = refs.pop(0) if k else None
    totals = [(refs.pop(0), refs.pop(0)) for _ in range(k)]
    raw = [[refs.pop(0) for _ in range(4)] for _ in range(max(k, 1))]
    images = [[refs.pop(0) for _ in range(4)] for _ in range(k)]
    precond = [refs.pop(0) for _ in range(4)] if k else []
    last = k + 1 == MATVECS
    halves = [refs.pop(0), refs.pop(0)] if last else []
    out_ref = None if last else refs.pop(0)
    early_ref = refs.pop(0)
    if k:
        new_refs = [refs.pop(0) for _ in range(4)]
    else:
        new_refs = raw[0]
        size_ref = refs.pop(0)
    if last:
        known_ref, state_ref, basis_out, images_out = [refs.pop(0) for _ in range(4)]
    high_ref, low_ref, tail_ref, mid_high, mid_low, order_ref = refs[:6]
    if last:
        out_ref, sems = refs[6:]
    states, width = out_ref.shape
    count, rows, cols = meta_ref[COUNT], meta_ref[ROWS], meta_ref[COLS]
    stride = packed_rows(rows)

    core = lax.axis_index("rsec")
    if not k:
        size_ref[2 * OWN], size_ref[2 * OWN + 1] = rows, cols
        size_ref[2 * SIB], size_ref[2 * SIB + 1] = meta_ref[SIB_ROWS], meta_ref[SIB_COLS]
        for slot in (FIRST_PAIR, SECOND_PAIR):
            note = raw[0][slot][pl.ds(states, NOTE), :HALF]
            size_ref[2 * slot] = jnp.max(note[:1]).astype(jnp.int32)
            size_ref[2 * slot + 1] = jnp.max(note[1:]).astype(jnp.int32)
    def list_bonds(narrow):
        def step(i, place):
            hit = (size_ref[2 * lax.rem(meta_ref[LIST + i], 4) + 1] <= HALF) == narrow

            @pl.when(hit)
            def _():
                order_ref[place] = i

            return place + hit.astype(jnp.int32)

        return step

    thin_sources = lax.fori_loop(0, count, list_bonds(True), jnp.int32(0))
    lax.fori_loop(0, count, list_bonds(False), thin_sources)
    if k:
        numbers = Scalars(totals, cells)
        theta = numbers.proj[k - 1, k - 1][:, :1]
    zero = jnp.zeros((8, width), F32)

    def prepare(slot, carry):
        def step(i, carry):
            at = pl.ds(pl.multiple_of(i * CHUNK, CHUNK), CHUNK)
            if k:
                basis = numbers.basis(k - 1, [r[slot][at, :] for r in raw])
                image = numbers.basis(k - 1, [r[slot][at, :] for r in images])
                value = (image[-1] - theta * basis[-1]) / jnp.maximum(
                    precond[slot][at, :] - theta, 1.0
                )
                new_refs[slot][at, :] = value
                if last and slot in (OWN, SIB):
                    for which, group in enumerate((basis, image)):
                        for j, block in enumerate(group):
                            block = jnp.where(core == 0, block[:, :HALF], block[:, HALF:])
                            known_ref[which, slot, j, at, :] = block
            else:
                basis, image = [], []
                value = raw[0][slot][at, :]
            high, low = split(value)
            high_ref[slot, at, :] = high
            low_ref[slot, at, :] = low
            terms = [value * value]
            if slot == OWN:
                terms += [value * b for b in basis] + [value * g for g in image]
            return tuple(c + fold(t) for c, t in zip(carry, terms))

        def dead(i, inner):
            at = pl.ds(pl.multiple_of(i * CHUNK, CHUNK), CHUNK)
            high_ref[slot, at, :] = jnp.zeros((CHUNK, width), BF16)
            low_ref[slot, at, :] = jnp.zeros((CHUNK, width), BF16)
            if last and slot in (OWN, SIB):
                for which in range(2):
                    for j in range(k):
                        known_ref[which, slot, j, at, :] = jnp.zeros((CHUNK, HALF), F32)
            return inner

        live = (size_ref[2 * slot] + CHUNK - 1) // CHUNK
        lax.fori_loop(live, states // CHUNK, dead, 0)
        return lax.fori_loop(0, live, step, carry)

    def dot(a, b):
        return jnp.dot(a, b, preferred_element_type=F32)

    def dot_nt(a, b):
        return lax.dot_general(a, b, (((1,), (1,)), ((), ())), preferred_element_type=F32)

    twice = functools.partial(jnp.concatenate, axis=0)

    def first_stage(slot, deep, narrow):
        begin, end = meta_ref[FIRST + slot], meta_ref[FIRST + 1 + slot]
        total = (end - begin) * stride
        top, rest = pl.ds(0, SIDE), pl.ds(SIDE, states - SIDE)
        if narrow:
            high_ref[slot, :, HALF:] = low_ref[slot, :, :HALF]
        if deep:
            tail = high_ref[slot, rest, :]
            tail_ref[...] = twice([tail, tail])

        def tile(first, size):
            at = pl.ds(pl.multiple_of(begin * stride + first, 16), size)
            high, low = left_high[at, :], left_low[at, :]
            mid = dot(high, high_ref[slot, top, :])
            if deep:
                mid = mid + dot(left_tail[at, :], tail_ref[...])
            if narrow:
                mid = mid[:, :HALF] + mid[:, HALF:] + dot(low, high_ref[slot, top, :HALF])
                mid_high[at, :] = jnp.concatenate(split(mid), axis=1)
            else:
                mid = mid + dot(low, high_ref[slot, top, :]) + dot(high, low_ref[slot, top, :])
                if deep:
                    mid = mid + dot(left_tail[at, : states - SIDE], low_ref[slot, rest, :])
                mid_high[at, :], mid_low[at, :] = split(mid)

        def step(t, carry):
            tile(t * PACK, PACK)
            return carry

        tiles = (total + PACK // 2 - 1) // PACK
        lax.fori_loop(0, tiles, step, 0)
        pl.when(total > tiles * PACK)(lambda: tile(tiles * PACK, PACK // 2))

    def both(test, action):
        pl.when(test)(lambda: action(True))
        pl.when(jnp.logical_not(test))(lambda: action(False))

    for slot in (OWN, SIB, FIRST_PAIR, SECOND_PAIR):
        if slot == OWN:
            own = prepare(slot, (zero,) * (1 + 2 * k))
        else:
            used = meta_ref[FIRST + 1 + slot] > meta_ref[FIRST + slot]
            pl.when(used | (slot == SIB))(lambda slot=slot: (prepare(slot, (zero,)), None)[1])

    def from_slot(slot, carry):
        both(
            size_ref[2 * slot] > SIDE,
            lambda deep: both(
                size_ref[2 * slot + 1] <= HALF, lambda narrow: first_stage(slot, deep, narrow)
            ),
        )
        return carry

    lax.fori_loop(0, 4, from_slot, 0)
    if last:
        sigma = meta_ref[SIGMA]
        outputs = [
            pltpu.make_async_copy(
                known_ref.at[which, slot],
                out.at[pl.ds(0, MATVECS - 1), sigma if slot == OWN else 1 - sigma],
                sems.at[which, slot],
            )
            for which, out in enumerate((basis_out, images_out))
            for slot in (OWN, SIB)
        ]
        for copy in outputs:
            copy.start()
        state_ref[...] = numbers.state(state_ref.shape)

    def clear(i, carry):
        at = pl.ds(pl.multiple_of(i * CHUNK, CHUNK), CHUNK)
        out_ref[at, :] = jnp.zeros((CHUNK, width), F32)
        return carry

    lax.fori_loop(0, states // CHUNK, clear, 0)
    zeros_at = mid_high.shape[0] - states
    for ref in (mid_high, mid_low):
        ref[pl.ds(zeros_at, states), :] = jnp.zeros((states, width), BF16)

    def second_stage(size, thin):
        to = pl.ds(0, size)

        def product(i, real, narrow):
            bond = order_ref[i]
            at = pl.ds(pl.multiple_of(jnp.where(real, bond * stride, zeros_at), 16), size)
            high = mid_high[at, :]
            lanes = pl.ds(0, HALF if narrow else width)
            right = right_high[bond, :, lanes]
            right_rest = None if thin else right_low[bond, :, lanes]
            if narrow:
                value = dot_nt(high, jnp.concatenate([right, right], axis=1))
                if not thin:
                    value = value + dot_nt(high[:, :HALF], right_rest)
            else:
                value = dot_nt(high, right)
                if not thin:
                    value = value + dot_nt(high, right_rest) + dot_nt(mid_low[at, :], right)
            if thin:
                value = value[:, :HALF] + value[:, HALF:]
                if not narrow:
                    value = value + dot_nt(mid_low[at, :], right[:HALF, :])
            return value

        def run(begin, end, narrow):
            def pair(p, carry):
                one = begin + 2 * p
                real = one + 1 < end
                two = jnp.where(real, one + 1, one)
                value = product(one, True, narrow) + product(two, real, narrow)
                if thin:
                    out_ref[to, :HALF] += value
                else:
                    out_ref[to, :] += value
                return carry

            lax.fori_loop(0, (end - begin + 1) // 2, pair, 0)

        run(0, thin_sources, True)
        run(thin_sources, count, False)

    for size in range(TILE, states + 1, TILE):
        pl.when((rows <= size) & (rows > size - TILE))(
            lambda size=size: both(cols <= HALF, functools.partial(second_stage, size))
        )

    def finish(i, carry):
        at = pl.ds(pl.multiple_of(i * CHUNK, CHUNK), CHUNK)
        mask = live_mask((CHUNK, width), i * CHUNK, rows, cols)
        value = jnp.where(mask, out_ref[at, :], 0.0)
        if last:
            halves[0][at, :] = jnp.where(core == 0, value[:, :HALF], value[:, HALF:])
            halves[1][at, :] = jnp.where(core == 0, value[:, HALF:], value[:, :HALF])
        else:
            out_ref[at, :] = value
        return carry

    lax.fori_loop(0, (rows + CHUNK - 1) // CHUNK, finish, 0)
    for index, entry in enumerate(own):
        early_ref[index] = entry
    if last:
        for copy in outputs:
            copy.wait()


def join_kernel(a_ref, b_ref, s0, s1, s2, s3, *refs):
    out_ref = refs[-1]
    states = a_ref.shape[0]
    total = (s0[...] + s1[...]) + (s2[...] + s3[...])
    out_ref[pl.ds(states, NOTE), :HALF] = total
    out_ref[pl.ds(states, NOTE), HALF:] = total

    def step(i, carry):
        at = pl.ds(pl.multiple_of(i * CHUNK, CHUNK), CHUNK)
        out_ref[at, :] = a_ref[at, :] + b_ref[at, :]
        return carry

    lax.fori_loop(0, states // CHUNK, step, 0)


def fill_kernel(cells, meta_ref, *refs):
    total, state_ref = refs[:2], refs[2]
    known_ref, raw_own, raw_sib, *parts = refs[3:9]
    basis_out, images_out, projected_ref, basis_buf, images_buf, sems = refs[-6:]
    last = MATVECS - 1
    sigma = meta_ref[SIGMA]
    numbers = Scalars([total], cells, state_ref[...])
    core = lax.axis_index("rsec")
    states, half = basis_buf.shape[1:]
    lanes = pl.ds(pl.multiple_of(core * half, half), half)
    inverse = 1.0 / numbers.norm[0][:, :1]
    corr = [a[:, :1] for a in numbers.corr[0]]
    copies = []
    chunks = states // CHUNK
    for slot, raw, image, rows in (
        (OWN, raw_own, parts[:2], meta_ref[ROWS]),
        (SIB, raw_sib, parts[2:], meta_ref[SIB_ROWS]),
    ):

        def step(i, carry, slot=slot, raw=raw, image=image):
            at = pl.ds(pl.multiple_of(i * CHUNK, CHUNK), CHUNK)
            fields = (raw[at, lanes], sum(ref[at, :] for ref in image[1:]) + image[0][at, :])
            for which, buf in enumerate((basis_buf, images_buf)):
                value = fields[which]
                for j in range(last):
                    value = value - corr[j] * known_ref[which, slot, j, at, :]
                buf[slot, at, :] = value * inverse
            return carry

        def dead(i, carry, slot=slot):
            at = pl.ds(pl.multiple_of(i * CHUNK, CHUNK), CHUNK)
            for buf in (basis_buf, images_buf):
                buf[slot, at, :] = jnp.zeros((CHUNK, half), F32)
            return carry

        live = (rows + CHUNK - 1) // CHUNK
        lax.fori_loop(0, live, step, 0)
        lax.fori_loop(live, chunks, dead, 0)
        sector = sigma if slot == OWN else 1 - sigma
        for which, (buf, out) in enumerate(((basis_buf, basis_out), (images_buf, images_out))):
            copies.append(
                pltpu.make_async_copy(buf.at[slot], out.at[last, sector], sems.at[which, slot])
            )
            copies[-1].start()
    shape = projected_ref.shape
    row_ids = lax.broadcasted_iota(jnp.int32, shape, 0)
    col_ids = lax.broadcasted_iota(jnp.int32, shape, 1)
    value = jnp.zeros(shape, F32)
    for i in range(MATVECS):
        for j in range(MATVECS):
            value = jnp.where((row_ids == i) & (col_ids == j), numbers.proj[i, j][:, :1], value)
    projected_ref[...] = value
    for copy in copies:
        copy.wait()


def per_device(
    wavefunction, left_env, right_env, precond_diag, down_charge, bond_mask, left_size, right_size
):
    sectors, states, columns = wavefunction.shape
    bonds = left_env.shape[0]
    lsec_count = lax.axis_size("lsec")
    mpo_count = lax.axis_size("mpo")
    assert sectors == 2 and lax.axis_size("rsec") == 2
    width = 2 * columns
    cells = float(lsec_count * sectors * states * width)
    field = jax.ShapeDtypeStruct((states, width), F32)
    noted = jax.ShapeDtypeStruct((states + NOTE, width), F32)
    half_field = jax.ShapeDtypeStruct((states, columns), F32)
    small = jax.ShapeDtypeStruct((8, 128), F32)
    params = pltpu.CompilerParams(vmem_limit_bytes=18 * 2**20)

    swap = [(0, 1), (1, 0)]
    first_pairs = [(i, i ^ 1) for i in range(lsec_count) if i ^ 1 < lsec_count]
    second_pairs = [(i, j) for a in range(1, lsec_count - 1, 2) for i, j in ((a, a + 1), (a + 1, a))]
    anywhere = pl.BlockSpec(memory_space=pl.ANY)
    in_hbm = pl.BlockSpec(memory_space=pltpu.HBM)

    def hold(value):
        return pltpu.with_memory_space_constraint(value, pltpu.HBM)

    def neighbours(value):
        return lax.ppermute(value, "lsec", first_pairs), lax.ppermute(value, "lsec", second_pairs)

    wave_far = lax.ppermute(wavefunction, "rsec", swap)
    mask_rows = bond_mask.T
    small_inputs = [down_charge, mask_rows, left_size, right_size]
    meta, wave_near = pl.pallas_call(
        functools.partial(prep_kernel, lsec_count, bonds),
        out_shape=(
            jax.ShapeDtypeStruct((LIST + bonds,), jnp.int32),
            jax.ShapeDtypeStruct(wavefunction.shape, F32),
        ),
        in_specs=[in_hbm] * 5,
        out_specs=(whole_smem(), whole_vmem()),
        scratch_shapes=[pltpu.SMEM(x.shape, jnp.int32) for x in small_inputs]
        + [pltpu.SemaphoreType.DMA((4,)), pltpu.SemaphoreType.DMA],
        compiler_params=params,
        cost_estimate=pl.CostEstimate(flops=0, transcendentals=0, bytes_accessed=10**6),
        name="prep",
    )(*[hold(x) for x in small_inputs], hold(wavefunction))
    right_send, _, _ = lax.optimization_barrier((right_env, wave_far, wave_near))
    right_far = lax.ppermute(right_send, "rsec", swap)
    own, sib = pl.pallas_call(
        first_kernel,
        out_shape=(noted, field),
        in_specs=[whole_smem()] + [whole_vmem()] * 2,
        out_specs=(whole_vmem(),) * 2,
        compiler_params=params,
        name="first",
    )(meta, wave_near, wave_far)
    near_waves = neighbours(own)
    raw = [(own, sib, *near_waves)]
    diag_send, _ = lax.optimization_barrier((precond_diag, sib))
    diag_far = lax.ppermute(diag_send, "rsec", swap)
    diag_own, diag_sib = pl.pallas_call(
        diag_kernel,
        out_shape=(field,) * 2,
        in_specs=[whole_smem()] + [whole_vmem()] * 2,
        out_specs=(whole_vmem(),) * 2,
        compiler_params=params,
        name="diag",
    )(meta, hold(precond_diag), diag_far)

    near_diags = neighbours(diag_own)

    def mpo_pair(value):
        if mpo_count != 2:
            value = lax.psum(value, "mpo")
            return value, jnp.zeros_like(value)
        return value, lax.ppermute(value, "mpo", swap)

    def lsec_parts(part):
        if lsec_count != 4:
            zero = jnp.zeros_like(part)
            return lax.psum(part, "lsec"), zero, zero, zero
        return (part, *[lax.ppermute(part, "lsec", [(i, i ^ x) for i in range(4)]) for x in (1, 2, 3)])

    def join(value, part, after):
        return pl.pallas_call(
            join_kernel,
            out_shape=noted,
            in_specs=[whole_vmem()] * 6 + [anywhere] * len(after),
            out_specs=whole_vmem(),
            compiler_params=params,
            name="join",
        )(*mpo_pair(value), *lsec_parts(part), *after)

    most = bonds - bonds // 5 if bonds % 5 == 0 else bonds
    packed = most * states + PACK
    lefts = pl.pallas_call(
        left_kernel,
        out_shape=(
            pltpu.VMEM((packed, SIDE), BF16),
            pltpu.VMEM((packed, SIDE), BF16),
            pltpu.VMEM((packed, 2 * (states - SIDE)), BF16),
        ),
        in_specs=[whole_smem(), anywhere],
        out_specs=(whole_vmem(),) * 3,
        scratch_shapes=[
            pltpu.VMEM((BUFFERS, states, states), F32),
            pltpu.SemaphoreType.DMA((states // TILE, BUFFERS)),
        ],
        compiler_params=params,
        cost_estimate=pl.CostEstimate(flops=0, transcendentals=0, bytes_accessed=bonds * states * states * 4),
        name="left",
    )(meta, hold(left_env))
    rights = pl.pallas_call(
        right_kernel,
        out_shape=(pltpu.VMEM((most, width, width), BF16),) * 2,
        in_specs=[whole_smem(), anywhere, anywhere],
        out_specs=(whole_vmem(),) * 2,
        scratch_shapes=[
            pltpu.VMEM((most, width, width), F32),
            pltpu.SemaphoreType.DMA((2, most)),
        ],
        compiler_params=params,
        cost_estimate=pl.CostEstimate(flops=0, transcendentals=0, bytes_accessed=bonds * width * width * 8),
        name="right",
    )(meta, hold(right_env), right_far)

    def dots(k, early, values):
        operands = [early, *totals, *[group[0] for group in raw], *values]
        return pl.pallas_call(
            functools.partial(dots_kernel, k, cells, mpo_count),
            out_shape=small,
            in_specs=[whole_smem()] + [whole_vmem()] * len(operands),
            out_specs=whole_vmem(),
            compiler_params=params,
            cost_estimate=pl.CostEstimate(
                flops=4 * states * width, transcendentals=0, bytes_accessed=4 * states * width
            ),
            name=f"dots{k}",
        )(meta, *operands)

    out = jax.ShapeDtypeStruct((MATVECS, sectors, states, columns), F32)
    known = jax.ShapeDtypeStruct((2, sectors, MATVECS - 1, states, columns), F32)

    def matvec(k, rights, inputs):
        last = k + 1 == MATVECS
        out_shape = [half_field] * 2 if last else [field]
        out_shape += [jax.ShapeDtypeStruct((1 + 2 * k, 8, width), F32)] + [field] * (4 if k else 0)
        out_specs = [whole_vmem()] * len(out_shape)
        scratch = [
            pltpu.VMEM((4, states, width), BF16),
            pltpu.VMEM((4, states, width), BF16),
            pltpu.VMEM((2 * (states - SIDE), width), BF16),
            pltpu.VMEM((packed + states, width), BF16),
            pltpu.VMEM((packed + states, width), BF16),
            pltpu.SMEM((bonds,), jnp.int32),
        ]
        right_specs = [whole_vmem()] * 2 + ([whole_smem()] if k else [])
        if k == 0:
            out_shape += [jax.ShapeDtypeStruct((8,), jnp.int32)]
            out_specs += [whole_smem()]
        if last:
            out_shape += [known, small, out, out]
            out_specs += [whole_vmem(), whole_vmem(), anywhere, anywhere]
            scratch += [pltpu.VMEM((states, width), F32), pltpu.SemaphoreType.DMA((2, 2))]
        return pl.pallas_call(
            functools.partial(matvec_kernel, k, cells),
            out_shape=tuple(out_shape),
            in_specs=[whole_smem()] + [whole_vmem()] * 3 + right_specs + [whole_vmem()] * len(inputs),
            out_specs=tuple(out_specs),
            scratch_shapes=scratch,
            compiler_params=params,
            cost_estimate=pl.CostEstimate(
                flops=2 * 3 * bonds * states * width * (states + width),
                transcendentals=0,
                bytes_accessed=bonds * states * states,
            ),
            name=f"matvec{k}",
        )(meta, *lefts, *rights, *inputs)

    def flatten(groups):
        return [x for group in groups for x in group]

    totals = []
    images = []
    for k in range(MATVECS - 1):
        if k == 0:
            value, early, sizes = matvec(0, rights, list(raw[0]))
            rights = [*rights, sizes]
            precond = (diag_own, diag_sib, *near_diags)
        else:
            value, early, *fresh = matvec(k, rights, [*totals, *flatten(raw), *flatten(images), *precond])
            raw.append(tuple(fresh))
        part = dots(k, early, [value])
        value = join(value, part, [] if k else near_diags)
        beside = lax.ppermute(value, "rsec", swap)
        images.append((value, beside, *neighbours(value)))
        totals += mpo_pair(value[states:, :HALF] + beside[states:, :HALF])

    inputs = [*totals, *flatten(raw), *flatten(images), *precond]
    near, away, early, own, sib, _, _, known_blocks, state, *outs = matvec(MATVECS - 1, rights, inputs)
    raw.append((own, sib))
    part = dots(MATVECS - 1, early, [near, away])
    away, far_away = mpo_pair(away)
    sib_half = lax.ppermute(away + far_away, "rsec", swap)
    own_half = mpo_pair(near)
    one, two, three, four = lsec_parts(part)
    part = (one + two) + (three + four)
    total = mpo_pair(part + lax.ppermute(part, "rsec", swap))
    operands = [*total, state, known_blocks, own, sib, *own_half, sib_half]
    return pl.pallas_call(
        functools.partial(fill_kernel, cells),
        out_shape=(out, out, jax.ShapeDtypeStruct((MATVECS, MATVECS), F32)),
        in_specs=[whole_smem()] + [whole_vmem()] * len(operands) + [anywhere] * 2,
        out_specs=(anywhere, anywhere, whole_vmem()),
        scratch_shapes=[
            pltpu.VMEM((sectors, states, columns), F32),
            pltpu.VMEM((sectors, states, columns), F32),
            pltpu.SemaphoreType.DMA((2, 2)),
        ],
        input_output_aliases={1 + len(operands): 0, 2 + len(operands): 1},
        compiler_params=params,
        name="fill",
    )(meta, *operands, *outs)


def solution(mesh):
    placed = (
        P(("grp", "lsec"), None, "rsec"),
        P("mpo", ("grp", "lsec"), None, None),
        P("mpo", ("grp", "lsec"), "rsec", None),
        P(("grp", "lsec"), None, "rsec"),
        P("grp"),
        P("mpo", ("grp", "lsec")),
        P(("grp", "lsec")),
        P(("grp", "lsec")),
    )
    return jax.shard_map(
        per_device,
        mesh=mesh,
        in_specs=placed,
        out_specs=(
            P(None, ("grp", "lsec"), None, "rsec"),
            P(None, ("grp", "lsec"), None, "rsec"),
            P("grp", None),
        ),
        check_vma=False,
    )
```

```python
import functools

import jax
import jax.numpy as jnp
from jax import lax
from jax.experimental import pallas as pl
from jax.experimental.pallas import tpu as pltpu
from jax.sharding import PartitionSpec as P

EPSILON = 1e-06
MATVECS = 3
F32 = jnp.float32
BF16 = jnp.bfloat16
SIGMA, COUNT, ROWS, COLS, FIRST, SIB_ROWS, SIB_COLS, LIST = 0, 1, 2, 3, 4, 9, 10, 16
OWN, SIB, FIRST_PAIR, SECOND_PAIR = 0, 1, 2, 3
CHUNK = 64
TILE = 128
SIDE = 256
HALF = 128
NOTE = 8
PACK = 512
BUFFERS = 8


def whole_vmem():
    return pl.BlockSpec(memory_space=pltpu.VMEM)


def whole_smem():
    return pl.BlockSpec(memory_space=pltpu.SMEM)


def split(value):
    high = value.astype(BF16)
    return high, (value - high.astype(F32)).astype(BF16)


def orientation(down_ref, place):
    def step(i, flips):
        straight = (down_ref[2 * i] == down_ref[2 * i - 2]) | (
            down_ref[2 * i + 1] == down_ref[2 * i - 1]
        )
        return jnp.where(straight, flips, 1 - flips)

    return lax.fori_loop(1, place + 1, step, jnp.int32(0))


def live_mask(shape, row0, rows, cols):
    row_ids = row0 + lax.broadcasted_iota(jnp.int32, shape, 0)
    col_ids = lax.broadcasted_iota(jnp.int32, shape, 1)
    return (row_ids < rows) & (col_ids < cols)


def read_small(pairs, sems):
    copies = [pltpu.make_async_copy(*pair, sems.at[i]) for i, pair in enumerate(pairs)]
    for copy in copies:
        copy.start()
    for copy in copies:
        copy.wait()


def first_kernel(meta_ref, wave_ref, wave_far, own_ref, sib_ref):
    states, half = wave_ref.shape[1:]
    sigma, core = meta_ref[SIGMA], lax.axis_index("rsec")
    for out_ref, slot, rows, cols in (
        (own_ref, sigma, meta_ref[ROWS], meta_ref[COLS]),
        (sib_ref, 1 - sigma, meta_ref[SIB_ROWS], meta_ref[SIB_COLS]),
    ):

        def fill(i, carry, out_ref=out_ref, slot=slot, rows=rows, cols=cols):
            at = pl.ds(pl.multiple_of(i * CHUNK, CHUNK), CHUNK)
            for place, wave in ((core, wave_ref), (1 - core, wave_far)):
                lanes = pl.ds(pl.multiple_of(place * half, half), half)
                mask = live_mask((CHUNK, half), i * CHUNK, rows, cols - place * half)
                out_ref[at, lanes] = jnp.where(mask, wave[slot, at, :], 0.0)
            return carry

        lax.fori_loop(0, states // CHUNK, fill, 0)
    note = (NOTE, own_ref.shape[1])
    row_ids = lax.broadcasted_iota(jnp.int32, note, 0)
    own_ref[pl.ds(states, NOTE), :] = jnp.where(
        row_ids == 0, meta_ref[ROWS], meta_ref[COLS]
    ).astype(F32)


def prep_kernel(lsec_count, bonds, down_in, mask_in, left_in, right_in, wave_in, meta_ref, wave_ref,
                down_ref, mask_ref, left_size_ref, right_size_ref, sems, wave_sem):
    wave_copy = pltpu.make_async_copy(wave_in, wave_ref, wave_sem)
    wave_copy.start()
    read_small(
        ((down_in, down_ref), (mask_in, mask_ref), (left_in, left_size_ref), (right_in, right_size_ref)),
        sems,
    )
    place = lax.axis_index("lsec")
    core = lax.axis_index("rsec")
    first_kind = lax.rem(lax.axis_index("mpo") * bonds, 5)
    sigma = core ^ orientation(down_ref, place)
    own_down = down_ref[2 * place + sigma]
    sib_down = down_ref[2 * place + 1 - sigma]
    before = jnp.maximum(place - 1, 0)
    after = jnp.minimum(place + 1, lsec_count - 1)
    prev_down = down_ref[2 * before + (core ^ orientation(down_ref, before))]
    next_down = down_ref[2 * after + (core ^ orientation(down_ref, after))]
    has_prev = (place > 0) & (prev_down == own_down)
    has_next = (place < lsec_count - 1) & (next_down == own_down)
    odd = lax.rem(place, 2)
    has_lower = sib_down == own_down - 1
    has_upper = sib_down == own_down + 1

    def gather(slot, count):
        meta_ref[FIRST + slot] = count

        def step(bond, carry):
            count, kind = carry
            if slot == OWN:
                there = kind == 0
            elif slot == SIB:
                there = ((kind == 3) & has_lower) | ((kind == 4) & has_upper)
            else:
                lower = odd if slot == FIRST_PAIR else 1 - odd
                there = ((kind == 1) & has_prev & (lower == 1)) | (
                    (kind == 2) & has_next & (lower == 0)
                )
            there = there & (mask_ref[sigma, bond] > 0)

            @pl.when(there)
            def _():
                meta_ref[LIST + count] = bond * 4 + slot

            return count + there.astype(jnp.int32), jnp.where(kind == 4, 0, kind + 1)

        return lax.fori_loop(0, bonds, step, (count, first_kind))[0]

    count = jnp.int32(0)
    for slot in (OWN, SIB, FIRST_PAIR, SECOND_PAIR):
        count = gather(slot, count)
    meta_ref[FIRST + 4] = count
    rows, cols = left_size_ref[sigma], right_size_ref[sigma]
    meta_ref[SIGMA] = sigma
    meta_ref[COUNT] = count
    meta_ref[ROWS] = rows
    meta_ref[COLS] = cols
    meta_ref[SIB_ROWS] = left_size_ref[1 - sigma]
    meta_ref[SIB_COLS] = right_size_ref[1 - sigma]
    wave_copy.wait()


def diag_kernel(meta_ref, diag_ref, diag_far, diag_own, diag_sib):
    states, width = diag_own.shape
    half = width // 2
    sigma, core = meta_ref[SIGMA], lax.axis_index("rsec")
    near = pl.ds(pl.multiple_of(core * half, half), half)
    away = pl.ds(pl.multiple_of((1 - core) * half, half), half)
    for out_ref, slot in ((diag_own, sigma), (diag_sib, 1 - sigma)):

        def fill(i, carry, out_ref=out_ref, slot=slot):
            at = pl.ds(pl.multiple_of(i * CHUNK, CHUNK), CHUNK)
            out_ref[at, near] = diag_ref[slot, at, :]
            out_ref[at, away] = diag_far[slot, at, :]
            return carry

        lax.fori_loop(0, states // CHUNK, fill, 0)


def row(value, index):
    return value[index : index + 1, :]


def stack_rows(shape, rows):
    row_ids = lax.broadcasted_iota(jnp.int32, shape, 0)
    value = jnp.zeros(shape, F32)
    for index, entry in enumerate(rows):
        if entry is not None:
            value = jnp.where(row_ids == index, entry, value)
    return value


class Scalars:
    def __init__(self, totals, cells, state=None):
        self.proj = {}
        self.gram = {}
        self.inverse = []
        self.corr = []
        known = 0
        if state is not None:
            known = MATVECS - 1
            places = [(i, j) for i in range(known) for j in range(known)]
            for index, place in enumerate(places):
                self.proj[place] = row(state, index)
                self.gram[place] = row(state, len(places) + index)
        for k, total in enumerate(totals, known):
            value = (total[0][...] + total[1][...]) / cells
            size, inner = row(value, 0), row(value, 1)
            a = [row(value, 2 + j) for j in range(k)]
            e = [row(value, 4 + j) for j in range(k)]
            f = [row(value, 6 + j) for j in range(k)]
            length = size
            theta = inner
            for j in range(k):
                length = length - 2.0 * a[j] * a[j]
                theta = theta - a[j] * e[j] - a[j] * f[j]
            for i in range(k):
                for j in range(k):
                    length = length + a[i] * a[j] * self.gram[i, j]
                    theta = theta + a[i] * a[j] * self.proj[i, j]
            length = jnp.maximum(length, 0.0)
            square = length + EPSILON
            norm = jnp.sqrt(square)
            for j in range(k):
                up, down, both = e[j], f[j], a[j]
                for i in range(k):
                    up = up - a[i] * self.proj[j, i]
                    down = down - a[i] * self.proj[i, j]
                    both = both - a[i] * self.gram[i, j]
                self.proj[j, k] = up / norm
                self.proj[k, j] = down / norm
                self.gram[j, k] = self.gram[k, j] = both / norm
            self.proj[k, k] = theta / square
            self.gram[k, k] = length / square
            self.inverse.append(1.0 / norm)
            self.corr.append(a)

    def state(self, shape):
        known = MATVECS - 1
        places = [(i, j) for i in range(known) for j in range(known)]
        rows = [self.proj[place] for place in places] + [self.gram[place] for place in places]
        return stack_rows(shape, rows)

    def basis(self, k, fields):
        done = []
        for step in range(k + 1):
            value = fields[step]
            for j in range(step):
                value = value - self.corr[step][j][:, :1] * done[j]
            done.append(value * self.inverse[step][:, :1])
        return done


def left_kernel(meta_ref, left_ref, left_high, left_low, left_tail, left_buf, sems):
    states = left_buf.shape[1]
    sigma, count, rows = meta_ref[SIGMA], meta_ref[COUNT], meta_ref[ROWS]
    stride = packed_rows(rows)

    def each(i, act):
        bond = (meta_ref[LIST + i] >> 2)
        at = i & (BUFFERS - 1)
        for p in range(states // TILE):
            part = pl.ds(p * TILE, TILE)

            @pl.when(rows > p * TILE)
            def _(part=part, p=p):
                act(
                    pltpu.make_async_copy(
                        left_ref.at[bond, sigma, part], left_buf.at[at, part], sems.at[p, at]
                    )
                )

    def start(i):
        @pl.when(i < count)
        def _():
            each(i, lambda copy: copy.start())

    for i in range(BUFFERS - 1):
        start(jnp.int32(i))

    def step(i, carry):
        at = i & (BUFFERS - 1)
        start(i + BUFFERS - 1)
        each(i, lambda copy: copy.wait())

        def chunk(t, inner):
            high, low = split(left_buf[at, pl.ds(pl.multiple_of(t * CHUNK, CHUNK), CHUNK), :])
            to = pl.ds(pl.multiple_of(i * stride + t * CHUNK, 16), CHUNK)
            left_high[to, :] = high[:, :SIDE]
            left_low[to, :] = low[:, :SIDE]
            left_tail[to, :] = jnp.concatenate([high[:, SIDE:], low[:, SIDE:]], axis=1)
            return inner

        lax.fori_loop(0, (rows + CHUNK - 1) // CHUNK, chunk, 0)
        return carry

    lax.fori_loop(0, count, step, 0)


def right_kernel(meta_ref, right_ref, far_ref, right_high, right_low, right_buf, sems):
    width, half = right_buf.shape[1], right_ref.shape[2]
    sigma, count = meta_ref[SIGMA], meta_ref[COUNT]
    core = lax.axis_index("rsec")
    thin = meta_ref[COLS] <= HALF

    def each(i, act):
        bond = (meta_ref[LIST + i] >> 2)
        for ref, place, sem in ((right_ref, core, 0), (far_ref, 1 - core, 1)):
            part = pl.ds(pl.multiple_of(place * half, half), half)

            @pl.when(jnp.logical_not(thin) | (place == 0))
            def _(ref=ref, part=part, sem=sem):
                act(
                    pltpu.make_async_copy(ref.at[bond, sigma], right_buf.at[i, part], sems.at[sem, i])
                )

    def start(i, carry):
        each(i, lambda copy: copy.start())
        return carry

    lax.fori_loop(0, count, start, 0)

    def step(i, carry):
        each(i, lambda copy: copy.wait())

        @pl.when(thin)
        def _():
            for first in range(0, HALF, CHUNK):
                high, low = split(right_buf[i, pl.ds(first, CHUNK), :])
                right_high[i, pl.ds(first, CHUNK), :] = high
                right_high[i, pl.ds(HALF + first, CHUNK), :] = low

        @pl.when(jnp.logical_not(thin))
        def _():
            for first in range(0, width, CHUNK):
                at = pl.ds(first, CHUNK)
                right_high[i, at, :], right_low[i, at, :] = split(right_buf[i, at, :])

        return carry

    lax.fori_loop(0, count, step, 0)


def packed_rows(rows):
    return ((rows + 15) // 16) * 16


def fold(value):
    return jnp.sum(value.reshape(CHUNK // 8, 8, value.shape[1]), axis=0)


def dots_kernel(k, cells, mpo_count, meta_ref, early_ref, *refs):
    refs, small_ref = list(refs[:-1]), refs[-1]
    totals = [(refs.pop(0), refs.pop(0)) for _ in range(k)]
    raw = [refs.pop(0) for _ in range(k + 1)]
    numbers = Scalars(totals, cells) if k else None
    core = lax.axis_index("rsec")
    zero = jnp.zeros(early_ref.shape[1:], F32)

    def step(i, carry):
        at = pl.ds(pl.multiple_of(i * CHUNK, CHUNK), CHUNK)
        blocks = [ref[at, :] for ref in refs]
        if len(blocks) == 2:
            near, away = blocks
            first, second = jnp.where(core == 0, near, away), jnp.where(core == 0, away, near)
            value = jnp.concatenate([first, second], axis=1)
        else:
            value = blocks[0]
        basis = numbers.basis(k - 1, [ref[at, :] for ref in raw[:k]]) if k else []
        return tuple(c + fold(value * b) for c, b in zip(carry, [raw[k][at, :], *basis]))

    live = (meta_ref[ROWS] + CHUNK - 1) // CHUNK
    late = lax.fori_loop(0, live, step, (zero,) * (1 + k))

    def whole(value):
        return jnp.sum(jnp.sum(value, axis=1, keepdims=True), axis=0, keepdims=True)

    share = 1.0 / mpo_count
    entries = [whole(early_ref[0]) * share, whole(late[0])]
    for j in range(2):
        entries.append(whole(early_ref[1 + j]) * share if j < k else None)
    for j in range(2):
        entries.append(whole(late[1 + j]) if j < k else None)
    for j in range(2):
        entries.append(whole(early_ref[1 + k + j]) * share if j < k else None)
    small_ref[...] = stack_rows(small_ref.shape, entries)


def matvec_kernel(k, cells, *refs):
    refs = list(refs)
    meta_ref = refs.pop(0)
    left_high, left_low, left_tail = [refs.pop(0) for _ in range(3)]
    right_high, right_low = refs.pop(0), refs.pop(0)
    size_ref = refs.pop(0) if k else None
    totals = [(refs.pop(0), refs.pop(0)) for _ in range(k)]
    raw = [[refs.pop(0) for _ in range(4)] for _ in range(max(k, 1))]
    images = [[refs.pop(0) for _ in range(4)] for _ in range(k)]
    precond = [refs.pop(0) for _ in range(4)] if k else []
    last = k + 1 == MATVECS
    halves = [refs.pop(0), refs.pop(0)] if last else []
    out_ref = None if last else refs.pop(0)
    early_ref = refs.pop(0)
    if k:
        new_refs = [refs.pop(0) for _ in range(4)]
    else:
        new_refs = raw[0]
        size_ref = refs.pop(0)
    if last:
        known_ref, state_ref, basis_out, images_out = [refs.pop(0) for _ in range(4)]
    high_ref, low_ref, tail_ref, mid_high, mid_low, order_ref = refs[:6]
    if last:
        out_ref, sems = refs[6:]
    states, width = out_ref.shape
    count, rows, cols = meta_ref[COUNT], meta_ref[ROWS], meta_ref[COLS]
    stride = packed_rows(rows)

    core = lax.axis_index("rsec")
    if not k:
        size_ref[2 * OWN], size_ref[2 * OWN + 1] = rows, cols
        size_ref[2 * SIB], size_ref[2 * SIB + 1] = meta_ref[SIB_ROWS], meta_ref[SIB_COLS]
        for slot in (FIRST_PAIR, SECOND_PAIR):
            note = raw[0][slot][pl.ds(states, NOTE), :HALF]
            size_ref[2 * slot] = jnp.max(note[:1]).astype(jnp.int32)
            size_ref[2 * slot + 1] = jnp.max(note[1:]).astype(jnp.int32)
    def list_bonds(narrow):
        def step(i, place):
            hit = (size_ref[2 * (meta_ref[LIST + i] & 3) + 1] <= HALF) == narrow

            @pl.when(hit)
            def _():
                order_ref[place] = i

            return place + hit.astype(jnp.int32)

        return step

    thin_sources = lax.fori_loop(0, count, list_bonds(True), jnp.int32(0))
    lax.fori_loop(0, count, list_bonds(False), thin_sources)
    if k:
        numbers = Scalars(totals, cells)
        theta = numbers.proj[k - 1, k - 1][:, :1]
    zero = jnp.zeros((8, width), F32)

    def prepare(slot, carry):
        def step(i, carry):
            at = pl.ds(pl.multiple_of(i * CHUNK, CHUNK), CHUNK)
            if k:
                basis = numbers.basis(k - 1, [r[slot][at, :] for r in raw])
                image = numbers.basis(k - 1, [r[slot][at, :] for r in images])
                value = (image[-1] - theta * basis[-1]) / jnp.maximum(
                    precond[slot][at, :] - theta, 1.0
                )
                new_refs[slot][at, :] = value
                if last and slot in (OWN, SIB):
                    for which, group in enumerate((basis, image)):
                        for j, block in enumerate(group):
                            block = jnp.where(core == 0, block[:, :HALF], block[:, HALF:])
                            known_ref[which, slot, j, at, :] = block
            else:
                basis, image = [], []
                value = raw[0][slot][at, :]
            high, low = split(value)
            high_ref[slot, at, :] = high
            low_ref[slot, at, :] = low
            terms = [value * value]
            if slot == OWN:
                terms += [value * b for b in basis] + [value * g for g in image]
            return tuple(c + fold(t) for c, t in zip(carry, terms))

        def dead(i, inner):
            at = pl.ds(pl.multiple_of(i * CHUNK, CHUNK), CHUNK)
            high_ref[slot, at, :] = jnp.zeros((CHUNK, width), BF16)
            low_ref[slot, at, :] = jnp.zeros((CHUNK, width), BF16)
            if last and slot in (OWN, SIB):
                for which in range(2):
                    for j in range(k):
                        known_ref[which, slot, j, at, :] = jnp.zeros((CHUNK, HALF), F32)
            return inner

        live = (size_ref[2 * slot] + CHUNK - 1) // CHUNK
        lax.fori_loop(live, states // CHUNK, dead, 0)
        return lax.fori_loop(0, live, step, carry)

    def dot(a, b):
        return jnp.dot(a, b, preferred_element_type=F32)

    def dot_nt(a, b):
        return lax.dot_general(a, b, (((1,), (1,)), ((), ())), preferred_element_type=F32)

    twice = functools.partial(jnp.concatenate, axis=0)

    def first_stage(slot, deep, narrow):
        begin, end = meta_ref[FIRST + slot], meta_ref[FIRST + 1 + slot]
        total = (end - begin) * stride
        top, rest = pl.ds(0, SIDE), pl.ds(SIDE, states - SIDE)
        if narrow:
            high_ref[slot, :, HALF:] = low_ref[slot, :, :HALF]
        if deep:
            tail = high_ref[slot, rest, :]
            tail_ref[...] = twice([tail, tail])

        def tile(first, size):
            at = pl.ds(pl.multiple_of(begin * stride + first, 16), size)
            high, low = left_high[at, :], left_low[at, :]
            mid = dot(high, high_ref[slot, top, :])
            if deep:
                mid = mid + dot(left_tail[at, :], tail_ref[...])
            if narrow:
                mid = mid[:, :HALF] + mid[:, HALF:] + dot(low, high_ref[slot, top, :HALF])
                mid_high[at, :] = jnp.concatenate(split(mid), axis=1)
            else:
                mid = mid + dot(low, high_ref[slot, top, :]) + dot(high, low_ref[slot, top, :])
                if deep:
                    mid = mid + dot(left_tail[at, : states - SIDE], low_ref[slot, rest, :])
                mid_high[at, :], mid_low[at, :] = split(mid)

        def step(t, carry):
            tile(t * PACK, PACK)
            return carry

        tiles = (total + PACK // 2 - 1) // PACK
        lax.fori_loop(0, tiles, step, 0)
        pl.when(total > tiles * PACK)(lambda: tile(tiles * PACK, PACK // 2))

    def both(test, action):
        pl.when(test)(lambda: action(True))
        pl.when(jnp.logical_not(test))(lambda: action(False))

    for slot in (OWN, SIB, FIRST_PAIR, SECOND_PAIR):
        if slot == OWN:
            own = prepare(slot, (zero,) * (1 + 2 * k))
        else:
            used = meta_ref[FIRST + 1 + slot] > meta_ref[FIRST + slot]
            pl.when(used | (slot == SIB))(lambda slot=slot: (prepare(slot, (zero,)), None)[1])

    def from_slot(slot, carry):
        both(
            size_ref[2 * slot] > SIDE,
            lambda deep: both(
                size_ref[2 * slot + 1] <= HALF, lambda narrow: first_stage(slot, deep, narrow)
            ),
        )
        return carry

    lax.fori_loop(0, 4, from_slot, 0)
    if last:
        sigma = meta_ref[SIGMA]
        outputs = [
            pltpu.make_async_copy(
                known_ref.at[which, slot],
                out.at[pl.ds(0, MATVECS - 1), sigma if slot == OWN else 1 - sigma],
                sems.at[which, slot],
            )
            for which, out in enumerate((basis_out, images_out))
            for slot in (OWN, SIB)
        ]
        for copy in outputs:
            copy.start()
        state_ref[...] = numbers.state(state_ref.shape)

    def clear(i, carry):
        at = pl.ds(pl.multiple_of(i * CHUNK, CHUNK), CHUNK)
        out_ref[at, :] = jnp.zeros((CHUNK, width), F32)
        return carry

    lax.fori_loop(0, states // CHUNK, clear, 0)
    zeros_at = mid_high.shape[0] - states
    for ref in (mid_high, mid_low):
        ref[pl.ds(zeros_at, states), :] = jnp.zeros((states, width), BF16)

    def second_stage(size, thin):
        to = pl.ds(0, size)

        def product(i, real, narrow):
            bond = order_ref[i]
            at = pl.ds(pl.multiple_of(jnp.where(real, bond * stride, zeros_at), 16), size)
            high = mid_high[at, :]
            lanes = pl.ds(0, HALF if narrow else width)
            right = right_high[bond, :, lanes]
            right_rest = None if thin else right_low[bond, :, lanes]
            if narrow:
                value = dot_nt(high, jnp.concatenate([right, right], axis=1))
                if not thin:
                    value = value + dot_nt(high[:, :HALF], right_rest)
            else:
                value = dot_nt(high, right)
                if not thin:
                    value = value + dot_nt(high, right_rest) + dot_nt(mid_low[at, :], right)
            if thin:
                value = value[:, :HALF] + value[:, HALF:]
                if not narrow:
                    value = value + dot_nt(mid_low[at, :], right[:HALF, :])
            return value

        def run(begin, end, narrow):
            def pair(p, carry):
                one = begin + 2 * p
                real = one + 1 < end
                two = jnp.where(real, one + 1, one)
                value = product(one, True, narrow) + product(two, real, narrow)
                if thin:
                    out_ref[to, :HALF] += value
                else:
                    out_ref[to, :] += value
                return carry

            lax.fori_loop(0, (end - begin + 1) // 2, pair, 0)

        run(0, thin_sources, True)
        run(thin_sources, count, False)

    for size in range(TILE, states + 1, TILE):
        pl.when((rows <= size) & (rows > size - TILE))(
            lambda size=size: both(cols <= HALF, functools.partial(second_stage, size))
        )

    def finish(i, carry):
        at = pl.ds(pl.multiple_of(i * CHUNK, CHUNK), CHUNK)
        mask = live_mask((CHUNK, width), i * CHUNK, rows, cols)
        value = jnp.where(mask, out_ref[at, :], 0.0)
        if last:
            halves[0][at, :] = jnp.where(core == 0, value[:, :HALF], value[:, HALF:])
            halves[1][at, :] = jnp.where(core == 0, value[:, HALF:], value[:, :HALF])
        else:
            out_ref[at, :] = value
        return carry

    lax.fori_loop(0, (rows + CHUNK - 1) // CHUNK, finish, 0)
    for index, entry in enumerate(own):
        early_ref[index] = entry
    if last:
        for copy in outputs:
            copy.wait()


def join_kernel(a_ref, b_ref, s0, s1, s2, s3, *refs):
    out_ref = refs[-1]
    states = a_ref.shape[0]
    total = (s0[...] + s1[...]) + (s2[...] + s3[...])
    out_ref[pl.ds(states, NOTE), :HALF] = total
    out_ref[pl.ds(states, NOTE), HALF:] = total

    def step(i, carry):
        at = pl.ds(pl.multiple_of(i * CHUNK, CHUNK), CHUNK)
        out_ref[at, :] = a_ref[at, :] + b_ref[at, :]
        return carry

    lax.fori_loop(0, states // CHUNK, step, 0)


def fill_kernel(cells, meta_ref, *refs):
    total, state_ref = refs[:2], refs[2]
    known_ref, raw_own, raw_sib, *parts = refs[3:9]
    basis_out, images_out, projected_ref, basis_buf, images_buf, sems = refs[-6:]
    last = MATVECS - 1
    sigma = meta_ref[SIGMA]
    numbers = Scalars([total], cells, state_ref[...])
    core = lax.axis_index("rsec")
    states, half = basis_buf.shape[1:]
    lanes = pl.ds(pl.multiple_of(core * half, half), half)
    inverse = numbers.inverse[0][:, :1]
    corr = [a[:, :1] for a in numbers.corr[0]]
    copies = []
    chunks = states // CHUNK
    for slot, raw, image, rows in (
        (OWN, raw_own, parts[:2], meta_ref[ROWS]),
        (SIB, raw_sib, parts[2:], meta_ref[SIB_ROWS]),
    ):

        def step(i, carry, slot=slot, raw=raw, image=image):
            at = pl.ds(pl.multiple_of(i * CHUNK, CHUNK), CHUNK)
            fields = (raw[at, lanes], sum(ref[at, :] for ref in image[1:]) + image[0][at, :])
            for which, buf in enumerate((basis_buf, images_buf)):
                value = fields[which]
                for j in range(last):
                    value = value - corr[j] * known_ref[which, slot, j, at, :]
                buf[slot, at, :] = value * inverse
            return carry

        def dead(i, carry, slot=slot):
            at = pl.ds(pl.multiple_of(i * CHUNK, CHUNK), CHUNK)
            for buf in (basis_buf, images_buf):
                buf[slot, at, :] = jnp.zeros((CHUNK, half), F32)
            return carry

        live = (rows + CHUNK - 1) // CHUNK
        lax.fori_loop(0, live, step, 0)
        lax.fori_loop(live, chunks, dead, 0)
        sector = sigma if slot == OWN else 1 - sigma
        for which, (buf, out) in enumerate(((basis_buf, basis_out), (images_buf, images_out))):
            copies.append(
                pltpu.make_async_copy(buf.at[slot], out.at[last, sector], sems.at[which, slot])
            )
            copies[-1].start()
    shape = projected_ref.shape
    row_ids = lax.broadcasted_iota(jnp.int32, shape, 0)
    col_ids = lax.broadcasted_iota(jnp.int32, shape, 1)
    value = jnp.zeros(shape, F32)
    for i in range(MATVECS):
        for j in range(MATVECS):
            value = jnp.where((row_ids == i) & (col_ids == j), numbers.proj[i, j][:, :1], value)
    projected_ref[...] = value
    for copy in copies:
        copy.wait()


def per_device(
    wavefunction, left_env, right_env, precond_diag, down_charge, bond_mask, left_size, right_size
):
    sectors, states, columns = wavefunction.shape
    bonds = left_env.shape[0]
    lsec_count = lax.axis_size("lsec")
    mpo_count = lax.axis_size("mpo")
    assert sectors == 2 and lax.axis_size("rsec") == 2
    width = 2 * columns
    cells = float(lsec_count * sectors * states * width)
    field = jax.ShapeDtypeStruct((states, width), F32)
    noted = jax.ShapeDtypeStruct((states + NOTE, width), F32)
    half_field = jax.ShapeDtypeStruct((states, columns), F32)
    small = jax.ShapeDtypeStruct((8, 128), F32)
    params = pltpu.CompilerParams(vmem_limit_bytes=18 * 2**20)

    swap = [(0, 1), (1, 0)]
    first_pairs = [(i, i ^ 1) for i in range(lsec_count) if i ^ 1 < lsec_count]
    second_pairs = [(i, j) for a in range(1, lsec_count - 1, 2) for i, j in ((a, a + 1), (a + 1, a))]
    anywhere = pl.BlockSpec(memory_space=pl.ANY)
    in_hbm = pl.BlockSpec(memory_space=pltpu.HBM)

    def hold(value):
        return pltpu.with_memory_space_constraint(value, pltpu.HBM)

    def neighbours(value):
        return lax.ppermute(value, "lsec", first_pairs), lax.ppermute(value, "lsec", second_pairs)

    wave_far = lax.ppermute(wavefunction, "rsec", swap)
    diag_far = lax.ppermute(precond_diag, "rsec", swap)
    mask_rows = bond_mask.T
    small_inputs = [down_charge, mask_rows, left_size, right_size]
    meta, wave_near = pl.pallas_call(
        functools.partial(prep_kernel, lsec_count, bonds),
        out_shape=(
            jax.ShapeDtypeStruct((LIST + bonds,), jnp.int32),
            jax.ShapeDtypeStruct(wavefunction.shape, F32),
        ),
        in_specs=[in_hbm] * 5,
        out_specs=(whole_smem(), whole_vmem()),
        scratch_shapes=[pltpu.SMEM(x.shape, jnp.int32) for x in small_inputs]
        + [pltpu.SemaphoreType.DMA((4,)), pltpu.SemaphoreType.DMA],
        compiler_params=params,
        cost_estimate=pl.CostEstimate(flops=0, transcendentals=0, bytes_accessed=10**6),
        name="prep",
    )(*[hold(x) for x in small_inputs], hold(wavefunction))
    right_send, _, _, _ = lax.optimization_barrier((right_env, wave_far, wave_near, diag_far))
    right_far = lax.ppermute(right_send, "rsec", swap)
    own, sib = pl.pallas_call(
        first_kernel,
        out_shape=(noted, field),
        in_specs=[whole_smem()] + [whole_vmem()] * 2,
        out_specs=(whole_vmem(),) * 2,
        compiler_params=params,
        name="first",
    )(meta, wave_near, wave_far)
    near_waves = neighbours(own)
    raw = [(own, sib, *near_waves)]
    diag_own, diag_sib = pl.pallas_call(
        diag_kernel,
        out_shape=(field,) * 2,
        in_specs=[whole_smem()] + [whole_vmem()] * 2,
        out_specs=(whole_vmem(),) * 2,
        compiler_params=params,
        name="diag",
    )(meta, hold(precond_diag), diag_far)

    near_diags = neighbours(diag_own)

    def mpo_pair(value):
        if mpo_count != 2:
            value = lax.psum(value, "mpo")
            return value, jnp.zeros_like(value)
        return value, lax.ppermute(value, "mpo", swap)

    def lsec_parts(part):
        if lsec_count != 4:
            zero = jnp.zeros_like(part)
            return lax.psum(part, "lsec"), zero, zero, zero
        return (part, *[lax.ppermute(part, "lsec", [(i, i ^ x) for i in range(4)]) for x in (1, 2, 3)])

    def join(value, part, after):
        return pl.pallas_call(
            join_kernel,
            out_shape=noted,
            in_specs=[whole_vmem()] * 6 + [anywhere] * len(after),
            out_specs=whole_vmem(),
            compiler_params=params,
            name="join",
        )(*mpo_pair(value), *lsec_parts(part), *after)

    most = bonds - bonds // 5 if bonds % 5 == 0 else bonds
    packed = most * states + PACK
    lefts = pl.pallas_call(
        left_kernel,
        out_shape=(
            pltpu.VMEM((packed, SIDE), BF16),
            pltpu.VMEM((packed, SIDE), BF16),
            pltpu.VMEM((packed, 2 * (states - SIDE)), BF16),
        ),
        in_specs=[whole_smem(), anywhere],
        out_specs=(whole_vmem(),) * 3,
        scratch_shapes=[
            pltpu.VMEM((BUFFERS, states, states), F32),
            pltpu.SemaphoreType.DMA((states // TILE, BUFFERS)),
        ],
        compiler_params=params,
        cost_estimate=pl.CostEstimate(flops=0, transcendentals=0, bytes_accessed=bonds * states * states * 4),
        name="left",
    )(meta, hold(left_env))
    rights = pl.pallas_call(
        right_kernel,
        out_shape=(pltpu.VMEM((most, width, width), BF16),) * 2,
        in_specs=[whole_smem(), anywhere, anywhere],
        out_specs=(whole_vmem(),) * 2,
        scratch_shapes=[
            pltpu.VMEM((most, width, width), F32),
            pltpu.SemaphoreType.DMA((2, most)),
        ],
        compiler_params=params,
        cost_estimate=pl.CostEstimate(flops=0, transcendentals=0, bytes_accessed=bonds * width * width * 8),
        name="right",
    )(meta, hold(right_env), right_far)

    def dots(k, early, values):
        operands = [early, *totals, *[group[0] for group in raw], *values]
        return pl.pallas_call(
            functools.partial(dots_kernel, k, cells, mpo_count),
            out_shape=small,
            in_specs=[whole_smem()] + [whole_vmem()] * len(operands),
            out_specs=whole_vmem(),
            compiler_params=params,
            cost_estimate=pl.CostEstimate(
                flops=4 * states * width, transcendentals=0, bytes_accessed=4 * states * width
            ),
            name=f"dots{k}",
        )(meta, *operands)

    out = jax.ShapeDtypeStruct((MATVECS, sectors, states, columns), F32)
    known = jax.ShapeDtypeStruct((2, sectors, MATVECS - 1, states, columns), F32)

    def matvec(k, rights, inputs):
        last = k + 1 == MATVECS
        out_shape = [half_field] * 2 if last else [field]
        out_shape += [jax.ShapeDtypeStruct((1 + 2 * k, 8, width), F32)] + [field] * (4 if k else 0)
        out_specs = [whole_vmem()] * len(out_shape)
        scratch = [
            pltpu.VMEM((4, states, width), BF16),
            pltpu.VMEM((4, states, width), BF16),
            pltpu.VMEM((2 * (states - SIDE), width), BF16),
            pltpu.VMEM((packed + states, width), BF16),
            pltpu.VMEM((packed + states, width), BF16),
            pltpu.SMEM((bonds,), jnp.int32),
        ]
        right_specs = [whole_vmem()] * 2 + ([whole_smem()] if k else [])
        if k == 0:
            out_shape += [jax.ShapeDtypeStruct((8,), jnp.int32)]
            out_specs += [whole_smem()]
        if last:
            out_shape += [known, small, out, out]
            out_specs += [whole_vmem(), whole_vmem(), anywhere, anywhere]
            scratch += [pltpu.VMEM((states, width), F32), pltpu.SemaphoreType.DMA((2, 2))]
        return pl.pallas_call(
            functools.partial(matvec_kernel, k, cells),
            out_shape=tuple(out_shape),
            in_specs=[whole_smem()] + [whole_vmem()] * 3 + right_specs + [whole_vmem()] * len(inputs),
            out_specs=tuple(out_specs),
            scratch_shapes=scratch,
            compiler_params=params,
            cost_estimate=pl.CostEstimate(
                flops=2 * 3 * bonds * states * width * (states + width),
                transcendentals=0,
                bytes_accessed=bonds * states * states,
            ),
            name=f"matvec{k}",
        )(meta, *lefts, *rights, *inputs)

    def flatten(groups):
        return [x for group in groups for x in group]

    totals = []
    images = []
    for k in range(MATVECS - 1):
        if k == 0:
            value, early, sizes = matvec(0, rights, list(raw[0]))
            rights = [*rights, sizes]
            precond = (diag_own, diag_sib, *near_diags)
        else:
            value, early, *fresh = matvec(k, rights, [*totals, *flatten(raw), *flatten(images), *precond])
            raw.append(tuple(fresh))
        part = dots(k, early, [value])
        value = join(value, part, [] if k else near_diags)
        beside = lax.ppermute(value, "rsec", swap)
        images.append((value, beside, *neighbours(value)))
        totals += mpo_pair(value[states:, :HALF] + beside[states:, :HALF])

    inputs = [*totals, *flatten(raw), *flatten(images), *precond]
    near, away, early, own, sib, _, _, known_blocks, state, *outs = matvec(MATVECS - 1, rights, inputs)
    raw.append((own, sib))
    part = dots(MATVECS - 1, early, [near, away])
    away, far_away = mpo_pair(away)
    sib_half = lax.ppermute(away + far_away, "rsec", swap)
    own_half = mpo_pair(near)
    one, two, three, four = lsec_parts(part)
    part = (one + two) + (three + four)
    total = mpo_pair(part + lax.ppermute(part, "rsec", swap))
    operands = [*total, state, known_blocks, own, sib, *own_half, sib_half]
    return pl.pallas_call(
        functools.partial(fill_kernel, cells),
        out_shape=(out, out, jax.ShapeDtypeStruct((MATVECS, MATVECS), F32)),
        in_specs=[whole_smem()] + [whole_vmem()] * len(operands) + [anywhere] * 2,
        out_specs=(anywhere, anywhere, whole_vmem()),
        scratch_shapes=[
            pltpu.VMEM((sectors, states, columns), F32),
            pltpu.VMEM((sectors, states, columns), F32),
            pltpu.SemaphoreType.DMA((2, 2)),
        ],
        input_output_aliases={1 + len(operands): 0, 2 + len(operands): 1},
        compiler_params=params,
        name="fill",
    )(meta, *operands, *outs)


def solution(mesh):
    placed = (
        P(("grp", "lsec"), None, "rsec"),
        P("mpo", ("grp", "lsec"), None, None),
        P("mpo", ("grp", "lsec"), "rsec", None),
        P(("grp", "lsec"), None, "rsec"),
        P("grp"),
        P("mpo", ("grp", "lsec")),
        P(("grp", "lsec")),
        P(("grp", "lsec")),
    )
    return jax.shard_map(
        per_device,
        mesh=mesh,
        in_specs=placed,
        out_specs=(
            P(None, ("grp", "lsec"), None, "rsec"),
            P(None, ("grp", "lsec"), None, "rsec"),
            P("grp", None),
        ),
        check_vma=False,
    )
```

```python
import functools

import jax
import jax.numpy as jnp
from jax import lax
from jax.experimental import pallas as pl
from jax.experimental.pallas import tpu as pltpu
from jax.sharding import PartitionSpec as P

EPSILON = 1e-06
MATVECS = 3
F32 = jnp.float32
BF16 = jnp.bfloat16
SIGMA, COUNT, ROWS, COLS, FIRST, SIB_ROWS, SIB_COLS, LIST = 0, 1, 2, 3, 4, 9, 10, 16
OWN, SIB, FIRST_PAIR, SECOND_PAIR = 0, 1, 2, 3
CHUNK = 64
TILE = 128
SIDE = 256
HALF = 128
NOTE = 8
PACK = 256
BUFFERS = 8


def whole_vmem():
    return pl.BlockSpec(memory_space=pltpu.VMEM)


def whole_smem():
    return pl.BlockSpec(memory_space=pltpu.SMEM)


def split(value):
    high = value.astype(BF16)
    return high, (value - high.astype(F32)).astype(BF16)


def orientation(down_ref, place):
    def step(i, flips):
        straight = (down_ref[2 * i] == down_ref[2 * i - 2]) | (
            down_ref[2 * i + 1] == down_ref[2 * i - 1]
        )
        return jnp.where(straight, flips, 1 - flips)

    return lax.fori_loop(1, place + 1, step, jnp.int32(0))


def live_mask(shape, row0, rows, cols):
    row_ids = row0 + lax.broadcasted_iota(jnp.int32, shape, 0)
    col_ids = lax.broadcasted_iota(jnp.int32, shape, 1)
    return (row_ids < rows) & (col_ids < cols)


def read_small(pairs, sems):
    copies = [pltpu.make_async_copy(*pair, sems.at[i]) for i, pair in enumerate(pairs)]
    for copy in copies:
        copy.start()
    for copy in copies:
        copy.wait()


def first_kernel(meta_ref, wave_ref, wave_far, own_ref, sib_ref):
    states, half = wave_ref.shape[1:]
    sigma, core = meta_ref[SIGMA], lax.axis_index("rsec")
    for out_ref, slot, rows, cols in (
        (own_ref, sigma, meta_ref[ROWS], meta_ref[COLS]),
        (sib_ref, 1 - sigma, meta_ref[SIB_ROWS], meta_ref[SIB_COLS]),
    ):

        def fill(i, carry, out_ref=out_ref, slot=slot, rows=rows, cols=cols):
            at = pl.ds(pl.multiple_of(i * CHUNK, CHUNK), CHUNK)
            for place, wave in ((core, wave_ref), (1 - core, wave_far)):
                lanes = pl.ds(pl.multiple_of(place * half, half), half)
                mask = live_mask((CHUNK, half), i * CHUNK, rows, cols - place * half)
                out_ref[at, lanes] = jnp.where(mask, wave[slot, at, :], 0.0)
            return carry

        lax.fori_loop(0, states // CHUNK, fill, 0)
    note = (NOTE, own_ref.shape[1])
    row_ids = lax.broadcasted_iota(jnp.int32, note, 0)
    own_ref[pl.ds(states, NOTE), :] = jnp.where(
        row_ids == 0, meta_ref[ROWS], meta_ref[COLS]
    ).astype(F32)


def prep_kernel(lsec_count, bonds, down_in, mask_in, left_in, right_in, wave_in, meta_ref, wave_ref,
                down_ref, mask_ref, left_size_ref, right_size_ref, sems, wave_sem):
    wave_copy = pltpu.make_async_copy(wave_in, wave_ref, wave_sem)
    wave_copy.start()
    read_small(
        ((down_in, down_ref), (mask_in, mask_ref), (left_in, left_size_ref), (right_in, right_size_ref)),
        sems,
    )
    place = lax.axis_index("lsec")
    core = lax.axis_index("rsec")
    first_kind = lax.rem(lax.axis_index("mpo") * bonds, 5)
    sigma = core ^ orientation(down_ref, place)
    own_down = down_ref[2 * place + sigma]
    sib_down = down_ref[2 * place + 1 - sigma]
    before = jnp.maximum(place - 1, 0)
    after = jnp.minimum(place + 1, lsec_count - 1)
    prev_down = down_ref[2 * before + (core ^ orientation(down_ref, before))]
    next_down = down_ref[2 * after + (core ^ orientation(down_ref, after))]
    has_prev = (place > 0) & (prev_down == own_down)
    has_next = (place < lsec_count - 1) & (next_down == own_down)
    odd = lax.rem(place, 2)
    has_lower = sib_down == own_down - 1
    has_upper = sib_down == own_down + 1

    def gather(slot, count):
        meta_ref[FIRST + slot] = count

        def step(bond, carry):
            count, kind = carry
            if slot == OWN:
                there = kind == 0
            elif slot == SIB:
                there = ((kind == 3) & has_lower) | ((kind == 4) & has_upper)
            else:
                lower = odd if slot == FIRST_PAIR else 1 - odd
                there = ((kind == 1) & has_prev & (lower == 1)) | (
                    (kind == 2) & has_next & (lower == 0)
                )
            there = there & (mask_ref[sigma, bond] > 0)

            @pl.when(there)
            def _():
                meta_ref[LIST + count] = bond * 4 + slot

            return count + there.astype(jnp.int32), jnp.where(kind == 4, 0, kind + 1)

        return lax.fori_loop(0, bonds, step, (count, first_kind))[0]

    count = jnp.int32(0)
    for slot in (OWN, SIB, FIRST_PAIR, SECOND_PAIR):
        count = gather(slot, count)
    meta_ref[FIRST + 4] = count
    rows, cols = left_size_ref[sigma], right_size_ref[sigma]
    meta_ref[SIGMA] = sigma
    meta_ref[COUNT] = count
    meta_ref[ROWS] = rows
    meta_ref[COLS] = cols
    meta_ref[SIB_ROWS] = left_size_ref[1 - sigma]
    meta_ref[SIB_COLS] = right_size_ref[1 - sigma]
    wave_copy.wait()


def diag_kernel(meta_ref, diag_ref, diag_far, diag_own, diag_sib):
    states, width = diag_own.shape
    half = width // 2
    sigma, core = meta_ref[SIGMA], lax.axis_index("rsec")
    near = pl.ds(pl.multiple_of(core * half, half), half)
    away = pl.ds(pl.multiple_of((1 - core) * half, half), half)
    for out_ref, slot in ((diag_own, sigma), (diag_sib, 1 - sigma)):

        def fill(i, carry, out_ref=out_ref, slot=slot):
            at = pl.ds(pl.multiple_of(i * CHUNK, CHUNK), CHUNK)
            out_ref[at, near] = diag_ref[slot, at, :]
            out_ref[at, away] = diag_far[slot, at, :]
            return carry

        lax.fori_loop(0, states // CHUNK, fill, 0)


def row(value, index):
    return value[index : index + 1, :]


def stack_rows(shape, rows):
    row_ids = lax.broadcasted_iota(jnp.int32, shape, 0)
    value = jnp.zeros(shape, F32)
    for index, entry in enumerate(rows):
        if entry is not None:
            value = jnp.where(row_ids == index, entry, value)
    return value


class Scalars:
    def __init__(self, totals, cells, state=None):
        self.proj = {}
        self.gram = {}
        self.inverse = []
        self.corr = []
        known = 0
        if state is not None:
            known = MATVECS - 1
            places = [(i, j) for i in range(known) for j in range(known)]
            for index, place in enumerate(places):
                self.proj[place] = row(state, index)
                self.gram[place] = row(state, len(places) + index)
        for k, total in enumerate(totals, known):
            value = (total[0][...] + total[1][...]) / cells
            size, inner = row(value, 0), row(value, 1)
            a = [row(value, 2 + j) for j in range(k)]
            e = [row(value, 4 + j) for j in range(k)]
            f = [row(value, 6 + j) for j in range(k)]
            length = size
            theta = inner
            for j in range(k):
                length = length - 2.0 * a[j] * a[j]
                theta = theta - a[j] * e[j] - a[j] * f[j]
            for i in range(k):
                for j in range(k):
                    length = length + a[i] * a[j] * self.gram[i, j]
                    theta = theta + a[i] * a[j] * self.proj[i, j]
            length = jnp.maximum(length, 0.0)
            square = length + EPSILON
            norm = jnp.sqrt(square)
            for j in range(k):
                up, down, both = e[j], f[j], a[j]
                for i in range(k):
                    up = up - a[i] * self.proj[j, i]
                    down = down - a[i] * self.proj[i, j]
                    both = both - a[i] * self.gram[i, j]
                self.proj[j, k] = up / norm
                self.proj[k, j] = down / norm
                self.gram[j, k] = self.gram[k, j] = both / norm
            self.proj[k, k] = theta / square
            self.gram[k, k] = length / square
            self.inverse.append(1.0 / norm)
            self.corr.append(a)

    def state(self, shape):
        known = MATVECS - 1
        places = [(i, j) for i in range(known) for j in range(known)]
        rows = [self.proj[place] for place in places] + [self.gram[place] for place in places]
        return stack_rows(shape, rows)

    def basis(self, k, fields):
        done = []
        for step in range(k + 1):
            value = fields[step]
            for j in range(step):
                value = value - self.corr[step][j][:, :1] * done[j]
            done.append(value * self.inverse[step][:, :1])
        return done


def left_kernel(meta_ref, left_ref, left_high, left_low, left_tail, left_buf, sems):
    states = left_buf.shape[1]
    sigma, count, rows = meta_ref[SIGMA], meta_ref[COUNT], meta_ref[ROWS]
    stride = packed_rows(rows)

    def each(i, act):
        bond = (meta_ref[LIST + i] >> 2)
        at = i & (BUFFERS - 1)
        for p in range(states // TILE):
            part = pl.ds(p * TILE, TILE)

            @pl.when(rows > p * TILE)
            def _(part=part, p=p):
                act(
                    pltpu.make_async_copy(
                        left_ref.at[bond, sigma, part], left_buf.at[at, part], sems.at[p, at]
                    )
                )

    def start(i):
        @pl.when(i < count)
        def _():
            each(i, lambda copy: copy.start())

    for i in range(BUFFERS - 1):
        start(jnp.int32(i))

    def step(i, carry):
        at = i & (BUFFERS - 1)
        start(i + BUFFERS - 1)
        each(i, lambda copy: copy.wait())

        def chunk(t, inner):
            high, low = split(left_buf[at, pl.ds(pl.multiple_of(t * CHUNK, CHUNK), CHUNK), :])
            to = pl.ds(pl.multiple_of(i * stride + t * CHUNK, 16), CHUNK)
            left_high[to, :] = high[:, :SIDE]
            left_low[to, :] = low[:, :SIDE]
            left_tail[to, :] = jnp.concatenate([high[:, SIDE:], low[:, SIDE:]], axis=1)
            return inner

        lax.fori_loop(0, (rows + CHUNK - 1) // CHUNK, chunk, 0)
        return carry

    lax.fori_loop(0, count, step, 0)


def right_kernel(meta_ref, right_ref, far_ref, right_high, right_low, right_buf, sems):
    width, half = right_buf.shape[1], right_ref.shape[2]
    sigma, count = meta_ref[SIGMA], meta_ref[COUNT]
    core = lax.axis_index("rsec")
    thin = meta_ref[COLS] <= HALF

    def each(i, act):
        bond = (meta_ref[LIST + i] >> 2)
        for ref, place, sem in ((right_ref, core, 0), (far_ref, 1 - core, 1)):
            part = pl.ds(pl.multiple_of(place * half, half), half)

            @pl.when(jnp.logical_not(thin) | (place == 0))
            def _(ref=ref, part=part, sem=sem):
                act(
                    pltpu.make_async_copy(ref.at[bond, sigma], right_buf.at[i, part], sems.at[sem, i])
                )

    def start(i, carry):
        each(i, lambda copy: copy.start())
        return carry

    lax.fori_loop(0, count, start, 0)

    def step(i, carry):
        each(i, lambda copy: copy.wait())

        @pl.when(thin)
        def _():
            for first in range(0, HALF, CHUNK):
                high, low = split(right_buf[i, pl.ds(first, CHUNK), :])
                right_high[i, pl.ds(first, CHUNK), :] = high
                right_high[i, pl.ds(HALF + first, CHUNK), :] = low

        @pl.when(jnp.logical_not(thin))
        def _():
            for first in range(0, width, CHUNK):
                at = pl.ds(first, CHUNK)
                right_high[i, at, :], right_low[i, at, :] = split(right_buf[i, at, :])

        return carry

    lax.fori_loop(0, count, step, 0)


def packed_rows(rows):
    return ((rows + 15) // 16) * 16


def fold(value):
    return jnp.sum(value.reshape(CHUNK // 8, 8, value.shape[1]), axis=0)


def dots_kernel(k, cells, mpo_count, meta_ref, early_ref, *refs):
    refs, small_ref = list(refs[:-1]), refs[-1]
    totals = [(refs.pop(0), refs.pop(0)) for _ in range(k)]
    raw = [refs.pop(0) for _ in range(k + 1)]
    numbers = Scalars(totals, cells) if k else None
    core = lax.axis_index("rsec")
    zero = jnp.zeros(early_ref.shape[1:], F32)

    def step(i, carry):
        at = pl.ds(pl.multiple_of(i * CHUNK, CHUNK), CHUNK)
        blocks = [ref[at, :] for ref in refs]
        if len(blocks) == 2:
            near, away = blocks
            first, second = jnp.where(core == 0, near, away), jnp.where(core == 0, away, near)
            value = jnp.concatenate([first, second], axis=1)
        else:
            value = blocks[0]
        basis = numbers.basis(k - 1, [ref[at, :] for ref in raw[:k]]) if k else []
        return tuple(c + fold(value * b) for c, b in zip(carry, [raw[k][at, :], *basis]))

    live = (meta_ref[ROWS] + CHUNK - 1) // CHUNK
    late = lax.fori_loop(0, live, step, (zero,) * (1 + k))

    def whole(value):
        return jnp.sum(jnp.sum(value, axis=1, keepdims=True), axis=0, keepdims=True)

    share = 1.0 / mpo_count
    entries = [whole(early_ref[0]) * share, whole(late[0])]
    for j in range(2):
        entries.append(whole(early_ref[1 + j]) * share if j < k else None)
    for j in range(2):
        entries.append(whole(late[1 + j]) if j < k else None)
    for j in range(2):
        entries.append(whole(early_ref[1 + k + j]) * share if j < k else None)
    small_ref[...] = stack_rows(small_ref.shape, entries)


def matvec_kernel(k, cells, near, *refs):
    refs = list(refs)
    slots = (OWN, SIB) if near else (FIRST_PAIR, SECOND_PAIR)
    base = slots[0]
    last = k + 1 == MATVECS
    meta_ref = refs.pop(0)
    left_high, left_low, left_tail = [refs.pop(0) for _ in range(3)]
    right_high, right_low = refs.pop(0), refs.pop(0)
    size_ref = refs.pop(0) if k and not near else None
    totals = [(refs.pop(0), refs.pop(0)) for _ in range(k)]
    raw = [{slot: refs.pop(0) for slot in slots} for _ in range(max(k, 1))]
    images = [{slot: refs.pop(0) for slot in slots} for _ in range(k)]
    precond = {slot: refs.pop(0) for slot in slots} if k else {}
    partial_ref = None if near else refs.pop(0)
    halves = [refs.pop(0), refs.pop(0)] if last and not near else []
    out_ref = None if halves else refs.pop(0)
    early_ref = refs.pop(0) if near else None
    new_refs = {slot: refs.pop(0) for slot in slots} if k else raw[0]
    if not k and not near:
        size_ref = refs.pop(0)
    if last and near:
        known_ref, state_ref, basis_out, images_out = [refs.pop(0) for _ in range(4)]
    high_ref, low_ref, tail_ref, mid_high, mid_low, order_ref = refs[:6]
    if near:
        size_ref = refs[6]
        sems = refs[7] if last else None
    elif last:
        out_ref = refs[6]
    states, width = out_ref.shape
    rows, cols = meta_ref[ROWS], meta_ref[COLS]
    first_bond, end_bond = meta_ref[FIRST + base], meta_ref[FIRST + base + 2]
    count = end_bond - first_bond
    stride = packed_rows(rows)

    core = lax.axis_index("rsec")
    if near:
        size_ref[2 * OWN], size_ref[2 * OWN + 1] = rows, cols
        size_ref[2 * SIB], size_ref[2 * SIB + 1] = meta_ref[SIB_ROWS], meta_ref[SIB_COLS]
    elif not k:
        for slot in slots:
            note = raw[0][slot][pl.ds(states, NOTE), :HALF]
            size_ref[2 * slot] = jnp.max(note[:1]).astype(jnp.int32)
            size_ref[2 * slot + 1] = jnp.max(note[1:]).astype(jnp.int32)
    def list_bonds(narrow):
        def step(i, place):
            hit = (size_ref[2 * (meta_ref[LIST + i] & 3) + 1] <= HALF) == narrow

            @pl.when(hit)
            def _():
                order_ref[place] = i

            return place + hit.astype(jnp.int32)

        return step

    thin_sources = lax.fori_loop(first_bond, end_bond, list_bonds(True), jnp.int32(0))
    lax.fori_loop(first_bond, end_bond, list_bonds(False), thin_sources)
    if k:
        numbers = Scalars(totals, cells)
        theta = numbers.proj[k - 1, k - 1][:, :1]
    zero = jnp.zeros((8, width), F32)

    def prepare(slot, carry):
        def step(i, carry):
            at = pl.ds(pl.multiple_of(i * CHUNK, CHUNK), CHUNK)
            if k:
                basis = numbers.basis(k - 1, [r[slot][at, :] for r in raw])
                image = numbers.basis(k - 1, [r[slot][at, :] for r in images])
                value = (image[-1] - theta * basis[-1]) / jnp.maximum(
                    precond[slot][at, :] - theta, 1.0
                )
                new_refs[slot][at, :] = value
                if last and near:
                    for which, group in enumerate((basis, image)):
                        for j, block in enumerate(group):
                            block = jnp.where(core == 0, block[:, :HALF], block[:, HALF:])
                            known_ref[which, slot, j, at, :] = block
            else:
                basis, image = [], []
                value = raw[0][slot][at, :]
            high, low = split(value)
            high_ref[slot - base, at, :] = high
            low_ref[slot - base, at, :] = low
            terms = [value * value]
            if slot == OWN:
                terms += [value * b for b in basis] + [value * g for g in image]
            return tuple(c + fold(t) for c, t in zip(carry, terms))

        def dead(i, inner):
            at = pl.ds(pl.multiple_of(i * CHUNK, CHUNK), CHUNK)
            high_ref[slot - base, at, :] = jnp.zeros((CHUNK, width), BF16)
            low_ref[slot - base, at, :] = jnp.zeros((CHUNK, width), BF16)
            if last and near:
                for which in range(2):
                    for j in range(k):
                        known_ref[which, slot, j, at, :] = jnp.zeros((CHUNK, HALF), F32)
            return inner

        live = (size_ref[2 * slot] + CHUNK - 1) // CHUNK
        lax.fori_loop(live, states // CHUNK, dead, 0)
        return lax.fori_loop(0, live, step, carry)

    def dot(a, b):
        return jnp.dot(a, b, preferred_element_type=F32)

    def dot_nt(a, b):
        return lax.dot_general(a, b, (((1,), (1,)), ((), ())), preferred_element_type=F32)

    twice = functools.partial(jnp.concatenate, axis=0)

    def first_stage(slot, deep, narrow):
        begin, end = meta_ref[FIRST + slot], meta_ref[FIRST + 1 + slot]
        at_slot = slot - base
        top, rest = pl.ds(0, SIDE), pl.ds(SIDE, states - SIDE)
        if narrow:
            high_ref[at_slot, :, HALF:] = low_ref[at_slot, :, :HALF]
        if deep:
            tail = high_ref[at_slot, rest, :]
            tail_ref[...] = twice([tail, tail])

        def step(t, carry):
            at = pl.ds(pl.multiple_of(begin * stride + t * PACK, 16), PACK)
            high, low = left_high[at, :], left_low[at, :]
            mid = dot(high, high_ref[at_slot, top, :])
            if deep:
                mid = mid + dot(left_tail[at, :], tail_ref[...])
            if narrow:
                mid = mid[:, :HALF] + mid[:, HALF:] + dot(low, high_ref[at_slot, top, :HALF])
                mid_high[at, :] = jnp.concatenate(split(mid), axis=1)
            else:
                mid = mid + dot(low, high_ref[at_slot, top, :]) + dot(high, low_ref[at_slot, top, :])
                if deep:
                    mid = mid + dot(left_tail[at, : states - SIDE], low_ref[at_slot, rest, :])
                mid_high[at, :], mid_low[at, :] = split(mid)
            return carry

        lax.fori_loop(0, ((end - begin) * stride + PACK - 1) // PACK, step, 0)

    def both(test, action):
        pl.when(test)(lambda: action(True))
        pl.when(jnp.logical_not(test))(lambda: action(False))

    if near:
        own = prepare(OWN, (zero,) * (1 + 2 * k))
        prepare(SIB, (zero,))
    else:
        for slot in slots:
            used = meta_ref[FIRST + 1 + slot] > meta_ref[FIRST + slot]
            pl.when(used)(lambda slot=slot: (prepare(slot, (zero,)), None)[1])

    def from_slot(slot, carry):
        both(
            size_ref[2 * slot] > SIDE,
            lambda deep: both(
                size_ref[2 * slot + 1] <= HALF, lambda narrow: first_stage(slot, deep, narrow)
            ),
        )
        return carry

    lax.fori_loop(base, base + 2, from_slot, 0)
    if last and near:
        sigma = meta_ref[SIGMA]
        outputs = [
            pltpu.make_async_copy(
                known_ref.at[which, slot],
                out.at[pl.ds(0, MATVECS - 1), sigma if slot == OWN else 1 - sigma],
                sems.at[which, slot],
            )
            for which, out in enumerate((basis_out, images_out))
            for slot in (OWN, SIB)
        ]
        for copy in outputs:
            copy.start()
        state_ref[...] = numbers.state(state_ref.shape)

    def clear(i, carry):
        at = pl.ds(pl.multiple_of(i * CHUNK, CHUNK), CHUNK)
        out_ref[at, :] = jnp.zeros((CHUNK, width), F32) if near else partial_ref[at, :]
        return carry

    lax.fori_loop(0, states // CHUNK, clear, 0)
    zeros_at = mid_high.shape[0] - states
    for ref in (mid_high, mid_low):
        ref[pl.ds(zeros_at, states), :] = jnp.zeros((states, width), BF16)

    def second_stage(size, thin):
        to = pl.ds(0, size)

        def product(i, real, narrow):
            bond = order_ref[i]
            at = pl.ds(pl.multiple_of(jnp.where(real, bond * stride, zeros_at), 16), size)
            high = mid_high[at, :]
            lanes = pl.ds(0, HALF if narrow else width)
            right = right_high[bond, :, lanes]
            right_rest = None if thin else right_low[bond, :, lanes]
            if narrow:
                value = dot_nt(high, jnp.concatenate([right, right], axis=1))
                if not thin:
                    value = value + dot_nt(high[:, :HALF], right_rest)
            else:
                value = dot_nt(high, right)
                if not thin:
                    value = value + dot_nt(high, right_rest) + dot_nt(mid_low[at, :], right)
            if thin:
                value = value[:, :HALF] + value[:, HALF:]
                if not narrow:
                    value = value + dot_nt(mid_low[at, :], right[:HALF, :])
            return value

        def run(begin, end, narrow):
            def pair(p, carry):
                one = begin + 2 * p
                real = one + 1 < end
                two = jnp.where(real, one + 1, one)
                value = product(one, True, narrow) + product(two, real, narrow)
                if thin:
                    out_ref[to, :HALF] += value
                else:
                    out_ref[to, :] += value
                return carry

            lax.fori_loop(0, (end - begin + 1) // 2, pair, 0)

        run(0, thin_sources, True)
        run(thin_sources, count, False)

    for size in range(TILE, states + 1, TILE):
        pl.when((rows <= size) & (rows > size - TILE))(
            lambda size=size: both(cols <= HALF, functools.partial(second_stage, size))
        )

    if near:
        for index, entry in enumerate(own):
            early_ref[index] = entry
        if last:
            for copy in outputs:
                copy.wait()
        return

    def finish(i, carry):
        at = pl.ds(pl.multiple_of(i * CHUNK, CHUNK), CHUNK)
        mask = live_mask((CHUNK, width), i * CHUNK, rows, cols)
        value = jnp.where(mask, out_ref[at, :], 0.0)
        if last:
            halves[0][at, :] = jnp.where(core == 0, value[:, :HALF], value[:, HALF:])
            halves[1][at, :] = jnp.where(core == 0, value[:, HALF:], value[:, :HALF])
        else:
            out_ref[at, :] = value
        return carry

    lax.fori_loop(0, (rows + CHUNK - 1) // CHUNK, finish, 0)


def join_kernel(a_ref, b_ref, s0, s1, s2, s3, *refs):
    out_ref = refs[-1]
    states = a_ref.shape[0]
    total = (s0[...] + s1[...]) + (s2[...] + s3[...])
    out_ref[pl.ds(states, NOTE), :HALF] = total
    out_ref[pl.ds(states, NOTE), HALF:] = total

    def step(i, carry):
        at = pl.ds(pl.multiple_of(i * CHUNK, CHUNK), CHUNK)
        out_ref[at, :] = a_ref[at, :] + b_ref[at, :]
        return carry

    lax.fori_loop(0, states // CHUNK, step, 0)


def fill_kernel(cells, meta_ref, *refs):
    total, state_ref = refs[:2], refs[2]
    known_ref, raw_own, raw_sib, *parts = refs[3:9]
    basis_out, images_out, projected_ref, basis_buf, images_buf, sems = refs[-6:]
    last = MATVECS - 1
    sigma = meta_ref[SIGMA]
    numbers = Scalars([total], cells, state_ref[...])
    core = lax.axis_index("rsec")
    states, half = basis_buf.shape[1:]
    lanes = pl.ds(pl.multiple_of(core * half, half), half)
    inverse = numbers.inverse[0][:, :1]
    corr = [a[:, :1] for a in numbers.corr[0]]
    copies = []
    chunks = states // CHUNK
    for slot, raw, image, rows in (
        (OWN, raw_own, parts[:2], meta_ref[ROWS]),
        (SIB, raw_sib, parts[2:], meta_ref[SIB_ROWS]),
    ):

        def step(i, carry, slot=slot, raw=raw, image=image):
            at = pl.ds(pl.multiple_of(i * CHUNK, CHUNK), CHUNK)
            fields = (raw[at, lanes], sum(ref[at, :] for ref in image[1:]) + image[0][at, :])
            for which, buf in enumerate((basis_buf, images_buf)):
                value = fields[which]
                for j in range(last):
                    value = value - corr[j] * known_ref[which, slot, j, at, :]
                buf[slot, at, :] = value * inverse
            return carry

        def dead(i, carry, slot=slot):
            at = pl.ds(pl.multiple_of(i * CHUNK, CHUNK), CHUNK)
            for buf in (basis_buf, images_buf):
                buf[slot, at, :] = jnp.zeros((CHUNK, half), F32)
            return carry

        live = (rows + CHUNK - 1) // CHUNK
        lax.fori_loop(0, live, step, 0)
        lax.fori_loop(live, chunks, dead, 0)
        sector = sigma if slot == OWN else 1 - sigma
        for which, (buf, out) in enumerate(((basis_buf, basis_out), (images_buf, images_out))):
            copies.append(
                pltpu.make_async_copy(buf.at[slot], out.at[last, sector], sems.at[which, slot])
            )
            copies[-1].start()
    shape = projected_ref.shape
    row_ids = lax.broadcasted_iota(jnp.int32, shape, 0)
    col_ids = lax.broadcasted_iota(jnp.int32, shape, 1)
    value = jnp.zeros(shape, F32)
    for i in range(MATVECS):
        for j in range(MATVECS):
            value = jnp.where((row_ids == i) & (col_ids == j), numbers.proj[i, j][:, :1], value)
    projected_ref[...] = value
    for copy in copies:
        copy.wait()


def per_device(
    wavefunction, left_env, right_env, precond_diag, down_charge, bond_mask, left_size, right_size
):
    sectors, states, columns = wavefunction.shape
    bonds = left_env.shape[0]
    lsec_count = lax.axis_size("lsec")
    mpo_count = lax.axis_size("mpo")
    assert sectors == 2 and lax.axis_size("rsec") == 2
    width = 2 * columns
    cells = float(lsec_count * sectors * states * width)
    field = jax.ShapeDtypeStruct((states, width), F32)
    noted = jax.ShapeDtypeStruct((states + NOTE, width), F32)
    half_field = jax.ShapeDtypeStruct((states, columns), F32)
    small = jax.ShapeDtypeStruct((8, 128), F32)
    params = pltpu.CompilerParams(vmem_limit_bytes=18 * 2**20)

    swap = [(0, 1), (1, 0)]
    first_pairs = [(i, i ^ 1) for i in range(lsec_count) if i ^ 1 < lsec_count]
    second_pairs = [(i, j) for a in range(1, lsec_count - 1, 2) for i, j in ((a, a + 1), (a + 1, a))]
    anywhere = pl.BlockSpec(memory_space=pl.ANY)
    in_hbm = pl.BlockSpec(memory_space=pltpu.HBM)

    def hold(value):
        return pltpu.with_memory_space_constraint(value, pltpu.HBM)

    def neighbours(value):
        return lax.ppermute(value, "lsec", first_pairs), lax.ppermute(value, "lsec", second_pairs)

    wave_far = lax.ppermute(wavefunction, "rsec", swap)
    diag_far = lax.ppermute(precond_diag, "rsec", swap)
    mask_rows = bond_mask.T
    small_inputs = [down_charge, mask_rows, left_size, right_size]
    meta, wave_near = pl.pallas_call(
        functools.partial(prep_kernel, lsec_count, bonds),
        out_shape=(
            jax.ShapeDtypeStruct((LIST + bonds,), jnp.int32),
            jax.ShapeDtypeStruct(wavefunction.shape, F32),
        ),
        in_specs=[in_hbm] * 5,
        out_specs=(whole_smem(), whole_vmem()),
        scratch_shapes=[pltpu.SMEM(x.shape, jnp.int32) for x in small_inputs]
        + [pltpu.SemaphoreType.DMA((4,)), pltpu.SemaphoreType.DMA],
        compiler_params=params,
        cost_estimate=pl.CostEstimate(flops=0, transcendentals=0, bytes_accessed=10**6),
        name="prep",
    )(*[hold(x) for x in small_inputs], hold(wavefunction))
    right_send, _, _, _ = lax.optimization_barrier((right_env, wave_far, wave_near, diag_far))
    right_far = lax.ppermute(right_send, "rsec", swap)
    own, sib = pl.pallas_call(
        first_kernel,
        out_shape=(noted, field),
        in_specs=[whole_smem()] + [whole_vmem()] * 2,
        out_specs=(whole_vmem(),) * 2,
        compiler_params=params,
        name="first",
    )(meta, wave_near, wave_far)
    near_waves = neighbours(own)
    raw = [(own, sib, *near_waves)]
    diag_own, diag_sib = pl.pallas_call(
        diag_kernel,
        out_shape=(field,) * 2,
        in_specs=[whole_smem()] + [whole_vmem()] * 2,
        out_specs=(whole_vmem(),) * 2,
        compiler_params=params,
        name="diag",
    )(meta, hold(precond_diag), diag_far)

    near_diags = neighbours(diag_own)

    def mpo_pair(value):
        if mpo_count != 2:
            value = lax.psum(value, "mpo")
            return value, jnp.zeros_like(value)
        return value, lax.ppermute(value, "mpo", swap)

    def lsec_parts(part):
        if lsec_count != 4:
            zero = jnp.zeros_like(part)
            return lax.psum(part, "lsec"), zero, zero, zero
        return (part, *[lax.ppermute(part, "lsec", [(i, i ^ x) for i in range(4)]) for x in (1, 2, 3)])

    def join(value, part, after):
        return pl.pallas_call(
            join_kernel,
            out_shape=noted,
            in_specs=[whole_vmem()] * 6 + [anywhere] * len(after),
            out_specs=whole_vmem(),
            compiler_params=params,
            name="join",
        )(*mpo_pair(value), *lsec_parts(part), *after)

    most = bonds - bonds // 5 if bonds % 5 == 0 else bonds
    packed = most * states + PACK
    lefts = pl.pallas_call(
        left_kernel,
        out_shape=(
            pltpu.VMEM((packed, SIDE), BF16),
            pltpu.VMEM((packed, SIDE), BF16),
            pltpu.VMEM((packed, 2 * (states - SIDE)), BF16),
        ),
        in_specs=[whole_smem(), anywhere],
        out_specs=(whole_vmem(),) * 3,
        scratch_shapes=[
            pltpu.VMEM((BUFFERS, states, states), F32),
            pltpu.SemaphoreType.DMA((states // TILE, BUFFERS)),
        ],
        compiler_params=params,
        cost_estimate=pl.CostEstimate(flops=0, transcendentals=0, bytes_accessed=bonds * states * states * 4),
        name="left",
    )(meta, hold(left_env))
    rights = pl.pallas_call(
        right_kernel,
        out_shape=(pltpu.VMEM((most, width, width), BF16),) * 2,
        in_specs=[whole_smem(), anywhere, anywhere],
        out_specs=(whole_vmem(),) * 2,
        scratch_shapes=[
            pltpu.VMEM((most, width, width), F32),
            pltpu.SemaphoreType.DMA((2, most)),
        ],
        compiler_params=params,
        cost_estimate=pl.CostEstimate(flops=0, transcendentals=0, bytes_accessed=bonds * width * width * 8),
        name="right",
    )(meta, hold(right_env), right_far)

    def dots(k, early, values):
        operands = [early, *totals, *[group[0] for group in raw], *values]
        return pl.pallas_call(
            functools.partial(dots_kernel, k, cells, mpo_count),
            out_shape=small,
            in_specs=[whole_smem()] + [whole_vmem()] * len(operands),
            out_specs=whole_vmem(),
            compiler_params=params,
            cost_estimate=pl.CostEstimate(
                flops=4 * states * width, transcendentals=0, bytes_accessed=4 * states * width
            ),
            name=f"dots{k}",
        )(meta, *operands)

    out = jax.ShapeDtypeStruct((MATVECS, sectors, states, columns), F32)
    known = jax.ShapeDtypeStruct((2, sectors, MATVECS - 1, states, columns), F32)

    def matvec(k, near, sizes, inputs):
        last = k + 1 == MATVECS
        vmem, scalars = whole_vmem(), whole_smem()
        scratch = [
            pltpu.VMEM((2, states, width), BF16),
            pltpu.VMEM((2, states, width), BF16),
            pltpu.VMEM((2 * (states - SIDE), width), BF16),
            pltpu.VMEM((packed + states, width), BF16),
            pltpu.VMEM((packed + states, width), BF16),
            pltpu.SMEM((bonds,), jnp.int32),
        ]
        fresh = [(field, vmem)] * (2 if k else 0)
        if near:
            outs = [(field, vmem), (jax.ShapeDtypeStruct((1 + 2 * k, 8, width), F32), vmem), *fresh]
            scratch.append(pltpu.SMEM((8,), jnp.int32))
            if last:
                outs += [(known, vmem), (small, vmem), (out, anywhere), (out, anywhere)]
                scratch.append(pltpu.SemaphoreType.DMA((2, 2)))
        else:
            outs = ([(half_field, vmem)] * 2 if last else [(field, vmem)]) + fresh
            if last:
                scratch.append(pltpu.VMEM((states, width), F32))
            if not k:
                outs.append((jax.ShapeDtypeStruct((8,), jnp.int32), scalars))
        return pl.pallas_call(
            functools.partial(matvec_kernel, k, cells, near),
            out_shape=tuple(shape for shape, _ in outs),
            in_specs=[scalars] + [vmem] * 5 + [scalars] * len(sizes) + [vmem] * len(inputs),
            out_specs=tuple(spec for _, spec in outs),
            scratch_shapes=scratch,
            compiler_params=params,
            cost_estimate=pl.CostEstimate(
                flops=3 * bonds * states * width * (states + width),
                transcendentals=0,
                bytes_accessed=bonds * states * states,
            ),
            name=f"matvec{k}_{'near' if near else 'far'}",
        )(meta, *lefts, *rights, *sizes, *inputs)

    def flatten(groups):
        return [x for group in groups for x in group]

    def step_inputs(slots):
        return [*totals, *flatten(group[slots] for group in (*raw, *images)), *precond[slots]]

    near_slots, far_slots = slice(0, 2), slice(2, 4)
    totals, images, sizes, precond = [], [], [], []
    for k in range(MATVECS):
        last = k + 1 == MATVECS
        inputs = step_inputs(far_slots)
        partial, early, *fresh = matvec(k, True, [], step_inputs(near_slots))
        value, *fresh_far = matvec(k, False, sizes, [*inputs, partial])
        if k == 0:
            sizes = fresh_far
            precond = (diag_own, diag_sib, *near_diags)
        elif not last:
            raw.append((*fresh, *fresh_far))
        if last:
            break
        part = dots(k, early, [value])
        value = join(value, part, [] if k else near_diags)
        beside = lax.ppermute(value, "rsec", swap)
        images.append((value, beside, *neighbours(value)))
        totals += mpo_pair(value[states:, :HALF] + beside[states:, :HALF])

    near, away = value, fresh_far[0]
    own, sib, known_blocks, state, *outs = fresh
    raw.append((own, sib))
    part = dots(MATVECS - 1, early, [near, away])
    away, far_away = mpo_pair(away)
    sib_half = lax.ppermute(away + far_away, "rsec", swap)
    own_half = mpo_pair(near)
    one, two, three, four = lsec_parts(part)
    part = (one + two) + (three + four)
    total = mpo_pair(part + lax.ppermute(part, "rsec", swap))
    operands = [*total, state, known_blocks, own, sib, *own_half, sib_half]
    return pl.pallas_call(
        functools.partial(fill_kernel, cells),
        out_shape=(out, out, jax.ShapeDtypeStruct((MATVECS, MATVECS), F32)),
        in_specs=[whole_smem()] + [whole_vmem()] * len(operands) + [anywhere] * 2,
        out_specs=(anywhere, anywhere, whole_vmem()),
        scratch_shapes=[
            pltpu.VMEM((sectors, states, columns), F32),
            pltpu.VMEM((sectors, states, columns), F32),
            pltpu.SemaphoreType.DMA((2, 2)),
        ],
        input_output_aliases={1 + len(operands): 0, 2 + len(operands): 1},
        compiler_params=params,
        name="fill",
    )(meta, *operands, *outs)


def solution(mesh):
    placed = (
        P(("grp", "lsec"), None, "rsec"),
        P("mpo", ("grp", "lsec"), None, None),
        P("mpo", ("grp", "lsec"), "rsec", None),
        P(("grp", "lsec"), None, "rsec"),
        P("grp"),
        P("mpo", ("grp", "lsec")),
        P(("grp", "lsec")),
        P(("grp", "lsec")),
    )
    return jax.shard_map(
        per_device,
        mesh=mesh,
        in_specs=placed,
        out_specs=(
            P(None, ("grp", "lsec"), None, "rsec"),
            P(None, ("grp", "lsec"), None, "rsec"),
            P("grp", None),
        ),
        check_vma=False,
    )
```

```python
import functools

import jax
import jax.numpy as jnp
from jax import lax
from jax.experimental import pallas as pl
from jax.experimental.pallas import tpu as pltpu
from jax.sharding import PartitionSpec as P

EPSILON = 1e-06
MATVECS = 3
F32 = jnp.float32
BF16 = jnp.bfloat16
SIGMA, COUNT, ROWS, COLS, FIRST, SIB_ROWS, SIB_COLS, LIST = 0, 1, 2, 3, 4, 9, 10, 16
OWN, SIB, FIRST_PAIR, SECOND_PAIR = 0, 1, 2, 3
CHUNK = 64
TILE = 128
SIDE = 256
HALF = 128
NOTE = 8
PACK = 256
BUFFERS = 8


def whole_vmem():
    return pl.BlockSpec(memory_space=pltpu.VMEM)


def whole_smem():
    return pl.BlockSpec(memory_space=pltpu.SMEM)


def split(value):
    high = value.astype(BF16)
    return high, (value - high.astype(F32)).astype(BF16)


def orientation(down_ref, place):
    def step(i, flips):
        straight = (down_ref[2 * i] == down_ref[2 * i - 2]) | (
            down_ref[2 * i + 1] == down_ref[2 * i - 1]
        )
        return jnp.where(straight, flips, 1 - flips)

    return lax.fori_loop(1, place + 1, step, jnp.int32(0))


def live_mask(shape, row0, rows, cols):
    row_ids = row0 + lax.broadcasted_iota(jnp.int32, shape, 0)
    col_ids = lax.broadcasted_iota(jnp.int32, shape, 1)
    return (row_ids < rows) & (col_ids < cols)


def read_small(pairs, sems):
    copies = [pltpu.make_async_copy(*pair, sems.at[i]) for i, pair in enumerate(pairs)]
    for copy in copies:
        copy.start()
    for copy in copies:
        copy.wait()


def first_kernel(meta_ref, wave_ref, wave_far, own_ref, sib_ref):
    states, half = wave_ref.shape[1:]
    sigma, core = meta_ref[SIGMA], lax.axis_index("rsec")
    for out_ref, slot, rows, cols in (
        (own_ref, sigma, meta_ref[ROWS], meta_ref[COLS]),
        (sib_ref, 1 - sigma, meta_ref[SIB_ROWS], meta_ref[SIB_COLS]),
    ):

        def fill(i, carry, out_ref=out_ref, slot=slot, rows=rows, cols=cols):
            at = pl.ds(pl.multiple_of(i * CHUNK, CHUNK), CHUNK)
            for place, wave in ((core, wave_ref), (1 - core, wave_far)):
                lanes = pl.ds(pl.multiple_of(place * half, half), half)
                mask = live_mask((CHUNK, half), i * CHUNK, rows, cols - place * half)
                out_ref[at, lanes] = jnp.where(mask, wave[slot, at, :], 0.0)
            return carry

        lax.fori_loop(0, states // CHUNK, fill, 0)
    note = (NOTE, own_ref.shape[1])
    row_ids = lax.broadcasted_iota(jnp.int32, note, 0)
    own_ref[pl.ds(states, NOTE), :] = jnp.where(
        row_ids == 0, meta_ref[ROWS], meta_ref[COLS]
    ).astype(F32)


def prep_kernel(lsec_count, bonds, down_in, mask_in, left_in, right_in, wave_in, meta_ref, wave_ref,
                down_ref, mask_ref, left_size_ref, right_size_ref, sems, wave_sem):
    wave_copy = pltpu.make_async_copy(wave_in, wave_ref, wave_sem)
    wave_copy.start()
    read_small(
        ((down_in, down_ref), (mask_in, mask_ref), (left_in, left_size_ref), (right_in, right_size_ref)),
        sems,
    )
    place = lax.axis_index("lsec")
    core = lax.axis_index("rsec")
    first_kind = lax.rem(lax.axis_index("mpo") * bonds, 5)
    sigma = core ^ orientation(down_ref, place)
    own_down = down_ref[2 * place + sigma]
    sib_down = down_ref[2 * place + 1 - sigma]
    before = jnp.maximum(place - 1, 0)
    after = jnp.minimum(place + 1, lsec_count - 1)
    prev_down = down_ref[2 * before + (core ^ orientation(down_ref, before))]
    next_down = down_ref[2 * after + (core ^ orientation(down_ref, after))]
    has_prev = (place > 0) & (prev_down == own_down)
    has_next = (place < lsec_count - 1) & (next_down == own_down)
    odd = lax.rem(place, 2)
    has_lower = sib_down == own_down - 1
    has_upper = sib_down == own_down + 1

    def gather(slot, count):
        meta_ref[FIRST + slot] = count

        def step(bond, carry):
            count, kind = carry
            if slot == OWN:
                there = kind == 0
            elif slot == SIB:
                there = ((kind == 3) & has_lower) | ((kind == 4) & has_upper)
            else:
                lower = odd if slot == FIRST_PAIR else 1 - odd
                there = ((kind == 1) & has_prev & (lower == 1)) | (
                    (kind == 2) & has_next & (lower == 0)
                )
            there = there & (mask_ref[sigma, bond] > 0)

            @pl.when(there)
            def _():
                meta_ref[LIST + count] = bond * 4 + slot

            return count + there.astype(jnp.int32), jnp.where(kind == 4, 0, kind + 1)

        return lax.fori_loop(0, bonds, step, (count, first_kind))[0]

    count = jnp.int32(0)
    for slot in (OWN, SIB, FIRST_PAIR, SECOND_PAIR):
        count = gather(slot, count)
    meta_ref[FIRST + 4] = count
    rows, cols = left_size_ref[sigma], right_size_ref[sigma]
    meta_ref[SIGMA] = sigma
    meta_ref[COUNT] = count
    meta_ref[ROWS] = rows
    meta_ref[COLS] = cols
    meta_ref[SIB_ROWS] = left_size_ref[1 - sigma]
    meta_ref[SIB_COLS] = right_size_ref[1 - sigma]
    wave_copy.wait()


def diag_kernel(meta_ref, diag_ref, diag_far, diag_own, diag_sib):
    states, width = diag_own.shape
    half = width // 2
    sigma, core = meta_ref[SIGMA], lax.axis_index("rsec")
    near = pl.ds(pl.multiple_of(core * half, half), half)
    away = pl.ds(pl.multiple_of((1 - core) * half, half), half)
    for out_ref, slot in ((diag_own, sigma), (diag_sib, 1 - sigma)):

        def fill(i, carry, out_ref=out_ref, slot=slot):
            at = pl.ds(pl.multiple_of(i * CHUNK, CHUNK), CHUNK)
            out_ref[at, near] = diag_ref[slot, at, :]
            out_ref[at, away] = diag_far[slot, at, :]
            return carry

        lax.fori_loop(0, states // CHUNK, fill, 0)


def row(value, index):
    return value[index : index + 1, :]


def stack_rows(shape, rows):
    row_ids = lax.broadcasted_iota(jnp.int32, shape, 0)
    value = jnp.zeros(shape, F32)
    for index, entry in enumerate(rows):
        if entry is not None:
            value = jnp.where(row_ids == index, entry, value)
    return value


class Scalars:
    def __init__(self, totals, cells, state=None):
        self.proj = {}
        self.gram = {}
        self.inverse = []
        self.corr = []
        known = 0
        if state is not None:
            known = MATVECS - 1
            places = [(i, j) for i in range(known) for j in range(known)]
            for index, place in enumerate(places):
                self.proj[place] = row(state, index)
                self.gram[place] = row(state, len(places) + index)
        for k, total in enumerate(totals, known):
            value = (total[0][...] + total[1][...]) / cells
            size, inner = row(value, 0), row(value, 1)
            a = [row(value, 2 + j) for j in range(k)]
            e = [row(value, 4 + j) for j in range(k)]
            f = [row(value, 6 + j) for j in range(k)]
            length = size
            theta = inner
            for j in range(k):
                length = length - 2.0 * a[j] * a[j]
                theta = theta - a[j] * e[j] - a[j] * f[j]
            for i in range(k):
                for j in range(k):
                    length = length + a[i] * a[j] * self.gram[i, j]
                    theta = theta + a[i] * a[j] * self.proj[i, j]
            length = jnp.maximum(length, 0.0)
            square = length + EPSILON
            norm = jnp.sqrt(square)
            for j in range(k):
                up, down, both = e[j], f[j], a[j]
                for i in range(k):
                    up = up - a[i] * self.proj[j, i]
                    down = down - a[i] * self.proj[i, j]
                    both = both - a[i] * self.gram[i, j]
                self.proj[j, k] = up / norm
                self.proj[k, j] = down / norm
                self.gram[j, k] = self.gram[k, j] = both / norm
            self.proj[k, k] = theta / square
            self.gram[k, k] = length / square
            self.inverse.append(1.0 / norm)
            self.corr.append(a)

    def state(self, shape):
        known = MATVECS - 1
        places = [(i, j) for i in range(known) for j in range(known)]
        rows = [self.proj[place] for place in places] + [self.gram[place] for place in places]
        return stack_rows(shape, rows)

    def pack(self, k, shape):
        rows = [self.proj[k - 1, k - 1], *self.inverse[:k]]
        for a in self.corr[:k]:
            rows += a
        return stack_rows(shape, rows)

    @classmethod
    def unpack(cls, k, ref):
        numbers = cls([], 1.0)
        value = ref[...]
        numbers.theta = row(value, 0)[:, :1]
        numbers.inverse = [row(value, 1 + i) for i in range(k)]
        place = 1 + k
        for step in range(k):
            numbers.corr.append([row(value, place + j) for j in range(step)])
            place += step
        return numbers

    def basis(self, k, fields):
        done = []
        for step in range(k + 1):
            value = fields[step]
            for j in range(step):
                value = value - self.corr[step][j][:, :1] * done[j]
            done.append(value * self.inverse[step][:, :1])
        return done


def left_kernel(meta_ref, left_ref, left_high, left_low, left_tail, left_buf, sems):
    states = left_buf.shape[1]
    sigma, count, rows = meta_ref[SIGMA], meta_ref[COUNT], meta_ref[ROWS]
    stride = packed_rows(rows)

    def each(i, act):
        bond = (meta_ref[LIST + i] >> 2)
        at = i & (BUFFERS - 1)
        for p in range(states // TILE):
            part = pl.ds(p * TILE, TILE)

            @pl.when(rows > p * TILE)
            def _(part=part, p=p):
                act(
                    pltpu.make_async_copy(
                        left_ref.at[bond, sigma, part], left_buf.at[at, part], sems.at[p, at]
                    )
                )

    def start(i):
        @pl.when(i < count)
        def _():
            each(i, lambda copy: copy.start())

    for i in range(BUFFERS - 1):
        start(jnp.int32(i))

    def step(i, carry):
        at = i & (BUFFERS - 1)
        start(i + BUFFERS - 1)
        each(i, lambda copy: copy.wait())

        def chunk(t, inner):
            high, low = split(left_buf[at, pl.ds(pl.multiple_of(t * CHUNK, CHUNK), CHUNK), :])
            to = pl.ds(pl.multiple_of(i * stride + t * CHUNK, 16), CHUNK)
            left_high[to, :] = high[:, :SIDE]
            left_low[to, :] = low[:, :SIDE]
            left_tail[to, :] = jnp.concatenate([high[:, SIDE:], low[:, SIDE:]], axis=1)
            return inner

        lax.fori_loop(0, (rows + CHUNK - 1) // CHUNK, chunk, 0)
        return carry

    lax.fori_loop(0, count, step, 0)


def right_kernel(meta_ref, right_ref, far_ref, right_high, right_low, right_buf, sems):
    width, half = right_buf.shape[1], right_ref.shape[2]
    sigma, count = meta_ref[SIGMA], meta_ref[COUNT]
    core = lax.axis_index("rsec")
    thin = meta_ref[COLS] <= HALF

    def each(i, act):
        bond = (meta_ref[LIST + i] >> 2)
        for ref, place, sem in ((right_ref, core, 0), (far_ref, 1 - core, 1)):
            part = pl.ds(pl.multiple_of(place * half, half), half)

            @pl.when(jnp.logical_not(thin) | (place == 0))
            def _(ref=ref, part=part, sem=sem):
                act(
                    pltpu.make_async_copy(ref.at[bond, sigma], right_buf.at[i, part], sems.at[sem, i])
                )

    def start(i, carry):
        each(i, lambda copy: copy.start())
        return carry

    lax.fori_loop(0, count, start, 0)

    def step(i, carry):
        each(i, lambda copy: copy.wait())

        @pl.when(thin)
        def _():
            for first in range(0, HALF, CHUNK):
                high, low = split(right_buf[i, pl.ds(first, CHUNK), :])
                right_high[i, pl.ds(first, CHUNK), :] = high
                right_high[i, pl.ds(HALF + first, CHUNK), :] = low

        @pl.when(jnp.logical_not(thin))
        def _():
            for first in range(0, width, CHUNK):
                at = pl.ds(first, CHUNK)
                right_high[i, at, :], right_low[i, at, :] = split(right_buf[i, at, :])

        return carry

    lax.fori_loop(0, count, step, 0)


def packed_rows(rows):
    return ((rows + 15) // 16) * 16


def fold(value):
    return jnp.sum(value.reshape(CHUNK // 8, 8, value.shape[1]), axis=0)


def dots_kernel(k, mpo_count, meta_ref, early_ref, *refs):
    refs, small_ref = list(refs[:-1]), refs[-1]
    numbers = Scalars.unpack(k, refs.pop(0)) if k else None
    raw = [refs.pop(0) for _ in range(k + 1)]
    core = lax.axis_index("rsec")
    zero = jnp.zeros(early_ref.shape[1:], F32)

    def step(i, carry):
        at = pl.ds(pl.multiple_of(i * CHUNK, CHUNK), CHUNK)
        blocks = [ref[at, :] for ref in refs]
        if len(blocks) == 2:
            near, away = blocks
            first, second = jnp.where(core == 0, near, away), jnp.where(core == 0, away, near)
            value = jnp.concatenate([first, second], axis=1)
        else:
            value = blocks[0]
        basis = numbers.basis(k - 1, [ref[at, :] for ref in raw[:k]]) if k else []
        return tuple(c + fold(value * b) for c, b in zip(carry, [raw[k][at, :], *basis]))

    live = (meta_ref[ROWS] + CHUNK - 1) // CHUNK
    late = lax.fori_loop(0, live, step, (zero,) * (1 + k))

    def whole(value):
        return jnp.sum(jnp.sum(value, axis=1, keepdims=True), axis=0, keepdims=True)

    share = 1.0 / mpo_count
    entries = [whole(early_ref[0]) * share, whole(late[0])]
    for j in range(2):
        entries.append(whole(early_ref[1 + j]) * share if j < k else None)
    for j in range(2):
        entries.append(whole(late[1 + j]) if j < k else None)
    for j in range(2):
        entries.append(whole(early_ref[1 + k + j]) * share if j < k else None)
    small_ref[...] = stack_rows(small_ref.shape, entries)


def matvec_kernel(k, cells, near, *refs):
    refs = list(refs)
    slots = (OWN, SIB) if near else (FIRST_PAIR, SECOND_PAIR)
    base = slots[0]
    last = k + 1 == MATVECS
    meta_ref = refs.pop(0)
    left_high, left_low, left_tail = [refs.pop(0) for _ in range(3)]
    right_high, right_low = refs.pop(0), refs.pop(0)
    size_ref = refs.pop(0) if k and not near else None
    totals = [(refs.pop(0), refs.pop(0)) for _ in range(k)] if near else []
    pack_ref = refs.pop(0) if k and not near else None
    raw = [{slot: refs.pop(0) for slot in slots} for _ in range(max(k, 1))]
    images = [{slot: refs.pop(0) for slot in slots} for _ in range(k)]
    precond = {slot: refs.pop(0) for slot in slots} if k else {}
    partial_ref = None if near else refs.pop(0)
    halves = [refs.pop(0), refs.pop(0)] if last and not near else []
    out_ref = None if halves else refs.pop(0)
    early_ref = refs.pop(0) if near else None
    pack_ref = refs.pop(0) if k and near else pack_ref
    new_refs = {slot: refs.pop(0) for slot in slots} if k else raw[0]
    if not k and not near:
        size_ref = refs.pop(0)
    if last and near:
        known_ref, state_ref, basis_out, images_out = [refs.pop(0) for _ in range(4)]
    high_ref, low_ref, tail_ref, mid_high, mid_low, order_ref = refs[:6]
    if near:
        size_ref = refs[6]
        sems = refs[7] if last else None
    elif last:
        out_ref = refs[6]
    states, width = out_ref.shape
    rows, cols = meta_ref[ROWS], meta_ref[COLS]
    first_bond, end_bond = meta_ref[FIRST + base], meta_ref[FIRST + base + 2]
    count = end_bond - first_bond
    stride = packed_rows(rows)

    core = lax.axis_index("rsec")
    if near:
        size_ref[2 * OWN], size_ref[2 * OWN + 1] = rows, cols
        size_ref[2 * SIB], size_ref[2 * SIB + 1] = meta_ref[SIB_ROWS], meta_ref[SIB_COLS]
    elif not k:
        for slot in slots:
            note = raw[0][slot][pl.ds(states, NOTE), :HALF]
            size_ref[2 * slot] = jnp.max(note[:1]).astype(jnp.int32)
            size_ref[2 * slot + 1] = jnp.max(note[1:]).astype(jnp.int32)
    def list_bonds(narrow):
        def step(i, place):
            hit = (size_ref[2 * (meta_ref[LIST + i] & 3) + 1] <= HALF) == narrow

            @pl.when(hit)
            def _():
                order_ref[place] = i

            return place + hit.astype(jnp.int32)

        return step

    thin_sources = lax.fori_loop(first_bond, end_bond, list_bonds(True), jnp.int32(0))
    lax.fori_loop(first_bond, end_bond, list_bonds(False), thin_sources)
    if k and near:
        numbers = Scalars(totals, cells)
        theta = numbers.proj[k - 1, k - 1][:, :1]
        pack_ref[...] = numbers.pack(k, pack_ref.shape)
    elif k:
        numbers = Scalars.unpack(k, pack_ref)
        theta = numbers.theta
    zero = jnp.zeros((8, width), F32)

    def prepare(slot, carry):
        def step(i, carry):
            at = pl.ds(pl.multiple_of(i * CHUNK, CHUNK), CHUNK)
            if k:
                basis = numbers.basis(k - 1, [r[slot][at, :] for r in raw])
                image = numbers.basis(k - 1, [r[slot][at, :] for r in images])
                value = (image[-1] - theta * basis[-1]) / jnp.maximum(
                    precond[slot][at, :] - theta, 1.0
                )
                new_refs[slot][at, :] = value
                if last and near:
                    for which, group in enumerate((basis, image)):
                        for j, block in enumerate(group):
                            block = jnp.where(core == 0, block[:, :HALF], block[:, HALF:])
                            known_ref[which, slot, j, at, :] = block
            else:
                basis, image = [], []
                value = raw[0][slot][at, :]
            high, low = split(value)
            high_ref[slot - base, at, :] = high
            low_ref[slot - base, at, :] = low
            terms = [value * value]
            if slot == OWN:
                terms += [value * b for b in basis] + [value * g for g in image]
            return tuple(c + fold(t) for c, t in zip(carry, terms))

        def dead(i, inner):
            at = pl.ds(pl.multiple_of(i * CHUNK, CHUNK), CHUNK)
            high_ref[slot - base, at, :] = jnp.zeros((CHUNK, width), BF16)
            low_ref[slot - base, at, :] = jnp.zeros((CHUNK, width), BF16)
            if last and near:
                for which in range(2):
                    for j in range(k):
                        known_ref[which, slot, j, at, :] = jnp.zeros((CHUNK, HALF), F32)
            return inner

        live = (size_ref[2 * slot] + CHUNK - 1) // CHUNK
        lax.fori_loop(live, states // CHUNK, dead, 0)
        return lax.fori_loop(0, live, step, carry)

    def dot(a, b):
        return jnp.dot(a, b, preferred_element_type=F32)

    def dot_nt(a, b):
        return lax.dot_general(a, b, (((1,), (1,)), ((), ())), preferred_element_type=F32)

    twice = functools.partial(jnp.concatenate, axis=0)

    def first_stage(slot, deep, narrow):
        begin, end = meta_ref[FIRST + slot], meta_ref[FIRST + 1 + slot]
        at_slot = slot - base
        top, rest = pl.ds(0, SIDE), pl.ds(SIDE, states - SIDE)
        if narrow:
            high_ref[at_slot, :, HALF:] = low_ref[at_slot, :, :HALF]
        if deep:
            tail = high_ref[at_slot, rest, :]
            tail_ref[...] = twice([tail, tail])

        def step(t, carry):
            at = pl.ds(pl.multiple_of(begin * stride + t * PACK, 16), PACK)
            high, low = left_high[at, :], left_low[at, :]
            mid = dot(high, high_ref[at_slot, top, :])
            if deep:
                mid = mid + dot(left_tail[at, :], tail_ref[...])
            if narrow:
                mid = mid[:, :HALF] + mid[:, HALF:] + dot(low, high_ref[at_slot, top, :HALF])
                mid_high[at, :] = jnp.concatenate(split(mid), axis=1)
            else:
                mid = mid + dot(low, high_ref[at_slot, top, :]) + dot(high, low_ref[at_slot, top, :])
                if deep:
                    mid = mid + dot(left_tail[at, : states - SIDE], low_ref[at_slot, rest, :])
                mid_high[at, :], mid_low[at, :] = split(mid)
            return carry

        lax.fori_loop(0, ((end - begin) * stride + PACK - 1) // PACK, step, 0)

    def both(test, action):
        pl.when(test)(lambda: action(True))
        pl.when(jnp.logical_not(test))(lambda: action(False))

    if near:
        own = prepare(OWN, (zero,) * (1 + 2 * k))
        prepare(SIB, (zero,))
    else:
        for slot in slots:
            used = meta_ref[FIRST + 1 + slot] > meta_ref[FIRST + slot]
            pl.when(used)(lambda slot=slot: (prepare(slot, (zero,)), None)[1])

    def from_slot(slot, carry):
        both(
            size_ref[2 * slot] > SIDE,
            lambda deep: both(
                size_ref[2 * slot + 1] <= HALF, lambda narrow: first_stage(slot, deep, narrow)
            ),
        )
        return carry

    lax.fori_loop(base, base + 2, from_slot, 0)
    if last and near:
        sigma = meta_ref[SIGMA]
        outputs = [
            pltpu.make_async_copy(
                known_ref.at[which, slot],
                out.at[pl.ds(0, MATVECS - 1), sigma if slot == OWN else 1 - sigma],
                sems.at[which, slot],
            )
            for which, out in enumerate((basis_out, images_out))
            for slot in (OWN, SIB)
        ]
        for copy in outputs:
            copy.start()
        state_ref[...] = numbers.state(state_ref.shape)

    def clear(i, carry):
        at = pl.ds(pl.multiple_of(i * CHUNK, CHUNK), CHUNK)
        out_ref[at, :] = jnp.zeros((CHUNK, width), F32) if near else partial_ref[at, :]
        return carry

    lax.fori_loop(0, states // CHUNK, clear, 0)
    zeros_at = mid_high.shape[0] - states
    for ref in (mid_high, mid_low):
        ref[pl.ds(zeros_at, states), :] = jnp.zeros((states, width), BF16)

    def second_stage(size, thin):
        to = pl.ds(0, size)

        def product(i, real, narrow):
            bond = order_ref[i]
            at = pl.ds(pl.multiple_of(jnp.where(real, bond * stride, zeros_at), 16), size)
            high = mid_high[at, :]
            lanes = pl.ds(0, HALF if narrow else width)
            right = right_high[bond, :, lanes]
            right_rest = None if thin else right_low[bond, :, lanes]
            if narrow:
                value = dot_nt(high, jnp.concatenate([right, right], axis=1))
                if not thin:
                    value = value + dot_nt(high[:, :HALF], right_rest)
            else:
                value = dot_nt(high, right)
                if not thin:
                    value = value + dot_nt(high, right_rest) + dot_nt(mid_low[at, :], right)
            if thin:
                value = value[:, :HALF] + value[:, HALF:]
                if not narrow:
                    value = value + dot_nt(mid_low[at, :], right[:HALF, :])
            return value

        def run(begin, end, narrow):
            def pair(p, carry):
                one = begin + 2 * p
                real = one + 1 < end
                two = jnp.where(real, one + 1, one)
                value = product(one, True, narrow) + product(two, real, narrow)
                if thin:
                    out_ref[to, :HALF] += value
                else:
                    out_ref[to, :] += value
                return carry

            lax.fori_loop(0, (end - begin + 1) // 2, pair, 0)

        run(0, thin_sources, True)
        run(thin_sources, count, False)

    for size in range(TILE, states + 1, TILE):
        pl.when((rows <= size) & (rows > size - TILE))(
            lambda size=size: both(cols <= HALF, functools.partial(second_stage, size))
        )

    if near:
        for index, entry in enumerate(own):
            early_ref[index] = entry
        if last:
            for copy in outputs:
                copy.wait()
        return

    def finish(i, carry):
        at = pl.ds(pl.multiple_of(i * CHUNK, CHUNK), CHUNK)
        mask = live_mask((CHUNK, width), i * CHUNK, rows, cols)
        value = jnp.where(mask, out_ref[at, :], 0.0)
        if last:
            halves[0][at, :] = jnp.where(core == 0, value[:, :HALF], value[:, HALF:])
            halves[1][at, :] = jnp.where(core == 0, value[:, HALF:], value[:, :HALF])
        else:
            out_ref[at, :] = value
        return carry

    lax.fori_loop(0, (rows + CHUNK - 1) // CHUNK, finish, 0)


def join_kernel(a_ref, b_ref, s0, s1, s2, s3, *refs):
    out_ref = refs[-1]
    states = a_ref.shape[0]
    total = (s0[...] + s1[...]) + (s2[...] + s3[...])
    out_ref[pl.ds(states, NOTE), :HALF] = total
    out_ref[pl.ds(states, NOTE), HALF:] = total

    def step(i, carry):
        at = pl.ds(pl.multiple_of(i * CHUNK, CHUNK), CHUNK)
        out_ref[at, :] = a_ref[at, :] + b_ref[at, :]
        return carry

    lax.fori_loop(0, states // CHUNK, step, 0)


def fill_kernel(cells, meta_ref, *refs):
    total, state_ref = refs[:2], refs[2]
    known_ref, raw_own, raw_sib, *parts = refs[3:9]
    basis_out, images_out, projected_ref, basis_buf, images_buf, sems = refs[-6:]
    last = MATVECS - 1
    sigma = meta_ref[SIGMA]
    numbers = Scalars([total], cells, state_ref[...])
    core = lax.axis_index("rsec")
    states, half = basis_buf.shape[1:]
    lanes = pl.ds(pl.multiple_of(core * half, half), half)
    inverse = numbers.inverse[0][:, :1]
    corr = [a[:, :1] for a in numbers.corr[0]]
    copies = []
    chunks = states // CHUNK
    for slot, raw, image, rows in (
        (OWN, raw_own, parts[:2], meta_ref[ROWS]),
        (SIB, raw_sib, parts[2:], meta_ref[SIB_ROWS]),
    ):

        def step(i, carry, slot=slot, raw=raw, image=image):
            at = pl.ds(pl.multiple_of(i * CHUNK, CHUNK), CHUNK)
            fields = (raw[at, lanes], sum(ref[at, :] for ref in image[1:]) + image[0][at, :])
            for which, buf in enumerate((basis_buf, images_buf)):
                value = fields[which]
                for j in range(last):
                    value = value - corr[j] * known_ref[which, slot, j, at, :]
                buf[slot, at, :] = value * inverse
            return carry

        def dead(i, carry, slot=slot):
            at = pl.ds(pl.multiple_of(i * CHUNK, CHUNK), CHUNK)
            for buf in (basis_buf, images_buf):
                buf[slot, at, :] = jnp.zeros((CHUNK, half), F32)
            return carry

        live = (rows + CHUNK - 1) // CHUNK
        lax.fori_loop(0, live, step, 0)
        lax.fori_loop(live, chunks, dead, 0)
        sector = sigma if slot == OWN else 1 - sigma
        for which, (buf, out) in enumerate(((basis_buf, basis_out), (images_buf, images_out))):
            copies.append(
                pltpu.make_async_copy(buf.at[slot], out.at[last, sector], sems.at[which, slot])
            )
            copies[-1].start()
    shape = projected_ref.shape
    row_ids = lax.broadcasted_iota(jnp.int32, shape, 0)
    col_ids = lax.broadcasted_iota(jnp.int32, shape, 1)
    value = jnp.zeros(shape, F32)
    for i in range(MATVECS):
        for j in range(MATVECS):
            value = jnp.where((row_ids == i) & (col_ids == j), numbers.proj[i, j][:, :1], value)
    projected_ref[...] = value
    for copy in copies:
        copy.wait()


def per_device(
    wavefunction, left_env, right_env, precond_diag, down_charge, bond_mask, left_size, right_size
):
    sectors, states, columns = wavefunction.shape
    bonds = left_env.shape[0]
    lsec_count = lax.axis_size("lsec")
    mpo_count = lax.axis_size("mpo")
    assert sectors == 2 and lax.axis_size("rsec") == 2
    width = 2 * columns
    cells = float(lsec_count * sectors * states * width)
    field = jax.ShapeDtypeStruct((states, width), F32)
    noted = jax.ShapeDtypeStruct((states + NOTE, width), F32)
    half_field = jax.ShapeDtypeStruct((states, columns), F32)
    small = jax.ShapeDtypeStruct((8, 128), F32)
    params = pltpu.CompilerParams(vmem_limit_bytes=18 * 2**20)

    swap = [(0, 1), (1, 0)]
    first_pairs = [(i, i ^ 1) for i in range(lsec_count) if i ^ 1 < lsec_count]
    second_pairs = [(i, j) for a in range(1, lsec_count - 1, 2) for i, j in ((a, a + 1), (a + 1, a))]
    anywhere = pl.BlockSpec(memory_space=pl.ANY)
    in_hbm = pl.BlockSpec(memory_space=pltpu.HBM)

    def hold(value):
        return pltpu.with_memory_space_constraint(value, pltpu.HBM)

    def neighbours(value):
        return lax.ppermute(value, "lsec", first_pairs), lax.ppermute(value, "lsec", second_pairs)

    wave_far = lax.ppermute(wavefunction, "rsec", swap)
    diag_far = lax.ppermute(precond_diag, "rsec", swap)
    mask_rows = bond_mask.T
    small_inputs = [down_charge, mask_rows, left_size, right_size]
    meta, wave_near = pl.pallas_call(
        functools.partial(prep_kernel, lsec_count, bonds),
        out_shape=(
            jax.ShapeDtypeStruct((LIST + bonds,), jnp.int32),
            jax.ShapeDtypeStruct(wavefunction.shape, F32),
        ),
        in_specs=[in_hbm] * 5,
        out_specs=(whole_smem(), whole_vmem()),
        scratch_shapes=[pltpu.SMEM(x.shape, jnp.int32) for x in small_inputs]
        + [pltpu.SemaphoreType.DMA((4,)), pltpu.SemaphoreType.DMA],
        compiler_params=params,
        cost_estimate=pl.CostEstimate(flops=0, transcendentals=0, bytes_accessed=10**6),
        name="prep",
    )(*[hold(x) for x in small_inputs], hold(wavefunction))
    right_send, _, _, _ = lax.optimization_barrier((right_env, wave_far, wave_near, diag_far))
    right_far = lax.ppermute(right_send, "rsec", swap)
    own, sib = pl.pallas_call(
        first_kernel,
        out_shape=(noted, field),
        in_specs=[whole_smem()] + [whole_vmem()] * 2,
        out_specs=(whole_vmem(),) * 2,
        compiler_params=params,
        name="first",
    )(meta, wave_near, wave_far)
    near_waves = neighbours(own)
    raw = [(own, sib, *near_waves)]
    diag_own, diag_sib = pl.pallas_call(
        diag_kernel,
        out_shape=(field,) * 2,
        in_specs=[whole_smem()] + [whole_vmem()] * 2,
        out_specs=(whole_vmem(),) * 2,
        compiler_params=params,
        name="diag",
    )(meta, hold(precond_diag), diag_far)

    near_diags = neighbours(diag_own)

    def mpo_pair(value):
        if mpo_count != 2:
            value = lax.psum(value, "mpo")
            return value, jnp.zeros_like(value)
        return value, lax.ppermute(value, "mpo", swap)

    def lsec_parts(part):
        if lsec_count != 4:
            zero = jnp.zeros_like(part)
            return lax.psum(part, "lsec"), zero, zero, zero
        return (part, *[lax.ppermute(part, "lsec", [(i, i ^ x) for i in range(4)]) for x in (1, 2, 3)])

    def join(value, part, after):
        return pl.pallas_call(
            join_kernel,
            out_shape=noted,
            in_specs=[whole_vmem()] * 6 + [anywhere] * len(after),
            out_specs=whole_vmem(),
            compiler_params=params,
            name="join",
        )(*mpo_pair(value), *lsec_parts(part), *after)

    most = bonds - bonds // 5 if bonds % 5 == 0 else bonds
    packed = most * states + PACK
    lefts = pl.pallas_call(
        left_kernel,
        out_shape=(
            pltpu.VMEM((packed, SIDE), BF16),
            pltpu.VMEM((packed, SIDE), BF16),
            pltpu.VMEM((packed, 2 * (states - SIDE)), BF16),
        ),
        in_specs=[whole_smem(), anywhere],
        out_specs=(whole_vmem(),) * 3,
        scratch_shapes=[
            pltpu.VMEM((BUFFERS, states, states), F32),
            pltpu.SemaphoreType.DMA((states // TILE, BUFFERS)),
        ],
        compiler_params=params,
        cost_estimate=pl.CostEstimate(flops=0, transcendentals=0, bytes_accessed=bonds * states * states * 4),
        name="left",
    )(meta, hold(left_env))
    rights = pl.pallas_call(
        right_kernel,
        out_shape=(pltpu.VMEM((most, width, width), BF16),) * 2,
        in_specs=[whole_smem(), anywhere, anywhere],
        out_specs=(whole_vmem(),) * 2,
        scratch_shapes=[
            pltpu.VMEM((most, width, width), F32),
            pltpu.SemaphoreType.DMA((2, most)),
        ],
        compiler_params=params,
        cost_estimate=pl.CostEstimate(flops=0, transcendentals=0, bytes_accessed=bonds * width * width * 8),
        name="right",
    )(meta, hold(right_env), right_far)

    def dots(k, early, pack, values):
        operands = [early, *pack, *[group[0] for group in raw], *values]
        return pl.pallas_call(
            functools.partial(dots_kernel, k, mpo_count),
            out_shape=small,
            in_specs=[whole_smem()] + [whole_vmem()] * len(operands),
            out_specs=whole_vmem(),
            compiler_params=params,
            cost_estimate=pl.CostEstimate(
                flops=4 * states * width, transcendentals=0, bytes_accessed=4 * states * width
            ),
            name=f"dots{k}",
        )(meta, *operands)

    out = jax.ShapeDtypeStruct((MATVECS, sectors, states, columns), F32)
    known = jax.ShapeDtypeStruct((2, sectors, MATVECS - 1, states, columns), F32)

    def matvec(k, near, sizes, inputs):
        last = k + 1 == MATVECS
        vmem, scalars = whole_vmem(), whole_smem()
        scratch = [
            pltpu.VMEM((2, states, width), BF16),
            pltpu.VMEM((2, states, width), BF16),
            pltpu.VMEM((2 * (states - SIDE), width), BF16),
            pltpu.VMEM((packed + states, width), BF16),
            pltpu.VMEM((packed + states, width), BF16),
            pltpu.SMEM((bonds,), jnp.int32),
        ]
        fresh = [(field, vmem)] * (2 if k else 0)
        if near:
            outs = [(field, vmem), (jax.ShapeDtypeStruct((1 + 2 * k, 8, width), F32), vmem)]
            outs += [(small, vmem)] * (1 if k else 0) + fresh
            scratch.append(pltpu.SMEM((8,), jnp.int32))
            if last:
                outs += [(known, vmem), (small, vmem), (out, anywhere), (out, anywhere)]
                scratch.append(pltpu.SemaphoreType.DMA((2, 2)))
        else:
            outs = ([(half_field, vmem)] * 2 if last else [(field, vmem)]) + fresh
            if last:
                scratch.append(pltpu.VMEM((states, width), F32))
            if not k:
                outs.append((jax.ShapeDtypeStruct((8,), jnp.int32), scalars))
        return pl.pallas_call(
            functools.partial(matvec_kernel, k, cells, near),
            out_shape=tuple(shape for shape, _ in outs),
            in_specs=[scalars] + [vmem] * 5 + [scalars] * len(sizes) + [vmem] * len(inputs),
            out_specs=tuple(spec for _, spec in outs),
            scratch_shapes=scratch,
            compiler_params=params,
            cost_estimate=pl.CostEstimate(
                flops=3 * bonds * states * width * (states + width),
                transcendentals=0,
                bytes_accessed=bonds * states * states,
            ),
            name=f"matvec{k}_{'near' if near else 'far'}",
        )(meta, *lefts, *rights, *sizes, *inputs)

    def flatten(groups):
        return [x for group in groups for x in group]

    def step_inputs(slots):
        return [*flatten(group[slots] for group in (*raw, *images)), *precond[slots]]

    near_slots, far_slots = slice(0, 2), slice(2, 4)
    totals, images, sizes, precond = [], [], [], []
    for k in range(MATVECS):
        last = k + 1 == MATVECS
        inputs = step_inputs(far_slots)
        partial, early, *fresh = matvec(k, True, [], [*totals, *step_inputs(near_slots)])
        pack, fresh = (fresh[:1], fresh[1:]) if k else ([], fresh)
        value, *fresh_far = matvec(k, False, sizes, [*pack, *inputs, partial])
        if k == 0:
            sizes = fresh_far
            precond = (diag_own, diag_sib, *near_diags)
        elif not last:
            raw.append((*fresh, *fresh_far))
        if last:
            break
        part = dots(k, early, pack, [value])
        value = join(value, part, [] if k else near_diags)
        beside = lax.ppermute(value, "rsec", swap)
        images.append((value, beside, *neighbours(value)))
        totals += mpo_pair(value[states:, :HALF] + beside[states:, :HALF])

    near, away = value, fresh_far[0]
    own, sib, known_blocks, state, *outs = fresh
    raw.append((own, sib))
    part = dots(MATVECS - 1, early, pack, [near, away])
    away, far_away = mpo_pair(away)
    sib_half = lax.ppermute(away + far_away, "rsec", swap)
    own_half = mpo_pair(near)
    one, two, three, four = lsec_parts(part)
    part = (one + two) + (three + four)
    total = mpo_pair(part + lax.ppermute(part, "rsec", swap))
    operands = [*total, state, known_blocks, own, sib, *own_half, sib_half]
    return pl.pallas_call(
        functools.partial(fill_kernel, cells),
        out_shape=(out, out, jax.ShapeDtypeStruct((MATVECS, MATVECS), F32)),
        in_specs=[whole_smem()] + [whole_vmem()] * len(operands) + [anywhere] * 2,
        out_specs=(anywhere, anywhere, whole_vmem()),
        scratch_shapes=[
            pltpu.VMEM((sectors, states, columns), F32),
            pltpu.VMEM((sectors, states, columns), F32),
            pltpu.SemaphoreType.DMA((2, 2)),
        ],
        input_output_aliases={1 + len(operands): 0, 2 + len(operands): 1},
        compiler_params=params,
        name="fill",
    )(meta, *operands, *outs)


def solution(mesh):
    placed = (
        P(("grp", "lsec"), None, "rsec"),
        P("mpo", ("grp", "lsec"), None, None),
        P("mpo", ("grp", "lsec"), "rsec", None),
        P(("grp", "lsec"), None, "rsec"),
        P("grp"),
        P("mpo", ("grp", "lsec")),
        P(("grp", "lsec")),
        P(("grp", "lsec")),
    )
    return jax.shard_map(
        per_device,
        mesh=mesh,
        in_specs=placed,
        out_specs=(
            P(None, ("grp", "lsec"), None, "rsec"),
            P(None, ("grp", "lsec"), None, "rsec"),
            P("grp", None),
        ),
        check_vma=False,
    )
```

```python
import functools

import jax
import jax.numpy as jnp
from jax import lax
from jax.experimental import pallas as pl
from jax.experimental.pallas import tpu as pltpu
from jax.sharding import PartitionSpec as P

EPSILON = 1e-06
MATVECS = 3
F32 = jnp.float32
BF16 = jnp.bfloat16
SIGMA, COUNT, ROWS, COLS, FIRST, SIB_ROWS, SIB_COLS, LIST = 0, 1, 2, 3, 4, 9, 10, 16
OWN, SIB, FIRST_PAIR, SECOND_PAIR = 0, 1, 2, 3
CHUNK = 64
TILE = 128
SIDE = 256
HALF = 128
NOTE = 8
PACK = 256
BUFFERS = 8


def whole_vmem():
    return pl.BlockSpec(memory_space=pltpu.VMEM)


def whole_smem():
    return pl.BlockSpec(memory_space=pltpu.SMEM)


def split(value):
    high = value.astype(BF16)
    return high, (value - high.astype(F32)).astype(BF16)


def orientation(down_ref, place):
    def step(i, flips):
        straight = (down_ref[2 * i] == down_ref[2 * i - 2]) | (
            down_ref[2 * i + 1] == down_ref[2 * i - 1]
        )
        return jnp.where(straight, flips, 1 - flips)

    return lax.fori_loop(1, place + 1, step, jnp.int32(0))


def live_mask(shape, row0, rows, cols):
    row_ids = row0 + lax.broadcasted_iota(jnp.int32, shape, 0)
    col_ids = lax.broadcasted_iota(jnp.int32, shape, 1)
    return (row_ids < rows) & (col_ids < cols)


def read_small(pairs, sems):
    copies = [pltpu.make_async_copy(*pair, sems.at[i]) for i, pair in enumerate(pairs)]
    for copy in copies:
        copy.start()
    for copy in copies:
        copy.wait()


def first_kernel(meta_ref, wave_ref, wave_far, own_ref, sib_ref):
    states, half = wave_ref.shape[1:]
    sigma, core = meta_ref[SIGMA], lax.axis_index("rsec")
    for out_ref, slot, rows, cols in (
        (own_ref, sigma, meta_ref[ROWS], meta_ref[COLS]),
        (sib_ref, 1 - sigma, meta_ref[SIB_ROWS], meta_ref[SIB_COLS]),
    ):

        def fill(i, carry, out_ref=out_ref, slot=slot, rows=rows, cols=cols):
            at = pl.ds(pl.multiple_of(i * CHUNK, CHUNK), CHUNK)
            for place, wave in ((core, wave_ref), (1 - core, wave_far)):
                lanes = pl.ds(pl.multiple_of(place * half, half), half)
                mask = live_mask((CHUNK, half), i * CHUNK, rows, cols - place * half)
                out_ref[at, lanes] = jnp.where(mask, wave[slot, at, :], 0.0)
            return carry

        lax.fori_loop(0, states // CHUNK, fill, 0)
    note = (NOTE, own_ref.shape[1])
    row_ids = lax.broadcasted_iota(jnp.int32, note, 0)
    own_ref[pl.ds(states, NOTE), :] = jnp.where(
        row_ids == 0, meta_ref[ROWS], meta_ref[COLS]
    ).astype(F32)


def prep_kernel(lsec_count, bonds, down_in, mask_in, left_in, right_in, wave_in, meta_ref, wave_ref,
                down_ref, mask_ref, left_size_ref, right_size_ref, sems, wave_sem):
    wave_copy = pltpu.make_async_copy(wave_in, wave_ref, wave_sem)
    wave_copy.start()
    read_small(
        ((down_in, down_ref), (mask_in, mask_ref), (left_in, left_size_ref), (right_in, right_size_ref)),
        sems,
    )
    place = lax.axis_index("lsec")
    core = lax.axis_index("rsec")
    first_kind = lax.rem(lax.axis_index("mpo") * bonds, 5)
    sigma = core ^ orientation(down_ref, place)
    own_down = down_ref[2 * place + sigma]
    sib_down = down_ref[2 * place + 1 - sigma]
    before = jnp.maximum(place - 1, 0)
    after = jnp.minimum(place + 1, lsec_count - 1)
    prev_down = down_ref[2 * before + (core ^ orientation(down_ref, before))]
    next_down = down_ref[2 * after + (core ^ orientation(down_ref, after))]
    has_prev = (place > 0) & (prev_down == own_down)
    has_next = (place < lsec_count - 1) & (next_down == own_down)
    odd = lax.rem(place, 2)
    has_lower = sib_down == own_down - 1
    has_upper = sib_down == own_down + 1

    def gather(slot, count):
        meta_ref[FIRST + slot] = count

        def step(bond, carry):
            count, kind = carry
            if slot == OWN:
                there = kind == 0
            elif slot == SIB:
                there = ((kind == 3) & has_lower) | ((kind == 4) & has_upper)
            else:
                lower = odd if slot == FIRST_PAIR else 1 - odd
                there = ((kind == 1) & has_prev & (lower == 1)) | (
                    (kind == 2) & has_next & (lower == 0)
                )
            there = there & (mask_ref[sigma, bond] > 0)

            @pl.when(there)
            def _():
                meta_ref[LIST + count] = bond * 4 + slot

            return count + there.astype(jnp.int32), jnp.where(kind == 4, 0, kind + 1)

        return lax.fori_loop(0, bonds, step, (count, first_kind))[0]

    count = jnp.int32(0)
    for slot in (OWN, SIB, FIRST_PAIR, SECOND_PAIR):
        count = gather(slot, count)
    meta_ref[FIRST + 4] = count
    rows, cols = left_size_ref[sigma], right_size_ref[sigma]
    meta_ref[SIGMA] = sigma
    meta_ref[COUNT] = count
    meta_ref[ROWS] = rows
    meta_ref[COLS] = cols
    meta_ref[SIB_ROWS] = left_size_ref[1 - sigma]
    meta_ref[SIB_COLS] = right_size_ref[1 - sigma]
    wave_copy.wait()


def diag_kernel(meta_ref, diag_ref, diag_far, diag_own, diag_sib):
    states, width = diag_own.shape
    half = width // 2
    sigma, core = meta_ref[SIGMA], lax.axis_index("rsec")
    near = pl.ds(pl.multiple_of(core * half, half), half)
    away = pl.ds(pl.multiple_of((1 - core) * half, half), half)
    for out_ref, slot in ((diag_own, sigma), (diag_sib, 1 - sigma)):

        def fill(i, carry, out_ref=out_ref, slot=slot):
            at = pl.ds(pl.multiple_of(i * CHUNK, CHUNK), CHUNK)
            out_ref[at, near] = diag_ref[slot, at, :]
            out_ref[at, away] = diag_far[slot, at, :]
            return carry

        lax.fori_loop(0, states // CHUNK, fill, 0)


def row(value, index):
    return value[index : index + 1, :]


def stack_rows(shape, rows):
    row_ids = lax.broadcasted_iota(jnp.int32, shape, 0)
    value = jnp.zeros(shape, F32)
    for index, entry in enumerate(rows):
        if entry is not None:
            value = jnp.where(row_ids == index, entry, value)
    return value


class Scalars:
    def __init__(self, totals, cells, state=None):
        self.proj = {}
        self.gram = {}
        self.inverse = []
        self.corr = []
        known = 0
        if state is not None:
            known = MATVECS - 1
            places = [(i, j) for i in range(known) for j in range(known)]
            for index, place in enumerate(places):
                self.proj[place] = row(state, index)
                self.gram[place] = row(state, len(places) + index)
        for k, total in enumerate(totals, known):
            value = (total[0][...] + total[1][...]) / cells
            size, inner = row(value, 0), row(value, 1)
            a = [row(value, 2 + j) for j in range(k)]
            e = [row(value, 4 + j) for j in range(k)]
            f = [row(value, 6 + j) for j in range(k)]
            length = size
            theta = inner
            for j in range(k):
                length = length - 2.0 * a[j] * a[j]
                theta = theta - a[j] * e[j] - a[j] * f[j]
            for i in range(k):
                for j in range(k):
                    length = length + a[i] * a[j] * self.gram[i, j]
                    theta = theta + a[i] * a[j] * self.proj[i, j]
            length = jnp.maximum(length, 0.0)
            square = length + EPSILON
            norm = jnp.sqrt(square)
            for j in range(k):
                up, down, both = e[j], f[j], a[j]
                for i in range(k):
                    up = up - a[i] * self.proj[j, i]
                    down = down - a[i] * self.proj[i, j]
                    both = both - a[i] * self.gram[i, j]
                self.proj[j, k] = up / norm
                self.proj[k, j] = down / norm
                self.gram[j, k] = self.gram[k, j] = both / norm
            self.proj[k, k] = theta / square
            self.gram[k, k] = length / square
            self.inverse.append(1.0 / norm)
            self.corr.append(a)

    def state(self, shape):
        known = MATVECS - 1
        places = [(i, j) for i in range(known) for j in range(known)]
        rows = [self.proj[place] for place in places] + [self.gram[place] for place in places]
        return stack_rows(shape, rows)

    def pack(self, k, shape):
        rows = [self.proj[k - 1, k - 1], *self.inverse[:k]]
        for a in self.corr[:k]:
            rows += a
        return stack_rows(shape, rows)

    @classmethod
    def unpack(cls, k, ref):
        numbers = cls([], 1.0)
        value = ref[...]
        numbers.theta = row(value, 0)[:, :1]
        numbers.inverse = [row(value, 1 + i) for i in range(k)]
        place = 1 + k
        for step in range(k):
            numbers.corr.append([row(value, place + j) for j in range(step)])
            place += step
        return numbers

    def basis(self, k, fields):
        done = []
        for step in range(k + 1):
            value = fields[step]
            for j in range(step):
                value = value - self.corr[step][j][:, :1] * done[j]
            done.append(value * self.inverse[step][:, :1])
        return done


def left_kernel(meta_ref, left_ref, _, left_high, left_low, left_tail, left_buf, sems):
    states = left_buf.shape[1]
    sigma, count, rows = meta_ref[SIGMA], meta_ref[COUNT], meta_ref[ROWS]
    stride = packed_rows(rows)

    def each(i, act):
        bond = (meta_ref[LIST + i] >> 2)
        at = i & (BUFFERS - 1)
        for p in range(states // TILE):
            part = pl.ds(p * TILE, TILE)

            @pl.when(rows > p * TILE)
            def _(part=part, p=p):
                act(
                    pltpu.make_async_copy(
                        left_ref.at[bond, sigma, part], left_buf.at[at, part], sems.at[p, at]
                    )
                )

    def start(i):
        @pl.when(i < count)
        def _():
            each(i, lambda copy: copy.start())

    for i in range(BUFFERS - 1):
        start(jnp.int32(i))

    def step(i, carry):
        at = i & (BUFFERS - 1)
        start(i + BUFFERS - 1)
        each(i, lambda copy: copy.wait())

        def chunk(t, inner):
            high, low = split(left_buf[at, pl.ds(pl.multiple_of(t * CHUNK, CHUNK), CHUNK), :])
            to = pl.ds(pl.multiple_of(i * stride + t * CHUNK, 16), CHUNK)
            left_high[to, :] = high[:, :SIDE]
            left_low[to, :] = low[:, :SIDE]
            left_tail[to, :] = jnp.concatenate([high[:, SIDE:], low[:, SIDE:]], axis=1)
            return inner

        lax.fori_loop(0, (rows + CHUNK - 1) // CHUNK, chunk, 0)
        return carry

    lax.fori_loop(0, count, step, 0)


def right_kernel(meta_ref, right_ref, far_ref, right_high, right_low, right_buf, sems):
    width, half = right_buf.shape[1], right_ref.shape[2]
    sigma, count = meta_ref[SIGMA], meta_ref[COUNT]
    core = lax.axis_index("rsec")
    thin = meta_ref[COLS] <= HALF

    def each(i, act):
        bond = (meta_ref[LIST + i] >> 2)
        for ref, place, sem in ((right_ref, core, 0), (far_ref, 1 - core, 1)):
            part = pl.ds(pl.multiple_of(place * half, half), half)

            @pl.when(jnp.logical_not(thin) | (place == 0))
            def _(ref=ref, part=part, sem=sem):
                act(
                    pltpu.make_async_copy(ref.at[bond, sigma], right_buf.at[i, part], sems.at[sem, i])
                )

    def start(i, carry):
        each(i, lambda copy: copy.start())
        return carry

    lax.fori_loop(0, count, start, 0)

    def step(i, carry):
        each(i, lambda copy: copy.wait())

        @pl.when(thin)
        def _():
            for first in range(0, HALF, CHUNK):
                high, low = split(right_buf[i, pl.ds(first, CHUNK), :])
                right_high[i, pl.ds(first, CHUNK), :] = high
                right_high[i, pl.ds(HALF + first, CHUNK), :] = low

        @pl.when(jnp.logical_not(thin))
        def _():
            for first in range(0, width, CHUNK):
                at = pl.ds(first, CHUNK)
                right_high[i, at, :], right_low[i, at, :] = split(right_buf[i, at, :])

        return carry

    lax.fori_loop(0, count, step, 0)


def packed_rows(rows):
    return ((rows + 15) // 16) * 16


def fold(value):
    return jnp.sum(value.reshape(CHUNK // 8, 8, value.shape[1]), axis=0)


def dots_kernel(k, mpo_count, meta_ref, early_ref, *refs):
    refs, small_ref = list(refs[:-1]), refs[-1]
    numbers = Scalars.unpack(k, refs.pop(0)) if k else None
    raw = [refs.pop(0) for _ in range(k + 1)]
    core = lax.axis_index("rsec")
    zero = jnp.zeros(early_ref.shape[1:], F32)

    def step(i, carry):
        at = pl.ds(pl.multiple_of(i * CHUNK, CHUNK), CHUNK)
        blocks = [ref[at, :] for ref in refs]
        if len(blocks) == 2:
            near, away = blocks
            first, second = jnp.where(core == 0, near, away), jnp.where(core == 0, away, near)
            value = jnp.concatenate([first, second], axis=1)
        else:
            value = blocks[0]
        basis = numbers.basis(k - 1, [ref[at, :] for ref in raw[:k]]) if k else []
        return tuple(c + fold(value * b) for c, b in zip(carry, [raw[k][at, :], *basis]))

    live = (meta_ref[ROWS] + CHUNK - 1) // CHUNK
    late = lax.fori_loop(0, live, step, (zero,) * (1 + k))

    def whole(value):
        return jnp.sum(jnp.sum(value, axis=1, keepdims=True), axis=0, keepdims=True)

    share = 1.0 / mpo_count
    entries = [whole(early_ref[0]) * share, whole(late[0])]
    for j in range(2):
        entries.append(whole(early_ref[1 + j]) * share if j < k else None)
    for j in range(2):
        entries.append(whole(late[1 + j]) if j < k else None)
    for j in range(2):
        entries.append(whole(early_ref[1 + k + j]) * share if j < k else None)
    small_ref[...] = stack_rows(small_ref.shape, entries)


def matvec_kernel(k, cells, near, *refs):
    refs = list(refs)
    slots = (OWN, SIB) if near else (FIRST_PAIR, SECOND_PAIR)
    base = slots[0]
    last = k + 1 == MATVECS
    meta_ref = refs.pop(0)
    left_high, left_low, left_tail = [refs.pop(0) for _ in range(3)]
    right_high, right_low = refs.pop(0), refs.pop(0)
    size_ref = refs.pop(0) if k and not near else None
    totals = [(refs.pop(0), refs.pop(0)) for _ in range(k)] if near else []
    pack_ref = refs.pop(0) if k and not near else None
    raw = [{slot: refs.pop(0) for slot in slots} for _ in range(max(k, 1))]
    images = [{slot: refs.pop(0) for slot in slots} for _ in range(k)]
    precond = {slot: refs.pop(0) for slot in slots} if k else {}
    partial_ref = None if near else refs.pop(0)
    halves = [refs.pop(0), refs.pop(0)] if last and not near else []
    out_ref = None if halves else refs.pop(0)
    early_ref = refs.pop(0) if near else None
    pack_ref = refs.pop(0) if k and near else pack_ref
    keep = near or not last
    new_refs = ({slot: refs.pop(0) for slot in slots} if keep else {}) if k else raw[0]
    if not k and not near:
        size_ref = refs.pop(0)
    if last and near:
        known_ref, state_ref, basis_out, images_out = [refs.pop(0) for _ in range(4)]
    high_ref, low_ref, tail_ref, mid_high, mid_low, order_ref = refs[:6]
    if near:
        size_ref = refs[6]
        sems = refs[7] if last else None
    elif last:
        out_ref = refs[6]
    states, width = out_ref.shape
    rows, cols = meta_ref[ROWS], meta_ref[COLS]
    first_bond, end_bond = meta_ref[FIRST + base], meta_ref[FIRST + base + 2]
    count = end_bond - first_bond
    stride = packed_rows(rows)

    core = lax.axis_index("rsec")
    if near:
        size_ref[2 * OWN], size_ref[2 * OWN + 1] = rows, cols
        size_ref[2 * SIB], size_ref[2 * SIB + 1] = meta_ref[SIB_ROWS], meta_ref[SIB_COLS]
    elif not k:
        for slot in slots:
            note = raw[0][slot][pl.ds(states, NOTE), :HALF]
            size_ref[2 * slot] = jnp.max(note[:1]).astype(jnp.int32)
            size_ref[2 * slot + 1] = jnp.max(note[1:]).astype(jnp.int32)
    def list_bonds(narrow):
        def step(i, place):
            hit = (size_ref[2 * (meta_ref[LIST + i] & 3) + 1] <= HALF) == narrow

            @pl.when(hit)
            def _():
                order_ref[place] = i

            return place + hit.astype(jnp.int32)

        return step

    thin_sources = lax.fori_loop(first_bond, end_bond, list_bonds(True), jnp.int32(0))
    lax.fori_loop(first_bond, end_bond, list_bonds(False), thin_sources)
    if k and near:
        numbers = Scalars(totals, cells)
        theta = numbers.proj[k - 1, k - 1][:, :1]
        pack_ref[...] = numbers.pack(k, pack_ref.shape)
    elif k:
        numbers = Scalars.unpack(k, pack_ref)
        theta = numbers.theta
    zero = jnp.zeros((8, width), F32)

    def prepare(slot, carry):
        def step(i, carry):
            at = pl.ds(pl.multiple_of(i * CHUNK, CHUNK), CHUNK)
            if k:
                basis = numbers.basis(k - 1, [r[slot][at, :] for r in raw])
                image = numbers.basis(k - 1, [r[slot][at, :] for r in images])
                value = (image[-1] - theta * basis[-1]) / jnp.maximum(
                    precond[slot][at, :] - theta, 1.0
                )
                if keep:
                    new_refs[slot][at, :] = value
                if last and near:
                    for which, group in enumerate((basis, image)):
                        for j, block in enumerate(group):
                            block = jnp.where(core == 0, block[:, :HALF], block[:, HALF:])
                            known_ref[which, slot, j, at, :] = block
            else:
                basis, image = [], []
                value = raw[0][slot][at, :]
            high, low = split(value)
            high_ref[slot - base, at, :] = high
            low_ref[slot - base, at, :] = low
            terms = [value * value]
            if slot == OWN:
                terms += [value * b for b in basis] + [value * g for g in image]
            return tuple(c + fold(t) for c, t in zip(carry, terms))

        def dead(i, inner):
            at = pl.ds(pl.multiple_of(i * CHUNK, CHUNK), CHUNK)
            high_ref[slot - base, at, :] = jnp.zeros((CHUNK, width), BF16)
            low_ref[slot - base, at, :] = jnp.zeros((CHUNK, width), BF16)
            if last and near:
                for which in range(2):
                    for j in range(k):
                        known_ref[which, slot, j, at, :] = jnp.zeros((CHUNK, HALF), F32)
            return inner

        live = (size_ref[2 * slot] + CHUNK - 1) // CHUNK
        lax.fori_loop(live, states // CHUNK, dead, 0)
        return lax.fori_loop(0, live, step, carry)

    def dot(a, b):
        return jnp.dot(a, b, preferred_element_type=F32)

    def dot_nt(a, b):
        return lax.dot_general(a, b, (((1,), (1,)), ((), ())), preferred_element_type=F32)

    twice = functools.partial(jnp.concatenate, axis=0)

    def first_stage(slot, deep, narrow):
        begin, end = meta_ref[FIRST + slot], meta_ref[FIRST + 1 + slot]
        at_slot = slot - base
        top, rest = pl.ds(0, SIDE), pl.ds(SIDE, states - SIDE)
        if narrow:
            high_ref[at_slot, :, HALF:] = low_ref[at_slot, :, :HALF]
        if deep:
            tail = high_ref[at_slot, rest, :]
            tail_ref[...] = twice([tail, tail])

        def step(t, carry):
            at = pl.ds(pl.multiple_of(begin * stride + t * PACK, 16), PACK)
            high, low = left_high[at, :], left_low[at, :]
            mid = dot(high, high_ref[at_slot, top, :])
            if deep:
                mid = mid + dot(left_tail[at, :], tail_ref[...])
            if narrow:
                mid = mid[:, :HALF] + mid[:, HALF:] + dot(low, high_ref[at_slot, top, :HALF])
                mid_high[at, :] = jnp.concatenate(split(mid), axis=1)
            else:
                mid = mid + dot(low, high_ref[at_slot, top, :]) + dot(high, low_ref[at_slot, top, :])
                if deep:
                    mid = mid + dot(left_tail[at, : states - SIDE], low_ref[at_slot, rest, :])
                mid_high[at, :], mid_low[at, :] = split(mid)
            return carry

        lax.fori_loop(0, ((end - begin) * stride + PACK - 1) // PACK, step, 0)

    def both(test, action):
        pl.when(test)(lambda: action(True))
        pl.when(jnp.logical_not(test))(lambda: action(False))

    if near:
        own = prepare(OWN, (zero,) * (1 + 2 * k))
        prepare(SIB, (zero,))
    else:
        for slot in slots:
            used = meta_ref[FIRST + 1 + slot] > meta_ref[FIRST + slot]
            pl.when(used)(lambda slot=slot: (prepare(slot, (zero,)), None)[1])

    def from_slot(slot, carry):
        both(
            size_ref[2 * slot] > SIDE,
            lambda deep: both(
                size_ref[2 * slot + 1] <= HALF, lambda narrow: first_stage(slot, deep, narrow)
            ),
        )
        return carry

    lax.fori_loop(base, base + 2, from_slot, 0)
    if last and near:
        sigma = meta_ref[SIGMA]
        outputs = [
            pltpu.make_async_copy(
                known_ref.at[which, slot],
                out.at[pl.ds(0, MATVECS - 1), sigma if slot == OWN else 1 - sigma],
                sems.at[which, slot],
            )
            for which, out in enumerate((basis_out, images_out))
            for slot in (OWN, SIB)
        ]
        for copy in outputs:
            copy.start()
        state_ref[...] = numbers.state(state_ref.shape)

    def clear(i, carry):
        at = pl.ds(pl.multiple_of(i * CHUNK, CHUNK), CHUNK)
        out_ref[at, :] = jnp.zeros((CHUNK, width), F32) if near else partial_ref[at, :]
        return carry

    lax.fori_loop(0, states // CHUNK, clear, 0)
    zeros_at = mid_high.shape[0] - states
    for ref in (mid_high, mid_low):
        ref[pl.ds(zeros_at, states), :] = jnp.zeros((states, width), BF16)

    def second_stage(size, thin):
        to = pl.ds(0, size)

        def product(i, real, narrow):
            bond = order_ref[i]
            at = pl.ds(pl.multiple_of(jnp.where(real, bond * stride, zeros_at), 16), size)
            high = mid_high[at, :]
            lanes = pl.ds(0, HALF if narrow else width)
            right = right_high[bond, :, lanes]
            right_rest = None if thin else right_low[bond, :, lanes]
            if narrow:
                value = dot_nt(high, jnp.concatenate([right, right], axis=1))
                if not thin:
                    value = value + dot_nt(high[:, :HALF], right_rest)
            else:
                value = dot_nt(high, right)
                if not thin:
                    value = value + dot_nt(high, right_rest) + dot_nt(mid_low[at, :], right)
            if thin:
                value = value[:, :HALF] + value[:, HALF:]
                if not narrow:
                    value = value + dot_nt(mid_low[at, :], right[:HALF, :])
            return value

        def run(begin, end, narrow):
            def pair(p, carry):
                one = begin + 2 * p
                real = one + 1 < end
                two = jnp.where(real, one + 1, one)
                value = product(one, True, narrow) + product(two, real, narrow)
                if thin:
                    out_ref[to, :HALF] += value
                else:
                    out_ref[to, :] += value
                return carry

            lax.fori_loop(0, (end - begin + 1) // 2, pair, 0)

        run(0, thin_sources, True)
        run(thin_sources, count, False)

    for size in range(TILE, states + 1, TILE):
        pl.when((rows <= size) & (rows > size - TILE))(
            lambda size=size: both(cols <= HALF, functools.partial(second_stage, size))
        )

    if near:
        for index, entry in enumerate(own):
            early_ref[index] = entry
        if last:
            for copy in outputs:
                copy.wait()
        return

    def finish(i, carry):
        at = pl.ds(pl.multiple_of(i * CHUNK, CHUNK), CHUNK)
        mask = live_mask((CHUNK, width), i * CHUNK, rows, cols)
        value = jnp.where(mask, out_ref[at, :], 0.0)
        if last:
            halves[0][at, :] = jnp.where(core == 0, value[:, :HALF], value[:, HALF:])
            halves[1][at, :] = jnp.where(core == 0, value[:, HALF:], value[:, :HALF])
        else:
            out_ref[at, :] = value
        return carry

    lax.fori_loop(0, (rows + CHUNK - 1) // CHUNK, finish, 0)


def join_kernel(a_ref, b_ref, s0, s1, s2, s3, *refs):
    out_ref = refs[-1]
    states = a_ref.shape[0]
    total = (s0[...] + s1[...]) + (s2[...] + s3[...])
    out_ref[pl.ds(states, NOTE), :HALF] = total
    out_ref[pl.ds(states, NOTE), HALF:] = total

    def step(i, carry):
        at = pl.ds(pl.multiple_of(i * CHUNK, CHUNK), CHUNK)
        out_ref[at, :] = a_ref[at, :] + b_ref[at, :]
        return carry

    lax.fori_loop(0, states // CHUNK, step, 0)


def fill_kernel(cells, meta_ref, *refs):
    total, state_ref = refs[:2], refs[2]
    known_ref, raw_own, raw_sib, *parts = refs[3:9]
    basis_out, images_out, projected_ref, basis_buf, images_buf, sems = refs[-6:]
    last = MATVECS - 1
    sigma = meta_ref[SIGMA]
    numbers = Scalars([total], cells, state_ref[...])
    core = lax.axis_index("rsec")
    states, half = basis_buf.shape[1:]
    lanes = pl.ds(pl.multiple_of(core * half, half), half)
    inverse = numbers.inverse[0][:, :1]
    corr = [a[:, :1] for a in numbers.corr[0]]
    copies = []
    chunks = states // CHUNK
    for slot, raw, image, rows in (
        (OWN, raw_own, parts[:2], meta_ref[ROWS]),
        (SIB, raw_sib, parts[2:], meta_ref[SIB_ROWS]),
    ):

        def step(i, carry, slot=slot, raw=raw, image=image):
            at = pl.ds(pl.multiple_of(i * CHUNK, CHUNK), CHUNK)
            fields = (raw[at, lanes], sum(ref[at, :] for ref in image[1:]) + image[0][at, :])
            for which, buf in enumerate((basis_buf, images_buf)):
                value = fields[which]
                for j in range(last):
                    value = value - corr[j] * known_ref[which, slot, j, at, :]
                buf[slot, at, :] = value * inverse
            return carry

        def dead(i, carry, slot=slot):
            at = pl.ds(pl.multiple_of(i * CHUNK, CHUNK), CHUNK)
            for buf in (basis_buf, images_buf):
                buf[slot, at, :] = jnp.zeros((CHUNK, half), F32)
            return carry

        live = (rows + CHUNK - 1) // CHUNK
        lax.fori_loop(0, live, step, 0)
        lax.fori_loop(live, chunks, dead, 0)
        sector = sigma if slot == OWN else 1 - sigma
        for which, (buf, out) in enumerate(((basis_buf, basis_out), (images_buf, images_out))):
            copies.append(
                pltpu.make_async_copy(buf.at[slot], out.at[last, sector], sems.at[which, slot])
            )
            copies[-1].start()
    shape = projected_ref.shape
    row_ids = lax.broadcasted_iota(jnp.int32, shape, 0)
    col_ids = lax.broadcasted_iota(jnp.int32, shape, 1)
    value = jnp.zeros(shape, F32)
    for i in range(MATVECS):
        for j in range(MATVECS):
            value = jnp.where((row_ids == i) & (col_ids == j), numbers.proj[i, j][:, :1], value)
    projected_ref[...] = value
    for copy in copies:
        copy.wait()


def per_device(
    wavefunction, left_env, right_env, precond_diag, down_charge, bond_mask, left_size, right_size
):
    sectors, states, columns = wavefunction.shape
    bonds = left_env.shape[0]
    lsec_count = lax.axis_size("lsec")
    mpo_count = lax.axis_size("mpo")
    assert sectors == 2 and lax.axis_size("rsec") == 2
    width = 2 * columns
    cells = float(lsec_count * sectors * states * width)
    field = jax.ShapeDtypeStruct((states, width), F32)
    noted = jax.ShapeDtypeStruct((states + NOTE, width), F32)
    half_field = jax.ShapeDtypeStruct((states, columns), F32)
    small = jax.ShapeDtypeStruct((8, 128), F32)
    params = pltpu.CompilerParams(vmem_limit_bytes=18 * 2**20)

    swap = [(0, 1), (1, 0)]
    first_pairs = [(i, i ^ 1) for i in range(lsec_count) if i ^ 1 < lsec_count]
    second_pairs = [(i, j) for a in range(1, lsec_count - 1, 2) for i, j in ((a, a + 1), (a + 1, a))]
    anywhere = pl.BlockSpec(memory_space=pl.ANY)
    in_hbm = pl.BlockSpec(memory_space=pltpu.HBM)

    def hold(value):
        return pltpu.with_memory_space_constraint(value, pltpu.HBM)

    def neighbours(value):
        return lax.ppermute(value, "lsec", first_pairs), lax.ppermute(value, "lsec", second_pairs)

    wave_far = lax.ppermute(wavefunction, "rsec", swap)
    diag_far = lax.ppermute(precond_diag, "rsec", swap)
    mask_rows = bond_mask.T
    small_inputs = [down_charge, mask_rows, left_size, right_size]
    meta, wave_near = pl.pallas_call(
        functools.partial(prep_kernel, lsec_count, bonds),
        out_shape=(
            jax.ShapeDtypeStruct((LIST + bonds,), jnp.int32),
            jax.ShapeDtypeStruct(wavefunction.shape, F32),
        ),
        in_specs=[in_hbm] * 5,
        out_specs=(whole_smem(), whole_vmem()),
        scratch_shapes=[pltpu.SMEM(x.shape, jnp.int32) for x in small_inputs]
        + [pltpu.SemaphoreType.DMA((4,)), pltpu.SemaphoreType.DMA],
        compiler_params=params,
        cost_estimate=pl.CostEstimate(flops=0, transcendentals=0, bytes_accessed=10**6),
        name="prep",
    )(*[hold(x) for x in small_inputs], hold(wavefunction))
    right_send, _, _, _ = lax.optimization_barrier((right_env, wave_far, wave_near, diag_far))
    right_far = lax.ppermute(right_send, "rsec", swap)
    own, sib = pl.pallas_call(
        first_kernel,
        out_shape=(noted, field),
        in_specs=[whole_smem()] + [whole_vmem()] * 2,
        out_specs=(whole_vmem(),) * 2,
        compiler_params=params,
        name="first",
    )(meta, wave_near, wave_far)
    near_waves = neighbours(own)
    raw = [(own, sib, *near_waves)]
    diag_own, diag_sib = pl.pallas_call(
        diag_kernel,
        out_shape=(field,) * 2,
        in_specs=[whole_smem()] + [whole_vmem()] * 2,
        out_specs=(whole_vmem(),) * 2,
        compiler_params=params,
        name="diag",
    )(meta, hold(precond_diag), diag_far)

    near_diags = neighbours(diag_own)

    def mpo_pair(value):
        if mpo_count != 2:
            value = lax.psum(value, "mpo")
            return value, jnp.zeros_like(value)
        return value, lax.ppermute(value, "mpo", swap)

    def lsec_parts(part):
        if lsec_count != 4:
            zero = jnp.zeros_like(part)
            return lax.psum(part, "lsec"), zero, zero, zero
        return (part, *[lax.ppermute(part, "lsec", [(i, i ^ x) for i in range(4)]) for x in (1, 2, 3)])

    def join(value, part, after):
        return pl.pallas_call(
            join_kernel,
            out_shape=noted,
            in_specs=[whole_vmem()] * 6 + [anywhere] * len(after),
            out_specs=whole_vmem(),
            compiler_params=params,
            name="join",
        )(*mpo_pair(value), *lsec_parts(part), *after)

    most = bonds - bonds // 5 if bonds % 5 == 0 else bonds
    packed = most * states + PACK
    lefts = pl.pallas_call(
        left_kernel,
        out_shape=(
            pltpu.VMEM((packed, SIDE), BF16),
            pltpu.VMEM((packed, SIDE), BF16),
            pltpu.VMEM((packed, 2 * (states - SIDE)), BF16),
        ),
        in_specs=[whole_smem(), anywhere, anywhere],
        out_specs=(whole_vmem(),) * 3,
        scratch_shapes=[
            pltpu.VMEM((BUFFERS, states, states), F32),
            pltpu.SemaphoreType.DMA((states // TILE, BUFFERS)),
        ],
        compiler_params=params,
        cost_estimate=pl.CostEstimate(flops=0, transcendentals=0, bytes_accessed=bonds * states * states * 4),
        name="left",
    )(meta, hold(left_env), diag_own)
    rights = pl.pallas_call(
        right_kernel,
        out_shape=(pltpu.VMEM((most, width, width), BF16),) * 2,
        in_specs=[whole_smem(), anywhere, anywhere],
        out_specs=(whole_vmem(),) * 2,
        scratch_shapes=[
            pltpu.VMEM((most, width, width), F32),
            pltpu.SemaphoreType.DMA((2, most)),
        ],
        compiler_params=params,
        cost_estimate=pl.CostEstimate(flops=0, transcendentals=0, bytes_accessed=bonds * width * width * 8),
        name="right",
    )(meta, hold(right_env), right_far)

    def dots(k, early, pack, values):
        operands = [early, *pack, *[group[0] for group in raw], *values]
        return pl.pallas_call(
            functools.partial(dots_kernel, k, mpo_count),
            out_shape=small,
            in_specs=[whole_smem()] + [whole_vmem()] * len(operands),
            out_specs=whole_vmem(),
            compiler_params=params,
            cost_estimate=pl.CostEstimate(
                flops=4 * states * width, transcendentals=0, bytes_accessed=4 * states * width
            ),
            name=f"dots{k}",
        )(meta, *operands)

    out = jax.ShapeDtypeStruct((MATVECS, sectors, states, columns), F32)
    known = jax.ShapeDtypeStruct((2, sectors, MATVECS - 1, states, columns), F32)

    def matvec(k, near, sizes, inputs):
        last = k + 1 == MATVECS
        vmem, scalars = whole_vmem(), whole_smem()
        scratch = [
            pltpu.VMEM((2, states, width), BF16),
            pltpu.VMEM((2, states, width), BF16),
            pltpu.VMEM((2 * (states - SIDE), width), BF16),
            pltpu.VMEM((packed + states, width), BF16),
            pltpu.VMEM((packed + states, width), BF16),
            pltpu.SMEM((bonds,), jnp.int32),
        ]
        fresh = [(field, vmem)] * (2 if k and (near or not last) else 0)
        if near:
            outs = [(field, vmem), (jax.ShapeDtypeStruct((1 + 2 * k, 8, width), F32), vmem)]
            outs += [(small, vmem)] * (1 if k else 0) + fresh
            scratch.append(pltpu.SMEM((8,), jnp.int32))
            if last:
                outs += [(known, vmem), (small, vmem), (out, anywhere), (out, anywhere)]
                scratch.append(pltpu.SemaphoreType.DMA((2, 2)))
        else:
            outs = ([(half_field, vmem)] * 2 if last else [(field, vmem)]) + fresh
            if last:
                scratch.append(pltpu.VMEM((states, width), F32))
            if not k:
                outs.append((jax.ShapeDtypeStruct((8,), jnp.int32), scalars))
        return pl.pallas_call(
            functools.partial(matvec_kernel, k, cells, near),
            out_shape=tuple(shape for shape, _ in outs),
            in_specs=[scalars] + [vmem] * 5 + [scalars] * len(sizes) + [vmem] * len(inputs),
            out_specs=tuple(spec for _, spec in outs),
            scratch_shapes=scratch,
            compiler_params=params,
            cost_estimate=pl.CostEstimate(
                flops=3 * bonds * states * width * (states + width),
                transcendentals=0,
                bytes_accessed=bonds * states * states,
            ),
            name=f"matvec{k}_{'near' if near else 'far'}",
        )(meta, *lefts, *rights, *sizes, *inputs)

    def flatten(groups):
        return [x for group in groups for x in group]

    def step_inputs(slots):
        return [*flatten(group[slots] for group in (*raw, *images)), *precond[slots]]

    near_slots, far_slots = slice(0, 2), slice(2, 4)
    totals, images, sizes, precond = [], [], [], []
    for k in range(MATVECS):
        last = k + 1 == MATVECS
        inputs = step_inputs(far_slots)
        partial, early, *fresh = matvec(k, True, [], [*totals, *step_inputs(near_slots)])
        pack, fresh = (fresh[:1], fresh[1:]) if k else ([], fresh)
        value, *fresh_far = matvec(k, False, sizes, [*pack, *inputs, partial])
        if k == 0:
            sizes = fresh_far
            precond = (diag_own, diag_sib, *near_diags)
        elif not last:
            raw.append((*fresh, *fresh_far))
        if last:
            break
        part = dots(k, early, pack, [value])
        value = join(value, part, [] if k else near_diags)
        beside = lax.ppermute(value, "rsec", swap)
        images.append((value, beside, *neighbours(value)))
        totals += mpo_pair(value[states:, :HALF] + beside[states:, :HALF])

    near, away = value, fresh_far[0]
    own, sib, known_blocks, state, *outs = fresh
    raw.append((own, sib))
    part = dots(MATVECS - 1, early, pack, [near, away])
    away, far_away = mpo_pair(away)
    sib_half = lax.ppermute(away + far_away, "rsec", swap)
    own_half = mpo_pair(near)
    one, two, three, four = lsec_parts(part)
    part = (one + two) + (three + four)
    total = mpo_pair(part + lax.ppermute(part, "rsec", swap))
    operands = [*total, state, known_blocks, own, sib, *own_half, sib_half]
    return pl.pallas_call(
        functools.partial(fill_kernel, cells),
        out_shape=(out, out, jax.ShapeDtypeStruct((MATVECS, MATVECS), F32)),
        in_specs=[whole_smem()] + [whole_vmem()] * len(operands) + [anywhere] * 2,
        out_specs=(anywhere, anywhere, whole_vmem()),
        scratch_shapes=[
            pltpu.VMEM((sectors, states, columns), F32),
            pltpu.VMEM((sectors, states, columns), F32),
            pltpu.SemaphoreType.DMA((2, 2)),
        ],
        input_output_aliases={1 + len(operands): 0, 2 + len(operands): 1},
        compiler_params=params,
        name="fill",
    )(meta, *operands, *outs)


def solution(mesh):
    placed = (
        P(("grp", "lsec"), None, "rsec"),
        P("mpo", ("grp", "lsec"), None, None),
        P("mpo", ("grp", "lsec"), "rsec", None),
        P(("grp", "lsec"), None, "rsec"),
        P("grp"),
        P("mpo", ("grp", "lsec")),
        P(("grp", "lsec")),
        P(("grp", "lsec")),
    )
    return jax.shard_map(
        per_device,
        mesh=mesh,
        in_specs=placed,
        out_specs=(
            P(None, ("grp", "lsec"), None, "rsec"),
            P(None, ("grp", "lsec"), None, "rsec"),
            P("grp", None),
        ),
        check_vma=False,
    )
```

```python
import functools

import jax
import jax.numpy as jnp
from jax import lax
from jax.experimental import pallas as pl
from jax.experimental.pallas import tpu as pltpu
from jax.sharding import PartitionSpec as P

EPSILON = 1e-06
MATVECS = 3
F32 = jnp.float32
BF16 = jnp.bfloat16
SIGMA, COUNT, ROWS, COLS, FIRST, SIB_ROWS, SIB_COLS, LIST = 0, 1, 2, 3, 4, 9, 10, 16
OWN, SIB, FIRST_PAIR, SECOND_PAIR = 0, 1, 2, 3
CHUNK = 64
TILE = 128
SIDE = 256
HALF = 128
NOTE = 8
PACK = 256
BUFFERS = 8


def whole_vmem():
    return pl.BlockSpec(memory_space=pltpu.VMEM)


def whole_smem():
    return pl.BlockSpec(memory_space=pltpu.SMEM)


def split(value):
    high = value.astype(BF16)
    return high, (value - high.astype(F32)).astype(BF16)


def orientation(down_ref, place):
    def step(i, flips):
        straight = (down_ref[2 * i] == down_ref[2 * i - 2]) | (
            down_ref[2 * i + 1] == down_ref[2 * i - 1]
        )
        return jnp.where(straight, flips, 1 - flips)

    return lax.fori_loop(1, place + 1, step, jnp.int32(0))


def live_mask(shape, row0, rows, cols):
    row_ids = row0 + lax.broadcasted_iota(jnp.int32, shape, 0)
    col_ids = lax.broadcasted_iota(jnp.int32, shape, 1)
    return (row_ids < rows) & (col_ids < cols)


def read_small(pairs, sems):
    copies = [pltpu.make_async_copy(*pair, sems.at[i]) for i, pair in enumerate(pairs)]
    for copy in copies:
        copy.start()
    for copy in copies:
        copy.wait()


def first_kernel(meta_ref, wave_ref, wave_far, own_ref, sib_ref):
    states, half = wave_ref.shape[1:]
    sigma, core = meta_ref[SIGMA], lax.axis_index("rsec")
    for out_ref, slot, rows, cols in (
        (own_ref, sigma, meta_ref[ROWS], meta_ref[COLS]),
        (sib_ref, 1 - sigma, meta_ref[SIB_ROWS], meta_ref[SIB_COLS]),
    ):

        def fill(i, carry, out_ref=out_ref, slot=slot, rows=rows, cols=cols):
            at = pl.ds(pl.multiple_of(i * CHUNK, CHUNK), CHUNK)
            for place, wave in ((core, wave_ref), (1 - core, wave_far)):
                lanes = pl.ds(pl.multiple_of(place * half, half), half)
                mask = live_mask((CHUNK, half), i * CHUNK, rows, cols - place * half)
                out_ref[at, lanes] = jnp.where(mask, wave[slot, at, :], 0.0)
            return carry

        lax.fori_loop(0, states // CHUNK, fill, 0)
    note = (NOTE, own_ref.shape[1])
    row_ids = lax.broadcasted_iota(jnp.int32, note, 0)
    own_ref[pl.ds(states, NOTE), :] = jnp.where(
        row_ids == 0, meta_ref[ROWS], meta_ref[COLS]
    ).astype(F32)


def prep_kernel(lsec_count, bonds, down_in, mask_in, left_in, right_in, wave_in, meta_ref, wave_ref,
                down_ref, mask_ref, left_size_ref, right_size_ref, sems, wave_sem):
    wave_copy = pltpu.make_async_copy(wave_in, wave_ref, wave_sem)
    wave_copy.start()
    read_small(
        ((down_in, down_ref), (mask_in, mask_ref), (left_in, left_size_ref), (right_in, right_size_ref)),
        sems,
    )
    place = lax.axis_index("lsec")
    core = lax.axis_index("rsec")
    first_kind = lax.rem(lax.axis_index("mpo") * bonds, 5)
    sigma = core ^ orientation(down_ref, place)
    own_down = down_ref[2 * place + sigma]
    sib_down = down_ref[2 * place + 1 - sigma]
    before = jnp.maximum(place - 1, 0)
    after = jnp.minimum(place + 1, lsec_count - 1)
    prev_down = down_ref[2 * before + (core ^ orientation(down_ref, before))]
    next_down = down_ref[2 * after + (core ^ orientation(down_ref, after))]
    has_prev = (place > 0) & (prev_down == own_down)
    has_next = (place < lsec_count - 1) & (next_down == own_down)
    odd = lax.rem(place, 2)
    has_lower = sib_down == own_down - 1
    has_upper = sib_down == own_down + 1

    def gather(slot, count):
        meta_ref[FIRST + slot] = count

        def step(bond, carry):
            count, kind = carry
            if slot == OWN:
                there = kind == 0
            elif slot == SIB:
                there = ((kind == 3) & has_lower) | ((kind == 4) & has_upper)
            else:
                lower = odd if slot == FIRST_PAIR else 1 - odd
                there = ((kind == 1) & has_prev & (lower == 1)) | (
                    (kind == 2) & has_next & (lower == 0)
                )
            there = there & (mask_ref[sigma, bond] > 0)

            @pl.when(there)
            def _():
                meta_ref[LIST + count] = bond * 4 + slot

            return count + there.astype(jnp.int32), jnp.where(kind == 4, 0, kind + 1)

        return lax.fori_loop(0, bonds, step, (count, first_kind))[0]

    count = jnp.int32(0)
    for slot in (OWN, SIB, FIRST_PAIR, SECOND_PAIR):
        count = gather(slot, count)
    meta_ref[FIRST + 4] = count
    rows, cols = left_size_ref[sigma], right_size_ref[sigma]
    meta_ref[SIGMA] = sigma
    meta_ref[COUNT] = count
    meta_ref[ROWS] = rows
    meta_ref[COLS] = cols
    meta_ref[SIB_ROWS] = left_size_ref[1 - sigma]
    meta_ref[SIB_COLS] = right_size_ref[1 - sigma]
    wave_copy.wait()


def diag_kernel(meta_ref, diag_ref, diag_far, _, diag_own, diag_sib):
    states, width = diag_own.shape
    half = width // 2
    sigma, core = meta_ref[SIGMA], lax.axis_index("rsec")
    near = pl.ds(pl.multiple_of(core * half, half), half)
    away = pl.ds(pl.multiple_of((1 - core) * half, half), half)
    for out_ref, slot in ((diag_own, sigma), (diag_sib, 1 - sigma)):

        def fill(i, carry, out_ref=out_ref, slot=slot):
            at = pl.ds(pl.multiple_of(i * CHUNK, CHUNK), CHUNK)
            out_ref[at, near] = diag_ref[slot, at, :]
            out_ref[at, away] = diag_far[slot, at, :]
            return carry

        lax.fori_loop(0, states // CHUNK, fill, 0)


def row(value, index):
    return value[index : index + 1, :]


def stack_rows(shape, rows):
    row_ids = lax.broadcasted_iota(jnp.int32, shape, 0)
    value = jnp.zeros(shape, F32)
    for index, entry in enumerate(rows):
        if entry is not None:
            value = jnp.where(row_ids == index, entry, value)
    return value


class Scalars:
    def __init__(self, totals, cells, state=None):
        self.proj = {}
        self.gram = {}
        self.inverse = []
        self.corr = []
        known = 0
        if state is not None:
            known = MATVECS - 1
            places = [(i, j) for i in range(known) for j in range(known)]
            for index, place in enumerate(places):
                self.proj[place] = row(state, index)
                self.gram[place] = row(state, len(places) + index)
        for k, total in enumerate(totals, known):
            value = (total[0][...] + total[1][...]) / cells
            size, inner = row(value, 0), row(value, 1)
            a = [row(value, 2 + j) for j in range(k)]
            e = [row(value, 4 + j) for j in range(k)]
            f = [row(value, 6 + j) for j in range(k)]
            length = size
            theta = inner
            for j in range(k):
                length = length - 2.0 * a[j] * a[j]
                theta = theta - a[j] * e[j] - a[j] * f[j]
            for i in range(k):
                for j in range(k):
                    length = length + a[i] * a[j] * self.gram[i, j]
                    theta = theta + a[i] * a[j] * self.proj[i, j]
            length = jnp.maximum(length, 0.0)
            square = length + EPSILON
            norm = jnp.sqrt(square)
            for j in range(k):
                up, down, both = e[j], f[j], a[j]
                for i in range(k):
                    up = up - a[i] * self.proj[j, i]
                    down = down - a[i] * self.proj[i, j]
                    both = both - a[i] * self.gram[i, j]
                self.proj[j, k] = up / norm
                self.proj[k, j] = down / norm
                self.gram[j, k] = self.gram[k, j] = both / norm
            self.proj[k, k] = theta / square
            self.gram[k, k] = length / square
            self.inverse.append(1.0 / norm)
            self.corr.append(a)

    def state(self, shape):
        known = MATVECS - 1
        places = [(i, j) for i in range(known) for j in range(known)]
        rows = [self.proj[place] for place in places] + [self.gram[place] for place in places]
        return stack_rows(shape, rows)

    def pack(self, k, shape):
        rows = [self.proj[k - 1, k - 1], *self.inverse[:k]]
        for a in self.corr[:k]:
            rows += a
        return stack_rows(shape, rows)

    @classmethod
    def unpack(cls, k, ref):
        numbers = cls([], 1.0)
        value = ref[...]
        numbers.theta = row(value, 0)[:, :1]
        numbers.inverse = [row(value, 1 + i) for i in range(k)]
        place = 1 + k
        for step in range(k):
            numbers.corr.append([row(value, place + j) for j in range(step)])
            place += step
        return numbers

    def basis(self, k, fields):
        done = []
        for step in range(k + 1):
            value = fields[step]
            for j in range(step):
                value = value - self.corr[step][j][:, :1] * done[j]
            done.append(value * self.inverse[step][:, :1])
        return done


def left_kernel(meta_ref, left_ref, left_high, left_low, left_tail, left_buf, sems):
    states = left_buf.shape[1]
    sigma, count, rows = meta_ref[SIGMA], meta_ref[COUNT], meta_ref[ROWS]
    stride = packed_rows(rows)

    def each(i, act):
        bond = (meta_ref[LIST + i] >> 2)
        at = i & (BUFFERS - 1)
        for p in range(states // TILE):
            part = pl.ds(p * TILE, TILE)

            @pl.when(rows > p * TILE)
            def _(part=part, p=p):
                act(
                    pltpu.make_async_copy(
                        left_ref.at[bond, sigma, part], left_buf.at[at, part], sems.at[p, at]
                    )
                )

    def start(i):
        @pl.when(i < count)
        def _():
            each(i, lambda copy: copy.start())

    for i in range(BUFFERS - 1):
        start(jnp.int32(i))

    def step(i, carry):
        at = i & (BUFFERS - 1)
        start(i + BUFFERS - 1)
        each(i, lambda copy: copy.wait())

        def chunk(t, inner):
            high, low = split(left_buf[at, pl.ds(pl.multiple_of(t * CHUNK, CHUNK), CHUNK), :])
            to = pl.ds(pl.multiple_of(i * stride + t * CHUNK, 16), CHUNK)
            left_high[to, :] = high[:, :SIDE]
            left_low[to, :] = low[:, :SIDE]
            left_tail[to, :] = jnp.concatenate([high[:, SIDE:], low[:, SIDE:]], axis=1)
            return inner

        lax.fori_loop(0, (rows + CHUNK - 1) // CHUNK, chunk, 0)
        return carry

    lax.fori_loop(0, count, step, 0)


def right_kernel(meta_ref, right_ref, far_ref, right_high, right_low, right_buf, sems):
    width, half = right_buf.shape[1], right_ref.shape[2]
    sigma, count = meta_ref[SIGMA], meta_ref[COUNT]
    core = lax.axis_index("rsec")
    thin = meta_ref[COLS] <= HALF

    def each(i, act):
        bond = (meta_ref[LIST + i] >> 2)
        for ref, place, sem in ((right_ref, core, 0), (far_ref, 1 - core, 1)):
            part = pl.ds(pl.multiple_of(place * half, half), half)

            @pl.when(jnp.logical_not(thin) | (place == 0))
            def _(ref=ref, part=part, sem=sem):
                act(
                    pltpu.make_async_copy(ref.at[bond, sigma], right_buf.at[i, part], sems.at[sem, i])
                )

    def start(i, carry):
        each(i, lambda copy: copy.start())
        return carry

    lax.fori_loop(0, count, start, 0)

    def step(i, carry):
        each(i, lambda copy: copy.wait())

        @pl.when(thin)
        def _():
            for first in range(0, HALF, CHUNK):
                high, low = split(right_buf[i, pl.ds(first, CHUNK), :])
                right_high[i, pl.ds(first, CHUNK), :] = high
                right_high[i, pl.ds(HALF + first, CHUNK), :] = low

        @pl.when(jnp.logical_not(thin))
        def _():
            for first in range(0, width, CHUNK):
                at = pl.ds(first, CHUNK)
                right_high[i, at, :], right_low[i, at, :] = split(right_buf[i, at, :])

        return carry

    lax.fori_loop(0, count, step, 0)


def packed_rows(rows):
    return ((rows + 15) // 16) * 16


def fold(value):
    return jnp.sum(value.reshape(CHUNK // 8, 8, value.shape[1]), axis=0)


def dots_kernel(k, mpo_count, meta_ref, early_ref, *refs):
    refs, small_ref = list(refs[:-1]), refs[-1]
    numbers = Scalars.unpack(k, refs.pop(0)) if k else None
    raw = [refs.pop(0) for _ in range(k + 1)]
    core = lax.axis_index("rsec")
    zero = jnp.zeros(early_ref.shape[1:], F32)

    def step(i, carry):
        at = pl.ds(pl.multiple_of(i * CHUNK, CHUNK), CHUNK)
        blocks = [ref[at, :] for ref in refs]
        if len(blocks) == 2:
            near, away = blocks
            first, second = jnp.where(core == 0, near, away), jnp.where(core == 0, away, near)
            value = jnp.concatenate([first, second], axis=1)
        else:
            value = blocks[0]
        basis = numbers.basis(k - 1, [ref[at, :] for ref in raw[:k]]) if k else []
        return tuple(c + fold(value * b) for c, b in zip(carry, [raw[k][at, :], *basis]))

    live = (meta_ref[ROWS] + CHUNK - 1) // CHUNK
    late = lax.fori_loop(0, live, step, (zero,) * (1 + k))

    def whole(value):
        return jnp.sum(jnp.sum(value, axis=1, keepdims=True), axis=0, keepdims=True)

    share = 1.0 / mpo_count
    entries = [whole(early_ref[0]) * share, whole(late[0])]
    for j in range(2):
        entries.append(whole(early_ref[1 + j]) * share if j < k else None)
    for j in range(2):
        entries.append(whole(late[1 + j]) if j < k else None)
    for j in range(2):
        entries.append(whole(early_ref[1 + k + j]) * share if j < k else None)
    small_ref[...] = stack_rows(small_ref.shape, entries)


def matvec_kernel(k, cells, near, *refs):
    refs = list(refs)
    slots = (OWN, SIB) if near else (FIRST_PAIR, SECOND_PAIR)
    base = slots[0]
    last = k + 1 == MATVECS
    meta_ref = refs.pop(0)
    left_high, left_low, left_tail = [refs.pop(0) for _ in range(3)]
    right_high, right_low = refs.pop(0), refs.pop(0)
    size_ref = refs.pop(0) if k and not near else None
    totals = [(refs.pop(0), refs.pop(0)) for _ in range(k)] if near else []
    pack_ref = refs.pop(0) if k and not near else None
    raw = [{slot: refs.pop(0) for slot in slots} for _ in range(max(k, 1))]
    images = [{slot: refs.pop(0) for slot in slots} for _ in range(k)]
    precond = {slot: refs.pop(0) for slot in slots} if k else {}
    partial_ref = None if near else refs.pop(0)
    if near and not k:
        refs.pop(0)
    halves = [refs.pop(0), refs.pop(0)] if last and not near else []
    out_ref = None if halves else refs.pop(0)
    early_ref = refs.pop(0) if near else None
    pack_ref = refs.pop(0) if k and near else pack_ref
    keep = near or not last
    new_refs = ({slot: refs.pop(0) for slot in slots} if keep else {}) if k else raw[0]
    if not k and not near:
        size_ref = refs.pop(0)
    if last and near:
        known_ref, state_ref, basis_out, images_out = [refs.pop(0) for _ in range(4)]
    high_ref, low_ref, tail_ref, mid_high, mid_low, order_ref = refs[:6]
    if near:
        size_ref = refs[6]
        sems = refs[7] if last else None
    elif last:
        out_ref = refs[6]
    states, width = out_ref.shape
    rows, cols = meta_ref[ROWS], meta_ref[COLS]
    first_bond, end_bond = meta_ref[FIRST + base], meta_ref[FIRST + base + 2]
    count = end_bond - first_bond
    stride = packed_rows(rows)

    core = lax.axis_index("rsec")
    if near:
        size_ref[2 * OWN], size_ref[2 * OWN + 1] = rows, cols
        size_ref[2 * SIB], size_ref[2 * SIB + 1] = meta_ref[SIB_ROWS], meta_ref[SIB_COLS]
    elif not k:
        for slot in slots:
            note = raw[0][slot][pl.ds(states, NOTE), :HALF]
            size_ref[2 * slot] = jnp.max(note[:1]).astype(jnp.int32)
            size_ref[2 * slot + 1] = jnp.max(note[1:]).astype(jnp.int32)
    def list_bonds(narrow):
        def step(i, place):
            hit = (size_ref[2 * (meta_ref[LIST + i] & 3) + 1] <= HALF) == narrow

            @pl.when(hit)
            def _():
                order_ref[place] = i

            return place + hit.astype(jnp.int32)

        return step

    thin_sources = lax.fori_loop(first_bond, end_bond, list_bonds(True), jnp.int32(0))
    lax.fori_loop(first_bond, end_bond, list_bonds(False), thin_sources)
    if k and near:
        numbers = Scalars(totals, cells)
        theta = numbers.proj[k - 1, k - 1][:, :1]
        pack_ref[...] = numbers.pack(k, pack_ref.shape)
    elif k:
        numbers = Scalars.unpack(k, pack_ref)
        theta = numbers.theta
    zero = jnp.zeros((8, width), F32)

    def prepare(slot, carry):
        def step(i, carry):
            at = pl.ds(pl.multiple_of(i * CHUNK, CHUNK), CHUNK)
            if k:
                basis = numbers.basis(k - 1, [r[slot][at, :] for r in raw])
                image = numbers.basis(k - 1, [r[slot][at, :] for r in images])
                value = (image[-1] - theta * basis[-1]) / jnp.maximum(
                    precond[slot][at, :] - theta, 1.0
                )
                if keep:
                    new_refs[slot][at, :] = value
                if last and near:
                    for which, group in enumerate((basis, image)):
                        for j, block in enumerate(group):
                            block = jnp.where(core == 0, block[:, :HALF], block[:, HALF:])
                            known_ref[which, slot, j, at, :] = block
            else:
                basis, image = [], []
                value = raw[0][slot][at, :]
            high, low = split(value)
            high_ref[slot - base, at, :] = high
            low_ref[slot - base, at, :] = low
            terms = [value * value]
            if slot == OWN:
                terms += [value * b for b in basis] + [value * g for g in image]
            return tuple(c + fold(t) for c, t in zip(carry, terms))

        def dead(i, inner):
            at = pl.ds(pl.multiple_of(i * CHUNK, CHUNK), CHUNK)
            high_ref[slot - base, at, :] = jnp.zeros((CHUNK, width), BF16)
            low_ref[slot - base, at, :] = jnp.zeros((CHUNK, width), BF16)
            if last and near:
                for which in range(2):
                    for j in range(k):
                        known_ref[which, slot, j, at, :] = jnp.zeros((CHUNK, HALF), F32)
            return inner

        live = (size_ref[2 * slot] + CHUNK - 1) // CHUNK
        lax.fori_loop(live, states // CHUNK, dead, 0)
        return lax.fori_loop(0, live, step, carry)

    def dot(a, b):
        return jnp.dot(a, b, preferred_element_type=F32)

    def dot_nt(a, b):
        return lax.dot_general(a, b, (((1,), (1,)), ((), ())), preferred_element_type=F32)

    twice = functools.partial(jnp.concatenate, axis=0)

    def first_stage(slot, deep, narrow):
        begin, end = meta_ref[FIRST + slot], meta_ref[FIRST + 1 + slot]
        at_slot = slot - base
        top, rest = pl.ds(0, SIDE), pl.ds(SIDE, states - SIDE)
        if narrow:
            high_ref[at_slot, :, HALF:] = low_ref[at_slot, :, :HALF]
        if deep:
            tail = high_ref[at_slot, rest, :]
            tail_ref[...] = twice([tail, tail])

        def step(t, carry):
            at = pl.ds(pl.multiple_of(begin * stride + t * PACK, 16), PACK)
            high, low = left_high[at, :], left_low[at, :]
            mid = dot(high, high_ref[at_slot, top, :])
            if deep:
                mid = mid + dot(left_tail[at, :], tail_ref[...])
            if narrow:
                mid = mid[:, :HALF] + mid[:, HALF:] + dot(low, high_ref[at_slot, top, :HALF])
                mid_high[at, :] = jnp.concatenate(split(mid), axis=1)
            else:
                mid = mid + dot(low, high_ref[at_slot, top, :]) + dot(high, low_ref[at_slot, top, :])
                if deep:
                    mid = mid + dot(left_tail[at, : states - SIDE], low_ref[at_slot, rest, :])
                mid_high[at, :], mid_low[at, :] = split(mid)
            return carry

        lax.fori_loop(0, ((end - begin) * stride + PACK - 1) // PACK, step, 0)

    def both(test, action):
        pl.when(test)(lambda: action(True))
        pl.when(jnp.logical_not(test))(lambda: action(False))

    if near:
        own = prepare(OWN, (zero,) * (1 + 2 * k))
        prepare(SIB, (zero,))
    else:
        for slot in slots:
            used = meta_ref[FIRST + 1 + slot] > meta_ref[FIRST + slot]
            pl.when(used)(lambda slot=slot: (prepare(slot, (zero,)), None)[1])

    def from_slot(slot, carry):
        both(
            size_ref[2 * slot] > SIDE,
            lambda deep: both(
                size_ref[2 * slot + 1] <= HALF, lambda narrow: first_stage(slot, deep, narrow)
            ),
        )
        return carry

    lax.fori_loop(base, base + 2, from_slot, 0)
    if last and near:
        sigma = meta_ref[SIGMA]
        outputs = [
            pltpu.make_async_copy(
                known_ref.at[which, slot],
                out.at[pl.ds(0, MATVECS - 1), sigma if slot == OWN else 1 - sigma],
                sems.at[which, slot],
            )
            for which, out in enumerate((basis_out, images_out))
            for slot in (OWN, SIB)
        ]
        for copy in outputs:
            copy.start()
        state_ref[...] = numbers.state(state_ref.shape)

    def clear(i, carry):
        at = pl.ds(pl.multiple_of(i * CHUNK, CHUNK), CHUNK)
        out_ref[at, :] = jnp.zeros((CHUNK, width), F32) if near else partial_ref[at, :]
        return carry

    lax.fori_loop(0, states // CHUNK, clear, 0)
    zeros_at = mid_high.shape[0] - states
    for ref in (mid_high, mid_low):
        ref[pl.ds(zeros_at, states), :] = jnp.zeros((states, width), BF16)

    def second_stage(size, thin):
        to = pl.ds(0, size)

        def product(i, real, narrow):
            bond = order_ref[i]
            at = pl.ds(pl.multiple_of(jnp.where(real, bond * stride, zeros_at), 16), size)
            high = mid_high[at, :]
            lanes = pl.ds(0, HALF if narrow else width)
            right = right_high[bond, :, lanes]
            right_rest = None if thin else right_low[bond, :, lanes]
            if narrow:
                value = dot_nt(high, jnp.concatenate([right, right], axis=1))
                if not thin:
                    value = value + dot_nt(high[:, :HALF], right_rest)
            else:
                value = dot_nt(high, right)
                if not thin:
                    value = value + dot_nt(high, right_rest) + dot_nt(mid_low[at, :], right)
            if thin:
                value = value[:, :HALF] + value[:, HALF:]
                if not narrow:
                    value = value + dot_nt(mid_low[at, :], right[:HALF, :])
            return value

        def run(begin, end, narrow):
            def pair(p, carry):
                one = begin + 2 * p
                real = one + 1 < end
                two = jnp.where(real, one + 1, one)
                value = product(one, True, narrow) + product(two, real, narrow)
                if thin:
                    out_ref[to, :HALF] += value
                else:
                    out_ref[to, :] += value
                return carry

            lax.fori_loop(0, (end - begin + 1) // 2, pair, 0)

        run(0, thin_sources, True)
        run(thin_sources, count, False)

    for size in range(TILE, states + 1, TILE):
        pl.when((rows <= size) & (rows > size - TILE))(
            lambda size=size: both(cols <= HALF, functools.partial(second_stage, size))
        )

    if near:
        for index, entry in enumerate(own):
            early_ref[index] = entry
        if last:
            for copy in outputs:
                copy.wait()
        return

    def finish(i, carry):
        at = pl.ds(pl.multiple_of(i * CHUNK, CHUNK), CHUNK)
        mask = live_mask((CHUNK, width), i * CHUNK, rows, cols)
        value = jnp.where(mask, out_ref[at, :], 0.0)
        if last:
            halves[0][at, :] = jnp.where(core == 0, value[:, :HALF], value[:, HALF:])
            halves[1][at, :] = jnp.where(core == 0, value[:, HALF:], value[:, :HALF])
        else:
            out_ref[at, :] = value
        return carry

    lax.fori_loop(0, (rows + CHUNK - 1) // CHUNK, finish, 0)


def join_kernel(a_ref, b_ref, s0, s1, s2, s3, *refs):
    out_ref = refs[-1]
    states = a_ref.shape[0]
    total = (s0[...] + s1[...]) + (s2[...] + s3[...])
    out_ref[pl.ds(states, NOTE), :HALF] = total
    out_ref[pl.ds(states, NOTE), HALF:] = total

    def step(i, carry):
        at = pl.ds(pl.multiple_of(i * CHUNK, CHUNK), CHUNK)
        out_ref[at, :] = a_ref[at, :] + b_ref[at, :]
        return carry

    lax.fori_loop(0, states // CHUNK, step, 0)


def fill_kernel(cells, meta_ref, *refs):
    total, state_ref = refs[:2], refs[2]
    known_ref, raw_own, raw_sib, *parts = refs[3:9]
    basis_out, images_out, projected_ref, basis_buf, images_buf, sems = refs[-6:]
    last = MATVECS - 1
    sigma = meta_ref[SIGMA]
    numbers = Scalars([total], cells, state_ref[...])
    core = lax.axis_index("rsec")
    states, half = basis_buf.shape[1:]
    lanes = pl.ds(pl.multiple_of(core * half, half), half)
    inverse = numbers.inverse[0][:, :1]
    corr = [a[:, :1] for a in numbers.corr[0]]
    copies = []
    chunks = states // CHUNK
    for slot, raw, image, rows in (
        (OWN, raw_own, parts[:2], meta_ref[ROWS]),
        (SIB, raw_sib, parts[2:], meta_ref[SIB_ROWS]),
    ):

        def step(i, carry, slot=slot, raw=raw, image=image):
            at = pl.ds(pl.multiple_of(i * CHUNK, CHUNK), CHUNK)
            fields = (raw[at, lanes], sum(ref[at, :] for ref in image[1:]) + image[0][at, :])
            for which, buf in enumerate((basis_buf, images_buf)):
                value = fields[which]
                for j in range(last):
                    value = value - corr[j] * known_ref[which, slot, j, at, :]
                buf[slot, at, :] = value * inverse
            return carry

        def dead(i, carry, slot=slot):
            at = pl.ds(pl.multiple_of(i * CHUNK, CHUNK), CHUNK)
            for buf in (basis_buf, images_buf):
                buf[slot, at, :] = jnp.zeros((CHUNK, half), F32)
            return carry

        live = (rows + CHUNK - 1) // CHUNK
        lax.fori_loop(0, live, step, 0)
        lax.fori_loop(live, chunks, dead, 0)
        sector = sigma if slot == OWN else 1 - sigma
        for which, (buf, out) in enumerate(((basis_buf, basis_out), (images_buf, images_out))):
            copies.append(
                pltpu.make_async_copy(buf.at[slot], out.at[last, sector], sems.at[which, slot])
            )
            copies[-1].start()
    shape = projected_ref.shape
    row_ids = lax.broadcasted_iota(jnp.int32, shape, 0)
    col_ids = lax.broadcasted_iota(jnp.int32, shape, 1)
    value = jnp.zeros(shape, F32)
    for i in range(MATVECS):
        for j in range(MATVECS):
            value = jnp.where((row_ids == i) & (col_ids == j), numbers.proj[i, j][:, :1], value)
    projected_ref[...] = value
    for copy in copies:
        copy.wait()


def per_device(
    wavefunction, left_env, right_env, precond_diag, down_charge, bond_mask, left_size, right_size
):
    sectors, states, columns = wavefunction.shape
    bonds = left_env.shape[0]
    lsec_count = lax.axis_size("lsec")
    mpo_count = lax.axis_size("mpo")
    assert sectors == 2 and lax.axis_size("rsec") == 2
    width = 2 * columns
    cells = float(lsec_count * sectors * states * width)
    field = jax.ShapeDtypeStruct((states, width), F32)
    noted = jax.ShapeDtypeStruct((states + NOTE, width), F32)
    half_field = jax.ShapeDtypeStruct((states, columns), F32)
    small = jax.ShapeDtypeStruct((8, 128), F32)
    params = pltpu.CompilerParams(vmem_limit_bytes=18 * 2**20)

    swap = [(0, 1), (1, 0)]
    first_pairs = [(i, i ^ 1) for i in range(lsec_count) if i ^ 1 < lsec_count]
    second_pairs = [(i, j) for a in range(1, lsec_count - 1, 2) for i, j in ((a, a + 1), (a + 1, a))]
    anywhere = pl.BlockSpec(memory_space=pl.ANY)
    in_hbm = pl.BlockSpec(memory_space=pltpu.HBM)

    def hold(value):
        return pltpu.with_memory_space_constraint(value, pltpu.HBM)

    def neighbours(value):
        return lax.ppermute(value, "lsec", first_pairs), lax.ppermute(value, "lsec", second_pairs)

    wave_far = lax.ppermute(wavefunction, "rsec", swap)
    diag_far = lax.ppermute(precond_diag, "rsec", swap)
    mask_rows = bond_mask.T
    small_inputs = [down_charge, mask_rows, left_size, right_size]
    meta, wave_near = pl.pallas_call(
        functools.partial(prep_kernel, lsec_count, bonds),
        out_shape=(
            jax.ShapeDtypeStruct((LIST + bonds,), jnp.int32),
            jax.ShapeDtypeStruct(wavefunction.shape, F32),
        ),
        in_specs=[in_hbm] * 5,
        out_specs=(whole_smem(), whole_vmem()),
        scratch_shapes=[pltpu.SMEM(x.shape, jnp.int32) for x in small_inputs]
        + [pltpu.SemaphoreType.DMA((4,)), pltpu.SemaphoreType.DMA],
        compiler_params=params,
        cost_estimate=pl.CostEstimate(flops=0, transcendentals=0, bytes_accessed=10**6),
        name="prep",
    )(*[hold(x) for x in small_inputs], hold(wavefunction))
    right_send, _, _, _ = lax.optimization_barrier((right_env, wave_far, wave_near, diag_far))
    right_far = lax.ppermute(right_send, "rsec", swap)
    own, sib = pl.pallas_call(
        first_kernel,
        out_shape=(noted, field),
        in_specs=[whole_smem()] + [whole_vmem()] * 2,
        out_specs=(whole_vmem(),) * 2,
        compiler_params=params,
        name="first",
    )(meta, wave_near, wave_far)
    near_waves = neighbours(own)
    raw = [(own, sib, *near_waves)]
    def mpo_pair(value):
        if mpo_count != 2:
            value = lax.psum(value, "mpo")
            return value, jnp.zeros_like(value)
        return value, lax.ppermute(value, "mpo", swap)

    def lsec_parts(part):
        if lsec_count != 4:
            zero = jnp.zeros_like(part)
            return lax.psum(part, "lsec"), zero, zero, zero
        return (part, *[lax.ppermute(part, "lsec", [(i, i ^ x) for i in range(4)]) for x in (1, 2, 3)])

    def join(value, part, after):
        return pl.pallas_call(
            join_kernel,
            out_shape=noted,
            in_specs=[whole_vmem()] * 6 + [anywhere] * len(after),
            out_specs=whole_vmem(),
            compiler_params=params,
            name="join",
        )(*mpo_pair(value), *lsec_parts(part), *after)

    most = bonds - bonds // 5 if bonds % 5 == 0 else bonds
    packed = most * states + PACK
    lefts = pl.pallas_call(
        left_kernel,
        out_shape=(
            pltpu.VMEM((packed, SIDE), BF16),
            pltpu.VMEM((packed, SIDE), BF16),
            pltpu.VMEM((packed, 2 * (states - SIDE)), BF16),
        ),
        in_specs=[whole_smem(), anywhere],
        out_specs=(whole_vmem(),) * 3,
        scratch_shapes=[
            pltpu.VMEM((BUFFERS, states, states), F32),
            pltpu.SemaphoreType.DMA((states // TILE, BUFFERS)),
        ],
        compiler_params=params,
        cost_estimate=pl.CostEstimate(flops=0, transcendentals=0, bytes_accessed=bonds * states * states * 4),
        name="left",
    )(meta, hold(left_env))
    rights = pl.pallas_call(
        right_kernel,
        out_shape=(pltpu.VMEM((most, width, width), BF16),) * 2,
        in_specs=[whole_smem(), anywhere, anywhere],
        out_specs=(whole_vmem(),) * 2,
        scratch_shapes=[
            pltpu.VMEM((most, width, width), F32),
            pltpu.SemaphoreType.DMA((2, most)),
        ],
        compiler_params=params,
        cost_estimate=pl.CostEstimate(flops=0, transcendentals=0, bytes_accessed=bonds * width * width * 8),
        name="right",
    )(meta, hold(right_env), right_far)

    diag_own, diag_sib = pl.pallas_call(
        diag_kernel,
        out_shape=(field,) * 2,
        in_specs=[whole_smem()] + [whole_vmem()] * 2 + [anywhere],
        out_specs=(whole_vmem(),) * 2,
        compiler_params=params,
        name="diag",
    )(meta, hold(precond_diag), diag_far, rights[0])
    near_diags = neighbours(diag_own)

    def dots(k, early, pack, values):
        operands = [early, *pack, *[group[0] for group in raw], *values]
        return pl.pallas_call(
            functools.partial(dots_kernel, k, mpo_count),
            out_shape=small,
            in_specs=[whole_smem()] + [whole_vmem()] * len(operands),
            out_specs=whole_vmem(),
            compiler_params=params,
            cost_estimate=pl.CostEstimate(
                flops=4 * states * width, transcendentals=0, bytes_accessed=4 * states * width
            ),
            name=f"dots{k}",
        )(meta, *operands)

    out = jax.ShapeDtypeStruct((MATVECS, sectors, states, columns), F32)
    known = jax.ShapeDtypeStruct((2, sectors, MATVECS - 1, states, columns), F32)

    def matvec(k, near, sizes, inputs, after=()):
        last = k + 1 == MATVECS
        vmem, scalars = whole_vmem(), whole_smem()
        scratch = [
            pltpu.VMEM((2, states, width), BF16),
            pltpu.VMEM((2, states, width), BF16),
            pltpu.VMEM((2 * (states - SIDE), width), BF16),
            pltpu.VMEM((packed + states, width), BF16),
            pltpu.VMEM((packed + states, width), BF16),
            pltpu.SMEM((bonds,), jnp.int32),
        ]
        fresh = [(field, vmem)] * (2 if k and (near or not last) else 0)
        if near:
            outs = [(field, vmem), (jax.ShapeDtypeStruct((1 + 2 * k, 8, width), F32), vmem)]
            outs += [(small, vmem)] * (1 if k else 0) + fresh
            scratch.append(pltpu.SMEM((8,), jnp.int32))
            if last:
                outs += [(known, vmem), (small, vmem), (out, anywhere), (out, anywhere)]
                scratch.append(pltpu.SemaphoreType.DMA((2, 2)))
        else:
            outs = ([(half_field, vmem)] * 2 if last else [(field, vmem)]) + fresh
            if last:
                scratch.append(pltpu.VMEM((states, width), F32))
            if not k:
                outs.append((jax.ShapeDtypeStruct((8,), jnp.int32), scalars))
        return pl.pallas_call(
            functools.partial(matvec_kernel, k, cells, near),
            out_shape=tuple(shape for shape, _ in outs),
            in_specs=[scalars] + [vmem] * 5 + [scalars] * len(sizes) + [vmem] * len(inputs)
            + [anywhere] * len(after),
            out_specs=tuple(spec for _, spec in outs),
            scratch_shapes=scratch,
            compiler_params=params,
            cost_estimate=pl.CostEstimate(
                flops=3 * bonds * states * width * (states + width),
                transcendentals=0,
                bytes_accessed=bonds * states * states,
            ),
            name=f"matvec{k}_{'near' if near else 'far'}",
        )(meta, *lefts, *rights, *sizes, *inputs, *after)

    def flatten(groups):
        return [x for group in groups for x in group]

    def step_inputs(slots):
        return [*flatten(group[slots] for group in (*raw, *images)), *precond[slots]]

    near_slots, far_slots = slice(0, 2), slice(2, 4)
    totals, images, sizes, precond = [], [], [], []
    for k in range(MATVECS):
        last = k + 1 == MATVECS
        inputs = step_inputs(far_slots)
        partial, early, *fresh = matvec(
            k, True, [], [*totals, *step_inputs(near_slots)], [] if k else [diag_own]
        )
        pack, fresh = (fresh[:1], fresh[1:]) if k else ([], fresh)
        value, *fresh_far = matvec(k, False, sizes, [*pack, *inputs, partial])
        if k == 0:
            sizes = fresh_far
            precond = (diag_own, diag_sib, *near_diags)
        elif not last:
            raw.append((*fresh, *fresh_far))
        if last:
            break
        part = dots(k, early, pack, [value])
        value = join(value, part, [] if k else near_diags)
        beside = lax.ppermute(value, "rsec", swap)
        images.append((value, beside, *neighbours(value)))
        totals += mpo_pair(value[states:, :HALF] + beside[states:, :HALF])

    near, away = value, fresh_far[0]
    own, sib, known_blocks, state, *outs = fresh
    raw.append((own, sib))
    part = dots(MATVECS - 1, early, pack, [near, away])
    away, far_away = mpo_pair(away)
    sib_half = lax.ppermute(away + far_away, "rsec", swap)
    own_half = mpo_pair(near)
    one, two, three, four = lsec_parts(part)
    part = (one + two) + (three + four)
    total = mpo_pair(part + lax.ppermute(part, "rsec", swap))
    operands = [*total, state, known_blocks, own, sib, *own_half, sib_half]
    return pl.pallas_call(
        functools.partial(fill_kernel, cells),
        out_shape=(out, out, jax.ShapeDtypeStruct((MATVECS, MATVECS), F32)),
        in_specs=[whole_smem()] + [whole_vmem()] * len(operands) + [anywhere] * 2,
        out_specs=(anywhere, anywhere, whole_vmem()),
        scratch_shapes=[
            pltpu.VMEM((sectors, states, columns), F32),
            pltpu.VMEM((sectors, states, columns), F32),
            pltpu.SemaphoreType.DMA((2, 2)),
        ],
        input_output_aliases={1 + len(operands): 0, 2 + len(operands): 1},
        compiler_params=params,
        name="fill",
    )(meta, *operands, *outs)


def solution(mesh):
    placed = (
        P(("grp", "lsec"), None, "rsec"),
        P("mpo", ("grp", "lsec"), None, None),
        P("mpo", ("grp", "lsec"), "rsec", None),
        P(("grp", "lsec"), None, "rsec"),
        P("grp"),
        P("mpo", ("grp", "lsec")),
        P(("grp", "lsec")),
        P(("grp", "lsec")),
    )
    return jax.shard_map(
        per_device,
        mesh=mesh,
        in_specs=placed,
        out_specs=(
            P(None, ("grp", "lsec"), None, "rsec"),
            P(None, ("grp", "lsec"), None, "rsec"),
            P("grp", None),
        ),
        check_vma=False,
    )
```

```python
import functools

import jax
import jax.numpy as jnp
from jax import lax
from jax.experimental import pallas as pl
from jax.experimental.pallas import tpu as pltpu
from jax.sharding import PartitionSpec as P

EPSILON = 1e-06
MATVECS = 3
F32 = jnp.float32
BF16 = jnp.bfloat16
SIGMA, COUNT, ROWS, COLS, FIRST, SIB_ROWS, SIB_COLS, LIST = 0, 1, 2, 3, 4, 9, 10, 16
OWN, SIB, FIRST_PAIR, SECOND_PAIR = 0, 1, 2, 3
CHUNK = 64
TILE = 128
SIDE = 256
HALF = 128
NOTE = 8
PACK = 256
BUFFERS = 8


def whole_vmem():
    return pl.BlockSpec(memory_space=pltpu.VMEM)


def whole_smem():
    return pl.BlockSpec(memory_space=pltpu.SMEM)


def split(value):
    high = value.astype(BF16)
    return high, (value - high.astype(F32)).astype(BF16)


def orientation(down_ref, place):
    def step(i, flips):
        straight = (down_ref[2 * i] == down_ref[2 * i - 2]) | (
            down_ref[2 * i + 1] == down_ref[2 * i - 1]
        )
        return jnp.where(straight, flips, 1 - flips)

    return lax.fori_loop(1, place + 1, step, jnp.int32(0))


def live_mask(shape, row0, rows, cols):
    row_ids = row0 + lax.broadcasted_iota(jnp.int32, shape, 0)
    col_ids = lax.broadcasted_iota(jnp.int32, shape, 1)
    return (row_ids < rows) & (col_ids < cols)


def read_small(pairs, sems):
    copies = [pltpu.make_async_copy(*pair, sems.at[i]) for i, pair in enumerate(pairs)]
    for copy in copies:
        copy.start()
    for copy in copies:
        copy.wait()


def first_kernel(meta_ref, wave_ref, wave_far, own_ref, sib_ref):
    states, half = wave_ref.shape[1:]
    sigma, core = meta_ref[SIGMA], lax.axis_index("rsec")
    for out_ref, slot, rows, cols in (
        (own_ref, sigma, meta_ref[ROWS], meta_ref[COLS]),
        (sib_ref, 1 - sigma, meta_ref[SIB_ROWS], meta_ref[SIB_COLS]),
    ):

        def fill(i, carry, out_ref=out_ref, slot=slot, rows=rows, cols=cols):
            at = pl.ds(pl.multiple_of(i * CHUNK, CHUNK), CHUNK)
            for place, wave in ((core, wave_ref), (1 - core, wave_far)):
                lanes = pl.ds(pl.multiple_of(place * half, half), half)
                mask = live_mask((CHUNK, half), i * CHUNK, rows, cols - place * half)
                out_ref[at, lanes] = jnp.where(mask, wave[slot, at, :], 0.0)
            return carry

        lax.fori_loop(0, states // CHUNK, fill, 0)
    note = (NOTE, own_ref.shape[1])
    row_ids = lax.broadcasted_iota(jnp.int32, note, 0)
    own_ref[pl.ds(states, NOTE), :] = jnp.where(
        row_ids == 0, meta_ref[ROWS], meta_ref[COLS]
    ).astype(F32)


def prep_kernel(lsec_count, bonds, down_in, mask_in, left_in, right_in, wave_in, meta_ref, wave_ref,
                down_ref, mask_ref, left_size_ref, right_size_ref, sems, wave_sem):
    wave_copy = pltpu.make_async_copy(wave_in, wave_ref, wave_sem)
    wave_copy.start()
    read_small(
        ((down_in, down_ref), (mask_in, mask_ref), (left_in, left_size_ref), (right_in, right_size_ref)),
        sems,
    )
    place = lax.axis_index("lsec")
    core = lax.axis_index("rsec")
    first_kind = lax.rem(lax.axis_index("mpo") * bonds, 5)
    sigma = core ^ orientation(down_ref, place)
    own_down = down_ref[2 * place + sigma]
    sib_down = down_ref[2 * place + 1 - sigma]
    before = jnp.maximum(place - 1, 0)
    after = jnp.minimum(place + 1, lsec_count - 1)
    prev_down = down_ref[2 * before + (core ^ orientation(down_ref, before))]
    next_down = down_ref[2 * after + (core ^ orientation(down_ref, after))]
    has_prev = (place > 0) & (prev_down == own_down)
    has_next = (place < lsec_count - 1) & (next_down == own_down)
    odd = lax.rem(place, 2)
    has_lower = sib_down == own_down - 1
    has_upper = sib_down == own_down + 1

    def gather(slot, count):
        meta_ref[FIRST + slot] = count

        def step(bond, carry):
            count, kind = carry
            if slot == OWN:
                there = kind == 0
            elif slot == SIB:
                there = ((kind == 3) & has_lower) | ((kind == 4) & has_upper)
            else:
                lower = odd if slot == FIRST_PAIR else 1 - odd
                there = ((kind == 1) & has_prev & (lower == 1)) | (
                    (kind == 2) & has_next & (lower == 0)
                )
            there = there & (mask_ref[sigma, bond] > 0)

            @pl.when(there)
            def _():
                meta_ref[LIST + count] = bond * 4 + slot

            return count + there.astype(jnp.int32), jnp.where(kind == 4, 0, kind + 1)

        return lax.fori_loop(0, bonds, step, (count, first_kind))[0]

    count = jnp.int32(0)
    for slot in (OWN, SIB, FIRST_PAIR, SECOND_PAIR):
        count = gather(slot, count)
    meta_ref[FIRST + 4] = count
    rows, cols = left_size_ref[sigma], right_size_ref[sigma]
    meta_ref[SIGMA] = sigma
    meta_ref[COUNT] = count
    meta_ref[ROWS] = rows
    meta_ref[COLS] = cols
    meta_ref[SIB_ROWS] = left_size_ref[1 - sigma]
    meta_ref[SIB_COLS] = right_size_ref[1 - sigma]
    wave_copy.wait()


def diag_kernel(meta_ref, diag_ref, diag_far, diag_own, diag_sib):
    states, width = diag_own.shape
    half = width // 2
    sigma, core = meta_ref[SIGMA], lax.axis_index("rsec")
    near = pl.ds(pl.multiple_of(core * half, half), half)
    away = pl.ds(pl.multiple_of((1 - core) * half, half), half)
    for out_ref, slot in ((diag_own, sigma), (diag_sib, 1 - sigma)):

        def fill(i, carry, out_ref=out_ref, slot=slot):
            at = pl.ds(pl.multiple_of(i * CHUNK, CHUNK), CHUNK)
            out_ref[at, near] = diag_ref[slot, at, :]
            out_ref[at, away] = diag_far[slot, at, :]
            return carry

        lax.fori_loop(0, states // CHUNK, fill, 0)


def row(value, index):
    return value[index : index + 1, :]


def stack_rows(shape, rows):
    row_ids = lax.broadcasted_iota(jnp.int32, shape, 0)
    value = jnp.zeros(shape, F32)
    for index, entry in enumerate(rows):
        if entry is not None:
            value = jnp.where(row_ids == index, entry, value)
    return value


class Scalars:
    def __init__(self, totals, cells, state=None):
        self.proj = {}
        self.gram = {}
        self.inverse = []
        self.corr = []
        known = 0
        if state is not None:
            known = MATVECS - 1
            places = [(i, j) for i in range(known) for j in range(known)]
            for index, place in enumerate(places):
                self.proj[place] = row(state, index)
                self.gram[place] = row(state, len(places) + index)
        for k, total in enumerate(totals, known):
            value = (total[0][...] + total[1][...]) / cells
            size, inner = row(value, 0), row(value, 1)
            a = [row(value, 2 + j) for j in range(k)]
            e = [row(value, 4 + j) for j in range(k)]
            f = [row(value, 6 + j) for j in range(k)]
            length = size
            theta = inner
            for j in range(k):
                length = length - 2.0 * a[j] * a[j]
                theta = theta - a[j] * e[j] - a[j] * f[j]
            for i in range(k):
                for j in range(k):
                    length = length + a[i] * a[j] * self.gram[i, j]
                    theta = theta + a[i] * a[j] * self.proj[i, j]
            length = jnp.maximum(length, 0.0)
            square = length + EPSILON
            norm = jnp.sqrt(square)
            for j in range(k):
                up, down, both = e[j], f[j], a[j]
                for i in range(k):
                    up = up - a[i] * self.proj[j, i]
                    down = down - a[i] * self.proj[i, j]
                    both = both - a[i] * self.gram[i, j]
                self.proj[j, k] = up / norm
                self.proj[k, j] = down / norm
                self.gram[j, k] = self.gram[k, j] = both / norm
            self.proj[k, k] = theta / square
            self.gram[k, k] = length / square
            self.inverse.append(1.0 / norm)
            self.corr.append(a)

    def state(self, shape):
        known = MATVECS - 1
        places = [(i, j) for i in range(known) for j in range(known)]
        rows = [self.proj[place] for place in places] + [self.gram[place] for place in places]
        return stack_rows(shape, rows)

    def pack(self, k, shape):
        rows = [self.proj[k - 1, k - 1], *self.inverse[:k]]
        for a in self.corr[:k]:
            rows += a
        return stack_rows(shape, rows)

    @classmethod
    def unpack(cls, k, ref):
        numbers = cls([], 1.0)
        value = ref[...]
        numbers.theta = row(value, 0)[:, :1]
        numbers.inverse = [row(value, 1 + i) for i in range(k)]
        place = 1 + k
        for step in range(k):
            numbers.corr.append([row(value, place + j) for j in range(step)])
            place += step
        return numbers

    def basis(self, k, fields):
        done = []
        for step in range(k + 1):
            value = fields[step]
            for j in range(step):
                value = value - self.corr[step][j][:, :1] * done[j]
            done.append(value * self.inverse[step][:, :1])
        return done


def left_kernel(meta_ref, left_ref, left_high, left_low, left_tail, left_buf, sems):
    states = left_buf.shape[1]
    sigma, count, rows = meta_ref[SIGMA], meta_ref[COUNT], meta_ref[ROWS]
    stride = packed_rows(rows)

    def each(i, act):
        bond = (meta_ref[LIST + i] >> 2)
        at = i & (BUFFERS - 1)
        for p in range(states // TILE):
            part = pl.ds(p * TILE, TILE)

            @pl.when(rows > p * TILE)
            def _(part=part, p=p):
                act(
                    pltpu.make_async_copy(
                        left_ref.at[bond, sigma, part], left_buf.at[at, part], sems.at[p, at]
                    )
                )

    def start(i):
        @pl.when(i < count)
        def _():
            each(i, lambda copy: copy.start())

    for i in range(BUFFERS - 1):
        start(jnp.int32(i))

    def step(i, carry):
        at = i & (BUFFERS - 1)
        start(i + BUFFERS - 1)
        each(i, lambda copy: copy.wait())

        def chunk(t, inner):
            high, low = split(left_buf[at, pl.ds(pl.multiple_of(t * CHUNK, CHUNK), CHUNK), :])
            to = pl.ds(pl.multiple_of(i * stride + t * CHUNK, 16), CHUNK)
            left_high[to, :] = high[:, :SIDE]
            left_low[to, :] = low[:, :SIDE]
            left_tail[to, :] = jnp.concatenate([high[:, SIDE:], low[:, SIDE:]], axis=1)
            return inner

        lax.fori_loop(0, (rows + CHUNK - 1) // CHUNK, chunk, 0)
        return carry

    lax.fori_loop(0, count, step, 0)


def right_kernel(meta_ref, right_ref, far_ref, right_high, right_low, right_buf, sems):
    width, half = right_buf.shape[1], right_ref.shape[2]
    sigma, count = meta_ref[SIGMA], meta_ref[COUNT]
    core = lax.axis_index("rsec")
    thin = meta_ref[COLS] <= HALF

    def each(i, act):
        bond = (meta_ref[LIST + i] >> 2)
        for ref, place, sem in ((right_ref, core, 0), (far_ref, 1 - core, 1)):
            part = pl.ds(pl.multiple_of(place * half, half), half)

            @pl.when(jnp.logical_not(thin) | (place == 0))
            def _(ref=ref, part=part, sem=sem):
                act(
                    pltpu.make_async_copy(ref.at[bond, sigma], right_buf.at[i, part], sems.at[sem, i])
                )

    def start(i, carry):
        each(i, lambda copy: copy.start())
        return carry

    lax.fori_loop(0, count, start, 0)

    def step(i, carry):
        each(i, lambda copy: copy.wait())

        @pl.when(thin)
        def _():
            for first in range(0, HALF, CHUNK):
                high, low = split(right_buf[i, pl.ds(first, CHUNK), :])
                right_high[i, pl.ds(first, CHUNK), :] = high
                right_high[i, pl.ds(HALF + first, CHUNK), :] = low

        @pl.when(jnp.logical_not(thin))
        def _():
            for first in range(0, width, CHUNK):
                at = pl.ds(first, CHUNK)
                right_high[i, at, :], right_low[i, at, :] = split(right_buf[i, at, :])

        return carry

    lax.fori_loop(0, count, step, 0)


def packed_rows(rows):
    return ((rows + 15) // 16) * 16


def fold(value):
    return jnp.sum(value.reshape(CHUNK // 8, 8, value.shape[1]), axis=0)


def dots_kernel(k, mpo_count, meta_ref, early_ref, *refs):
    refs, small_ref = list(refs[:-1]), refs[-1]
    numbers = Scalars.unpack(k, refs.pop(0)) if k else None
    raw = [refs.pop(0) for _ in range(k + 1)]
    core = lax.axis_index("rsec")
    zero = jnp.zeros(early_ref.shape[1:], F32)

    def step(i, carry):
        at = pl.ds(pl.multiple_of(i * CHUNK, CHUNK), CHUNK)
        blocks = [ref[at, :] for ref in refs]
        if len(blocks) == 2:
            near, away = blocks
            first, second = jnp.where(core == 0, near, away), jnp.where(core == 0, away, near)
            value = jnp.concatenate([first, second], axis=1)
        else:
            value = blocks[0]
        basis = numbers.basis(k - 1, [ref[at, :] for ref in raw[:k]]) if k else []
        return tuple(c + fold(value * b) for c, b in zip(carry, [raw[k][at, :], *basis]))

    live = (meta_ref[ROWS] + CHUNK - 1) // CHUNK
    late = lax.fori_loop(0, live, step, (zero,) * (1 + k))

    def whole(value):
        return jnp.sum(jnp.sum(value, axis=1, keepdims=True), axis=0, keepdims=True)

    share = 1.0 / mpo_count
    entries = [whole(early_ref[0]) * share, whole(late[0])]
    for j in range(2):
        entries.append(whole(early_ref[1 + j]) * share if j < k else None)
    for j in range(2):
        entries.append(whole(late[1 + j]) if j < k else None)
    for j in range(2):
        entries.append(whole(early_ref[1 + k + j]) * share if j < k else None)
    small_ref[...] = stack_rows(small_ref.shape, entries)


def matvec_kernel(k, cells, near, *refs):
    refs = list(refs)
    slots = (OWN, SIB) if near else (FIRST_PAIR, SECOND_PAIR)
    base = slots[0]
    last = k + 1 == MATVECS
    meta_ref = refs.pop(0)
    left_high, left_low, left_tail = [refs.pop(0) for _ in range(3)]
    right_high, right_low = refs.pop(0), refs.pop(0)
    size_ref = refs.pop(0) if k and not near else None
    totals = [(refs.pop(0), refs.pop(0)) for _ in range(k)] if near else []
    pack_ref = refs.pop(0) if k and not near else None
    raw = [{slot: refs.pop(0) for slot in slots} for _ in range(max(k, 1))]
    images = [{slot: refs.pop(0) for slot in slots} for _ in range(k)]
    precond = {slot: refs.pop(0) for slot in slots} if k else {}
    partial_ref = None if near else refs.pop(0)
    halves = [refs.pop(0), refs.pop(0)] if last and not near else []
    out_ref = None if halves else refs.pop(0)
    early_ref = refs.pop(0) if near else None
    pack_ref = refs.pop(0) if k and near else pack_ref
    keep = near or not last
    new_refs = ({slot: refs.pop(0) for slot in slots} if keep else {}) if k else raw[0]
    if not k and not near:
        size_ref = refs.pop(0)
    if last and near:
        known_ref, state_ref, basis_out, images_out = [refs.pop(0) for _ in range(4)]
    high_ref, low_ref, tail_ref, mid_high, mid_low, order_ref = refs[:6]
    if near:
        size_ref = refs[6]
        sems = refs[7] if last else None
    elif last:
        out_ref = refs[6]
    states, width = out_ref.shape
    rows, cols = meta_ref[ROWS], meta_ref[COLS]
    first_bond, end_bond = meta_ref[FIRST + base], meta_ref[FIRST + base + 2]
    count = end_bond - first_bond
    stride = packed_rows(rows)

    core = lax.axis_index("rsec")
    if near:
        size_ref[2 * OWN], size_ref[2 * OWN + 1] = rows, cols
        size_ref[2 * SIB], size_ref[2 * SIB + 1] = meta_ref[SIB_ROWS], meta_ref[SIB_COLS]
    elif not k:
        for slot in slots:
            note = raw[0][slot][pl.ds(states, NOTE), :HALF]
            size_ref[2 * slot] = jnp.max(note[:1]).astype(jnp.int32)
            size_ref[2 * slot + 1] = jnp.max(note[1:]).astype(jnp.int32)
    def list_bonds(narrow):
        def step(i, place):
            hit = (size_ref[2 * (meta_ref[LIST + i] & 3) + 1] <= HALF) == narrow

            @pl.when(hit)
            def _():
                order_ref[place] = i

            return place + hit.astype(jnp.int32)

        return step

    thin_sources = lax.fori_loop(first_bond, end_bond, list_bonds(True), jnp.int32(0))
    lax.fori_loop(first_bond, end_bond, list_bonds(False), thin_sources)
    if k and near:
        numbers = Scalars(totals, cells)
        theta = numbers.proj[k - 1, k - 1][:, :1]
        pack_ref[...] = numbers.pack(k, pack_ref.shape)
    elif k:
        numbers = Scalars.unpack(k, pack_ref)
        theta = numbers.theta
    zero = jnp.zeros((8, width), F32)

    def prepare(slot, carry):
        def step(i, carry):
            at = pl.ds(pl.multiple_of(i * CHUNK, CHUNK), CHUNK)
            if k:
                basis = numbers.basis(k - 1, [r[slot][at, :] for r in raw])
                image = numbers.basis(k - 1, [r[slot][at, :] for r in images])
                value = (image[-1] - theta * basis[-1]) / jnp.maximum(
                    precond[slot][at, :] - theta, 1.0
                )
                if keep:
                    new_refs[slot][at, :] = value
                if last and near:
                    for which, group in enumerate((basis, image)):
                        for j, block in enumerate(group):
                            block = jnp.where(core == 0, block[:, :HALF], block[:, HALF:])
                            known_ref[which, slot, j, at, :] = block
            else:
                basis, image = [], []
                value = raw[0][slot][at, :]
            high, low = split(value)
            high_ref[slot - base, at, :] = high
            low_ref[slot - base, at, :] = low
            terms = [value * value]
            if slot == OWN:
                terms += [value * b for b in basis] + [value * g for g in image]
            return tuple(c + fold(t) for c, t in zip(carry, terms))

        def dead(i, inner):
            at = pl.ds(pl.multiple_of(i * CHUNK, CHUNK), CHUNK)
            high_ref[slot - base, at, :] = jnp.zeros((CHUNK, width), BF16)
            low_ref[slot - base, at, :] = jnp.zeros((CHUNK, width), BF16)
            if last and near:
                for which in range(2):
                    for j in range(k):
                        known_ref[which, slot, j, at, :] = jnp.zeros((CHUNK, HALF), F32)
            return inner

        live = (size_ref[2 * slot] + CHUNK - 1) // CHUNK
        lax.fori_loop(live, states // CHUNK, dead, 0)
        return lax.fori_loop(0, live, step, carry)

    def dot(a, b):
        return jnp.dot(a, b, preferred_element_type=F32)

    def dot_nt(a, b):
        return lax.dot_general(a, b, (((1,), (1,)), ((), ())), preferred_element_type=F32)

    twice = functools.partial(jnp.concatenate, axis=0)

    def first_stage(slot, deep, narrow):
        begin, end = meta_ref[FIRST + slot], meta_ref[FIRST + 1 + slot]
        at_slot = slot - base
        top, rest = pl.ds(0, SIDE), pl.ds(SIDE, states - SIDE)
        if narrow:
            high_ref[at_slot, :, HALF:] = low_ref[at_slot, :, :HALF]
        if deep:
            tail = high_ref[at_slot, rest, :]
            tail_ref[...] = twice([tail, tail])

        def step(t, carry):
            at = pl.ds(pl.multiple_of(begin * stride + t * PACK, 16), PACK)
            high, low = left_high[at, :], left_low[at, :]
            mid = dot(high, high_ref[at_slot, top, :])
            if deep:
                mid = mid + dot(left_tail[at, :], tail_ref[...])
            if narrow:
                mid = mid[:, :HALF] + mid[:, HALF:] + dot(low, high_ref[at_slot, top, :HALF])
                mid_high[at, :] = jnp.concatenate(split(mid), axis=1)
            else:
                mid = mid + dot(low, high_ref[at_slot, top, :]) + dot(high, low_ref[at_slot, top, :])
                if deep:
                    mid = mid + dot(left_tail[at, : states - SIDE], low_ref[at_slot, rest, :])
                mid_high[at, :], mid_low[at, :] = split(mid)
            return carry

        lax.fori_loop(0, ((end - begin) * stride + PACK - 1) // PACK, step, 0)

    def both(test, action):
        pl.when(test)(lambda: action(True))
        pl.when(jnp.logical_not(test))(lambda: action(False))

    if near:
        own = prepare(OWN, (zero,) * (1 + 2 * k))
        prepare(SIB, (zero,))
    else:
        for slot in slots:
            used = meta_ref[FIRST + 1 + slot] > meta_ref[FIRST + slot]
            pl.when(used)(lambda slot=slot: (prepare(slot, (zero,)), None)[1])

    def from_slot(slot, carry):
        both(
            size_ref[2 * slot] > SIDE,
            lambda deep: both(
                size_ref[2 * slot + 1] <= HALF, lambda narrow: first_stage(slot, deep, narrow)
            ),
        )
        return carry

    lax.fori_loop(base, base + 2, from_slot, 0)
    if last and near:
        sigma = meta_ref[SIGMA]
        outputs = [
            pltpu.make_async_copy(
                known_ref.at[which, slot],
                out.at[pl.ds(0, MATVECS - 1), sigma if slot == OWN else 1 - sigma],
                sems.at[which, slot],
            )
            for which, out in enumerate((basis_out, images_out))
            for slot in (OWN, SIB)
        ]
        for copy in outputs:
            copy.start()
        state_ref[...] = numbers.state(state_ref.shape)

    def clear(i, carry):
        at = pl.ds(pl.multiple_of(i * CHUNK, CHUNK), CHUNK)
        out_ref[at, :] = jnp.zeros((CHUNK, width), F32) if near else partial_ref[at, :]
        return carry

    lax.fori_loop(0, states // CHUNK, clear, 0)
    zeros_at = mid_high.shape[0] - states
    for ref in (mid_high, mid_low):
        ref[pl.ds(zeros_at, states), :] = jnp.zeros((states, width), BF16)

    def second_stage(size, thin):
        to = pl.ds(0, size)

        def product(i, real, narrow):
            bond = order_ref[i]
            at = pl.ds(pl.multiple_of(jnp.where(real, bond * stride, zeros_at), 16), size)
            high = mid_high[at, :]
            lanes = pl.ds(0, HALF if narrow else width)
            right = right_high[bond, :, lanes]
            right_rest = None if thin else right_low[bond, :, lanes]
            if narrow:
                value = dot_nt(high, jnp.concatenate([right, right], axis=1))
                if not thin:
                    value = value + dot_nt(high[:, :HALF], right_rest)
            else:
                value = dot_nt(high, right)
                if not thin:
                    value = value + dot_nt(high, right_rest) + dot_nt(mid_low[at, :], right)
            if thin:
                value = value[:, :HALF] + value[:, HALF:]
                if not narrow:
                    value = value + dot_nt(mid_low[at, :], right[:HALF, :])
            return value

        def run(begin, end, narrow):
            def pair(p, carry):
                one = begin + 2 * p
                real = one + 1 < end
                two = jnp.where(real, one + 1, one)
                value = product(one, True, narrow) + product(two, real, narrow)
                if thin:
                    out_ref[to, :HALF] += value
                else:
                    out_ref[to, :] += value
                return carry

            lax.fori_loop(0, (end - begin + 1) // 2, pair, 0)

        run(0, thin_sources, True)
        run(thin_sources, count, False)

    for size in range(TILE, states + 1, TILE):
        pl.when((rows <= size) & (rows > size - TILE))(
            lambda size=size: both(cols <= HALF, functools.partial(second_stage, size))
        )

    if near:
        for index, entry in enumerate(own):
            early_ref[index] = entry
        if last:
            for copy in outputs:
                copy.wait()
        return

    def finish(i, carry):
        at = pl.ds(pl.multiple_of(i * CHUNK, CHUNK), CHUNK)
        mask = live_mask((CHUNK, width), i * CHUNK, rows, cols)
        value = jnp.where(mask, out_ref[at, :], 0.0)
        if last:
            halves[0][at, :] = jnp.where(core == 0, value[:, :HALF], value[:, HALF:])
            halves[1][at, :] = jnp.where(core == 0, value[:, HALF:], value[:, :HALF])
        else:
            out_ref[at, :] = value
        return carry

    lax.fori_loop(0, (rows + CHUNK - 1) // CHUNK, finish, 0)


def join_kernel(a_ref, b_ref, s0, s1, s2, s3, *refs):
    out_ref = refs[-1]
    states = a_ref.shape[0]
    total = (s0[...] + s1[...]) + (s2[...] + s3[...])
    out_ref[pl.ds(states, NOTE), :HALF] = total
    out_ref[pl.ds(states, NOTE), HALF:] = total

    def step(i, carry):
        at = pl.ds(pl.multiple_of(i * CHUNK, CHUNK), CHUNK)
        out_ref[at, :] = a_ref[at, :] + b_ref[at, :]
        return carry

    lax.fori_loop(0, states // CHUNK, step, 0)


def fill_kernel(cells, meta_ref, *refs):
    total, state_ref = refs[:2], refs[2]
    known_ref, raw_own, raw_sib, *parts = refs[3:9]
    basis_out, images_out, projected_ref, basis_buf, images_buf, sems = refs[-6:]
    last = MATVECS - 1
    sigma = meta_ref[SIGMA]
    numbers = Scalars([total], cells, state_ref[...])
    core = lax.axis_index("rsec")
    states, half = basis_buf.shape[1:]
    lanes = pl.ds(pl.multiple_of(core * half, half), half)
    inverse = numbers.inverse[0][:, :1]
    corr = [a[:, :1] for a in numbers.corr[0]]
    copies = []
    chunks = states // CHUNK
    for slot, raw, image, rows in (
        (OWN, raw_own, parts[:2], meta_ref[ROWS]),
        (SIB, raw_sib, parts[2:], meta_ref[SIB_ROWS]),
    ):

        def step(i, carry, slot=slot, raw=raw, image=image):
            at = pl.ds(pl.multiple_of(i * CHUNK, CHUNK), CHUNK)
            fields = (raw[at, lanes], sum(ref[at, :] for ref in image[1:]) + image[0][at, :])
            for which, buf in enumerate((basis_buf, images_buf)):
                value = fields[which]
                for j in range(last):
                    value = value - corr[j] * known_ref[which, slot, j, at, :]
                buf[slot, at, :] = value * inverse
            return carry

        def dead(i, carry, slot=slot):
            at = pl.ds(pl.multiple_of(i * CHUNK, CHUNK), CHUNK)
            for buf in (basis_buf, images_buf):
                buf[slot, at, :] = jnp.zeros((CHUNK, half), F32)
            return carry

        live = (rows + CHUNK - 1) // CHUNK
        lax.fori_loop(0, live, step, 0)
        lax.fori_loop(live, chunks, dead, 0)
        sector = sigma if slot == OWN else 1 - sigma
        for which, (buf, out) in enumerate(((basis_buf, basis_out), (images_buf, images_out))):
            copies.append(
                pltpu.make_async_copy(buf.at[slot], out.at[last, sector], sems.at[which, slot])
            )
            copies[-1].start()
    shape = projected_ref.shape
    row_ids = lax.broadcasted_iota(jnp.int32, shape, 0)
    col_ids = lax.broadcasted_iota(jnp.int32, shape, 1)
    value = jnp.zeros(shape, F32)
    for i in range(MATVECS):
        for j in range(MATVECS):
            value = jnp.where((row_ids == i) & (col_ids == j), numbers.proj[i, j][:, :1], value)
    projected_ref[...] = value
    for copy in copies:
        copy.wait()


def per_device(
    wavefunction, left_env, right_env, precond_diag, down_charge, bond_mask, left_size, right_size
):
    sectors, states, columns = wavefunction.shape
    bonds = left_env.shape[0]
    lsec_count = lax.axis_size("lsec")
    mpo_count = lax.axis_size("mpo")
    assert sectors == 2 and lax.axis_size("rsec") == 2
    width = 2 * columns
    cells = float(lsec_count * sectors * states * width)
    field = jax.ShapeDtypeStruct((states, width), F32)
    noted = jax.ShapeDtypeStruct((states + NOTE, width), F32)
    half_field = jax.ShapeDtypeStruct((states, columns), F32)
    small = jax.ShapeDtypeStruct((8, 128), F32)
    params = pltpu.CompilerParams(vmem_limit_bytes=18 * 2**20)

    swap = [(0, 1), (1, 0)]
    first_pairs = [(i, i ^ 1) for i in range(lsec_count) if i ^ 1 < lsec_count]
    second_pairs = [(i, j) for a in range(1, lsec_count - 1, 2) for i, j in ((a, a + 1), (a + 1, a))]
    anywhere = pl.BlockSpec(memory_space=pl.ANY)
    in_hbm = pl.BlockSpec(memory_space=pltpu.HBM)

    def hold(value):
        return pltpu.with_memory_space_constraint(value, pltpu.HBM)

    def neighbours(value):
        return lax.ppermute(value, "lsec", first_pairs), lax.ppermute(value, "lsec", second_pairs)

    wave_far = lax.ppermute(wavefunction, "rsec", swap)
    diag_far = lax.ppermute(precond_diag, "rsec", swap)
    mask_rows = bond_mask.T
    small_inputs = [down_charge, mask_rows, left_size, right_size]
    meta, wave_near = pl.pallas_call(
        functools.partial(prep_kernel, lsec_count, bonds),
        out_shape=(
            jax.ShapeDtypeStruct((LIST + bonds,), jnp.int32),
            jax.ShapeDtypeStruct(wavefunction.shape, F32),
        ),
        in_specs=[in_hbm] * 5,
        out_specs=(whole_smem(), whole_vmem()),
        scratch_shapes=[pltpu.SMEM(x.shape, jnp.int32) for x in small_inputs]
        + [pltpu.SemaphoreType.DMA((4,)), pltpu.SemaphoreType.DMA],
        compiler_params=params,
        cost_estimate=pl.CostEstimate(flops=0, transcendentals=0, bytes_accessed=10**6),
        name="prep",
    )(*[hold(x) for x in small_inputs], hold(wavefunction))
    right_send, _, _, _ = lax.optimization_barrier((right_env, wave_far, wave_near, diag_far))
    right_far = lax.ppermute(right_send, "rsec", swap)
    own, sib = pl.pallas_call(
        first_kernel,
        out_shape=(noted, field),
        in_specs=[whole_smem()] + [whole_vmem()] * 2,
        out_specs=(whole_vmem(),) * 2,
        compiler_params=params,
        name="first",
    )(meta, wave_near, wave_far)
    near_waves = neighbours(own)
    raw = [(own, sib, *near_waves)]
    diag_own, diag_sib = pl.pallas_call(
        diag_kernel,
        out_shape=(field,) * 2,
        in_specs=[whole_smem()] + [whole_vmem()] * 2,
        out_specs=(whole_vmem(),) * 2,
        compiler_params=params,
        name="diag",
    )(meta, hold(precond_diag), diag_far)

    near_diags = neighbours(diag_own)

    def mpo_pair(value):
        if mpo_count != 2:
            value = lax.psum(value, "mpo")
            return value, jnp.zeros_like(value)
        return value, lax.ppermute(value, "mpo", swap)

    def lsec_parts(part):
        if lsec_count != 4:
            zero = jnp.zeros_like(part)
            return lax.psum(part, "lsec"), zero, zero, zero
        return (part, *[lax.ppermute(part, "lsec", [(i, i ^ x) for i in range(4)]) for x in (1, 2, 3)])

    def join(value, part, after):
        return pl.pallas_call(
            join_kernel,
            out_shape=noted,
            in_specs=[whole_vmem()] * 6 + [anywhere] * len(after),
            out_specs=whole_vmem(),
            compiler_params=params,
            name="join",
        )(*mpo_pair(value), *lsec_parts(part), *after)

    most = bonds - bonds // 5 if bonds % 5 == 0 else bonds
    packed = most * states + PACK
    lefts = pl.pallas_call(
        left_kernel,
        out_shape=(
            pltpu.VMEM((packed, SIDE), BF16),
            pltpu.VMEM((packed, SIDE), BF16),
            pltpu.VMEM((packed, 2 * (states - SIDE)), BF16),
        ),
        in_specs=[whole_smem(), anywhere],
        out_specs=(whole_vmem(),) * 3,
        scratch_shapes=[
            pltpu.VMEM((BUFFERS, states, states), F32),
            pltpu.SemaphoreType.DMA((states // TILE, BUFFERS)),
        ],
        compiler_params=params,
        cost_estimate=pl.CostEstimate(flops=0, transcendentals=0, bytes_accessed=bonds * states * states * 4),
        name="left",
    )(meta, hold(left_env))
    rights = pl.pallas_call(
        right_kernel,
        out_shape=(pltpu.VMEM((most, width, width), BF16),) * 2,
        in_specs=[whole_smem(), anywhere, anywhere],
        out_specs=(whole_vmem(),) * 2,
        scratch_shapes=[
            pltpu.VMEM((most, width, width), F32),
            pltpu.SemaphoreType.DMA((2, most)),
        ],
        compiler_params=params,
        cost_estimate=pl.CostEstimate(flops=0, transcendentals=0, bytes_accessed=bonds * width * width * 8),
        name="right",
    )(meta, hold(right_env), right_far)

    def dots(k, early, pack, values):
        operands = [early, *pack, *[group[0] for group in raw], *values]
        return pl.pallas_call(
            functools.partial(dots_kernel, k, mpo_count),
            out_shape=small,
            in_specs=[whole_smem()] + [whole_vmem()] * len(operands),
            out_specs=whole_vmem(),
            compiler_params=params,
            cost_estimate=pl.CostEstimate(
                flops=4 * states * width, transcendentals=0, bytes_accessed=4 * states * width
            ),
            name=f"dots{k}",
        )(meta, *operands)

    out = jax.ShapeDtypeStruct((MATVECS, sectors, states, columns), F32)
    known = jax.ShapeDtypeStruct((2, sectors, MATVECS - 1, states, columns), F32)

    def matvec(k, near, sizes, inputs):
        last = k + 1 == MATVECS
        vmem, scalars = whole_vmem(), whole_smem()
        scratch = [
            pltpu.VMEM((2, states, width), BF16),
            pltpu.VMEM((2, states, width), BF16),
            pltpu.VMEM((2 * (states - SIDE), width), BF16),
            pltpu.VMEM((packed + states, width), BF16),
            pltpu.VMEM((packed + states, width), BF16),
            pltpu.SMEM((bonds,), jnp.int32),
        ]
        fresh = [(field, vmem)] * (2 if k and (near or not last) else 0)
        if near:
            outs = [(field, vmem), (jax.ShapeDtypeStruct((1 + 2 * k, 8, width), F32), vmem)]
            outs += [(small, vmem)] * (1 if k else 0) + fresh
            scratch.append(pltpu.SMEM((8,), jnp.int32))
            if last:
                outs += [(known, vmem), (small, vmem), (out, anywhere), (out, anywhere)]
                scratch.append(pltpu.SemaphoreType.DMA((2, 2)))
        else:
            outs = ([(half_field, vmem)] * 2 if last else [(field, vmem)]) + fresh
            if last:
                scratch.append(pltpu.VMEM((states, width), F32))
            if not k:
                outs.append((jax.ShapeDtypeStruct((8,), jnp.int32), scalars))
        return pl.pallas_call(
            functools.partial(matvec_kernel, k, cells, near),
            out_shape=tuple(shape for shape, _ in outs),
            in_specs=[scalars] + [vmem] * 5 + [scalars] * len(sizes) + [vmem] * len(inputs),
            out_specs=tuple(spec for _, spec in outs),
            scratch_shapes=scratch,
            compiler_params=params,
            cost_estimate=pl.CostEstimate(
                flops=3 * bonds * states * width * (states + width),
                transcendentals=0,
                bytes_accessed=bonds * states * states,
            ),
            name=f"matvec{k}_{'near' if near else 'far'}",
        )(meta, *lefts, *rights, *sizes, *inputs)

    def flatten(groups):
        return [x for group in groups for x in group]

    def step_inputs(slots):
        return [*flatten(group[slots] for group in (*raw, *images)), *precond[slots]]

    near_slots, far_slots = slice(0, 2), slice(2, 4)
    totals, images, sizes, precond = [], [], [], []
    for k in range(MATVECS):
        last = k + 1 == MATVECS
        inputs = step_inputs(far_slots)
        partial, early, *fresh = matvec(k, True, [], [*totals, *step_inputs(near_slots)])
        pack, fresh = (fresh[:1], fresh[1:]) if k else ([], fresh)
        value, *fresh_far = matvec(k, False, sizes, [*pack, *inputs, partial])
        if k == 0:
            sizes = fresh_far
            precond = (diag_own, diag_sib, *near_diags)
        elif not last:
            raw.append((*fresh, *fresh_far))
        if last:
            break
        part = dots(k, early, pack, [value])
        value = join(value, part, [] if k else near_diags)
        beside = lax.ppermute(value, "rsec", swap)
        images.append((value, beside, *neighbours(value)))
        totals += mpo_pair(value[states:, :HALF] + beside[states:, :HALF])

    near, away = value, fresh_far[0]
    own, sib, known_blocks, state, *outs = fresh
    raw.append((own, sib))
    part = dots(MATVECS - 1, early, pack, [near, away])
    away, far_away = mpo_pair(away)
    sib_half = lax.ppermute(away + far_away, "rsec", swap)
    own_half = mpo_pair(near)
    one, two, three, four = lsec_parts(part)
    part = (one + two) + (three + four)
    total = mpo_pair(part + lax.ppermute(part, "rsec", swap))
    operands = [*total, state, known_blocks, own, sib, *own_half, sib_half]
    return pl.pallas_call(
        functools.partial(fill_kernel, cells),
        out_shape=(out, out, jax.ShapeDtypeStruct((MATVECS, MATVECS), F32)),
        in_specs=[whole_smem()] + [whole_vmem()] * len(operands) + [anywhere] * 2,
        out_specs=(anywhere, anywhere, whole_vmem()),
        scratch_shapes=[
            pltpu.VMEM((sectors, states, columns), F32),
            pltpu.VMEM((sectors, states, columns), F32),
            pltpu.SemaphoreType.DMA((2, 2)),
        ],
        input_output_aliases={1 + len(operands): 0, 2 + len(operands): 1},
        compiler_params=params,
        name="fill",
    )(meta, *operands, *outs)


def solution(mesh):
    placed = (
        P(("grp", "lsec"), None, "rsec"),
        P("mpo", ("grp", "lsec"), None, None),
        P("mpo", ("grp", "lsec"), "rsec", None),
        P(("grp", "lsec"), None, "rsec"),
        P("grp"),
        P("mpo", ("grp", "lsec")),
        P(("grp", "lsec")),
        P(("grp", "lsec")),
    )
    return jax.shard_map(
        per_device,
        mesh=mesh,
        in_specs=placed,
        out_specs=(
            P(None, ("grp", "lsec"), None, "rsec"),
            P(None, ("grp", "lsec"), None, "rsec"),
            P("grp", None),
        ),
        check_vma=False,
    )
```

```python
import functools

import jax
import jax.numpy as jnp
from jax import lax
from jax.experimental import pallas as pl
from jax.experimental.pallas import tpu as pltpu
from jax.sharding import PartitionSpec as P

EPSILON = 1e-06
MATVECS = 3
F32 = jnp.float32
BF16 = jnp.bfloat16
SIGMA, COUNT, ROWS, COLS, FIRST, SIB_ROWS, SIB_COLS, LIST = 0, 1, 2, 3, 4, 9, 10, 16
OWN, SIB, FIRST_PAIR, SECOND_PAIR = 0, 1, 2, 3
CHUNK = 64
TILE = 128
SIDE = 256
HALF = 128
NOTE = 8
PACK = 256
BUFFERS = 8


def whole_vmem():
    return pl.BlockSpec(memory_space=pltpu.VMEM)


def whole_smem():
    return pl.BlockSpec(memory_space=pltpu.SMEM)


def split(value):
    high = value.astype(BF16)
    return high, (value - high.astype(F32)).astype(BF16)


def orientation(down_ref, place):
    def step(i, flips):
        straight = (down_ref[2 * i] == down_ref[2 * i - 2]) | (
            down_ref[2 * i + 1] == down_ref[2 * i - 1]
        )
        return jnp.where(straight, flips, 1 - flips)

    return lax.fori_loop(1, place + 1, step, jnp.int32(0))


def live_mask(shape, row0, rows, cols):
    row_ids = row0 + lax.broadcasted_iota(jnp.int32, shape, 0)
    col_ids = lax.broadcasted_iota(jnp.int32, shape, 1)
    return (row_ids < rows) & (col_ids < cols)


def read_small(pairs, sems):
    copies = [pltpu.make_async_copy(*pair, sems.at[i]) for i, pair in enumerate(pairs)]
    for copy in copies:
        copy.start()
    for copy in copies:
        copy.wait()


def first_kernel(meta_ref, wave_ref, wave_far, own_ref, sib_ref):
    states, half = wave_ref.shape[1:]
    sigma, core = meta_ref[SIGMA], lax.axis_index("rsec")
    for out_ref, slot, rows, cols in (
        (own_ref, sigma, meta_ref[ROWS], meta_ref[COLS]),
        (sib_ref, 1 - sigma, meta_ref[SIB_ROWS], meta_ref[SIB_COLS]),
    ):

        def fill(i, carry, out_ref=out_ref, slot=slot, rows=rows, cols=cols):
            at = pl.ds(pl.multiple_of(i * CHUNK, CHUNK), CHUNK)
            for place, wave in ((core, wave_ref), (1 - core, wave_far)):
                lanes = pl.ds(pl.multiple_of(place * half, half), half)
                mask = live_mask((CHUNK, half), i * CHUNK, rows, cols - place * half)
                out_ref[at, lanes] = jnp.where(mask, wave[slot, at, :], 0.0)
            return carry

        lax.fori_loop(0, states // CHUNK, fill, 0)
    note = (NOTE, own_ref.shape[1])
    row_ids = lax.broadcasted_iota(jnp.int32, note, 0)
    own_ref[pl.ds(states, NOTE), :] = jnp.where(
        row_ids == 0, meta_ref[ROWS], meta_ref[COLS]
    ).astype(F32)


def prep_kernel(lsec_count, bonds, down_in, mask_in, left_in, right_in, wave_in, meta_ref, wave_ref,
                down_ref, mask_ref, left_size_ref, right_size_ref, sems, wave_sem):
    wave_copy = pltpu.make_async_copy(wave_in, wave_ref, wave_sem)
    wave_copy.start()
    read_small(
        ((down_in, down_ref), (mask_in, mask_ref), (left_in, left_size_ref), (right_in, right_size_ref)),
        sems,
    )
    place = lax.axis_index("lsec")
    core = lax.axis_index("rsec")
    first_kind = lax.rem(lax.axis_index("mpo") * bonds, 5)
    sigma = core ^ orientation(down_ref, place)
    own_down = down_ref[2 * place + sigma]
    sib_down = down_ref[2 * place + 1 - sigma]
    before = jnp.maximum(place - 1, 0)
    after = jnp.minimum(place + 1, lsec_count - 1)
    prev_down = down_ref[2 * before + (core ^ orientation(down_ref, before))]
    next_down = down_ref[2 * after + (core ^ orientation(down_ref, after))]
    has_prev = (place > 0) & (prev_down == own_down)
    has_next = (place < lsec_count - 1) & (next_down == own_down)
    odd = lax.rem(place, 2)
    has_lower = sib_down == own_down - 1
    has_upper = sib_down == own_down + 1

    def gather(slot, count):
        meta_ref[FIRST + slot] = count

        def step(bond, carry):
            count, kind = carry
            if slot == OWN:
                there = kind == 0
            elif slot == SIB:
                there = ((kind == 3) & has_lower) | ((kind == 4) & has_upper)
            else:
                lower = odd if slot == FIRST_PAIR else 1 - odd
                there = ((kind == 1) & has_prev & (lower == 1)) | (
                    (kind == 2) & has_next & (lower == 0)
                )
            there = there & (mask_ref[sigma, bond] > 0)

            @pl.when(there)
            def _():
                meta_ref[LIST + count] = bond * 4 + slot

            return count + there.astype(jnp.int32), jnp.where(kind == 4, 0, kind + 1)

        return lax.fori_loop(0, bonds, step, (count, first_kind))[0]

    count = jnp.int32(0)
    for slot in (OWN, SIB, FIRST_PAIR, SECOND_PAIR):
        count = gather(slot, count)
    meta_ref[FIRST + 4] = count
    rows, cols = left_size_ref[sigma], right_size_ref[sigma]
    meta_ref[SIGMA] = sigma
    meta_ref[COUNT] = count
    meta_ref[ROWS] = rows
    meta_ref[COLS] = cols
    meta_ref[SIB_ROWS] = left_size_ref[1 - sigma]
    meta_ref[SIB_COLS] = right_size_ref[1 - sigma]
    wave_copy.wait()


def diag_kernel(meta_ref, diag_ref, diag_far, _, diag_own, diag_sib):
    states, width = diag_own.shape
    half = width // 2
    sigma, core = meta_ref[SIGMA], lax.axis_index("rsec")
    near = pl.ds(pl.multiple_of(core * half, half), half)
    away = pl.ds(pl.multiple_of((1 - core) * half, half), half)
    for out_ref, slot in ((diag_own, sigma), (diag_sib, 1 - sigma)):

        def fill(i, carry, out_ref=out_ref, slot=slot):
            at = pl.ds(pl.multiple_of(i * CHUNK, CHUNK), CHUNK)
            out_ref[at, near] = diag_ref[slot, at, :]
            out_ref[at, away] = diag_far[slot, at, :]
            return carry

        lax.fori_loop(0, states // CHUNK, fill, 0)


def row(value, index):
    return value[index : index + 1, :]


def stack_rows(shape, rows):
    row_ids = lax.broadcasted_iota(jnp.int32, shape, 0)
    value = jnp.zeros(shape, F32)
    for index, entry in enumerate(rows):
        if entry is not None:
            value = jnp.where(row_ids == index, entry, value)
    return value


class Scalars:
    def __init__(self, totals, cells, state=None):
        self.proj = {}
        self.gram = {}
        self.inverse = []
        self.corr = []
        known = 0
        if state is not None:
            known = MATVECS - 1
            places = [(i, j) for i in range(known) for j in range(known)]
            for index, place in enumerate(places):
                self.proj[place] = row(state, index)
                self.gram[place] = row(state, len(places) + index)
        for k, total in enumerate(totals, known):
            value = (total[0][...] + total[1][...]) / cells
            size, inner = row(value, 0), row(value, 1)
            a = [row(value, 2 + j) for j in range(k)]
            e = [row(value, 4 + j) for j in range(k)]
            f = [row(value, 6 + j) for j in range(k)]
            length = size
            theta = inner
            for j in range(k):
                length = length - 2.0 * a[j] * a[j]
                theta = theta - a[j] * e[j] - a[j] * f[j]
            for i in range(k):
                for j in range(k):
                    length = length + a[i] * a[j] * self.gram[i, j]
                    theta = theta + a[i] * a[j] * self.proj[i, j]
            length = jnp.maximum(length, 0.0)
            square = length + EPSILON
            norm = jnp.sqrt(square)
            for j in range(k):
                up, down, both = e[j], f[j], a[j]
                for i in range(k):
                    up = up - a[i] * self.proj[j, i]
                    down = down - a[i] * self.proj[i, j]
                    both = both - a[i] * self.gram[i, j]
                self.proj[j, k] = up / norm
                self.proj[k, j] = down / norm
                self.gram[j, k] = self.gram[k, j] = both / norm
            self.proj[k, k] = theta / square
            self.gram[k, k] = length / square
            self.inverse.append(1.0 / norm)
            self.corr.append(a)

    def state(self, shape):
        known = MATVECS - 1
        places = [(i, j) for i in range(known) for j in range(known)]
        rows = [self.proj[place] for place in places] + [self.gram[place] for place in places]
        return stack_rows(shape, rows)

    def pack(self, k, shape):
        rows = [self.proj[k - 1, k - 1], *self.inverse[:k]]
        for a in self.corr[:k]:
            rows += a
        return stack_rows(shape, rows)

    @classmethod
    def unpack(cls, k, ref):
        numbers = cls([], 1.0)
        value = ref[...]
        numbers.theta = row(value, 0)[:, :1]
        numbers.inverse = [row(value, 1 + i) for i in range(k)]
        place = 1 + k
        for step in range(k):
            numbers.corr.append([row(value, place + j) for j in range(step)])
            place += step
        return numbers

    def basis(self, k, fields):
        done = []
        for step in range(k + 1):
            value = fields[step]
            for j in range(step):
                value = value - self.corr[step][j][:, :1] * done[j]
            done.append(value * self.inverse[step][:, :1])
        return done


def left_kernel(meta_ref, left_ref, left_high, left_low, left_tail, left_buf, sems):
    states = left_buf.shape[1]
    sigma, count, rows = meta_ref[SIGMA], meta_ref[COUNT], meta_ref[ROWS]
    stride = packed_rows(rows)

    def each(i, act):
        bond = (meta_ref[LIST + i] >> 2)
        at = i & (BUFFERS - 1)
        for p in range(states // TILE):
            part = pl.ds(p * TILE, TILE)

            @pl.when(rows > p * TILE)
            def _(part=part, p=p):
                act(
                    pltpu.make_async_copy(
                        left_ref.at[bond, sigma, part], left_buf.at[at, part], sems.at[p, at]
                    )
                )

    def start(i):
        @pl.when(i < count)
        def _():
            each(i, lambda copy: copy.start())

    for i in range(BUFFERS - 1):
        start(jnp.int32(i))

    def step(i, carry):
        at = i & (BUFFERS - 1)
        start(i + BUFFERS - 1)
        each(i, lambda copy: copy.wait())

        def chunk(t, inner):
            high, low = split(left_buf[at, pl.ds(pl.multiple_of(t * CHUNK, CHUNK), CHUNK), :])
            to = pl.ds(pl.multiple_of(i * stride + t * CHUNK, 16), CHUNK)
            left_high[to, :] = high[:, :SIDE]
            left_low[to, :] = low[:, :SIDE]
            left_tail[to, :] = jnp.concatenate([high[:, SIDE:], low[:, SIDE:]], axis=1)
            return inner

        lax.fori_loop(0, (rows + CHUNK - 1) // CHUNK, chunk, 0)
        return carry

    lax.fori_loop(0, count, step, 0)


def right_kernel(meta_ref, right_ref, far_ref, right_high, right_low, right_buf, sems):
    width, half = right_buf.shape[1], right_ref.shape[2]
    sigma, count = meta_ref[SIGMA], meta_ref[COUNT]
    core = lax.axis_index("rsec")
    thin = meta_ref[COLS] <= HALF

    def each(i, act):
        bond = (meta_ref[LIST + i] >> 2)
        for ref, place, sem in ((right_ref, core, 0), (far_ref, 1 - core, 1)):
            part = pl.ds(pl.multiple_of(place * half, half), half)

            @pl.when(jnp.logical_not(thin) | (place == 0))
            def _(ref=ref, part=part, sem=sem):
                act(
                    pltpu.make_async_copy(ref.at[bond, sigma], right_buf.at[i, part], sems.at[sem, i])
                )

    def start(i, carry):
        each(i, lambda copy: copy.start())
        return carry

    lax.fori_loop(0, count, start, 0)

    def step(i, carry):
        each(i, lambda copy: copy.wait())

        @pl.when(thin)
        def _():
            for first in range(0, HALF, CHUNK):
                high, low = split(right_buf[i, pl.ds(first, CHUNK), :])
                right_high[i, pl.ds(first, CHUNK), :] = high
                right_high[i, pl.ds(HALF + first, CHUNK), :] = low

        @pl.when(jnp.logical_not(thin))
        def _():
            for first in range(0, width, CHUNK):
                at = pl.ds(first, CHUNK)
                right_high[i, at, :], right_low[i, at, :] = split(right_buf[i, at, :])

        return carry

    lax.fori_loop(0, count, step, 0)


def packed_rows(rows):
    return ((rows + 15) // 16) * 16


def fold(value):
    return jnp.sum(value.reshape(CHUNK // 8, 8, value.shape[1]), axis=0)


def dots_kernel(k, mpo_count, meta_ref, early_ref, *refs):
    refs, small_ref = list(refs[:-1]), refs[-1]
    numbers = Scalars.unpack(k, refs.pop(0)) if k else None
    raw = [refs.pop(0) for _ in range(k + 1)]
    core = lax.axis_index("rsec")
    zero = jnp.zeros(early_ref.shape[1:], F32)

    def step(i, carry):
        at = pl.ds(pl.multiple_of(i * CHUNK, CHUNK), CHUNK)
        blocks = [ref[at, :] for ref in refs]
        if len(blocks) == 2:
            near, away = blocks
            first, second = jnp.where(core == 0, near, away), jnp.where(core == 0, away, near)
            value = jnp.concatenate([first, second], axis=1)
        else:
            value = blocks[0]
        basis = numbers.basis(k - 1, [ref[at, :] for ref in raw[:k]]) if k else []
        return tuple(c + fold(value * b) for c, b in zip(carry, [raw[k][at, :], *basis]))

    live = (meta_ref[ROWS] + CHUNK - 1) // CHUNK
    late = lax.fori_loop(0, live, step, (zero,) * (1 + k))

    def whole(value):
        return jnp.sum(jnp.sum(value, axis=1, keepdims=True), axis=0, keepdims=True)

    share = 1.0 / mpo_count
    entries = [whole(early_ref[0]) * share, whole(late[0])]
    for j in range(2):
        entries.append(whole(early_ref[1 + j]) * share if j < k else None)
    for j in range(2):
        entries.append(whole(late[1 + j]) if j < k else None)
    for j in range(2):
        entries.append(whole(early_ref[1 + k + j]) * share if j < k else None)
    small_ref[...] = stack_rows(small_ref.shape, entries)


def matvec_kernel(k, cells, near, *refs):
    refs = list(refs)
    slots = (OWN, SIB) if near else (FIRST_PAIR, SECOND_PAIR)
    base = slots[0]
    last = k + 1 == MATVECS
    meta_ref = refs.pop(0)
    left_high, left_low, left_tail = [refs.pop(0) for _ in range(3)]
    right_high, right_low = refs.pop(0), refs.pop(0)
    size_ref = refs.pop(0) if k and not near else None
    totals = [(refs.pop(0), refs.pop(0)) for _ in range(k)] if near else []
    pack_ref = refs.pop(0) if k and not near else None
    raw = [{slot: refs.pop(0) for slot in slots} for _ in range(max(k, 1))]
    images = [{slot: refs.pop(0) for slot in slots} for _ in range(k)]
    precond = {slot: refs.pop(0) for slot in slots} if k else {}
    partial_ref = None if near else refs.pop(0)
    halves = [refs.pop(0), refs.pop(0)] if last and not near else []
    out_ref = None if halves else refs.pop(0)
    early_ref = refs.pop(0) if near else None
    pack_ref = refs.pop(0) if k and near else pack_ref
    keep = near or not last
    new_refs = ({slot: refs.pop(0) for slot in slots} if keep else {}) if k else raw[0]
    if not k and not near:
        size_ref = refs.pop(0)
    if last and near:
        known_ref, state_ref, basis_out, images_out = [refs.pop(0) for _ in range(4)]
    high_ref, low_ref, tail_ref, mid_high, mid_low, order_ref = refs[:6]
    if near:
        size_ref = refs[6]
        sems = refs[7] if last else None
    elif last:
        out_ref = refs[6]
    states, width = out_ref.shape
    rows, cols = meta_ref[ROWS], meta_ref[COLS]
    first_bond, end_bond = meta_ref[FIRST + base], meta_ref[FIRST + base + 2]
    count = end_bond - first_bond
    stride = packed_rows(rows)

    core = lax.axis_index("rsec")
    if near:
        size_ref[2 * OWN], size_ref[2 * OWN + 1] = rows, cols
        size_ref[2 * SIB], size_ref[2 * SIB + 1] = meta_ref[SIB_ROWS], meta_ref[SIB_COLS]
    elif not k:
        for slot in slots:
            note = raw[0][slot][pl.ds(states, NOTE), :HALF]
            size_ref[2 * slot] = jnp.max(note[:1]).astype(jnp.int32)
            size_ref[2 * slot + 1] = jnp.max(note[1:]).astype(jnp.int32)
    def list_bonds(narrow):
        def step(i, place):
            hit = (size_ref[2 * (meta_ref[LIST + i] & 3) + 1] <= HALF) == narrow

            @pl.when(hit)
            def _():
                order_ref[place] = i

            return place + hit.astype(jnp.int32)

        return step

    thin_sources = lax.fori_loop(first_bond, end_bond, list_bonds(True), jnp.int32(0))
    lax.fori_loop(first_bond, end_bond, list_bonds(False), thin_sources)
    if k and near:
        numbers = Scalars(totals, cells)
        theta = numbers.proj[k - 1, k - 1][:, :1]
        pack_ref[...] = numbers.pack(k, pack_ref.shape)
    elif k:
        numbers = Scalars.unpack(k, pack_ref)
        theta = numbers.theta
    zero = jnp.zeros((8, width), F32)

    def prepare(slot, carry):
        def step(i, carry):
            at = pl.ds(pl.multiple_of(i * CHUNK, CHUNK), CHUNK)
            if k:
                basis = numbers.basis(k - 1, [r[slot][at, :] for r in raw])
                image = numbers.basis(k - 1, [r[slot][at, :] for r in images])
                value = (image[-1] - theta * basis[-1]) / jnp.maximum(
                    precond[slot][at, :] - theta, 1.0
                )
                if keep:
                    new_refs[slot][at, :] = value
                if last and near:
                    for which, group in enumerate((basis, image)):
                        for j, block in enumerate(group):
                            block = jnp.where(core == 0, block[:, :HALF], block[:, HALF:])
                            known_ref[which, slot, j, at, :] = block
            else:
                basis, image = [], []
                value = raw[0][slot][at, :]
            high, low = split(value)
            high_ref[slot - base, at, :] = high
            low_ref[slot - base, at, :] = low
            terms = [value * value]
            if slot == OWN:
                terms += [value * b for b in basis] + [value * g for g in image]
            return tuple(c + fold(t) for c, t in zip(carry, terms))

        def dead(i, inner):
            at = pl.ds(pl.multiple_of(i * CHUNK, CHUNK), CHUNK)
            high_ref[slot - base, at, :] = jnp.zeros((CHUNK, width), BF16)
            low_ref[slot - base, at, :] = jnp.zeros((CHUNK, width), BF16)
            if last and near:
                for which in range(2):
                    for j in range(k):
                        known_ref[which, slot, j, at, :] = jnp.zeros((CHUNK, HALF), F32)
            return inner

        live = (size_ref[2 * slot] + CHUNK - 1) // CHUNK
        lax.fori_loop(live, states // CHUNK, dead, 0)
        return lax.fori_loop(0, live, step, carry)

    def dot(a, b):
        return jnp.dot(a, b, preferred_element_type=F32)

    def dot_nt(a, b):
        return lax.dot_general(a, b, (((1,), (1,)), ((), ())), preferred_element_type=F32)

    twice = functools.partial(jnp.concatenate, axis=0)

    def first_stage(slot, deep, narrow):
        begin, end = meta_ref[FIRST + slot], meta_ref[FIRST + 1 + slot]
        at_slot = slot - base
        top, rest = pl.ds(0, SIDE), pl.ds(SIDE, states - SIDE)
        if narrow:
            high_ref[at_slot, :, HALF:] = low_ref[at_slot, :, :HALF]
        if deep:
            tail = high_ref[at_slot, rest, :]
            tail_ref[...] = twice([tail, tail])

        def step(t, carry):
            at = pl.ds(pl.multiple_of(begin * stride + t * PACK, 16), PACK)
            high, low = left_high[at, :], left_low[at, :]
            mid = dot(high, high_ref[at_slot, top, :])
            if deep:
                mid = mid + dot(left_tail[at, :], tail_ref[...])
            if narrow:
                mid = mid[:, :HALF] + mid[:, HALF:] + dot(low, high_ref[at_slot, top, :HALF])
                mid_high[at, :] = jnp.concatenate(split(mid), axis=1)
            else:
                mid = mid + dot(low, high_ref[at_slot, top, :]) + dot(high, low_ref[at_slot, top, :])
                if deep:
                    mid = mid + dot(left_tail[at, : states - SIDE], low_ref[at_slot, rest, :])
                mid_high[at, :], mid_low[at, :] = split(mid)
            return carry

        lax.fori_loop(0, ((end - begin) * stride + PACK - 1) // PACK, step, 0)

    def both(test, action):
        pl.when(test)(lambda: action(True))
        pl.when(jnp.logical_not(test))(lambda: action(False))

    if near:
        own = prepare(OWN, (zero,) * (1 + 2 * k))
        prepare(SIB, (zero,))
    else:
        for slot in slots:
            used = meta_ref[FIRST + 1 + slot] > meta_ref[FIRST + slot]
            pl.when(used)(lambda slot=slot: (prepare(slot, (zero,)), None)[1])

    def from_slot(slot, carry):
        both(
            size_ref[2 * slot] > SIDE,
            lambda deep: both(
                size_ref[2 * slot + 1] <= HALF, lambda narrow: first_stage(slot, deep, narrow)
            ),
        )
        return carry

    lax.fori_loop(base, base + 2, from_slot, 0)
    if last and near:
        sigma = meta_ref[SIGMA]
        outputs = [
            pltpu.make_async_copy(
                known_ref.at[which, slot],
                out.at[pl.ds(0, MATVECS - 1), sigma if slot == OWN else 1 - sigma],
                sems.at[which, slot],
            )
            for which, out in enumerate((basis_out, images_out))
            for slot in (OWN, SIB)
        ]
        for copy in outputs:
            copy.start()
        state_ref[...] = numbers.state(state_ref.shape)

    def clear(i, carry):
        at = pl.ds(pl.multiple_of(i * CHUNK, CHUNK), CHUNK)
        out_ref[at, :] = jnp.zeros((CHUNK, width), F32) if near else partial_ref[at, :]
        return carry

    lax.fori_loop(0, states // CHUNK, clear, 0)
    zeros_at = mid_high.shape[0] - states
    for ref in (mid_high, mid_low):
        ref[pl.ds(zeros_at, states), :] = jnp.zeros((states, width), BF16)

    def second_stage(size, thin):
        to = pl.ds(0, size)

        def product(i, real, narrow):
            bond = order_ref[i]
            at = pl.ds(pl.multiple_of(jnp.where(real, bond * stride, zeros_at), 16), size)
            high = mid_high[at, :]
            lanes = pl.ds(0, HALF if narrow else width)
            right = right_high[bond, :, lanes]
            right_rest = None if thin else right_low[bond, :, lanes]
            if narrow:
                value = dot_nt(high, jnp.concatenate([right, right], axis=1))
                if not thin:
                    value = value + dot_nt(high[:, :HALF], right_rest)
            else:
                value = dot_nt(high, right)
                if not thin:
                    value = value + dot_nt(high, right_rest) + dot_nt(mid_low[at, :], right)
            if thin:
                value = value[:, :HALF] + value[:, HALF:]
                if not narrow:
                    value = value + dot_nt(mid_low[at, :], right[:HALF, :])
            return value

        def run(begin, end, narrow):
            def pair(p, carry):
                one = begin + 2 * p
                real = one + 1 < end
                two = jnp.where(real, one + 1, one)
                value = product(one, True, narrow) + product(two, real, narrow)
                if thin:
                    out_ref[to, :HALF] += value
                else:
                    out_ref[to, :] += value
                return carry

            lax.fori_loop(0, (end - begin + 1) // 2, pair, 0)

        run(0, thin_sources, True)
        run(thin_sources, count, False)

    for size in range(TILE, states + 1, TILE):
        pl.when((rows <= size) & (rows > size - TILE))(
            lambda size=size: both(cols <= HALF, functools.partial(second_stage, size))
        )

    if near:
        for index, entry in enumerate(own):
            early_ref[index] = entry
        if last:
            for copy in outputs:
                copy.wait()
        return

    def finish(i, carry):
        at = pl.ds(pl.multiple_of(i * CHUNK, CHUNK), CHUNK)
        mask = live_mask((CHUNK, width), i * CHUNK, rows, cols)
        value = jnp.where(mask, out_ref[at, :], 0.0)
        if last:
            halves[0][at, :] = jnp.where(core == 0, value[:, :HALF], value[:, HALF:])
            halves[1][at, :] = jnp.where(core == 0, value[:, HALF:], value[:, :HALF])
        else:
            out_ref[at, :] = value
        return carry

    lax.fori_loop(0, (rows + CHUNK - 1) // CHUNK, finish, 0)


def join_kernel(a_ref, b_ref, s0, s1, s2, s3, *refs):
    out_ref = refs[-1]
    states = a_ref.shape[0]
    total = (s0[...] + s1[...]) + (s2[...] + s3[...])
    out_ref[pl.ds(states, NOTE), :HALF] = total
    out_ref[pl.ds(states, NOTE), HALF:] = total

    def step(i, carry):
        at = pl.ds(pl.multiple_of(i * CHUNK, CHUNK), CHUNK)
        out_ref[at, :] = a_ref[at, :] + b_ref[at, :]
        return carry

    lax.fori_loop(0, states // CHUNK, step, 0)


def fill_kernel(cells, meta_ref, *refs):
    total, state_ref = refs[:2], refs[2]
    known_ref, raw_own, raw_sib, *parts = refs[3:9]
    basis_out, images_out, projected_ref, basis_buf, images_buf, sems = refs[-6:]
    last = MATVECS - 1
    sigma = meta_ref[SIGMA]
    numbers = Scalars([total], cells, state_ref[...])
    core = lax.axis_index("rsec")
    states, half = basis_buf.shape[1:]
    lanes = pl.ds(pl.multiple_of(core * half, half), half)
    inverse = numbers.inverse[0][:, :1]
    corr = [a[:, :1] for a in numbers.corr[0]]
    copies = []
    chunks = states // CHUNK
    for slot, raw, image, rows in (
        (OWN, raw_own, parts[:2], meta_ref[ROWS]),
        (SIB, raw_sib, parts[2:], meta_ref[SIB_ROWS]),
    ):

        def step(i, carry, slot=slot, raw=raw, image=image):
            at = pl.ds(pl.multiple_of(i * CHUNK, CHUNK), CHUNK)
            fields = (raw[at, lanes], sum(ref[at, :] for ref in image[1:]) + image[0][at, :])
            for which, buf in enumerate((basis_buf, images_buf)):
                value = fields[which]
                for j in range(last):
                    value = value - corr[j] * known_ref[which, slot, j, at, :]
                buf[slot, at, :] = value * inverse
            return carry

        def dead(i, carry, slot=slot):
            at = pl.ds(pl.multiple_of(i * CHUNK, CHUNK), CHUNK)
            for buf in (basis_buf, images_buf):
                buf[slot, at, :] = jnp.zeros((CHUNK, half), F32)
            return carry

        live = (rows + CHUNK - 1) // CHUNK
        lax.fori_loop(0, live, step, 0)
        lax.fori_loop(live, chunks, dead, 0)
        sector = sigma if slot == OWN else 1 - sigma
        for which, (buf, out) in enumerate(((basis_buf, basis_out), (images_buf, images_out))):
            copies.append(
                pltpu.make_async_copy(buf.at[slot], out.at[last, sector], sems.at[which, slot])
            )
            copies[-1].start()
    shape = projected_ref.shape
    row_ids = lax.broadcasted_iota(jnp.int32, shape, 0)
    col_ids = lax.broadcasted_iota(jnp.int32, shape, 1)
    value = jnp.zeros(shape, F32)
    for i in range(MATVECS):
        for j in range(MATVECS):
            value = jnp.where((row_ids == i) & (col_ids == j), numbers.proj[i, j][:, :1], value)
    projected_ref[...] = value
    for copy in copies:
        copy.wait()


def per_device(
    wavefunction, left_env, right_env, precond_diag, down_charge, bond_mask, left_size, right_size
):
    sectors, states, columns = wavefunction.shape
    bonds = left_env.shape[0]
    lsec_count = lax.axis_size("lsec")
    mpo_count = lax.axis_size("mpo")
    assert sectors == 2 and lax.axis_size("rsec") == 2
    width = 2 * columns
    cells = float(lsec_count * sectors * states * width)
    field = jax.ShapeDtypeStruct((states, width), F32)
    noted = jax.ShapeDtypeStruct((states + NOTE, width), F32)
    half_field = jax.ShapeDtypeStruct((states, columns), F32)
    small = jax.ShapeDtypeStruct((8, 128), F32)
    params = pltpu.CompilerParams(vmem_limit_bytes=18 * 2**20)

    swap = [(0, 1), (1, 0)]
    first_pairs = [(i, i ^ 1) for i in range(lsec_count) if i ^ 1 < lsec_count]
    second_pairs = [(i, j) for a in range(1, lsec_count - 1, 2) for i, j in ((a, a + 1), (a + 1, a))]
    anywhere = pl.BlockSpec(memory_space=pl.ANY)
    in_hbm = pl.BlockSpec(memory_space=pltpu.HBM)

    def hold(value):
        return pltpu.with_memory_space_constraint(value, pltpu.HBM)

    def neighbours(value):
        return lax.ppermute(value, "lsec", first_pairs), lax.ppermute(value, "lsec", second_pairs)

    wave_far = lax.ppermute(wavefunction, "rsec", swap)
    diag_far = lax.ppermute(precond_diag, "rsec", swap)
    mask_rows = bond_mask.T
    small_inputs = [down_charge, mask_rows, left_size, right_size]
    meta, wave_near = pl.pallas_call(
        functools.partial(prep_kernel, lsec_count, bonds),
        out_shape=(
            jax.ShapeDtypeStruct((LIST + bonds,), jnp.int32),
            jax.ShapeDtypeStruct(wavefunction.shape, F32),
        ),
        in_specs=[in_hbm] * 5,
        out_specs=(whole_smem(), whole_vmem()),
        scratch_shapes=[pltpu.SMEM(x.shape, jnp.int32) for x in small_inputs]
        + [pltpu.SemaphoreType.DMA((4,)), pltpu.SemaphoreType.DMA],
        compiler_params=params,
        cost_estimate=pl.CostEstimate(flops=0, transcendentals=0, bytes_accessed=10**6),
        name="prep",
    )(*[hold(x) for x in small_inputs], hold(wavefunction))
    right_send, _, _, _ = lax.optimization_barrier((right_env, wave_far, wave_near, diag_far))
    right_far = lax.ppermute(right_send, "rsec", swap)
    own, sib = pl.pallas_call(
        first_kernel,
        out_shape=(noted, field),
        in_specs=[whole_smem()] + [whole_vmem()] * 2,
        out_specs=(whole_vmem(),) * 2,
        compiler_params=params,
        name="first",
    )(meta, wave_near, wave_far)
    near_waves = neighbours(own)
    raw = [(own, sib, *near_waves)]
    def mpo_pair(value):
        if mpo_count != 2:
            value = lax.psum(value, "mpo")
            return value, jnp.zeros_like(value)
        return value, lax.ppermute(value, "mpo", swap)

    def lsec_parts(part):
        if lsec_count != 4:
            zero = jnp.zeros_like(part)
            return lax.psum(part, "lsec"), zero, zero, zero
        return (part, *[lax.ppermute(part, "lsec", [(i, i ^ x) for i in range(4)]) for x in (1, 2, 3)])

    def join(value, part, after):
        return pl.pallas_call(
            join_kernel,
            out_shape=noted,
            in_specs=[whole_vmem()] * 6 + [anywhere] * len(after),
            out_specs=whole_vmem(),
            compiler_params=params,
            name="join",
        )(*mpo_pair(value), *lsec_parts(part), *after)

    most = bonds - bonds // 5 if bonds % 5 == 0 else bonds
    packed = most * states + PACK
    lefts = pl.pallas_call(
        left_kernel,
        out_shape=(
            pltpu.VMEM((packed, SIDE), BF16),
            pltpu.VMEM((packed, SIDE), BF16),
            pltpu.VMEM((packed, 2 * (states - SIDE)), BF16),
        ),
        in_specs=[whole_smem(), anywhere],
        out_specs=(whole_vmem(),) * 3,
        scratch_shapes=[
            pltpu.VMEM((BUFFERS, states, states), F32),
            pltpu.SemaphoreType.DMA((states // TILE, BUFFERS)),
        ],
        compiler_params=params,
        cost_estimate=pl.CostEstimate(flops=0, transcendentals=0, bytes_accessed=bonds * states * states * 4),
        name="left",
    )(meta, hold(left_env))
    rights = pl.pallas_call(
        right_kernel,
        out_shape=(pltpu.VMEM((most, width, width), BF16),) * 2,
        in_specs=[whole_smem(), anywhere, anywhere],
        out_specs=(whole_vmem(),) * 2,
        scratch_shapes=[
            pltpu.VMEM((most, width, width), F32),
            pltpu.SemaphoreType.DMA((2, most)),
        ],
        compiler_params=params,
        cost_estimate=pl.CostEstimate(flops=0, transcendentals=0, bytes_accessed=bonds * width * width * 8),
        name="right",
    )(meta, hold(right_env), right_far)

    diag_own, diag_sib = pl.pallas_call(
        diag_kernel,
        out_shape=(field,) * 2,
        in_specs=[whole_smem()] + [whole_vmem()] * 2 + [anywhere],
        out_specs=(whole_vmem(),) * 2,
        compiler_params=params,
        name="diag",
    )(meta, hold(precond_diag), diag_far, rights[0])

    near_diags = neighbours(diag_own)
    near_diags = neighbours(diag_own)

    def dots(k, early, pack, values):
        operands = [early, *pack, *[group[0] for group in raw], *values]
        return pl.pallas_call(
            functools.partial(dots_kernel, k, mpo_count),
            out_shape=small,
            in_specs=[whole_smem()] + [whole_vmem()] * len(operands),
            out_specs=whole_vmem(),
            compiler_params=params,
            cost_estimate=pl.CostEstimate(
                flops=4 * states * width, transcendentals=0, bytes_accessed=4 * states * width
            ),
            name=f"dots{k}",
        )(meta, *operands)

    out = jax.ShapeDtypeStruct((MATVECS, sectors, states, columns), F32)
    known = jax.ShapeDtypeStruct((2, sectors, MATVECS - 1, states, columns), F32)

    def matvec(k, near, sizes, inputs):
        last = k + 1 == MATVECS
        vmem, scalars = whole_vmem(), whole_smem()
        scratch = [
            pltpu.VMEM((2, states, width), BF16),
            pltpu.VMEM((2, states, width), BF16),
            pltpu.VMEM((2 * (states - SIDE), width), BF16),
            pltpu.VMEM((packed + states, width), BF16),
            pltpu.VMEM((packed + states, width), BF16),
            pltpu.SMEM((bonds,), jnp.int32),
        ]
        fresh = [(field, vmem)] * (2 if k and (near or not last) else 0)
        if near:
            outs = [(field, vmem), (jax.ShapeDtypeStruct((1 + 2 * k, 8, width), F32), vmem)]
            outs += [(small, vmem)] * (1 if k else 0) + fresh
            scratch.append(pltpu.SMEM((8,), jnp.int32))
            if last:
                outs += [(known, vmem), (small, vmem), (out, anywhere), (out, anywhere)]
                scratch.append(pltpu.SemaphoreType.DMA((2, 2)))
        else:
            outs = ([(half_field, vmem)] * 2 if last else [(field, vmem)]) + fresh
            if last:
                scratch.append(pltpu.VMEM((states, width), F32))
            if not k:
                outs.append((jax.ShapeDtypeStruct((8,), jnp.int32), scalars))
        return pl.pallas_call(
            functools.partial(matvec_kernel, k, cells, near),
            out_shape=tuple(shape for shape, _ in outs),
            in_specs=[scalars] + [vmem] * 5 + [scalars] * len(sizes) + [vmem] * len(inputs),
            out_specs=tuple(spec for _, spec in outs),
            scratch_shapes=scratch,
            compiler_params=params,
            cost_estimate=pl.CostEstimate(
                flops=3 * bonds * states * width * (states + width),
                transcendentals=0,
                bytes_accessed=bonds * states * states,
            ),
            name=f"matvec{k}_{'near' if near else 'far'}",
        )(meta, *lefts, *rights, *sizes, *inputs)

    def flatten(groups):
        return [x for group in groups for x in group]

    def step_inputs(slots):
        return [*flatten(group[slots] for group in (*raw, *images)), *precond[slots]]

    near_slots, far_slots = slice(0, 2), slice(2, 4)
    totals, images, sizes, precond = [], [], [], []
    for k in range(MATVECS):
        last = k + 1 == MATVECS
        inputs = step_inputs(far_slots)
        partial, early, *fresh = matvec(k, True, [], [*totals, *step_inputs(near_slots)])
        pack, fresh = (fresh[:1], fresh[1:]) if k else ([], fresh)
        value, *fresh_far = matvec(k, False, sizes, [*pack, *inputs, partial])
        if k == 0:
            sizes = fresh_far
            value, near_diags = lax.optimization_barrier((value, near_diags))
            precond = (diag_own, diag_sib, *near_diags)
        elif not last:
            raw.append((*fresh, *fresh_far))
        if last:
            break
        part = dots(k, early, pack, [value])
        value = join(value, part, [])
        beside = lax.ppermute(value, "rsec", swap)
        images.append((value, beside, *neighbours(value)))
        totals += mpo_pair(value[states:, :HALF] + beside[states:, :HALF])

    near, away = value, fresh_far[0]
    own, sib, known_blocks, state, *outs = fresh
    raw.append((own, sib))
    part = dots(MATVECS - 1, early, pack, [near, away])
    away, far_away = mpo_pair(away)
    sib_half = lax.ppermute(away + far_away, "rsec", swap)
    own_half = mpo_pair(near)
    one, two, three, four = lsec_parts(part)
    part = (one + two) + (three + four)
    total = mpo_pair(part + lax.ppermute(part, "rsec", swap))
    operands = [*total, state, known_blocks, own, sib, *own_half, sib_half]
    return pl.pallas_call(
        functools.partial(fill_kernel, cells),
        out_shape=(out, out, jax.ShapeDtypeStruct((MATVECS, MATVECS), F32)),
        in_specs=[whole_smem()] + [whole_vmem()] * len(operands) + [anywhere] * 2,
        out_specs=(anywhere, anywhere, whole_vmem()),
        scratch_shapes=[
            pltpu.VMEM((sectors, states, columns), F32),
            pltpu.VMEM((sectors, states, columns), F32),
            pltpu.SemaphoreType.DMA((2, 2)),
        ],
        input_output_aliases={1 + len(operands): 0, 2 + len(operands): 1},
        compiler_params=params,
        name="fill",
    )(meta, *operands, *outs)


def solution(mesh):
    placed = (
        P(("grp", "lsec"), None, "rsec"),
        P("mpo", ("grp", "lsec"), None, None),
        P("mpo", ("grp", "lsec"), "rsec", None),
        P(("grp", "lsec"), None, "rsec"),
        P("grp"),
        P("mpo", ("grp", "lsec")),
        P(("grp", "lsec")),
        P(("grp", "lsec")),
    )
    return jax.shard_map(
        per_device,
        mesh=mesh,
        in_specs=placed,
        out_specs=(
            P(None, ("grp", "lsec"), None, "rsec"),
            P(None, ("grp", "lsec"), None, "rsec"),
            P("grp", None),
        ),
        check_vma=False,
    )
```

```python
import functools

import jax
import jax.numpy as jnp
from jax import lax
from jax.experimental import pallas as pl
from jax.experimental.pallas import tpu as pltpu
from jax.sharding import PartitionSpec as P

EPSILON = 1e-06
MATVECS = 3
F32 = jnp.float32
BF16 = jnp.bfloat16
SIGMA, COUNT, ROWS, COLS, FIRST, SIB_ROWS, SIB_COLS, LIST = 0, 1, 2, 3, 4, 9, 10, 16
OWN, SIB, FIRST_PAIR, SECOND_PAIR = 0, 1, 2, 3
CHUNK = 64
TILE = 128
SIDE = 256
HALF = 128
NOTE = 8
PACK = 256
BUFFERS = 8


def whole_vmem():
    return pl.BlockSpec(memory_space=pltpu.VMEM)


def whole_smem():
    return pl.BlockSpec(memory_space=pltpu.SMEM)


def split(value):
    high = value.astype(BF16)
    return high, (value - high.astype(F32)).astype(BF16)


def orientation(down_ref, place):
    def step(i, flips):
        straight = (down_ref[2 * i] == down_ref[2 * i - 2]) | (
            down_ref[2 * i + 1] == down_ref[2 * i - 1]
        )
        return jnp.where(straight, flips, 1 - flips)

    return lax.fori_loop(1, place + 1, step, jnp.int32(0))


def live_mask(shape, row0, rows, cols):
    row_ids = row0 + lax.broadcasted_iota(jnp.int32, shape, 0)
    col_ids = lax.broadcasted_iota(jnp.int32, shape, 1)
    return (row_ids < rows) & (col_ids < cols)


def read_small(pairs, sems):
    copies = [pltpu.make_async_copy(*pair, sems.at[i]) for i, pair in enumerate(pairs)]
    for copy in copies:
        copy.start()
    for copy in copies:
        copy.wait()


def first_kernel(meta_ref, wave_ref, wave_far, own_ref, sib_ref):
    states, half = wave_ref.shape[1:]
    sigma, core = meta_ref[SIGMA], lax.axis_index("rsec")
    for out_ref, slot, rows, cols in (
        (own_ref, sigma, meta_ref[ROWS], meta_ref[COLS]),
        (sib_ref, 1 - sigma, meta_ref[SIB_ROWS], meta_ref[SIB_COLS]),
    ):

        def fill(i, carry, out_ref=out_ref, slot=slot, rows=rows, cols=cols):
            at = pl.ds(pl.multiple_of(i * CHUNK, CHUNK), CHUNK)
            for place, wave in ((core, wave_ref), (1 - core, wave_far)):
                lanes = pl.ds(pl.multiple_of(place * half, half), half)
                mask = live_mask((CHUNK, half), i * CHUNK, rows, cols - place * half)
                out_ref[at, lanes] = jnp.where(mask, wave[slot, at, :], 0.0)
            return carry

        lax.fori_loop(0, states // CHUNK, fill, 0)
    note = (NOTE, own_ref.shape[1])
    row_ids = lax.broadcasted_iota(jnp.int32, note, 0)
    own_ref[pl.ds(states, NOTE), :] = jnp.where(
        row_ids == 0, meta_ref[ROWS], meta_ref[COLS]
    ).astype(F32)


def order_kernel(down_in, left_in, right_in, wave_in, meta_ref, wave_ref, down_ref, left_size_ref,
                 right_size_ref, sems, wave_sem):
    wave_copy = pltpu.make_async_copy(wave_in, wave_ref, wave_sem)
    wave_copy.start()
    read_small(((down_in, down_ref), (left_in, left_size_ref), (right_in, right_size_ref)), sems)
    sigma = lax.axis_index("rsec") ^ orientation(down_ref, lax.axis_index("lsec"))
    meta_ref[SIGMA] = sigma
    meta_ref[ROWS] = left_size_ref[sigma]
    meta_ref[COLS] = right_size_ref[sigma]
    meta_ref[SIB_ROWS] = left_size_ref[1 - sigma]
    meta_ref[SIB_COLS] = right_size_ref[1 - sigma]
    wave_copy.wait()


def prep_kernel(lsec_count, bonds, down_in, mask_in, left_in, right_in, _, meta_ref, down_ref, mask_ref,
                left_size_ref, right_size_ref, sems):
    read_small(
        ((down_in, down_ref), (mask_in, mask_ref), (left_in, left_size_ref), (right_in, right_size_ref)),
        sems,
    )
    place = lax.axis_index("lsec")
    core = lax.axis_index("rsec")
    first_kind = lax.rem(lax.axis_index("mpo") * bonds, 5)
    sigma = core ^ orientation(down_ref, place)
    own_down = down_ref[2 * place + sigma]
    sib_down = down_ref[2 * place + 1 - sigma]
    before = jnp.maximum(place - 1, 0)
    after = jnp.minimum(place + 1, lsec_count - 1)
    prev_down = down_ref[2 * before + (core ^ orientation(down_ref, before))]
    next_down = down_ref[2 * after + (core ^ orientation(down_ref, after))]
    has_prev = (place > 0) & (prev_down == own_down)
    has_next = (place < lsec_count - 1) & (next_down == own_down)
    odd = lax.rem(place, 2)
    has_lower = sib_down == own_down - 1
    has_upper = sib_down == own_down + 1

    def gather(slot, count):
        meta_ref[FIRST + slot] = count

        def step(bond, carry):
            count, kind = carry
            if slot == OWN:
                there = kind == 0
            elif slot == SIB:
                there = ((kind == 3) & has_lower) | ((kind == 4) & has_upper)
            else:
                lower = odd if slot == FIRST_PAIR else 1 - odd
                there = ((kind == 1) & has_prev & (lower == 1)) | (
                    (kind == 2) & has_next & (lower == 0)
                )
            there = there & (mask_ref[sigma, bond] > 0)

            @pl.when(there)
            def _():
                meta_ref[LIST + count] = bond * 4 + slot

            return count + there.astype(jnp.int32), jnp.where(kind == 4, 0, kind + 1)

        return lax.fori_loop(0, bonds, step, (count, first_kind))[0]

    count = jnp.int32(0)
    for slot in (OWN, SIB, FIRST_PAIR, SECOND_PAIR):
        count = gather(slot, count)
    meta_ref[FIRST + 4] = count
    rows, cols = left_size_ref[sigma], right_size_ref[sigma]
    meta_ref[SIGMA] = sigma
    meta_ref[COUNT] = count
    meta_ref[ROWS] = rows
    meta_ref[COLS] = cols
    meta_ref[SIB_ROWS] = left_size_ref[1 - sigma]
    meta_ref[SIB_COLS] = right_size_ref[1 - sigma]


def diag_kernel(meta_ref, diag_ref, diag_far, diag_own, diag_sib):
    states, width = diag_own.shape
    half = width // 2
    sigma, core = meta_ref[SIGMA], lax.axis_index("rsec")
    near = pl.ds(pl.multiple_of(core * half, half), half)
    away = pl.ds(pl.multiple_of((1 - core) * half, half), half)
    for out_ref, slot in ((diag_own, sigma), (diag_sib, 1 - sigma)):

        def fill(i, carry, out_ref=out_ref, slot=slot):
            at = pl.ds(pl.multiple_of(i * CHUNK, CHUNK), CHUNK)
            out_ref[at, near] = diag_ref[slot, at, :]
            out_ref[at, away] = diag_far[slot, at, :]
            return carry

        lax.fori_loop(0, states // CHUNK, fill, 0)


def row(value, index):
    return value[index : index + 1, :]


def stack_rows(shape, rows):
    row_ids = lax.broadcasted_iota(jnp.int32, shape, 0)
    value = jnp.zeros(shape, F32)
    for index, entry in enumerate(rows):
        if entry is not None:
            value = jnp.where(row_ids == index, entry, value)
    return value


class Scalars:
    def __init__(self, totals, cells, state=None):
        self.proj = {}
        self.gram = {}
        self.inverse = []
        self.corr = []
        known = 0
        if state is not None:
            known = MATVECS - 1
            places = [(i, j) for i in range(known) for j in range(known)]
            for index, place in enumerate(places):
                self.proj[place] = row(state, index)
                self.gram[place] = row(state, len(places) + index)
        for k, total in enumerate(totals, known):
            value = (total[0][...] + total[1][...]) / cells
            size, inner = row(value, 0), row(value, 1)
            a = [row(value, 2 + j) for j in range(k)]
            e = [row(value, 4 + j) for j in range(k)]
            f = [row(value, 6 + j) for j in range(k)]
            length = size
            theta = inner
            for j in range(k):
                length = length - 2.0 * a[j] * a[j]
                theta = theta - a[j] * e[j] - a[j] * f[j]
            for i in range(k):
                for j in range(k):
                    length = length + a[i] * a[j] * self.gram[i, j]
                    theta = theta + a[i] * a[j] * self.proj[i, j]
            length = jnp.maximum(length, 0.0)
            square = length + EPSILON
            norm = jnp.sqrt(square)
            for j in range(k):
                up, down, both = e[j], f[j], a[j]
                for i in range(k):
                    up = up - a[i] * self.proj[j, i]
                    down = down - a[i] * self.proj[i, j]
                    both = both - a[i] * self.gram[i, j]
                self.proj[j, k] = up / norm
                self.proj[k, j] = down / norm
                self.gram[j, k] = self.gram[k, j] = both / norm
            self.proj[k, k] = theta / square
            self.gram[k, k] = length / square
            self.inverse.append(1.0 / norm)
            self.corr.append(a)

    def state(self, shape):
        known = MATVECS - 1
        places = [(i, j) for i in range(known) for j in range(known)]
        rows = [self.proj[place] for place in places] + [self.gram[place] for place in places]
        return stack_rows(shape, rows)

    def pack(self, k, shape):
        rows = [self.proj[k - 1, k - 1], *self.inverse[:k]]
        for a in self.corr[:k]:
            rows += a
        return stack_rows(shape, rows)

    @classmethod
    def unpack(cls, k, ref):
        numbers = cls([], 1.0)
        value = ref[...]
        numbers.theta = row(value, 0)[:, :1]
        numbers.inverse = [row(value, 1 + i) for i in range(k)]
        place = 1 + k
        for step in range(k):
            numbers.corr.append([row(value, place + j) for j in range(step)])
            place += step
        return numbers

    def basis(self, k, fields):
        done = []
        for step in range(k + 1):
            value = fields[step]
            for j in range(step):
                value = value - self.corr[step][j][:, :1] * done[j]
            done.append(value * self.inverse[step][:, :1])
        return done


def left_kernel(meta_ref, left_ref, left_high, left_low, left_tail, left_buf, sems):
    states = left_buf.shape[1]
    sigma, count, rows = meta_ref[SIGMA], meta_ref[COUNT], meta_ref[ROWS]
    stride = packed_rows(rows)

    def each(i, act):
        bond = (meta_ref[LIST + i] >> 2)
        at = i & (BUFFERS - 1)
        for p in range(states // TILE):
            part = pl.ds(p * TILE, TILE)

            @pl.when(rows > p * TILE)
            def _(part=part, p=p):
                act(
                    pltpu.make_async_copy(
                        left_ref.at[bond, sigma, part], left_buf.at[at, part], sems.at[p, at]
                    )
                )

    def start(i):
        @pl.when(i < count)
        def _():
            each(i, lambda copy: copy.start())

    for i in range(BUFFERS - 1):
        start(jnp.int32(i))

    def step(i, carry):
        at = i & (BUFFERS - 1)
        start(i + BUFFERS - 1)
        each(i, lambda copy: copy.wait())

        def chunk(t, inner):
            high, low = split(left_buf[at, pl.ds(pl.multiple_of(t * CHUNK, CHUNK), CHUNK), :])
            to = pl.ds(pl.multiple_of(i * stride + t * CHUNK, 16), CHUNK)
            left_high[to, :] = high[:, :SIDE]
            left_low[to, :] = low[:, :SIDE]
            left_tail[to, :] = jnp.concatenate([high[:, SIDE:], low[:, SIDE:]], axis=1)
            return inner

        lax.fori_loop(0, (rows + CHUNK - 1) // CHUNK, chunk, 0)
        return carry

    lax.fori_loop(0, count, step, 0)


def right_kernel(meta_ref, right_ref, far_ref, right_high, right_low, right_buf, sems):
    width, half = right_buf.shape[1], right_ref.shape[2]
    sigma, count = meta_ref[SIGMA], meta_ref[COUNT]
    core = lax.axis_index("rsec")
    thin = meta_ref[COLS] <= HALF

    def each(i, act):
        bond = (meta_ref[LIST + i] >> 2)
        for ref, place, sem in ((right_ref, core, 0), (far_ref, 1 - core, 1)):
            part = pl.ds(pl.multiple_of(place * half, half), half)

            @pl.when(jnp.logical_not(thin) | (place == 0))
            def _(ref=ref, part=part, sem=sem):
                act(
                    pltpu.make_async_copy(ref.at[bond, sigma], right_buf.at[i, part], sems.at[sem, i])
                )

    def start(i, carry):
        each(i, lambda copy: copy.start())
        return carry

    lax.fori_loop(0, count, start, 0)

    def step(i, carry):
        each(i, lambda copy: copy.wait())

        @pl.when(thin)
        def _():
            for first in range(0, HALF, CHUNK):
                high, low = split(right_buf[i, pl.ds(first, CHUNK), :])
                right_high[i, pl.ds(first, CHUNK), :] = high
                right_high[i, pl.ds(HALF + first, CHUNK), :] = low

        @pl.when(jnp.logical_not(thin))
        def _():
            for first in range(0, width, CHUNK):
                at = pl.ds(first, CHUNK)
                right_high[i, at, :], right_low[i, at, :] = split(right_buf[i, at, :])

        return carry

    lax.fori_loop(0, count, step, 0)


def packed_rows(rows):
    return ((rows + 15) // 16) * 16


def fold(value):
    return jnp.sum(value.reshape(CHUNK // 8, 8, value.shape[1]), axis=0)


def dots_kernel(k, mpo_count, meta_ref, early_ref, *refs):
    refs, small_ref = list(refs[:-1]), refs[-1]
    numbers = Scalars.unpack(k, refs.pop(0)) if k else None
    raw = [refs.pop(0) for _ in range(k + 1)]
    core = lax.axis_index("rsec")
    zero = jnp.zeros(early_ref.shape[1:], F32)

    def step(i, carry):
        at = pl.ds(pl.multiple_of(i * CHUNK, CHUNK), CHUNK)
        blocks = [ref[at, :] for ref in refs]
        if len(blocks) == 2:
            near, away = blocks
            first, second = jnp.where(core == 0, near, away), jnp.where(core == 0, away, near)
            value = jnp.concatenate([first, second], axis=1)
        else:
            value = blocks[0]
        basis = numbers.basis(k - 1, [ref[at, :] for ref in raw[:k]]) if k else []
        return tuple(c + fold(value * b) for c, b in zip(carry, [raw[k][at, :], *basis]))

    live = (meta_ref[ROWS] + CHUNK - 1) // CHUNK
    late = lax.fori_loop(0, live, step, (zero,) * (1 + k))

    def whole(value):
        return jnp.sum(jnp.sum(value, axis=1, keepdims=True), axis=0, keepdims=True)

    share = 1.0 / mpo_count
    entries = [whole(early_ref[0]) * share, whole(late[0])]
    for j in range(2):
        entries.append(whole(early_ref[1 + j]) * share if j < k else None)
    for j in range(2):
        entries.append(whole(late[1 + j]) if j < k else None)
    for j in range(2):
        entries.append(whole(early_ref[1 + k + j]) * share if j < k else None)
    small_ref[...] = stack_rows(small_ref.shape, entries)


def matvec_kernel(k, cells, near, *refs):
    refs = list(refs)
    slots = (OWN, SIB) if near else (FIRST_PAIR, SECOND_PAIR)
    base = slots[0]
    last = k + 1 == MATVECS
    meta_ref = refs.pop(0)
    left_high, left_low, left_tail = [refs.pop(0) for _ in range(3)]
    right_high, right_low = refs.pop(0), refs.pop(0)
    size_ref = refs.pop(0) if k and not near else None
    totals = [(refs.pop(0), refs.pop(0)) for _ in range(k)] if near else []
    pack_ref = refs.pop(0) if k and not near else None
    raw = [{slot: refs.pop(0) for slot in slots} for _ in range(max(k, 1))]
    images = [{slot: refs.pop(0) for slot in slots} for _ in range(k)]
    precond = {slot: refs.pop(0) for slot in slots} if k else {}
    partial_ref = None if near else refs.pop(0)
    halves = [refs.pop(0), refs.pop(0)] if last and not near else []
    out_ref = None if halves else refs.pop(0)
    early_ref = refs.pop(0) if near else None
    pack_ref = refs.pop(0) if k and near else pack_ref
    keep = near or not last
    new_refs = ({slot: refs.pop(0) for slot in slots} if keep else {}) if k else raw[0]
    if not k and not near:
        size_ref = refs.pop(0)
    if last and near:
        known_ref, state_ref, basis_out, images_out = [refs.pop(0) for _ in range(4)]
    high_ref, low_ref, tail_ref, mid_high, mid_low, order_ref = refs[:6]
    if near:
        size_ref = refs[6]
        sems = refs[7] if last else None
    elif last:
        out_ref = refs[6]
    states, width = out_ref.shape
    rows, cols = meta_ref[ROWS], meta_ref[COLS]
    first_bond, end_bond = meta_ref[FIRST + base], meta_ref[FIRST + base + 2]
    count = end_bond - first_bond
    stride = packed_rows(rows)

    core = lax.axis_index("rsec")
    if near:
        size_ref[2 * OWN], size_ref[2 * OWN + 1] = rows, cols
        size_ref[2 * SIB], size_ref[2 * SIB + 1] = meta_ref[SIB_ROWS], meta_ref[SIB_COLS]
    elif not k:
        for slot in slots:
            note = raw[0][slot][pl.ds(states, NOTE), :HALF]
            size_ref[2 * slot] = jnp.max(note[:1]).astype(jnp.int32)
            size_ref[2 * slot + 1] = jnp.max(note[1:]).astype(jnp.int32)
    def list_bonds(narrow):
        def step(i, place):
            hit = (size_ref[2 * (meta_ref[LIST + i] & 3) + 1] <= HALF) == narrow

            @pl.when(hit)
            def _():
                order_ref[place] = i

            return place + hit.astype(jnp.int32)

        return step

    thin_sources = lax.fori_loop(first_bond, end_bond, list_bonds(True), jnp.int32(0))
    lax.fori_loop(first_bond, end_bond, list_bonds(False), thin_sources)
    if k and near:
        numbers = Scalars(totals, cells)
        theta = numbers.proj[k - 1, k - 1][:, :1]
        pack_ref[...] = numbers.pack(k, pack_ref.shape)
    elif k:
        numbers = Scalars.unpack(k, pack_ref)
        theta = numbers.theta
    zero = jnp.zeros((8, width), F32)

    def prepare(slot, carry):
        def step(i, carry):
            at = pl.ds(pl.multiple_of(i * CHUNK, CHUNK), CHUNK)
            if k:
                basis = numbers.basis(k - 1, [r[slot][at, :] for r in raw])
                image = numbers.basis(k - 1, [r[slot][at, :] for r in images])
                value = (image[-1] - theta * basis[-1]) / jnp.maximum(
                    precond[slot][at, :] - theta, 1.0
                )
                if keep:
                    new_refs[slot][at, :] = value
                if last and near:
                    for which, group in enumerate((basis, image)):
                        for j, block in enumerate(group):
                            block = jnp.where(core == 0, block[:, :HALF], block[:, HALF:])
                            known_ref[which, slot, j, at, :] = block
            else:
                basis, image = [], []
                value = raw[0][slot][at, :]
            high, low = split(value)
            high_ref[slot - base, at, :] = high
            low_ref[slot - base, at, :] = low
            terms = [value * value]
            if slot == OWN:
                terms += [value * b for b in basis] + [value * g for g in image]
            return tuple(c + fold(t) for c, t in zip(carry, terms))

        def dead(i, inner):
            at = pl.ds(pl.multiple_of(i * CHUNK, CHUNK), CHUNK)
            high_ref[slot - base, at, :] = jnp.zeros((CHUNK, width), BF16)
            low_ref[slot - base, at, :] = jnp.zeros((CHUNK, width), BF16)
            if last and near:
                for which in range(2):
                    for j in range(k):
                        known_ref[which, slot, j, at, :] = jnp.zeros((CHUNK, HALF), F32)
            return inner

        live = (size_ref[2 * slot] + CHUNK - 1) // CHUNK
        lax.fori_loop(live, states // CHUNK, dead, 0)
        return lax.fori_loop(0, live, step, carry)

    def dot(a, b):
        return jnp.dot(a, b, preferred_element_type=F32)

    def dot_nt(a, b):
        return lax.dot_general(a, b, (((1,), (1,)), ((), ())), preferred_element_type=F32)

    twice = functools.partial(jnp.concatenate, axis=0)

    def first_stage(slot, deep, narrow):
        begin, end = meta_ref[FIRST + slot], meta_ref[FIRST + 1 + slot]
        at_slot = slot - base
        top, rest = pl.ds(0, SIDE), pl.ds(SIDE, states - SIDE)
        if narrow:
            high_ref[at_slot, :, HALF:] = low_ref[at_slot, :, :HALF]
        if deep:
            tail = high_ref[at_slot, rest, :]
            tail_ref[...] = twice([tail, tail])

        def step(t, carry):
            at = pl.ds(pl.multiple_of(begin * stride + t * PACK, 16), PACK)
            high, low = left_high[at, :], left_low[at, :]
            mid = dot(high, high_ref[at_slot, top, :])
            if deep:
                mid = mid + dot(left_tail[at, :], tail_ref[...])
            if narrow:
                mid = mid[:, :HALF] + mid[:, HALF:] + dot(low, high_ref[at_slot, top, :HALF])
                mid_high[at, :] = jnp.concatenate(split(mid), axis=1)
            else:
                mid = mid + dot(low, high_ref[at_slot, top, :]) + dot(high, low_ref[at_slot, top, :])
                if deep:
                    mid = mid + dot(left_tail[at, : states - SIDE], low_ref[at_slot, rest, :])
                mid_high[at, :], mid_low[at, :] = split(mid)
            return carry

        lax.fori_loop(0, ((end - begin) * stride + PACK - 1) // PACK, step, 0)

    def both(test, action):
        pl.when(test)(lambda: action(True))
        pl.when(jnp.logical_not(test))(lambda: action(False))

    if near:
        own = prepare(OWN, (zero,) * (1 + 2 * k))
        prepare(SIB, (zero,))
    else:
        for slot in slots:
            used = meta_ref[FIRST + 1 + slot] > meta_ref[FIRST + slot]
            pl.when(used)(lambda slot=slot: (prepare(slot, (zero,)), None)[1])

    def from_slot(slot, carry):
        both(
            size_ref[2 * slot] > SIDE,
            lambda deep: both(
                size_ref[2 * slot + 1] <= HALF, lambda narrow: first_stage(slot, deep, narrow)
            ),
        )
        return carry

    lax.fori_loop(base, base + 2, from_slot, 0)
    if last and near:
        sigma = meta_ref[SIGMA]
        outputs = [
            pltpu.make_async_copy(
                known_ref.at[which, slot],
                out.at[pl.ds(0, MATVECS - 1), sigma if slot == OWN else 1 - sigma],
                sems.at[which, slot],
            )
            for which, out in enumerate((basis_out, images_out))
            for slot in (OWN, SIB)
        ]
        for copy in outputs:
            copy.start()
        state_ref[...] = numbers.state(state_ref.shape)

    def clear(i, carry):
        at = pl.ds(pl.multiple_of(i * CHUNK, CHUNK), CHUNK)
        out_ref[at, :] = jnp.zeros((CHUNK, width), F32) if near else partial_ref[at, :]
        return carry

    lax.fori_loop(0, states // CHUNK, clear, 0)
    zeros_at = mid_high.shape[0] - states
    for ref in (mid_high, mid_low):
        ref[pl.ds(zeros_at, states), :] = jnp.zeros((states, width), BF16)

    def second_stage(size, thin):
        to = pl.ds(0, size)

        def product(i, real, narrow):
            bond = order_ref[i]
            at = pl.ds(pl.multiple_of(jnp.where(real, bond * stride, zeros_at), 16), size)
            high = mid_high[at, :]
            lanes = pl.ds(0, HALF if narrow else width)
            right = right_high[bond, :, lanes]
            right_rest = None if thin else right_low[bond, :, lanes]
            if narrow:
                value = dot_nt(high, jnp.concatenate([right, right], axis=1))
                if not thin:
                    value = value + dot_nt(high[:, :HALF], right_rest)
            else:
                value = dot_nt(high, right)
                if not thin:
                    value = value + dot_nt(high, right_rest) + dot_nt(mid_low[at, :], right)
            if thin:
                value = value[:, :HALF] + value[:, HALF:]
                if not narrow:
                    value = value + dot_nt(mid_low[at, :], right[:HALF, :])
            return value

        def run(begin, end, narrow):
            def pair(p, carry):
                one = begin + 2 * p
                real = one + 1 < end
                two = jnp.where(real, one + 1, one)
                value = product(one, True, narrow) + product(two, real, narrow)
                if thin:
                    out_ref[to, :HALF] += value
                else:
                    out_ref[to, :] += value
                return carry

            lax.fori_loop(0, (end - begin + 1) // 2, pair, 0)

        run(0, thin_sources, True)
        run(thin_sources, count, False)

    for size in range(TILE, states + 1, TILE):
        pl.when((rows <= size) & (rows > size - TILE))(
            lambda size=size: both(cols <= HALF, functools.partial(second_stage, size))
        )

    if near:
        for index, entry in enumerate(own):
            early_ref[index] = entry
        if last:
            for copy in outputs:
                copy.wait()
        return

    def finish(i, carry):
        at = pl.ds(pl.multiple_of(i * CHUNK, CHUNK), CHUNK)
        mask = live_mask((CHUNK, width), i * CHUNK, rows, cols)
        value = jnp.where(mask, out_ref[at, :], 0.0)
        if last:
            halves[0][at, :] = jnp.where(core == 0, value[:, :HALF], value[:, HALF:])
            halves[1][at, :] = jnp.where(core == 0, value[:, HALF:], value[:, :HALF])
        else:
            out_ref[at, :] = value
        return carry

    lax.fori_loop(0, (rows + CHUNK - 1) // CHUNK, finish, 0)


def join_kernel(a_ref, b_ref, s0, s1, s2, s3, *refs):
    out_ref = refs[-1]
    states = a_ref.shape[0]
    total = (s0[...] + s1[...]) + (s2[...] + s3[...])
    out_ref[pl.ds(states, NOTE), :HALF] = total
    out_ref[pl.ds(states, NOTE), HALF:] = total

    def step(i, carry):
        at = pl.ds(pl.multiple_of(i * CHUNK, CHUNK), CHUNK)
        out_ref[at, :] = a_ref[at, :] + b_ref[at, :]
        return carry

    lax.fori_loop(0, states // CHUNK, step, 0)


def fill_kernel(cells, meta_ref, *refs):
    total, state_ref = refs[:2], refs[2]
    known_ref, raw_own, raw_sib, *parts = refs[3:9]
    basis_out, images_out, projected_ref, basis_buf, images_buf, sems = refs[-6:]
    last = MATVECS - 1
    sigma = meta_ref[SIGMA]
    numbers = Scalars([total], cells, state_ref[...])
    core = lax.axis_index("rsec")
    states, half = basis_buf.shape[1:]
    lanes = pl.ds(pl.multiple_of(core * half, half), half)
    inverse = numbers.inverse[0][:, :1]
    corr = [a[:, :1] for a in numbers.corr[0]]
    copies = []
    chunks = states // CHUNK
    for slot, raw, image, rows in (
        (OWN, raw_own, parts[:2], meta_ref[ROWS]),
        (SIB, raw_sib, parts[2:], meta_ref[SIB_ROWS]),
    ):

        def step(i, carry, slot=slot, raw=raw, image=image):
            at = pl.ds(pl.multiple_of(i * CHUNK, CHUNK), CHUNK)
            fields = (raw[at, lanes], sum(ref[at, :] for ref in image[1:]) + image[0][at, :])
            for which, buf in enumerate((basis_buf, images_buf)):
                value = fields[which]
                for j in range(last):
                    value = value - corr[j] * known_ref[which, slot, j, at, :]
                buf[slot, at, :] = value * inverse
            return carry

        def dead(i, carry, slot=slot):
            at = pl.ds(pl.multiple_of(i * CHUNK, CHUNK), CHUNK)
            for buf in (basis_buf, images_buf):
                buf[slot, at, :] = jnp.zeros((CHUNK, half), F32)
            return carry

        live = (rows + CHUNK - 1) // CHUNK
        lax.fori_loop(0, live, step, 0)
        lax.fori_loop(live, chunks, dead, 0)
        sector = sigma if slot == OWN else 1 - sigma
        for which, (buf, out) in enumerate(((basis_buf, basis_out), (images_buf, images_out))):
            copies.append(
                pltpu.make_async_copy(buf.at[slot], out.at[last, sector], sems.at[which, slot])
            )
            copies[-1].start()
    shape = projected_ref.shape
    row_ids = lax.broadcasted_iota(jnp.int32, shape, 0)
    col_ids = lax.broadcasted_iota(jnp.int32, shape, 1)
    value = jnp.zeros(shape, F32)
    for i in range(MATVECS):
        for j in range(MATVECS):
            value = jnp.where((row_ids == i) & (col_ids == j), numbers.proj[i, j][:, :1], value)
    projected_ref[...] = value
    for copy in copies:
        copy.wait()


def per_device(
    wavefunction, left_env, right_env, precond_diag, down_charge, bond_mask, left_size, right_size
):
    sectors, states, columns = wavefunction.shape
    bonds = left_env.shape[0]
    lsec_count = lax.axis_size("lsec")
    mpo_count = lax.axis_size("mpo")
    assert sectors == 2 and lax.axis_size("rsec") == 2
    width = 2 * columns
    cells = float(lsec_count * sectors * states * width)
    field = jax.ShapeDtypeStruct((states, width), F32)
    noted = jax.ShapeDtypeStruct((states + NOTE, width), F32)
    half_field = jax.ShapeDtypeStruct((states, columns), F32)
    small = jax.ShapeDtypeStruct((8, 128), F32)
    params = pltpu.CompilerParams(vmem_limit_bytes=18 * 2**20)

    swap = [(0, 1), (1, 0)]
    first_pairs = [(i, i ^ 1) for i in range(lsec_count) if i ^ 1 < lsec_count]
    second_pairs = [(i, j) for a in range(1, lsec_count - 1, 2) for i, j in ((a, a + 1), (a + 1, a))]
    anywhere = pl.BlockSpec(memory_space=pl.ANY)
    in_hbm = pl.BlockSpec(memory_space=pltpu.HBM)

    def hold(value):
        return pltpu.with_memory_space_constraint(value, pltpu.HBM)

    def neighbours(value):
        return lax.ppermute(value, "lsec", first_pairs), lax.ppermute(value, "lsec", second_pairs)

    wave_far = lax.ppermute(wavefunction, "rsec", swap)
    diag_far = lax.ppermute(precond_diag, "rsec", swap)
    mask_rows = bond_mask.T
    small_inputs = [down_charge, mask_rows, left_size, right_size]
    small_inputs = [hold(x) for x in small_inputs]
    order_inputs = [small_inputs[0], small_inputs[2], small_inputs[3]]
    order_meta, wave_near = pl.pallas_call(
        order_kernel,
        out_shape=(
            jax.ShapeDtypeStruct((LIST,), jnp.int32),
            jax.ShapeDtypeStruct(wavefunction.shape, F32),
        ),
        in_specs=[in_hbm] * 4,
        out_specs=(whole_smem(), whole_vmem()),
        scratch_shapes=[pltpu.SMEM(x.shape, jnp.int32) for x in order_inputs]
        + [pltpu.SemaphoreType.DMA((3,)), pltpu.SemaphoreType.DMA],
        compiler_params=params,
        cost_estimate=pl.CostEstimate(flops=0, transcendentals=0, bytes_accessed=10**6),
        name="order",
    )(*order_inputs, hold(wavefunction))
    right_send, _, _, _ = lax.optimization_barrier((right_env, wave_far, wave_near, diag_far))
    right_far = lax.ppermute(right_send, "rsec", swap)
    own, sib = pl.pallas_call(
        first_kernel,
        out_shape=(noted, field),
        in_specs=[whole_smem()] + [whole_vmem()] * 2,
        out_specs=(whole_vmem(),) * 2,
        compiler_params=params,
        name="first",
    )(order_meta, wave_near, wave_far)
    meta = pl.pallas_call(
        functools.partial(prep_kernel, lsec_count, bonds),
        out_shape=jax.ShapeDtypeStruct((LIST + bonds,), jnp.int32),
        in_specs=[in_hbm] * 4 + [anywhere],
        out_specs=whole_smem(),
        scratch_shapes=[pltpu.SMEM(x.shape, jnp.int32) for x in small_inputs]
        + [pltpu.SemaphoreType.DMA((4,))],
        compiler_params=params,
        name="prep",
    )(*small_inputs, own)
    near_waves = neighbours(own)
    raw = [(own, sib, *near_waves)]
    diag_own, diag_sib = pl.pallas_call(
        diag_kernel,
        out_shape=(field,) * 2,
        in_specs=[whole_smem()] + [whole_vmem()] * 2,
        out_specs=(whole_vmem(),) * 2,
        compiler_params=params,
        name="diag",
    )(meta, hold(precond_diag), diag_far)

    near_diags = neighbours(diag_own)

    def mpo_pair(value):
        if mpo_count != 2:
            value = lax.psum(value, "mpo")
            return value, jnp.zeros_like(value)
        return value, lax.ppermute(value, "mpo", swap)

    def lsec_parts(part):
        if lsec_count != 4:
            zero = jnp.zeros_like(part)
            return lax.psum(part, "lsec"), zero, zero, zero
        return (part, *[lax.ppermute(part, "lsec", [(i, i ^ x) for i in range(4)]) for x in (1, 2, 3)])

    def join(value, part, after):
        return pl.pallas_call(
            join_kernel,
            out_shape=noted,
            in_specs=[whole_vmem()] * 6 + [anywhere] * len(after),
            out_specs=whole_vmem(),
            compiler_params=params,
            name="join",
        )(*mpo_pair(value), *lsec_parts(part), *after)

    most = bonds - bonds // 5 if bonds % 5 == 0 else bonds
    packed = most * states + PACK
    lefts = pl.pallas_call(
        left_kernel,
        out_shape=(
            pltpu.VMEM((packed, SIDE), BF16),
            pltpu.VMEM((packed, SIDE), BF16),
            pltpu.VMEM((packed, 2 * (states - SIDE)), BF16),
        ),
        in_specs=[whole_smem(), anywhere],
        out_specs=(whole_vmem(),) * 3,
        scratch_shapes=[
            pltpu.VMEM((BUFFERS, states, states), F32),
            pltpu.SemaphoreType.DMA((states // TILE, BUFFERS)),
        ],
        compiler_params=params,
        cost_estimate=pl.CostEstimate(flops=0, transcendentals=0, bytes_accessed=bonds * states * states * 4),
        name="left",
    )(meta, hold(left_env))
    rights = pl.pallas_call(
        right_kernel,
        out_shape=(pltpu.VMEM((most, width, width), BF16),) * 2,
        in_specs=[whole_smem(), anywhere, anywhere],
        out_specs=(whole_vmem(),) * 2,
        scratch_shapes=[
            pltpu.VMEM((most, width, width), F32),
            pltpu.SemaphoreType.DMA((2, most)),
        ],
        compiler_params=params,
        cost_estimate=pl.CostEstimate(flops=0, transcendentals=0, bytes_accessed=bonds * width * width * 8),
        name="right",
    )(meta, hold(right_env), right_far)

    def dots(k, early, pack, values):
        operands = [early, *pack, *[group[0] for group in raw], *values]
        return pl.pallas_call(
            functools.partial(dots_kernel, k, mpo_count),
            out_shape=small,
            in_specs=[whole_smem()] + [whole_vmem()] * len(operands),
            out_specs=whole_vmem(),
            compiler_params=params,
            cost_estimate=pl.CostEstimate(
                flops=4 * states * width, transcendentals=0, bytes_accessed=4 * states * width
            ),
            name=f"dots{k}",
        )(meta, *operands)

    out = jax.ShapeDtypeStruct((MATVECS, sectors, states, columns), F32)
    known = jax.ShapeDtypeStruct((2, sectors, MATVECS - 1, states, columns), F32)

    def matvec(k, near, sizes, inputs):
        last = k + 1 == MATVECS
        vmem, scalars = whole_vmem(), whole_smem()
        scratch = [
            pltpu.VMEM((2, states, width), BF16),
            pltpu.VMEM((2, states, width), BF16),
            pltpu.VMEM((2 * (states - SIDE), width), BF16),
            pltpu.VMEM((packed + states, width), BF16),
            pltpu.VMEM((packed + states, width), BF16),
            pltpu.SMEM((bonds,), jnp.int32),
        ]
        fresh = [(field, vmem)] * (2 if k and (near or not last) else 0)
        if near:
            outs = [(field, vmem), (jax.ShapeDtypeStruct((1 + 2 * k, 8, width), F32), vmem)]
            outs += [(small, vmem)] * (1 if k else 0) + fresh
            scratch.append(pltpu.SMEM((8,), jnp.int32))
            if last:
                outs += [(known, vmem), (small, vmem), (out, anywhere), (out, anywhere)]
                scratch.append(pltpu.SemaphoreType.DMA((2, 2)))
        else:
            outs = ([(half_field, vmem)] * 2 if last else [(field, vmem)]) + fresh
            if last:
                scratch.append(pltpu.VMEM((states, width), F32))
            if not k:
                outs.append((jax.ShapeDtypeStruct((8,), jnp.int32), scalars))
        return pl.pallas_call(
            functools.partial(matvec_kernel, k, cells, near),
            out_shape=tuple(shape for shape, _ in outs),
            in_specs=[scalars] + [vmem] * 5 + [scalars] * len(sizes) + [vmem] * len(inputs),
            out_specs=tuple(spec for _, spec in outs),
            scratch_shapes=scratch,
            compiler_params=params,
            cost_estimate=pl.CostEstimate(
                flops=3 * bonds * states * width * (states + width),
                transcendentals=0,
                bytes_accessed=bonds * states * states,
            ),
            name=f"matvec{k}_{'near' if near else 'far'}",
        )(meta, *lefts, *rights, *sizes, *inputs)

    def flatten(groups):
        return [x for group in groups for x in group]

    def step_inputs(slots):
        return [*flatten(group[slots] for group in (*raw, *images)), *precond[slots]]

    near_slots, far_slots = slice(0, 2), slice(2, 4)
    totals, images, sizes, precond = [], [], [], []
    for k in range(MATVECS):
        last = k + 1 == MATVECS
        inputs = step_inputs(far_slots)
        partial, early, *fresh = matvec(k, True, [], [*totals, *step_inputs(near_slots)])
        pack, fresh = (fresh[:1], fresh[1:]) if k else ([], fresh)
        value, *fresh_far = matvec(k, False, sizes, [*pack, *inputs, partial])
        if k == 0:
            sizes = fresh_far
            precond = (diag_own, diag_sib, *near_diags)
        elif not last:
            raw.append((*fresh, *fresh_far))
        if last:
            break
        part = dots(k, early, pack, [value])
        value = join(value, part, [] if k else near_diags)
        beside = lax.ppermute(value, "rsec", swap)
        images.append((value, beside, *neighbours(value)))
        totals += mpo_pair(value[states:, :HALF] + beside[states:, :HALF])

    near, away = value, fresh_far[0]
    own, sib, known_blocks, state, *outs = fresh
    raw.append((own, sib))
    part = dots(MATVECS - 1, early, pack, [near, away])
    away, far_away = mpo_pair(away)
    sib_half = lax.ppermute(away + far_away, "rsec", swap)
    own_half = mpo_pair(near)
    one, two, three, four = lsec_parts(part)
    part = (one + two) + (three + four)
    total = mpo_pair(part + lax.ppermute(part, "rsec", swap))
    operands = [*total, state, known_blocks, own, sib, *own_half, sib_half]
    return pl.pallas_call(
        functools.partial(fill_kernel, cells),
        out_shape=(out, out, jax.ShapeDtypeStruct((MATVECS, MATVECS), F32)),
        in_specs=[whole_smem()] + [whole_vmem()] * len(operands) + [anywhere] * 2,
        out_specs=(anywhere, anywhere, whole_vmem()),
        scratch_shapes=[
            pltpu.VMEM((sectors, states, columns), F32),
            pltpu.VMEM((sectors, states, columns), F32),
            pltpu.SemaphoreType.DMA((2, 2)),
        ],
        input_output_aliases={1 + len(operands): 0, 2 + len(operands): 1},
        compiler_params=params,
        name="fill",
    )(meta, *operands, *outs)


def solution(mesh):
    placed = (
        P(("grp", "lsec"), None, "rsec"),
        P("mpo", ("grp", "lsec"), None, None),
        P("mpo", ("grp", "lsec"), "rsec", None),
        P(("grp", "lsec"), None, "rsec"),
        P("grp"),
        P("mpo", ("grp", "lsec")),
        P(("grp", "lsec")),
        P(("grp", "lsec")),
    )
    return jax.shard_map(
        per_device,
        mesh=mesh,
        in_specs=placed,
        out_specs=(
            P(None, ("grp", "lsec"), None, "rsec"),
            P(None, ("grp", "lsec"), None, "rsec"),
            P("grp", None),
        ),
        check_vma=False,
    )
```

```python
import functools

import jax
import jax.numpy as jnp
from jax import lax
from jax.experimental import pallas as pl
from jax.experimental.pallas import tpu as pltpu
from jax.sharding import PartitionSpec as P

EPSILON = 1e-06
MATVECS = 3
F32 = jnp.float32
BF16 = jnp.bfloat16
SIGMA, COUNT, ROWS, COLS, FIRST, SIB_ROWS, SIB_COLS, LIST = 0, 1, 2, 3, 4, 9, 10, 16
OWN, SIB, FIRST_PAIR, SECOND_PAIR = 0, 1, 2, 3
CHUNK = 64
TILE = 128
SIDE = 256
HALF = 128
NOTE = 8
PACK = 512
BUFFERS = 8


def whole_vmem():
    return pl.BlockSpec(memory_space=pltpu.VMEM)


def whole_smem():
    return pl.BlockSpec(memory_space=pltpu.SMEM)


def split(value):
    high = value.astype(BF16)
    return high, (value - high.astype(F32)).astype(BF16)


def orientation(down_ref, place):
    def step(i, flips):
        straight = (down_ref[2 * i] == down_ref[2 * i - 2]) | (
            down_ref[2 * i + 1] == down_ref[2 * i - 1]
        )
        return jnp.where(straight, flips, 1 - flips)

    return lax.fori_loop(1, place + 1, step, jnp.int32(0))


def live_mask(shape, row0, rows, cols):
    row_ids = row0 + lax.broadcasted_iota(jnp.int32, shape, 0)
    col_ids = lax.broadcasted_iota(jnp.int32, shape, 1)
    return (row_ids < rows) & (col_ids < cols)


def read_small(pairs, sems):
    copies = [pltpu.make_async_copy(*pair, sems.at[i]) for i, pair in enumerate(pairs)]
    for copy in copies:
        copy.start()
    for copy in copies:
        copy.wait()


def first_kernel(meta_ref, wave_ref, wave_far, own_ref, sib_ref):
    states, half = wave_ref.shape[1:]
    sigma, core = meta_ref[SIGMA], lax.axis_index("rsec")
    for out_ref, slot, rows, cols in (
        (own_ref, sigma, meta_ref[ROWS], meta_ref[COLS]),
        (sib_ref, 1 - sigma, meta_ref[SIB_ROWS], meta_ref[SIB_COLS]),
    ):

        def fill(i, carry, out_ref=out_ref, slot=slot, rows=rows, cols=cols):
            at = pl.ds(pl.multiple_of(i * CHUNK, CHUNK), CHUNK)
            for place, wave in ((core, wave_ref), (1 - core, wave_far)):
                lanes = pl.ds(pl.multiple_of(place * half, half), half)
                mask = live_mask((CHUNK, half), i * CHUNK, rows, cols - place * half)
                out_ref[at, lanes] = jnp.where(mask, wave[slot, at, :], 0.0)
            return carry

        lax.fori_loop(0, states // CHUNK, fill, 0)
    note = (NOTE, own_ref.shape[1])
    row_ids = lax.broadcasted_iota(jnp.int32, note, 0)
    own_ref[pl.ds(states, NOTE), :] = jnp.where(
        row_ids == 0, meta_ref[ROWS], meta_ref[COLS]
    ).astype(F32)


def prep_kernel(lsec_count, bonds, down_in, mask_in, left_in, right_in, wave_in, meta_ref, wave_ref,
                down_ref, mask_ref, left_size_ref, right_size_ref, sems, wave_sem):
    wave_copy = pltpu.make_async_copy(wave_in, wave_ref, wave_sem)
    wave_copy.start()
    read_small(
        ((down_in, down_ref), (mask_in, mask_ref), (left_in, left_size_ref), (right_in, right_size_ref)),
        sems,
    )
    place = lax.axis_index("lsec")
    core = lax.axis_index("rsec")
    first_kind = lax.rem(lax.axis_index("mpo") * bonds, 5)
    sigma = core ^ orientation(down_ref, place)
    own_down = down_ref[2 * place + sigma]
    sib_down = down_ref[2 * place + 1 - sigma]
    before = jnp.maximum(place - 1, 0)
    after = jnp.minimum(place + 1, lsec_count - 1)
    prev_down = down_ref[2 * before + (core ^ orientation(down_ref, before))]
    next_down = down_ref[2 * after + (core ^ orientation(down_ref, after))]
    has_prev = (place > 0) & (prev_down == own_down)
    has_next = (place < lsec_count - 1) & (next_down == own_down)
    odd = lax.rem(place, 2)
    has_lower = sib_down == own_down - 1
    has_upper = sib_down == own_down + 1

    def gather(slot, count):
        meta_ref[FIRST + slot] = count

        def step(bond, carry):
            count, kind = carry
            if slot == OWN:
                there = kind == 0
            elif slot == SIB:
                there = ((kind == 3) & has_lower) | ((kind == 4) & has_upper)
            else:
                lower = odd if slot == FIRST_PAIR else 1 - odd
                there = ((kind == 1) & has_prev & (lower == 1)) | (
                    (kind == 2) & has_next & (lower == 0)
                )
            there = there & (mask_ref[sigma, bond] > 0)

            @pl.when(there)
            def _():
                meta_ref[LIST + count] = bond * 4 + slot

            return count + there.astype(jnp.int32), jnp.where(kind == 4, 0, kind + 1)

        return lax.fori_loop(0, bonds, step, (count, first_kind))[0]

    count = jnp.int32(0)
    for slot in (OWN, SIB, FIRST_PAIR, SECOND_PAIR):
        count = gather(slot, count)
    meta_ref[FIRST + 4] = count
    rows, cols = left_size_ref[sigma], right_size_ref[sigma]
    meta_ref[SIGMA] = sigma
    meta_ref[COUNT] = count
    meta_ref[ROWS] = rows
    meta_ref[COLS] = cols
    meta_ref[SIB_ROWS] = left_size_ref[1 - sigma]
    meta_ref[SIB_COLS] = right_size_ref[1 - sigma]
    wave_copy.wait()


def diag_kernel(meta_ref, diag_ref, diag_far, diag_own, diag_sib):
    states, width = diag_own.shape
    half = width // 2
    sigma, core = meta_ref[SIGMA], lax.axis_index("rsec")
    near = pl.ds(pl.multiple_of(core * half, half), half)
    away = pl.ds(pl.multiple_of((1 - core) * half, half), half)
    for out_ref, slot in ((diag_own, sigma), (diag_sib, 1 - sigma)):

        def fill(i, carry, out_ref=out_ref, slot=slot):
            at = pl.ds(pl.multiple_of(i * CHUNK, CHUNK), CHUNK)
            out_ref[at, near] = diag_ref[slot, at, :]
            out_ref[at, away] = diag_far[slot, at, :]
            return carry

        lax.fori_loop(0, states // CHUNK, fill, 0)


def row(value, index):
    return value[index : index + 1, :]


def stack_rows(shape, rows):
    row_ids = lax.broadcasted_iota(jnp.int32, shape, 0)
    value = jnp.zeros(shape, F32)
    for index, entry in enumerate(rows):
        if entry is not None:
            value = jnp.where(row_ids == index, entry, value)
    return value


class Scalars:
    def __init__(self, totals, cells, state=None):
        self.proj = {}
        self.gram = {}
        self.inverse = []
        self.corr = []
        known = 0
        if state is not None:
            known = MATVECS - 1
            places = [(i, j) for i in range(known) for j in range(known)]
            for index, place in enumerate(places):
                self.proj[place] = row(state, index)
                self.gram[place] = row(state, len(places) + index)
        for k, total in enumerate(totals, known):
            value = (total[0][...] + total[1][...]) / cells
            size, inner = row(value, 0), row(value, 1)
            a = [row(value, 2 + j) for j in range(k)]
            e = [row(value, 4 + j) for j in range(k)]
            f = [row(value, 6 + j) for j in range(k)]
            length = size
            theta = inner
            for j in range(k):
                length = length - 2.0 * a[j] * a[j]
                theta = theta - a[j] * e[j] - a[j] * f[j]
            for i in range(k):
                for j in range(k):
                    length = length + a[i] * a[j] * self.gram[i, j]
                    theta = theta + a[i] * a[j] * self.proj[i, j]
            length = jnp.maximum(length, 0.0)
            square = length + EPSILON
            norm = jnp.sqrt(square)
            for j in range(k):
                up, down, both = e[j], f[j], a[j]
                for i in range(k):
                    up = up - a[i] * self.proj[j, i]
                    down = down - a[i] * self.proj[i, j]
                    both = both - a[i] * self.gram[i, j]
                self.proj[j, k] = up / norm
                self.proj[k, j] = down / norm
                self.gram[j, k] = self.gram[k, j] = both / norm
            self.proj[k, k] = theta / square
            self.gram[k, k] = length / square
            self.inverse.append(1.0 / norm)
            self.corr.append(a)

    def state(self, shape):
        known = MATVECS - 1
        places = [(i, j) for i in range(known) for j in range(known)]
        rows = [self.proj[place] for place in places] + [self.gram[place] for place in places]
        return stack_rows(shape, rows)

    def pack(self, k, shape):
        rows = [self.proj[k - 1, k - 1], *self.inverse[:k]]
        for a in self.corr[:k]:
            rows += a
        return stack_rows(shape, rows)

    @classmethod
    def unpack(cls, k, ref):
        numbers = cls([], 1.0)
        value = ref[...]
        numbers.theta = row(value, 0)[:, :1]
        numbers.inverse = [row(value, 1 + i) for i in range(k)]
        place = 1 + k
        for step in range(k):
            numbers.corr.append([row(value, place + j) for j in range(step)])
            place += step
        return numbers

    def basis(self, k, fields):
        done = []
        for step in range(k + 1):
            value = fields[step]
            for j in range(step):
                value = value - self.corr[step][j][:, :1] * done[j]
            done.append(value * self.inverse[step][:, :1])
        return done


def left_kernel(meta_ref, left_ref, left_high, left_low, left_tail, left_buf, sems):
    states = left_buf.shape[1]
    sigma, count, rows = meta_ref[SIGMA], meta_ref[COUNT], meta_ref[ROWS]
    stride = packed_rows(rows)

    def each(i, act):
        bond = (meta_ref[LIST + i] >> 2)
        at = i & (BUFFERS - 1)
        for p in range(states // TILE):
            part = pl.ds(p * TILE, TILE)

            @pl.when(rows > p * TILE)
            def _(part=part, p=p):
                act(
                    pltpu.make_async_copy(
                        left_ref.at[bond, sigma, part], left_buf.at[at, part], sems.at[p, at]
                    )
                )

    def start(i):
        @pl.when(i < count)
        def _():
            each(i, lambda copy: copy.start())

    for i in range(BUFFERS - 1):
        start(jnp.int32(i))

    def step(i, carry):
        at = i & (BUFFERS - 1)
        start(i + BUFFERS - 1)
        each(i, lambda copy: copy.wait())

        def chunk(t, inner):
            high, low = split(left_buf[at, pl.ds(pl.multiple_of(t * CHUNK, CHUNK), CHUNK), :])
            to = pl.ds(pl.multiple_of(i * stride + t * CHUNK, 16), CHUNK)
            left_high[to, :] = high[:, :SIDE]
            left_low[to, :] = low[:, :SIDE]
            left_tail[to, :] = jnp.concatenate([high[:, SIDE:], low[:, SIDE:]], axis=1)
            return inner

        lax.fori_loop(0, (rows + CHUNK - 1) // CHUNK, chunk, 0)
        return carry

    lax.fori_loop(0, count, step, 0)


def right_kernel(meta_ref, right_ref, far_ref, right_high, right_low, right_buf, sems):
    width, half = right_buf.shape[1], right_ref.shape[2]
    sigma, count = meta_ref[SIGMA], meta_ref[COUNT]
    core = lax.axis_index("rsec")
    thin = meta_ref[COLS] <= HALF

    def each(i, act):
        bond = (meta_ref[LIST + i] >> 2)
        for ref, place, sem in ((right_ref, core, 0), (far_ref, 1 - core, 1)):
            part = pl.ds(pl.multiple_of(place * half, half), half)

            @pl.when(jnp.logical_not(thin) | (place == 0))
            def _(ref=ref, part=part, sem=sem):
                act(
                    pltpu.make_async_copy(ref.at[bond, sigma], right_buf.at[i, part], sems.at[sem, i])
                )

    def start(i, carry):
        each(i, lambda copy: copy.start())
        return carry

    lax.fori_loop(0, count, start, 0)

    def step(i, carry):
        each(i, lambda copy: copy.wait())

        @pl.when(thin)
        def _():
            for first in range(0, HALF, CHUNK):
                high, low = split(right_buf[i, pl.ds(first, CHUNK), :])
                right_high[i, pl.ds(first, CHUNK), :] = high
                right_high[i, pl.ds(HALF + first, CHUNK), :] = low

        @pl.when(jnp.logical_not(thin))
        def _():
            for first in range(0, width, CHUNK):
                at = pl.ds(first, CHUNK)
                right_high[i, at, :], right_low[i, at, :] = split(right_buf[i, at, :])

        return carry

    lax.fori_loop(0, count, step, 0)


def packed_rows(rows):
    return ((rows + 15) // 16) * 16


def fold(value):
    return jnp.sum(value.reshape(CHUNK // 8, 8, value.shape[1]), axis=0)


def dots_kernel(k, mpo_count, meta_ref, early_ref, *refs):
    refs, small_ref = list(refs[:-1]), refs[-1]
    numbers = Scalars.unpack(k, refs.pop(0)) if k else None
    raw = [refs.pop(0) for _ in range(k + 1)]
    core = lax.axis_index("rsec")
    zero = jnp.zeros(early_ref.shape[1:], F32)

    def step(i, carry):
        at = pl.ds(pl.multiple_of(i * CHUNK, CHUNK), CHUNK)
        blocks = [ref[at, :] for ref in refs]
        if len(blocks) == 2:
            near, away = blocks
            first, second = jnp.where(core == 0, near, away), jnp.where(core == 0, away, near)
            value = jnp.concatenate([first, second], axis=1)
        else:
            value = blocks[0]
        basis = numbers.basis(k - 1, [ref[at, :] for ref in raw[:k]]) if k else []
        return tuple(c + fold(value * b) for c, b in zip(carry, [raw[k][at, :], *basis]))

    live = (meta_ref[ROWS] + CHUNK - 1) // CHUNK
    late = lax.fori_loop(0, live, step, (zero,) * (1 + k))

    def whole(value):
        return jnp.sum(jnp.sum(value, axis=1, keepdims=True), axis=0, keepdims=True)

    share = 1.0 / mpo_count
    entries = [whole(early_ref[0]) * share, whole(late[0])]
    for j in range(2):
        entries.append(whole(early_ref[1 + j]) * share if j < k else None)
    for j in range(2):
        entries.append(whole(late[1 + j]) if j < k else None)
    for j in range(2):
        entries.append(whole(early_ref[1 + k + j]) * share if j < k else None)
    small_ref[...] = stack_rows(small_ref.shape, entries)


def matvec_kernel(k, cells, near, *refs):
    refs = list(refs)
    slots = (OWN, SIB) if near else (FIRST_PAIR, SECOND_PAIR)
    base = slots[0]
    last = k + 1 == MATVECS
    meta_ref = refs.pop(0)
    left_high, left_low, left_tail = [refs.pop(0) for _ in range(3)]
    right_high, right_low = refs.pop(0), refs.pop(0)
    size_ref = refs.pop(0) if k and not near else None
    totals = [(refs.pop(0), refs.pop(0)) for _ in range(k)] if near else []
    pack_ref = refs.pop(0) if k and not near else None
    raw = [{slot: refs.pop(0) for slot in slots} for _ in range(max(k, 1))]
    images = [{slot: refs.pop(0) for slot in slots} for _ in range(k)]
    precond = {slot: refs.pop(0) for slot in slots} if k else {}
    partial_ref = None if near else refs.pop(0)
    halves = [refs.pop(0), refs.pop(0)] if last and not near else []
    out_ref = None if halves else refs.pop(0)
    early_ref = refs.pop(0) if near else None
    pack_ref = refs.pop(0) if k and near else pack_ref
    keep = near or not last
    new_refs = ({slot: refs.pop(0) for slot in slots} if keep else {}) if k else raw[0]
    if not k and not near:
        size_ref = refs.pop(0)
    if last and near:
        known_ref, state_ref, basis_out, images_out = [refs.pop(0) for _ in range(4)]
    high_ref, low_ref, tail_ref, mid_high, mid_low, order_ref = refs[:6]
    if near:
        size_ref = refs[6]
        sems = refs[7] if last else None
    elif last:
        out_ref = refs[6]
    states, width = out_ref.shape
    rows, cols = meta_ref[ROWS], meta_ref[COLS]
    first_bond, end_bond = meta_ref[FIRST + base], meta_ref[FIRST + base + 2]
    count = end_bond - first_bond
    stride = packed_rows(rows)

    core = lax.axis_index("rsec")
    if near:
        size_ref[2 * OWN], size_ref[2 * OWN + 1] = rows, cols
        size_ref[2 * SIB], size_ref[2 * SIB + 1] = meta_ref[SIB_ROWS], meta_ref[SIB_COLS]
    elif not k:
        for slot in slots:
            note = raw[0][slot][pl.ds(states, NOTE), :HALF]
            size_ref[2 * slot] = jnp.max(note[:1]).astype(jnp.int32)
            size_ref[2 * slot + 1] = jnp.max(note[1:]).astype(jnp.int32)
    def list_bonds(narrow):
        def step(i, place):
            hit = (size_ref[2 * (meta_ref[LIST + i] & 3) + 1] <= HALF) == narrow

            @pl.when(hit)
            def _():
                order_ref[place] = i

            return place + hit.astype(jnp.int32)

        return step

    thin_sources = lax.fori_loop(first_bond, end_bond, list_bonds(True), jnp.int32(0))
    lax.fori_loop(first_bond, end_bond, list_bonds(False), thin_sources)
    if k and near:
        numbers = Scalars(totals, cells)
        theta = numbers.proj[k - 1, k - 1][:, :1]
        pack_ref[...] = numbers.pack(k, pack_ref.shape)
    elif k:
        numbers = Scalars.unpack(k, pack_ref)
        theta = numbers.theta
    zero = jnp.zeros((8, width), F32)

    def prepare(slot, carry):
        def step(i, carry):
            at = pl.ds(pl.multiple_of(i * CHUNK, CHUNK), CHUNK)
            if k:
                basis = numbers.basis(k - 1, [r[slot][at, :] for r in raw])
                image = numbers.basis(k - 1, [r[slot][at, :] for r in images])
                value = (image[-1] - theta * basis[-1]) / jnp.maximum(
                    precond[slot][at, :] - theta, 1.0
                )
                if keep:
                    new_refs[slot][at, :] = value
                if last and near:
                    for which, group in enumerate((basis, image)):
                        for j, block in enumerate(group):
                            block = jnp.where(core == 0, block[:, :HALF], block[:, HALF:])
                            known_ref[which, slot, j, at, :] = block
            else:
                basis, image = [], []
                value = raw[0][slot][at, :]
            high, low = split(value)
            high_ref[slot - base, at, :] = high
            low_ref[slot - base, at, :] = low
            terms = [value * value]
            if slot == OWN:
                terms += [value * b for b in basis] + [value * g for g in image]
            return tuple(c + fold(t) for c, t in zip(carry, terms))

        def dead(i, inner):
            at = pl.ds(pl.multiple_of(i * CHUNK, CHUNK), CHUNK)
            high_ref[slot - base, at, :] = jnp.zeros((CHUNK, width), BF16)
            low_ref[slot - base, at, :] = jnp.zeros((CHUNK, width), BF16)
            if last and near:
                for which in range(2):
                    for j in range(k):
                        known_ref[which, slot, j, at, :] = jnp.zeros((CHUNK, HALF), F32)
            return inner

        live = (size_ref[2 * slot] + CHUNK - 1) // CHUNK
        lax.fori_loop(live, states // CHUNK, dead, 0)
        return lax.fori_loop(0, live, step, carry)

    def dot(a, b):
        return jnp.dot(a, b, preferred_element_type=F32)

    def dot_nt(a, b):
        return lax.dot_general(a, b, (((1,), (1,)), ((), ())), preferred_element_type=F32)

    twice = functools.partial(jnp.concatenate, axis=0)

    def first_stage(slot, deep, narrow):
        begin, end = meta_ref[FIRST + slot], meta_ref[FIRST + 1 + slot]
        at_slot = slot - base
        top, rest = pl.ds(0, SIDE), pl.ds(SIDE, states - SIDE)
        if narrow:
            high_ref[at_slot, :, HALF:] = low_ref[at_slot, :, :HALF]
        if deep:
            tail = high_ref[at_slot, rest, :]
            tail_ref[...] = twice([tail, tail])

        def step(t, carry):
            at = pl.ds(pl.multiple_of(begin * stride + t * PACK, 16), PACK)
            high, low = left_high[at, :], left_low[at, :]
            mid = dot(high, high_ref[at_slot, top, :])
            if deep:
                mid = mid + dot(left_tail[at, :], tail_ref[...])
            if narrow:
                mid = mid[:, :HALF] + mid[:, HALF:] + dot(low, high_ref[at_slot, top, :HALF])
                mid_high[at, :] = jnp.concatenate(split(mid), axis=1)
            else:
                mid = mid + dot(low, high_ref[at_slot, top, :]) + dot(high, low_ref[at_slot, top, :])
                if deep:
                    mid = mid + dot(left_tail[at, : states - SIDE], low_ref[at_slot, rest, :])
                mid_high[at, :], mid_low[at, :] = split(mid)
            return carry

        lax.fori_loop(0, ((end - begin) * stride + PACK - 1) // PACK, step, 0)

    def both(test, action):
        pl.when(test)(lambda: action(True))
        pl.when(jnp.logical_not(test))(lambda: action(False))

    if near:
        own = prepare(OWN, (zero,) * (1 + 2 * k))
        prepare(SIB, (zero,))
    else:
        for slot in slots:
            used = meta_ref[FIRST + 1 + slot] > meta_ref[FIRST + slot]
            pl.when(used)(lambda slot=slot: (prepare(slot, (zero,)), None)[1])

    def from_slot(slot, carry):
        both(
            size_ref[2 * slot] > SIDE,
            lambda deep: both(
                size_ref[2 * slot + 1] <= HALF, lambda narrow: first_stage(slot, deep, narrow)
            ),
        )
        return carry

    lax.fori_loop(base, base + 2, from_slot, 0)
    if last and near:
        sigma = meta_ref[SIGMA]
        outputs = [
            pltpu.make_async_copy(
                known_ref.at[which, slot],
                out.at[pl.ds(0, MATVECS - 1), sigma if slot == OWN else 1 - sigma],
                sems.at[which, slot],
            )
            for which, out in enumerate((basis_out, images_out))
            for slot in (OWN, SIB)
        ]
        for copy in outputs:
            copy.start()
        state_ref[...] = numbers.state(state_ref.shape)

    def clear(i, carry):
        at = pl.ds(pl.multiple_of(i * CHUNK, CHUNK), CHUNK)
        out_ref[at, :] = jnp.zeros((CHUNK, width), F32) if near else partial_ref[at, :]
        return carry

    lax.fori_loop(0, states // CHUNK, clear, 0)
    zeros_at = mid_high.shape[0] - states
    for ref in (mid_high, mid_low):
        ref[pl.ds(zeros_at, states), :] = jnp.zeros((states, width), BF16)

    def second_stage(size, thin):
        to = pl.ds(0, size)

        def product(i, real, narrow):
            bond = order_ref[i]
            at = pl.ds(pl.multiple_of(jnp.where(real, bond * stride, zeros_at), 16), size)
            high = mid_high[at, :]
            lanes = pl.ds(0, HALF if narrow else width)
            right = right_high[bond, :, lanes]
            right_rest = None if thin else right_low[bond, :, lanes]
            if narrow:
                value = dot_nt(high, jnp.concatenate([right, right], axis=1))
                if not thin:
                    value = value + dot_nt(high[:, :HALF], right_rest)
            else:
                value = dot_nt(high, right)
                if not thin:
                    value = value + dot_nt(high, right_rest) + dot_nt(mid_low[at, :], right)
            if thin:
                value = value[:, :HALF] + value[:, HALF:]
                if not narrow:
                    value = value + dot_nt(mid_low[at, :], right[:HALF, :])
            return value

        def run(begin, end, narrow):
            def pair(p, carry):
                one = begin + 2 * p
                real = one + 1 < end
                two = jnp.where(real, one + 1, one)
                value = product(one, True, narrow) + product(two, real, narrow)
                if thin:
                    out_ref[to, :HALF] += value
                else:
                    out_ref[to, :] += value
                return carry

            lax.fori_loop(0, (end - begin + 1) // 2, pair, 0)

        run(0, thin_sources, True)
        run(thin_sources, count, False)

    for size in range(TILE, states + 1, TILE):
        pl.when((rows <= size) & (rows > size - TILE))(
            lambda size=size: both(cols <= HALF, functools.partial(second_stage, size))
        )

    if near:
        for index, entry in enumerate(own):
            early_ref[index] = entry
        if last:
            for copy in outputs:
                copy.wait()
        return

    def finish(i, carry):
        at = pl.ds(pl.multiple_of(i * CHUNK, CHUNK), CHUNK)
        mask = live_mask((CHUNK, width), i * CHUNK, rows, cols)
        value = jnp.where(mask, out_ref[at, :], 0.0)
        if last:
            halves[0][at, :] = jnp.where(core == 0, value[:, :HALF], value[:, HALF:])
            halves[1][at, :] = jnp.where(core == 0, value[:, HALF:], value[:, :HALF])
        else:
            out_ref[at, :] = value
        return carry

    lax.fori_loop(0, (rows + CHUNK - 1) // CHUNK, finish, 0)


def join_kernel(a_ref, b_ref, s0, s1, s2, s3, *refs):
    out_ref = refs[-1]
    states = a_ref.shape[0]
    total = (s0[...] + s1[...]) + (s2[...] + s3[...])
    out_ref[pl.ds(states, NOTE), :HALF] = total
    out_ref[pl.ds(states, NOTE), HALF:] = total

    def step(i, carry):
        at = pl.ds(pl.multiple_of(i * CHUNK, CHUNK), CHUNK)
        out_ref[at, :] = a_ref[at, :] + b_ref[at, :]
        return carry

    lax.fori_loop(0, states // CHUNK, step, 0)


def fill_kernel(cells, meta_ref, *refs):
    total, state_ref = refs[:2], refs[2]
    known_ref, raw_own, raw_sib, *parts = refs[3:9]
    basis_out, images_out, projected_ref, basis_buf, images_buf, sems = refs[-6:]
    last = MATVECS - 1
    sigma = meta_ref[SIGMA]
    numbers = Scalars([total], cells, state_ref[...])
    core = lax.axis_index("rsec")
    states, half = basis_buf.shape[1:]
    lanes = pl.ds(pl.multiple_of(core * half, half), half)
    inverse = numbers.inverse[0][:, :1]
    corr = [a[:, :1] for a in numbers.corr[0]]
    copies = []
    chunks = states // CHUNK
    for slot, raw, image, rows in (
        (OWN, raw_own, parts[:2], meta_ref[ROWS]),
        (SIB, raw_sib, parts[2:], meta_ref[SIB_ROWS]),
    ):

        def step(i, carry, slot=slot, raw=raw, image=image):
            at = pl.ds(pl.multiple_of(i * CHUNK, CHUNK), CHUNK)
            fields = (raw[at, lanes], sum(ref[at, :] for ref in image[1:]) + image[0][at, :])
            for which, buf in enumerate((basis_buf, images_buf)):
                value = fields[which]
                for j in range(last):
                    value = value - corr[j] * known_ref[which, slot, j, at, :]
                buf[slot, at, :] = value * inverse
            return carry

        def dead(i, carry, slot=slot):
            at = pl.ds(pl.multiple_of(i * CHUNK, CHUNK), CHUNK)
            for buf in (basis_buf, images_buf):
                buf[slot, at, :] = jnp.zeros((CHUNK, half), F32)
            return carry

        live = (rows + CHUNK - 1) // CHUNK
        lax.fori_loop(0, live, step, 0)
        lax.fori_loop(live, chunks, dead, 0)
        sector = sigma if slot == OWN else 1 - sigma
        for which, (buf, out) in enumerate(((basis_buf, basis_out), (images_buf, images_out))):
            copies.append(
                pltpu.make_async_copy(buf.at[slot], out.at[last, sector], sems.at[which, slot])
            )
            copies[-1].start()
    shape = projected_ref.shape
    row_ids = lax.broadcasted_iota(jnp.int32, shape, 0)
    col_ids = lax.broadcasted_iota(jnp.int32, shape, 1)
    value = jnp.zeros(shape, F32)
    for i in range(MATVECS):
        for j in range(MATVECS):
            value = jnp.where((row_ids == i) & (col_ids == j), numbers.proj[i, j][:, :1], value)
    projected_ref[...] = value
    for copy in copies:
        copy.wait()


def per_device(
    wavefunction, left_env, right_env, precond_diag, down_charge, bond_mask, left_size, right_size
):
    sectors, states, columns = wavefunction.shape
    bonds = left_env.shape[0]
    lsec_count = lax.axis_size("lsec")
    mpo_count = lax.axis_size("mpo")
    assert sectors == 2 and lax.axis_size("rsec") == 2
    width = 2 * columns
    cells = float(lsec_count * sectors * states * width)
    field = jax.ShapeDtypeStruct((states, width), F32)
    noted = jax.ShapeDtypeStruct((states + NOTE, width), F32)
    half_field = jax.ShapeDtypeStruct((states, columns), F32)
    small = jax.ShapeDtypeStruct((8, 128), F32)
    params = pltpu.CompilerParams(vmem_limit_bytes=18 * 2**20)

    swap = [(0, 1), (1, 0)]
    first_pairs = [(i, i ^ 1) for i in range(lsec_count) if i ^ 1 < lsec_count]
    second_pairs = [(i, j) for a in range(1, lsec_count - 1, 2) for i, j in ((a, a + 1), (a + 1, a))]
    anywhere = pl.BlockSpec(memory_space=pl.ANY)
    in_hbm = pl.BlockSpec(memory_space=pltpu.HBM)

    def hold(value):
        return pltpu.with_memory_space_constraint(value, pltpu.HBM)

    def neighbours(value):
        return lax.ppermute(value, "lsec", first_pairs), lax.ppermute(value, "lsec", second_pairs)

    wave_far = lax.ppermute(wavefunction, "rsec", swap)
    diag_far = lax.ppermute(precond_diag, "rsec", swap)
    mask_rows = bond_mask.T
    small_inputs = [down_charge, mask_rows, left_size, right_size]
    meta, wave_near = pl.pallas_call(
        functools.partial(prep_kernel, lsec_count, bonds),
        out_shape=(
            jax.ShapeDtypeStruct((LIST + bonds,), jnp.int32),
            jax.ShapeDtypeStruct(wavefunction.shape, F32),
        ),
        in_specs=[in_hbm] * 5,
        out_specs=(whole_smem(), whole_vmem()),
        scratch_shapes=[pltpu.SMEM(x.shape, jnp.int32) for x in small_inputs]
        + [pltpu.SemaphoreType.DMA((4,)), pltpu.SemaphoreType.DMA],
        compiler_params=params,
        cost_estimate=pl.CostEstimate(flops=0, transcendentals=0, bytes_accessed=10**6),
        name="prep",
    )(*[hold(x) for x in small_inputs], hold(wavefunction))
    right_send, _, _, _ = lax.optimization_barrier((right_env, wave_far, wave_near, diag_far))
    right_far = lax.ppermute(right_send, "rsec", swap)
    own, sib = pl.pallas_call(
        first_kernel,
        out_shape=(noted, field),
        in_specs=[whole_smem()] + [whole_vmem()] * 2,
        out_specs=(whole_vmem(),) * 2,
        compiler_params=params,
        name="first",
    )(meta, wave_near, wave_far)
    near_waves = neighbours(own)
    raw = [(own, sib, *near_waves)]
    diag_own, diag_sib = pl.pallas_call(
        diag_kernel,
        out_shape=(field,) * 2,
        in_specs=[whole_smem()] + [whole_vmem()] * 2,
        out_specs=(whole_vmem(),) * 2,
        compiler_params=params,
        name="diag",
    )(meta, hold(precond_diag), diag_far)

    near_diags = neighbours(diag_own)

    def mpo_pair(value):
        if mpo_count != 2:
            value = lax.psum(value, "mpo")
            return value, jnp.zeros_like(value)
        return value, lax.ppermute(value, "mpo", swap)

    def lsec_parts(part):
        if lsec_count != 4:
            zero = jnp.zeros_like(part)
            return lax.psum(part, "lsec"), zero, zero, zero
        return (part, *[lax.ppermute(part, "lsec", [(i, i ^ x) for i in range(4)]) for x in (1, 2, 3)])

    def join(value, part, after):
        return pl.pallas_call(
            join_kernel,
            out_shape=noted,
            in_specs=[whole_vmem()] * 6 + [anywhere] * len(after),
            out_specs=whole_vmem(),
            compiler_params=params,
            name="join",
        )(*mpo_pair(value), *lsec_parts(part), *after)

    most = bonds - bonds // 5 if bonds % 5 == 0 else bonds
    packed = most * states + PACK
    lefts = pl.pallas_call(
        left_kernel,
        out_shape=(
            pltpu.VMEM((packed, SIDE), BF16),
            pltpu.VMEM((packed, SIDE), BF16),
            pltpu.VMEM((packed, 2 * (states - SIDE)), BF16),
        ),
        in_specs=[whole_smem(), anywhere],
        out_specs=(whole_vmem(),) * 3,
        scratch_shapes=[
            pltpu.VMEM((BUFFERS, states, states), F32),
            pltpu.SemaphoreType.DMA((states // TILE, BUFFERS)),
        ],
        compiler_params=params,
        cost_estimate=pl.CostEstimate(flops=0, transcendentals=0, bytes_accessed=bonds * states * states * 4),
        name="left",
    )(meta, hold(left_env))
    rights = pl.pallas_call(
        right_kernel,
        out_shape=(pltpu.VMEM((most, width, width), BF16),) * 2,
        in_specs=[whole_smem(), anywhere, anywhere],
        out_specs=(whole_vmem(),) * 2,
        scratch_shapes=[
            pltpu.VMEM((most, width, width), F32),
            pltpu.SemaphoreType.DMA((2, most)),
        ],
        compiler_params=params,
        cost_estimate=pl.CostEstimate(flops=0, transcendentals=0, bytes_accessed=bonds * width * width * 8),
        name="right",
    )(meta, hold(right_env), right_far)

    def dots(k, early, pack, values):
        operands = [early, *pack, *[group[0] for group in raw], *values]
        return pl.pallas_call(
            functools.partial(dots_kernel, k, mpo_count),
            out_shape=small,
            in_specs=[whole_smem()] + [whole_vmem()] * len(operands),
            out_specs=whole_vmem(),
            compiler_params=params,
            cost_estimate=pl.CostEstimate(
                flops=4 * states * width, transcendentals=0, bytes_accessed=4 * states * width
            ),
            name=f"dots{k}",
        )(meta, *operands)

    out = jax.ShapeDtypeStruct((MATVECS, sectors, states, columns), F32)
    known = jax.ShapeDtypeStruct((2, sectors, MATVECS - 1, states, columns), F32)

    def matvec(k, near, sizes, inputs):
        last = k + 1 == MATVECS
        vmem, scalars = whole_vmem(), whole_smem()
        scratch = [
            pltpu.VMEM((2, states, width), BF16),
            pltpu.VMEM((2, states, width), BF16),
            pltpu.VMEM((2 * (states - SIDE), width), BF16),
            pltpu.VMEM((packed + states, width), BF16),
            pltpu.VMEM((packed + states, width), BF16),
            pltpu.SMEM((bonds,), jnp.int32),
        ]
        fresh = [(field, vmem)] * (2 if k and (near or not last) else 0)
        if near:
            outs = [(field, vmem), (jax.ShapeDtypeStruct((1 + 2 * k, 8, width), F32), vmem)]
            outs += [(small, vmem)] * (1 if k else 0) + fresh
            scratch.append(pltpu.SMEM((8,), jnp.int32))
            if last:
                outs += [(known, vmem), (small, vmem), (out, anywhere), (out, anywhere)]
                scratch.append(pltpu.SemaphoreType.DMA((2, 2)))
        else:
            outs = ([(half_field, vmem)] * 2 if last else [(field, vmem)]) + fresh
            if last:
                scratch.append(pltpu.VMEM((states, width), F32))
            if not k:
                outs.append((jax.ShapeDtypeStruct((8,), jnp.int32), scalars))
        return pl.pallas_call(
            functools.partial(matvec_kernel, k, cells, near),
            out_shape=tuple(shape for shape, _ in outs),
            in_specs=[scalars] + [vmem] * 5 + [scalars] * len(sizes) + [vmem] * len(inputs),
            out_specs=tuple(spec for _, spec in outs),
            scratch_shapes=scratch,
            compiler_params=params,
            cost_estimate=pl.CostEstimate(
                flops=3 * bonds * states * width * (states + width),
                transcendentals=0,
                bytes_accessed=bonds * states * states,
            ),
            name=f"matvec{k}_{'near' if near else 'far'}",
        )(meta, *lefts, *rights, *sizes, *inputs)

    def flatten(groups):
        return [x for group in groups for x in group]

    def step_inputs(slots):
        return [*flatten(group[slots] for group in (*raw, *images)), *precond[slots]]

    near_slots, far_slots = slice(0, 2), slice(2, 4)
    totals, images, sizes, precond = [], [], [], []
    for k in range(MATVECS):
        last = k + 1 == MATVECS
        inputs = step_inputs(far_slots)
        partial, early, *fresh = matvec(k, True, [], [*totals, *step_inputs(near_slots)])
        pack, fresh = (fresh[:1], fresh[1:]) if k else ([], fresh)
        value, *fresh_far = matvec(k, False, sizes, [*pack, *inputs, partial])
        if k == 0:
            sizes = fresh_far
            precond = (diag_own, diag_sib, *near_diags)
        elif not last:
            raw.append((*fresh, *fresh_far))
        if last:
            break
        part = dots(k, early, pack, [value])
        value = join(value, part, [] if k else near_diags)
        beside = lax.ppermute(value, "rsec", swap)
        images.append((value, beside, *neighbours(value)))
        totals += mpo_pair(value[states:, :HALF] + beside[states:, :HALF])

    near, away = value, fresh_far[0]
    own, sib, known_blocks, state, *outs = fresh
    raw.append((own, sib))
    part = dots(MATVECS - 1, early, pack, [near, away])
    away, far_away = mpo_pair(away)
    sib_half = lax.ppermute(away + far_away, "rsec", swap)
    own_half = mpo_pair(near)
    one, two, three, four = lsec_parts(part)
    part = (one + two) + (three + four)
    total = mpo_pair(part + lax.ppermute(part, "rsec", swap))
    operands = [*total, state, known_blocks, own, sib, *own_half, sib_half]
    return pl.pallas_call(
        functools.partial(fill_kernel, cells),
        out_shape=(out, out, jax.ShapeDtypeStruct((MATVECS, MATVECS), F32)),
        in_specs=[whole_smem()] + [whole_vmem()] * len(operands) + [anywhere] * 2,
        out_specs=(anywhere, anywhere, whole_vmem()),
        scratch_shapes=[
            pltpu.VMEM((sectors, states, columns), F32),
            pltpu.VMEM((sectors, states, columns), F32),
            pltpu.SemaphoreType.DMA((2, 2)),
        ],
        input_output_aliases={1 + len(operands): 0, 2 + len(operands): 1},
        compiler_params=params,
        name="fill",
    )(meta, *operands, *outs)


def solution(mesh):
    placed = (
        P(("grp", "lsec"), None, "rsec"),
        P("mpo", ("grp", "lsec"), None, None),
        P("mpo", ("grp", "lsec"), "rsec", None),
        P(("grp", "lsec"), None, "rsec"),
        P("grp"),
        P("mpo", ("grp", "lsec")),
        P(("grp", "lsec")),
        P(("grp", "lsec")),
    )
    return jax.shard_map(
        per_device,
        mesh=mesh,
        in_specs=placed,
        out_specs=(
            P(None, ("grp", "lsec"), None, "rsec"),
            P(None, ("grp", "lsec"), None, "rsec"),
            P("grp", None),
        ),
        check_vma=False,
    )
```
